32 devices in a mesh: harm: 4 (over x, core), space: 2 (over y), samp: 4 (over z).
Axes of the slice: x: 2, y: 2, z: 4, core: 2. Of those that a mesh axis runs over, the one named last changes fastest.
Arguments:
- coeffs: bfloat16 [32, 4096], P(('harm', 'samp'), 'space'), may hold values from -1.5 to 1.5
- curl_tiles: bfloat16 [32, 4, 128, 384], P('space'), may hold values from -0.25 to 0.25
- pattern: int32 [32, 4], P('space'), may hold values from 0 to 17, as said below
- region_ids: int32 [32], P('space'), may hold values from 0 to 3
- material_law: float32 [3, 4], replicated, may hold values from 0.3 to 3
- source: float32 [32, 4096], P(('harm', 'samp'), 'space'), may hold values from -6 to 6
Outputs:
- residual: float32 [32, 4096], P(('harm', 'samp'), 'space')
The draws below stay inside these ranges and needn't reach their ends.
Inputs may be any that keep to these rules, and one draw needn't show every extreme that they name: `pattern`: entries index a space shard's window of 18 edge tiles: 0 is the last tile of the previous shard, 17 the first of the next, cyclically over the sector; the first entry of every row is the element tile's own position in its shard plus one.
All inputs are finite; a program needn't handle non-finite values.
Results may differ from the reference program's by a relative error of at most 0.0015.
Values may be sent and summed in bfloat16 or wider, within the bound.
No kernel may reach another device: no remote copies, remote signals or barrier semaphores. Data moves between devices by JAX's collectives and lax.ppermute only.
A program may use at most 64 MiB of HBM per device.

```python
import math
import jax
import jax.numpy as jnp
from jax import lax

SAMPLES = 64
TILE = 128
LINKS = 4
REGIONS = 4
TILES = 16
PARTS_SIZE = 32
ELEM_TILES = 32
EDGES = 4096


def draw_pattern(key, part):
    owners = jnp.arange(ELEM_TILES, dtype=jnp.int32) % TILES
    nearby = owners[:, None] + jax.random.randint(jax.random.fold_in(key, 11), (ELEM_TILES, 2), 0, 3).astype(jnp.int32)
    distant = jax.random.randint(jax.random.fold_in(key, 23), (ELEM_TILES, LINKS - 3), 0, TILES + 2).astype(jnp.int32)
    return jnp.concatenate([owners[:, None] + 1, nearby, distant], axis=1).astype(jnp.int32)


def touch_ends(values, key, smallest, high):
    spot = [jax.random.randint(jax.random.fold_in(key, axis), (), 0, length) for axis, length in enumerate(values.shape)]
    widest = values.shape.index(max(values.shape))
    neighbour = spot[:widest] + [(spot[widest] + 1) % values.shape[widest]] + spot[widest + 1:]
    return values.at[tuple(spot)].set(smallest).at[tuple(neighbour)].set(high)


def shard_levels(rng, extent, shards, least, top_value):
    level = 1.0
    for axis_at, parts in shards:
        heights = jax.random.uniform(jax.random.fold_in(jax.random.fold_in(rng, 6), axis_at), (parts,), jnp.float32, least / len(shards), top_value / len(shards))
        level = level * jnp.repeat(jnp.exp(heights), extent[axis_at] // parts).reshape((-1,) + (1,) * (len(extent) - 1 - axis_at))
    return level


def noise(own_key, extent, width, bound, cuts=(), kind=jnp.bfloat16):
    level = shard_levels(own_key, extent, cuts, -0.22, 0.18) if cuts else 1.0
    entries = jax.random.normal(own_key, extent, jnp.float32) * width * level
    return jnp.minimum(jnp.maximum(entries, -bound), bound).astype(kind)


def setup_inputs(seed: int = 0) -> dict:
    key_list = jax.random.split(jax.random.key(seed), 7)
    coeffs = noise(key_list[0], (PARTS_SIZE, EDGES), 0.25, 1.5, ((0, 16), (1, 2)))
    curl_tiles = noise(key_list[1], (ELEM_TILES, LINKS, TILE, 3 * TILE), (LINKS * TILE) ** -0.5, 0.25, ((0, 2),))
    pattern = draw_pattern(jax.random.fold_in(key_list[6], 71), 0)
    region_ids = touch_ends(jax.random.randint(key_list[3], (ELEM_TILES,), 0, REGIONS), jax.random.fold_in(key_list[3], 1), 0, REGIONS - 1).astype(jnp.int32)
    material_law = jnp.clip(jnp.exp(jax.random.uniform(key_list[4], (3, REGIONS), jnp.float32, math.log(0.3), math.log(3.0))), 0.3, 3.0)
    source = noise(key_list[5], (PARTS_SIZE, EDGES), 1.0, 6.0, ((0, 16), (1, 2)), jnp.float32)
    return dict(coeffs=coeffs, curl_tiles=curl_tiles, pattern=pattern, region_ids=region_ids, material_law=material_law, source=source)


def transform_table():
    sample_ids = jnp.arange(SAMPLES, dtype=jnp.int32)[:, None]
    part_ids = jnp.arange(PARTS_SIZE, dtype=jnp.int32)[None, :]
    orders = 2 * (part_ids // 2) + 1
    phase = ((orders * sample_ids) % SAMPLES).astype(jnp.float32) * (2.0 * math.pi / SAMPLES)
    return jnp.where(part_ids % 2 == 0, jnp.cos(phase), jnp.sin(phase))


def reference(coeffs, curl_tiles, pattern, region_ids, material_law, source):
    transform = transform_table()
    shard_of = jnp.arange(ELEM_TILES, dtype=jnp.int32) // TILES
    edge_index = ((shard_of[:, None] * TILES + pattern - 1) % ELEM_TILES).astype(jnp.int32)
    coeff_tiles = coeffs.reshape(PARTS_SIZE, ELEM_TILES, TILE)
    picked = coeff_tiles[:, edge_index.reshape(-1)].reshape(PARTS_SIZE, ELEM_TILES, LINKS, TILE)
    curl_wide = curl_tiles.astype(jnp.float32)
    flux_rows = jnp.einsum("pgki,gkij->pgj", picked.astype(jnp.float32), curl_wide, precision=lax.Precision.HIGHEST)
    flux_rows = flux_rows.reshape(PARTS_SIZE, ELEM_TILES * 3 * TILE)
    density = jnp.dot(transform, flux_rows, precision=lax.Precision.HIGHEST, preferred_element_type=jnp.float32)
    density = density.reshape(SAMPLES, ELEM_TILES, 3, TILE)
    magnitude = jnp.sum(density * density, axis=2)
    region_hits = (region_ids[:, None] == jnp.arange(REGIONS, dtype=jnp.int32)[None, :]).astype(jnp.float32)
    region_law = jnp.dot(region_hits, material_law.T, precision=lax.Precision.HIGHEST, preferred_element_type=jnp.float32)
    base_value = region_law[:, 0][None, :, None]
    knee_value = region_law[:, 1][None, :, None]
    rise_value = region_law[:, 2][None, :, None]
    reluct = base_value + rise_value * magnitude / (magnitude + knee_value)
    field = (reluct[:, :, None, :] * density).reshape(SAMPLES, ELEM_TILES * 3 * TILE)
    harm_field = (2.0 / SAMPLES) * jnp.dot(transform.T, field, precision=lax.Precision.HIGHEST, preferred_element_type=jnp.float32)
    field_half = harm_field.astype(jnp.bfloat16).reshape(PARTS_SIZE, ELEM_TILES, 3 * TILE)
    contrib = jnp.einsum("pgj,gkij->pgki", field_half.astype(jnp.float32), curl_wide, precision=lax.Precision.HIGHEST)
    accumulated = jnp.zeros((PARTS_SIZE, ELEM_TILES, TILE), jnp.float32)
    accumulated = accumulated.at[:, edge_index.reshape(-1)].add(contrib.reshape(PARTS_SIZE, ELEM_TILES * LINKS, TILE))
    return accumulated.reshape(PARTS_SIZE, EDGES) - source
```

```python
import math

import jax
import jax.numpy as jnp
import ml_dtypes
import numpy as np
from jax import lax
from jax.experimental import pallas as pl
from jax.experimental.pallas import tpu as pltpu
from jax.sharding import PartitionSpec as P

SAMPLES = 64
HALF = SAMPLES // 2
GROUP = ("harm", "samp")


def half_table(parts):
    sample_ids = np.arange(HALF)[:, None]
    part_ids = np.arange(parts)[None, :]
    phase = ((2 * (part_ids // 2) + 1) * sample_ids % SAMPLES) * (2.0 * math.pi / SAMPLES)
    return np.where(part_ids % 2 == 0, np.cos(phase), np.sin(phase))


def bf16_pieces(table):
    rest = table
    pieces = []
    for _ in range(3):
        piece = rest.astype(ml_dtypes.bfloat16)
        pieces.append(piece)
        rest = rest - piece.astype(np.float64)
    return np.concatenate(pieces, axis=1)


def ring(axis, by):
    count = lax.axis_size(axis)
    return [(i, (i + by) % count) for i in range(count)]


def exchange(to_left, to_right, axis):
    if lax.axis_size(axis) == 2:
        width = to_left.shape[1]
        both = lax.ppermute(jnp.concatenate([to_left, to_right], axis=1), axis, ring(axis, 1))
        return both[:, :width], both[:, width:]
    return lax.ppermute(to_left, axis, ring(axis, -1)), lax.ppermute(to_right, axis, ring(axis, 1))


def shard_kernel(
    pattern, region_ids, law, window, pieces, table, curl, source, out, halo, timed, sums
):
    tile_count, links, tile, comps = curl.shape
    parts_here = out.shape[0]
    rank = lax.axis_index(GROUP)
    stacked = jnp.concatenate([window[...]] * 3, axis=0)
    samples = jnp.dot(pieces[...], stacked, preferred_element_type=jnp.float32)
    high = samples.astype(jnp.bfloat16)
    timed[:HALF, :] = high
    timed[HALF:, :] = (samples - high.astype(jnp.float32)).astype(jnp.bfloat16)
    sums[...] = jnp.zeros_like(sums)
    lanes = lax.broadcasted_iota(jnp.int32, table.shape, 1)
    columns = [
        jnp.sum(
            jnp.where(lanes == rank * parts_here + part, table[...], 0.0), axis=1, keepdims=True
        )
        for part in range(parts_here)
    ]
    for elem in range(tile_count):
        places = [pattern[elem, link] for link in range(links)]
        picked = jnp.concatenate(
            [timed[:, pl.ds(pl.multiple_of(place * tile, tile), tile)] for place in places], axis=1
        )
        blocks = curl[elem].reshape(links * tile, comps)
        split = jnp.dot(picked, blocks, preferred_element_type=jnp.float32)
        density = split[:HALF] + split[HALF:]
        comp = [density[:, c * tile : (c + 1) * tile] for c in range(comps // tile)]
        square = comp[0] * comp[0]
        for c in comp[1:]:
            square = square + c * c
        region = region_ids[elem]
        reluct = law[0, region] + law[2, region] * square / (square + law[1, region])
        field = jnp.concatenate([reluct * c for c in comp], axis=1)
        projected = jnp.concatenate(
            [jnp.sum(column * field, axis=0, keepdims=True) for column in columns], axis=0
        )
        projected = (projected * (4.0 / SAMPLES)).astype(jnp.bfloat16)
        contrib = lax.dot_general(
            projected, blocks, (((1,), (1,)), ((), ())), preferred_element_type=jnp.float32
        )
        for link, place in enumerate(places):
            sums[place] += contrib[:, link * tile : (link + 1) * tile]
    for w in range(tile_count):
        at = slice(w * tile, (w + 1) * tile)
        out[:, at] = sums[w + 1] - source[:, at]
    halo[:, :tile] = sums[0]
    halo[:, tile:] = sums[tile_count + 1]


def per_device(coeffs, curl_tiles, pattern, region_ids, material_law, source):
    parts_here = coeffs.shape[0]
    tile_count, links, tile, comps = curl_tiles.shape
    parts = parts_here * lax.axis_size(GROUP)
    high, low = exchange(coeffs[:, :tile], coeffs[:, -tile:], "space")
    window = lax.all_gather(
        jnp.concatenate([low, coeffs, high], axis=1), GROUP, axis=0, tiled=True
    )
    table = half_table(parts)
    vmem, smem = pl.BlockSpec(memory_space=pltpu.VMEM), pl.BlockSpec(memory_space=pltpu.SMEM)
    own, halo = pl.pallas_call(
        shard_kernel,
        out_shape=(
            jax.ShapeDtypeStruct(source.shape, jnp.float32),
            jax.ShapeDtypeStruct((parts_here, 2 * tile), jnp.float32),
        ),
        in_specs=[smem] * 3 + [vmem] * 5,
        out_specs=(vmem, vmem),
        scratch_shapes=[
            pltpu.VMEM((SAMPLES, (tile_count + 2) * tile), jnp.bfloat16),
            pltpu.VMEM((tile_count + 2, parts_here, tile), jnp.float32),
        ],
        compiler_params=pltpu.CompilerParams(vmem_limit_bytes=32 * 1024 * 1024),
        cost_estimate=pl.CostEstimate(
            flops=4 * SAMPLES * tile_count * links * tile * comps,
            bytes_accessed=2 * curl_tiles.size,
            transcendentals=0,
        ),
        name="shard_residual",
    )(
        pattern,
        region_ids,
        material_law,
        window,
        jnp.asarray(bf16_pieces(table)),
        jnp.asarray(table.astype(np.float32)),
        curl_tiles,
        source,
    )
    from_right, from_left = exchange(halo[:, :tile], halo[:, tile:], "space")
    return own.at[:, :tile].add(from_left).at[:, -tile:].add(from_right)


def solution(mesh):
    placed = (
        P(GROUP, "space"),
        P("space", None, None, None),
        P("space", None),
        P("space"),
        P(),
        P(GROUP, "space"),
    )
    return jax.shard_map(
        per_device,
        mesh=mesh,
        in_specs=placed,
        out_specs=P(GROUP, "space"),
        check_vma=False,
    )
```

```python
import math

import jax
import jax.numpy as jnp
import ml_dtypes
import numpy as np
from jax import lax
from jax.experimental import pallas as pl
from jax.experimental.pallas import tpu as pltpu
from jax.sharding import PartitionSpec as P

SAMPLES = 64
HALF = SAMPLES // 2
GROUP = ("harm", "samp")


def half_table(parts):
    sample_ids = np.arange(HALF)[:, None]
    part_ids = np.arange(parts)[None, :]
    phase = ((2 * (part_ids // 2) + 1) * sample_ids % SAMPLES) * (2.0 * math.pi / SAMPLES)
    return np.where(part_ids % 2 == 0, np.cos(phase), np.sin(phase))


def bf16_pieces(table):
    rest = table
    pieces = []
    for _ in range(3):
        piece = rest.astype(ml_dtypes.bfloat16)
        pieces.append(piece)
        rest = rest - piece.astype(np.float64)
    return np.concatenate(pieces, axis=1)


def ring(axis, by):
    count = lax.axis_size(axis)
    return [(i, (i + by) % count) for i in range(count)]


def exchange(to_left, to_right, axis):
    if lax.axis_size(axis) == 2:
        width = to_left.shape[1]
        both = lax.ppermute(jnp.concatenate([to_left, to_right], axis=1), axis, ring(axis, 1))
        return both[:, :width], both[:, width:]
    return lax.ppermute(to_left, axis, ring(axis, -1)), lax.ppermute(to_right, axis, ring(axis, 1))


def shard_kernel(
    window,
    pattern_hbm,
    region_hbm,
    law_hbm,
    pieces_hbm,
    table_hbm,
    source_hbm,
    curl_hbm,
    out,
    halo,
    pattern,
    region_ids,
    law,
    pieces,
    table,
    source,
    curl,
    timed,
    sums,
    small_sems,
    curl_sems,
):
    tile_count, links, tile, comps = curl.shape
    parts_here = out.shape[0]
    fetched = [
        (pieces_hbm, pieces),
        (table_hbm, table),
        (pattern_hbm, pattern),
        (region_hbm, region_ids),
        (law_hbm, law),
        (source_hbm, source),
    ]
    small = [
        pltpu.make_async_copy(src, dst, small_sems.at[i]) for i, (src, dst) in enumerate(fetched)
    ]
    blocks_in = [
        pltpu.make_async_copy(curl_hbm.at[elem], curl.at[elem], curl_sems.at[elem])
        for elem in range(tile_count)
    ]
    for copy in small + blocks_in:
        copy.start()
    rank = lax.axis_index(GROUP)
    sums[...] = jnp.zeros_like(sums)
    small[0].wait()
    stacked = jnp.concatenate([window[...]] * 3, axis=0)
    samples = jnp.dot(pieces[...], stacked, preferred_element_type=jnp.float32)
    high = samples.astype(jnp.bfloat16)
    timed[:HALF, :] = high
    timed[HALF:, :] = (samples - high.astype(jnp.float32)).astype(jnp.bfloat16)
    for copy in small[1:]:
        copy.wait()
    lanes = lax.broadcasted_iota(jnp.int32, table.shape, 1)
    columns = [
        jnp.sum(
            jnp.where(lanes == rank * parts_here + part, table[...], 0.0), axis=1, keepdims=True
        )
        for part in range(parts_here)
    ]
    for elem in range(tile_count):
        places = [pattern[link, elem] for link in range(links)]
        picked = jnp.concatenate(
            [timed[:, pl.ds(pl.multiple_of(place * tile, tile), tile)] for place in places], axis=1
        )
        blocks_in[elem].wait()
        blocks = curl[elem].reshape(links * tile, comps)
        split = jnp.dot(picked, blocks, preferred_element_type=jnp.float32)
        density = split[:HALF] + split[HALF:]
        comp = [density[:, c * tile : (c + 1) * tile] for c in range(comps // tile)]
        square = comp[0] * comp[0]
        for c in comp[1:]:
            square = square + c * c
        region = region_ids[elem]
        reluct = law[0, region] + law[2, region] * square / (square + law[1, region])
        field = jnp.concatenate([reluct * c for c in comp], axis=1)
        projected = jnp.concatenate(
            [jnp.sum(column * field, axis=0, keepdims=True) for column in columns], axis=0
        )
        projected = (projected * (4.0 / SAMPLES)).astype(jnp.bfloat16)
        contrib = lax.dot_general(
            projected, blocks, (((1,), (1,)), ((), ())), preferred_element_type=jnp.float32
        )
        for link, place in enumerate(places):
            sums[place] += contrib[:, link * tile : (link + 1) * tile]
    for w in range(tile_count):
        at = slice(w * tile, (w + 1) * tile)
        out[:, at] = sums[w + 1] - source[:, at]
    halo[:, :tile] = sums[0]
    halo[:, tile:] = sums[tile_count + 1]


def halo_kernel(own, from_right, from_left, out):
    tile = from_left.shape[1]
    out[...] = own[...]
    out[:, :tile] += from_left[...]
    out[:, -tile:] += from_right[...]


def per_device(coeffs, curl_tiles, pattern, region_ids, material_law, source):
    parts_here = coeffs.shape[0]
    tile_count, links, tile, comps = curl_tiles.shape
    group_size = lax.axis_size(GROUP)
    parts = parts_here * group_size
    high, low = exchange(coeffs[:, :tile], coeffs[:, -tile:], "space")
    block = jnp.concatenate([low, coeffs, high], axis=1)
    window = lax.all_to_all(
        jnp.broadcast_to(block[None], (group_size,) + block.shape), GROUP, 0, 0
    ).reshape(parts, block.shape[1])
    table = half_table(parts)
    pieces = bf16_pieces(table)
    vmem, hbm = pl.BlockSpec(memory_space=pltpu.VMEM), pl.BlockSpec(memory_space=pltpu.HBM)
    own, halo = pl.pallas_call(
        shard_kernel,
        out_shape=(
            jax.ShapeDtypeStruct(source.shape, jnp.float32),
            jax.ShapeDtypeStruct((parts_here, 2 * tile), jnp.float32),
        ),
        in_specs=[vmem] + [hbm] * 7,
        out_specs=(vmem, vmem),
        scratch_shapes=[
            pltpu.SMEM((links, tile_count), jnp.int32),
            pltpu.SMEM(region_ids.shape, jnp.int32),
            pltpu.SMEM(material_law.shape, jnp.float32),
            pltpu.VMEM(pieces.shape, jnp.bfloat16),
            pltpu.VMEM(table.shape, jnp.float32),
            pltpu.VMEM(source.shape, jnp.float32),
            pltpu.VMEM(curl_tiles.shape, jnp.bfloat16),
            pltpu.VMEM((SAMPLES, (tile_count + 2) * tile), jnp.bfloat16),
            pltpu.VMEM((tile_count + 2, parts_here, tile), jnp.float32),
            pltpu.SemaphoreType.DMA((6,)),
            pltpu.SemaphoreType.DMA((tile_count,)),
        ],
        compiler_params=pltpu.CompilerParams(vmem_limit_bytes=32 * 1024 * 1024),
        cost_estimate=pl.CostEstimate(
            flops=4 * SAMPLES * tile_count * links * tile * comps,
            bytes_accessed=2 * curl_tiles.size,
            transcendentals=0,
        ),
        name="shard_residual",
    )(
        window,
        *[
            pltpu.with_memory_space_constraint(operand, pltpu.HBM)
            for operand in (
                pattern.T,
                region_ids,
                material_law,
                jnp.asarray(pieces),
                jnp.asarray(table.astype(np.float32)),
                source,
                curl_tiles,
            )
        ],
    )
    from_right, from_left = exchange(halo[:, :tile], halo[:, tile:], "space")
    return pl.pallas_call(
        halo_kernel,
        out_shape=jax.ShapeDtypeStruct(source.shape, jnp.float32),
        in_specs=[vmem] * 3,
        out_specs=vmem,
        name="halo_sum",
    )(own, from_right, from_left)


def solution(mesh):
    placed = (
        P(GROUP, "space"),
        P("space", None, None, None),
        P("space", None),
        P("space"),
        P(),
        P(GROUP, "space"),
    )
    return jax.shard_map(
        per_device,
        mesh=mesh,
        in_specs=placed,
        out_specs=P(GROUP, "space"),
        check_vma=False,
    )
```

```python
import math

import jax
import jax.numpy as jnp
import ml_dtypes
import numpy as np
from jax import lax
from jax.experimental import pallas as pl
from jax.experimental.pallas import tpu as pltpu
from jax.sharding import PartitionSpec as P

SAMPLES = 64
HALF = SAMPLES // 2
GROUP = ("harm", "samp")


def half_table(parts):
    sample_ids = np.arange(HALF)[:, None]
    part_ids = np.arange(parts)[None, :]
    phase = ((2 * (part_ids // 2) + 1) * sample_ids % SAMPLES) * (2.0 * math.pi / SAMPLES)
    return np.where(part_ids % 2 == 0, np.cos(phase), np.sin(phase))


def bf16_pieces(table):
    rest = table
    pieces = []
    for _ in range(3):
        piece = rest.astype(ml_dtypes.bfloat16)
        pieces.append(piece)
        rest = rest - piece.astype(np.float64)
    return np.concatenate(pieces, axis=-1)


def arrival_order(harm, samp, parts_here):
    order = np.empty((harm * samp, harm * samp * parts_here), np.int32)
    for h in range(harm):
        for s in range(samp):
            ranks = [
                (h - j) % harm * samp + (s - k) % samp for j in range(harm) for k in range(samp)
            ]
            order[h * samp + s] = (
                np.array(ranks)[:, None] * parts_here + np.arange(parts_here)
            ).reshape(-1)
    return order


def shifted(array, axes, by):
    sizes = [lax.axis_size(axis) for axis in axes]
    places = list(np.ndindex(*sizes))
    pairs = []
    for place in places:
        target = tuple((p + step) % size for p, step, size in zip(place, by, sizes))
        pairs.append((places.index(place), places.index(target)))
    return lax.ppermute(array, axes, pairs)


def from_neighbours(edges, samp_step):
    axes, tile = ("space", "samp"), edges.shape[1] // 2
    if lax.axis_size("space") == 2:
        return shifted(edges, axes, (1, samp_step))
    return jnp.concatenate(
        [
            shifted(edges[:, :tile], axes, (-1, samp_step)),
            shifted(edges[:, tile:], axes, (1, samp_step)),
        ],
        axis=1,
    )


def fetch_kernel(curl_hbm, curl, sem):
    copy = pltpu.make_async_copy(curl_hbm.at[: curl.shape[0]], curl, sem)
    copy.start()
    copy.wait()


def shard_kernel(
    window,
    first_curl,
    curl_hbm,
    pattern_hbm,
    region_hbm,
    law_hbm,
    pieces_hbm,
    table_hbm,
    source_hbm,
    out,
    halo,
    pattern,
    region_ids,
    law,
    pieces,
    table,
    source,
    later_curl,
    timed,
    sums,
    small_sems,
    curl_sem,
):
    tile_count, links, tile, comps = curl_hbm.shape
    early = first_curl.shape[0]
    parts_here = out.shape[0]
    rank = lax.axis_index(GROUP)
    fetched = [
        (pieces_hbm.at[rank], pieces),
        (table_hbm.at[rank], table),
        (pattern_hbm, pattern),
        (region_hbm, region_ids),
        (law_hbm, law),
        (source_hbm, source),
    ]
    small = [
        pltpu.make_async_copy(src, dst, small_sems.at[i]) for i, (src, dst) in enumerate(fetched)
    ]
    rest = pltpu.make_async_copy(curl_hbm.at[early:], later_curl, curl_sem)
    for copy in small + [rest]:
        copy.start()
    sums[...] = jnp.zeros_like(sums)
    for copy in small:
        copy.wait()
    stacked = jnp.concatenate([window[...]] * 3, axis=0)
    samples = jnp.dot(pieces[...], stacked, preferred_element_type=jnp.float32)
    high = samples.astype(jnp.bfloat16)
    timed[:HALF, :] = high
    timed[HALF:, :] = (samples - high.astype(jnp.float32)).astype(jnp.bfloat16)
    columns = [
        jnp.broadcast_to(table[:, part : part + 1], (HALF, comps)) for part in range(parts_here)
    ]
    for elem in range(tile_count):
        places = [pattern[link, elem] for link in range(links)]
        picked = jnp.concatenate(
            [timed[:, pl.ds(pl.multiple_of(place * tile, tile), tile)] for place in places], axis=1
        )
        if elem == early:
            rest.wait()
        curl = first_curl[elem] if elem < early else later_curl[elem - early]
        blocks = curl.reshape(links * tile, comps)
        split = jnp.dot(picked, blocks, preferred_element_type=jnp.float32)
        density = split[:HALF] + split[HALF:]
        comp = [density[:, c * tile : (c + 1) * tile] for c in range(comps // tile)]
        square = comp[0] * comp[0]
        for c in comp[1:]:
            square = square + c * c
        region = region_ids[elem]
        reluct = law[0, region] + law[2, region] * square / (square + law[1, region])
        field = jnp.concatenate([reluct * c for c in comp], axis=1)
        projected = jnp.concatenate(
            [jnp.sum(column * field, axis=0, keepdims=True) for column in columns], axis=0
        )
        projected = (projected * (4.0 / SAMPLES)).astype(jnp.bfloat16)
        contrib = lax.dot_general(
            projected, blocks, (((1,), (1,)), ((), ())), preferred_element_type=jnp.float32
        )
        for link, place in enumerate(places):
            sums[place] += contrib[:, link * tile : (link + 1) * tile]
    for w in range(tile_count):
        at = slice(w * tile, (w + 1) * tile)
        out[:, at] = sums[w + 1] - source[:, at]
    halo[:, :tile] = sums[0]
    halo[:, tile:] = sums[tile_count + 1]


def halo_kernel(own, received, out):
    tile = received.shape[1] // 2
    out[...] = own[...]
    out[:, :tile] += received[:, tile:]
    out[:, -tile:] += received[:, :tile]


def per_device(coeffs, curl_tiles, pattern, region_ids, material_law, source):
    parts_here = coeffs.shape[0]
    tile_count, links, tile, comps = curl_tiles.shape
    harm, samp = lax.axis_size("harm"), lax.axis_size("samp")
    parts = parts_here * harm * samp
    order = arrival_order(harm, samp, parts_here)
    table = half_table(parts)[:, order].transpose(1, 0, 2)
    pieces = bf16_pieces(table)
    own_columns = table[:, :, :parts_here].astype(np.float32)
    vmem, hbm = pl.BlockSpec(memory_space=pltpu.VMEM), pl.BlockSpec(memory_space=pltpu.HBM)

    edges = jnp.concatenate([coeffs[:, :tile], coeffs[:, -tile:]], axis=1)
    blocks = []
    for k in range(samp):
        beside = from_neighbours(edges, k)
        block = shifted(coeffs, ("samp",), (k,)) if k else coeffs
        blocks.append(jnp.concatenate([beside[:, tile:], block, beside[:, :tile]], axis=1))
    curl_hbm = pltpu.with_memory_space_constraint(curl_tiles, pltpu.HBM)
    early = 3 * tile_count // 8
    first_curl = pl.pallas_call(
        fetch_kernel,
        out_shape=pltpu.VMEM((early,) + curl_tiles.shape[1:], curl_tiles.dtype),
        in_specs=[hbm],
        out_specs=vmem,
        scratch_shapes=[pltpu.SemaphoreType.DMA],
        compiler_params=pltpu.CompilerParams(vmem_limit_bytes=16 * 1024 * 1024),
        cost_estimate=pl.CostEstimate(
            flops=0, bytes_accessed=4 * early * links * tile * comps, transcendentals=0
        ),
        name="fetch_curl",
    )(curl_hbm)
    near = jnp.stack(blocks)
    far = [near] + [shifted(near, ("harm",), (j,)) for j in range(1, harm)]
    window = jnp.concatenate(far, axis=0).reshape(parts, near.shape[-1])
    own, halo = pl.pallas_call(
        shard_kernel,
        out_shape=(
            pltpu.VMEM(source.shape, jnp.float32),
            pltpu.VMEM((parts_here, 2 * tile), jnp.float32),
        ),
        in_specs=[vmem] * 2 + [hbm] * 7,
        out_specs=(vmem, vmem),
        scratch_shapes=[
            pltpu.SMEM((links, tile_count), jnp.int32),
            pltpu.SMEM(region_ids.shape, jnp.int32),
            pltpu.SMEM(material_law.shape, jnp.float32),
            pltpu.VMEM(pieces.shape[1:], jnp.bfloat16),
            pltpu.VMEM(own_columns.shape[1:], jnp.float32),
            pltpu.VMEM(source.shape, jnp.float32),
            pltpu.VMEM((tile_count - early,) + curl_tiles.shape[1:], curl_tiles.dtype),
            pltpu.VMEM((SAMPLES, (tile_count + 2) * tile), jnp.bfloat16),
            pltpu.VMEM((tile_count + 2, parts_here, tile), jnp.float32),
            pltpu.SemaphoreType.DMA((6,)),
            pltpu.SemaphoreType.DMA,
        ],
        compiler_params=pltpu.CompilerParams(vmem_limit_bytes=32 * 1024 * 1024),
        cost_estimate=pl.CostEstimate(
            flops=4 * SAMPLES * tile_count * links * tile * comps,
            bytes_accessed=2 * curl_tiles.size,
            transcendentals=0,
        ),
        name="shard_residual",
    )(
        window,
        pltpu.with_memory_space_constraint(first_curl, pltpu.VMEM),
        curl_hbm,
        *[
            pltpu.with_memory_space_constraint(operand, pltpu.HBM)
            for operand in (
                pattern.T,
                region_ids,
                material_law,
                jnp.asarray(pieces),
                jnp.asarray(own_columns),
                source,
            )
        ],
    )
    return pl.pallas_call(
        halo_kernel,
        out_shape=jax.ShapeDtypeStruct(source.shape, jnp.float32),
        in_specs=[vmem] * 2,
        out_specs=vmem,
        compiler_params=pltpu.CompilerParams(vmem_limit_bytes=16 * 1024 * 1024),
        name="halo_sum",
    )(pltpu.with_memory_space_constraint(own, pltpu.VMEM), from_neighbours(halo, 0))


def solution(mesh):
    placed = (
        P(GROUP, "space"),
        P("space", None, None, None),
        P("space", None),
        P("space"),
        P(),
        P(GROUP, "space"),
    )
    return jax.shard_map(
        per_device,
        mesh=mesh,
        in_specs=placed,
        out_specs=P(GROUP, "space"),
        check_vma=False,
    )
```

```python
import math

import jax
import jax.numpy as jnp
import ml_dtypes
import numpy as np
from jax import lax
from jax.experimental import pallas as pl
from jax.experimental.pallas import tpu as pltpu
from jax.sharding import PartitionSpec as P

SAMPLES = 64
HALF = SAMPLES // 2
GROUP = ("harm", "samp")


def half_table(parts):
    sample_ids = np.arange(HALF)[:, None]
    part_ids = np.arange(parts)[None, :]
    phase = ((2 * (part_ids // 2) + 1) * sample_ids % SAMPLES) * (2.0 * math.pi / SAMPLES)
    return np.where(part_ids % 2 == 0, np.cos(phase), np.sin(phase))


def bf16_pieces(table):
    rest = table
    pieces = []
    for _ in range(3):
        piece = rest.astype(ml_dtypes.bfloat16)
        pieces.append(piece)
        rest = rest - piece.astype(np.float64)
    return np.concatenate(pieces, axis=-1)


def shifted(array, axis, by):
    count = lax.axis_size(axis)
    return lax.ppermute(array, axis, [(i, (i + by) % count) for i in range(count)])


def from_neighbours(edges, axis):
    tile = edges.shape[1] // 2
    if lax.axis_size(axis) == 2:
        return shifted(edges, axis, 1)
    return jnp.concatenate(
        [shifted(edges[:, :tile], axis, -1), shifted(edges[:, tile:], axis, 1)], axis=1
    )


def gathered(block, axis):
    copies = jnp.broadcast_to(block[None], (lax.axis_size(axis),) + block.shape)
    return lax.all_to_all(copies, axis, 0, 0)


def fetch_kernel(curl_hbm, curl, sem):
    copy = pltpu.make_async_copy(curl_hbm.at[: curl.shape[0]], curl, sem)
    copy.start()
    copy.wait()


def shard_kernel(
    window,
    first_curl,
    curl_hbm,
    pattern_hbm,
    region_hbm,
    law_hbm,
    pieces_hbm,
    table_hbm,
    source_hbm,
    out,
    halo,
    pattern,
    region_ids,
    law,
    pieces,
    table,
    source,
    later_curl,
    timed,
    sums,
    small_sems,
    curl_sem,
):
    tile_count, links, tile, comps = curl_hbm.shape
    early = first_curl.shape[0]
    parts_here = out.shape[0]
    rank = lax.axis_index(GROUP)
    fetched = [
        (pieces_hbm, pieces),
        (table_hbm.at[rank], table),
        (pattern_hbm, pattern),
        (region_hbm, region_ids),
        (law_hbm, law),
        (source_hbm, source),
    ]
    small = [
        pltpu.make_async_copy(src, dst, small_sems.at[i]) for i, (src, dst) in enumerate(fetched)
    ]
    rest = pltpu.make_async_copy(curl_hbm.at[early:], later_curl, curl_sem)
    for copy in small + [rest]:
        copy.start()
    sums[...] = jnp.zeros_like(sums)
    for copy in small:
        copy.wait()
    stacked = jnp.concatenate([window[...]] * 3, axis=0)
    samples = jnp.dot(pieces[...], stacked, preferred_element_type=jnp.float32)
    high = samples.astype(jnp.bfloat16)
    timed[:HALF, :] = high
    timed[HALF:, :] = (samples - high.astype(jnp.float32)).astype(jnp.bfloat16)
    columns = [
        jnp.broadcast_to(table[:, part : part + 1], (HALF, comps)) for part in range(parts_here)
    ]
    for elem in range(tile_count):
        places = [pattern[link, elem] for link in range(links)]
        picked = jnp.concatenate(
            [timed[:, pl.ds(pl.multiple_of(place * tile, tile), tile)] for place in places], axis=1
        )
        if elem == early:
            rest.wait()
        curl = first_curl[elem] if elem < early else later_curl[elem - early]
        blocks = curl.reshape(links * tile, comps)
        split = jnp.dot(picked, blocks, preferred_element_type=jnp.float32)
        density = split[:HALF] + split[HALF:]
        comp = [density[:, c * tile : (c + 1) * tile] for c in range(comps // tile)]
        square = comp[0] * comp[0]
        for c in comp[1:]:
            square = square + c * c
        region = region_ids[elem]
        reluct = law[0, region] + law[2, region] * square / (square + law[1, region])
        field = jnp.concatenate([reluct * c for c in comp], axis=1)
        projected = jnp.concatenate(
            [jnp.sum(column * field, axis=0, keepdims=True) for column in columns], axis=0
        )
        projected = (projected * (4.0 / SAMPLES)).astype(jnp.bfloat16)
        contrib = lax.dot_general(
            projected, blocks, (((1,), (1,)), ((), ())), preferred_element_type=jnp.float32
        )
        for link, place in enumerate(places):
            sums[place] += contrib[:, link * tile : (link + 1) * tile]
    for w in range(tile_count):
        at = slice(w * tile, (w + 1) * tile)
        out[:, at] = sums[w + 1] - source[:, at]
    halo[:, :tile] = sums[0]
    halo[:, tile:] = sums[tile_count + 1]


def halo_kernel(own, received, out):
    tile = received.shape[1] // 2
    out[...] = own[...]
    out[:, :tile] += received[:, tile:]
    out[:, -tile:] += received[:, :tile]


def per_device(coeffs, curl_tiles, pattern, region_ids, material_law, source):
    parts_here = coeffs.shape[0]
    tile_count, links, tile, comps = curl_tiles.shape
    group_size = lax.axis_size(GROUP)
    parts = parts_here * group_size
    table = half_table(parts)
    pieces = bf16_pieces(table)
    own_columns = table.reshape(HALF, group_size, parts_here).transpose(1, 0, 2)
    vmem, hbm = pl.BlockSpec(memory_space=pltpu.VMEM), pl.BlockSpec(memory_space=pltpu.HBM)

    edges = jnp.concatenate([coeffs[:, :tile], coeffs[:, -tile:]], axis=1)
    beside = from_neighbours(edges, "space")
    curl_hbm = pltpu.with_memory_space_constraint(curl_tiles, pltpu.HBM)
    early = 3 * tile_count // 8
    first_curl = pl.pallas_call(
        fetch_kernel,
        out_shape=pltpu.VMEM((early,) + curl_tiles.shape[1:], curl_tiles.dtype),
        in_specs=[hbm],
        out_specs=vmem,
        scratch_shapes=[pltpu.SemaphoreType.DMA],
        compiler_params=pltpu.CompilerParams(vmem_limit_bytes=16 * 1024 * 1024),
        cost_estimate=pl.CostEstimate(
            flops=0, bytes_accessed=4 * early * links * tile * comps, transcendentals=0
        ),
        name="fetch_curl",
    )(curl_hbm)
    block = jnp.concatenate([beside[:, tile:], coeffs, beside[:, :tile]], axis=1)
    window = gathered(gathered(block, "samp"), "harm").reshape(parts, block.shape[1])
    own, halo = pl.pallas_call(
        shard_kernel,
        out_shape=(
            pltpu.VMEM(source.shape, jnp.float32),
            pltpu.VMEM((parts_here, 2 * tile), jnp.float32),
        ),
        in_specs=[vmem] * 2 + [hbm] * 7,
        out_specs=(vmem, vmem),
        scratch_shapes=[
            pltpu.SMEM((links, tile_count), jnp.int32),
            pltpu.SMEM(region_ids.shape, jnp.int32),
            pltpu.SMEM(material_law.shape, jnp.float32),
            pltpu.VMEM(pieces.shape, jnp.bfloat16),
            pltpu.VMEM(own_columns.shape[1:], jnp.float32),
            pltpu.VMEM(source.shape, jnp.float32),
            pltpu.VMEM((tile_count - early,) + curl_tiles.shape[1:], curl_tiles.dtype),
            pltpu.VMEM((SAMPLES, (tile_count + 2) * tile), jnp.bfloat16),
            pltpu.VMEM((tile_count + 2, parts_here, tile), jnp.float32),
            pltpu.SemaphoreType.DMA((6,)),
            pltpu.SemaphoreType.DMA,
        ],
        compiler_params=pltpu.CompilerParams(vmem_limit_bytes=32 * 1024 * 1024),
        cost_estimate=pl.CostEstimate(
            flops=4 * SAMPLES * tile_count * links * tile * comps,
            bytes_accessed=2 * curl_tiles.size,
            transcendentals=0,
        ),
        name="shard_residual",
    )(
        window,
        pltpu.with_memory_space_constraint(first_curl, pltpu.VMEM),
        curl_hbm,
        *[
            pltpu.with_memory_space_constraint(operand, pltpu.HBM)
            for operand in (
                pattern.T,
                region_ids,
                material_law,
                jnp.asarray(pieces),
                jnp.asarray(own_columns.astype(np.float32)),
                source,
            )
        ],
    )
    return pl.pallas_call(
        halo_kernel,
        out_shape=jax.ShapeDtypeStruct(source.shape, jnp.float32),
        in_specs=[vmem] * 2,
        out_specs=vmem,
        compiler_params=pltpu.CompilerParams(vmem_limit_bytes=16 * 1024 * 1024),
        name="halo_sum",
    )(pltpu.with_memory_space_constraint(own, pltpu.VMEM), from_neighbours(halo, "space"))


def solution(mesh):
    placed = (
        P(GROUP, "space"),
        P("space", None, None, None),
        P("space", None),
        P("space"),
        P(),
        P(GROUP, "space"),
    )
    return jax.shard_map(
        per_device,
        mesh=mesh,
        in_specs=placed,
        out_specs=P(GROUP, "space"),
        check_vma=False,
    )
```

```python
import math

import jax
import jax.numpy as jnp
import ml_dtypes
import numpy as np
from jax import lax
from jax.experimental import pallas as pl
from jax.experimental.pallas import tpu as pltpu
from jax.sharding import PartitionSpec as P

SAMPLES = 64
HALF = SAMPLES // 2
GROUP = ("harm", "samp")


def half_table(parts):
    sample_ids = np.arange(HALF)[:, None]
    part_ids = np.arange(parts)[None, :]
    phase = ((2 * (part_ids // 2) + 1) * sample_ids % SAMPLES) * (2.0 * math.pi / SAMPLES)
    return np.where(part_ids % 2 == 0, np.cos(phase), np.sin(phase))


def bf16_pieces(table):
    rest = table
    pieces = []
    for _ in range(3):
        piece = rest.astype(ml_dtypes.bfloat16)
        pieces.append(piece)
        rest = rest - piece.astype(np.float64)
    return np.concatenate(pieces, axis=-1)


def partner(index, step, size):
    return index ^ step if size & (size - 1) == 0 else (index + step) % size


def sender(index, step, size):
    return index ^ step if size & (size - 1) == 0 else (index - step) % size


def send(array, axis, step, along=None, by=0):
    size = lax.axis_size(axis)
    if along is None:
        return lax.ppermute(array, axis, [(i, partner(i, step, size)) for i in range(size)])
    count = lax.axis_size(along)
    pairs = [
        (i * count + n, partner(i, step, size) * count + (n + by) % count)
        for i in range(size)
        for n in range(count)
    ]
    return lax.ppermute(array, (axis, along), pairs)


def from_neighbours(edges, axis, step):
    tile = edges.shape[-1] // 2
    if lax.axis_size("space") == 2:
        return send(edges, axis, step, "space", 1)
    return jnp.concatenate(
        [
            send(edges[..., :tile], axis, step, "space", -1),
            send(edges[..., tile:], axis, step, "space", 1),
        ],
        axis=-1,
    )


def arrival_order(harm, samp, parts_here):
    ranks = [
        [
            sender(h, j, harm) * samp + sender(s, k, samp)
            for j in range(harm)
            for k in range(samp)
        ]
        for h in range(harm)
        for s in range(samp)
    ]
    rows = np.array(ranks)[:, :, None] * parts_here + np.arange(parts_here)
    return rows.reshape(harm * samp, -1)


def fetch_kernel(curl_hbm, curl, sem):
    copy = pltpu.make_async_copy(curl_hbm.at[: curl.shape[0]], curl, sem)
    copy.start()
    copy.wait()


def shard_kernel(
    window,
    first_curl,
    curl_hbm,
    pattern_hbm,
    region_hbm,
    law_hbm,
    pieces_hbm,
    table_hbm,
    source_hbm,
    out,
    halo,
    pattern,
    region_ids,
    law,
    pieces,
    table,
    source,
    later_curl,
    timed,
    sums,
    small_sems,
    curl_sem,
):
    tile_count, links, tile, comps = curl_hbm.shape
    early = first_curl.shape[0]
    parts_here = out.shape[0]
    rank = lax.axis_index(GROUP)
    fetched = [
        (pieces_hbm.at[rank], pieces),
        (table_hbm.at[rank], table),
        (pattern_hbm, pattern),
        (region_hbm, region_ids),
        (law_hbm, law),
        (source_hbm, source),
    ]
    small = [
        pltpu.make_async_copy(src, dst, small_sems.at[i]) for i, (src, dst) in enumerate(fetched)
    ]
    rest = pltpu.make_async_copy(curl_hbm.at[early:], later_curl, curl_sem)
    for copy in small + [rest]:
        copy.start()
    sums[...] = jnp.zeros_like(sums)
    for copy in small:
        copy.wait()
    stacked = jnp.concatenate([window[...]] * 3, axis=0)
    samples = jnp.dot(pieces[...], stacked, preferred_element_type=jnp.float32)
    high = samples.astype(jnp.bfloat16)
    timed[:HALF, :] = high
    timed[HALF:, :] = (samples - high.astype(jnp.float32)).astype(jnp.bfloat16)
    columns = [
        jnp.broadcast_to(table[:, part : part + 1], (HALF, comps)) for part in range(parts_here)
    ]
    for elem in range(tile_count):
        places = [pattern[link, elem] for link in range(links)]
        picked = jnp.concatenate(
            [timed[:, pl.ds(pl.multiple_of(place * tile, tile), tile)] for place in places], axis=1
        )
        if elem == early:
            rest.wait()
        curl = first_curl[elem] if elem < early else later_curl[elem - early]
        blocks = curl.reshape(links * tile, comps)
        split = jnp.dot(picked, blocks, preferred_element_type=jnp.float32)
        density = split[:HALF] + split[HALF:]
        comp = [density[:, c * tile : (c + 1) * tile] for c in range(comps // tile)]
        square = comp[0] * comp[0]
        for c in comp[1:]:
            square = square + c * c
        region = region_ids[elem]
        reluct = law[0, region] + law[2, region] * square / (square + law[1, region])
        field = jnp.concatenate([reluct * c for c in comp], axis=1)
        projected = jnp.concatenate(
            [jnp.sum(column * field, axis=0, keepdims=True) for column in columns], axis=0
        )
        projected = (projected * (4.0 / SAMPLES)).astype(jnp.bfloat16)
        contrib = lax.dot_general(
            projected, blocks, (((1,), (1,)), ((), ())), preferred_element_type=jnp.float32
        )
        for link, place in enumerate(places):
            sums[place] += contrib[:, link * tile : (link + 1) * tile]
    for w in range(tile_count):
        at = slice(w * tile, (w + 1) * tile)
        out[:, at] = sums[w + 1] - source[:, at]
    halo[:, :tile] = sums[0]
    halo[:, tile:] = sums[tile_count + 1]


def halo_kernel(own, received, out):
    tile = received.shape[1] // 2
    out[...] = own[...]
    out[:, :tile] += received[:, tile:]
    out[:, -tile:] += received[:, :tile]


def per_device(coeffs, curl_tiles, pattern, region_ids, material_law, source):
    parts_here = coeffs.shape[0]
    tile_count, links, tile, comps = curl_tiles.shape
    harm, samp = lax.axis_size("harm"), lax.axis_size("samp")
    parts = parts_here * harm * samp
    table = half_table(parts)[:, arrival_order(harm, samp, parts_here)].transpose(1, 0, 2)
    pieces = bf16_pieces(table)
    own_columns = table[:, :, :parts_here]
    vmem, hbm = pl.BlockSpec(memory_space=pltpu.VMEM), pl.BlockSpec(memory_space=pltpu.HBM)

    near = jnp.stack([coeffs] + [send(coeffs, "samp", k) for k in range(1, samp)])
    edges = jnp.concatenate([near[..., :tile], near[..., -tile:]], axis=-1)
    curl_hbm = pltpu.with_memory_space_constraint(curl_tiles, pltpu.HBM)
    early = 3 * tile_count // 8
    first_curl = pl.pallas_call(
        fetch_kernel,
        out_shape=pltpu.VMEM((early,) + curl_tiles.shape[1:], curl_tiles.dtype),
        in_specs=[hbm],
        out_specs=vmem,
        scratch_shapes=[pltpu.SemaphoreType.DMA],
        compiler_params=pltpu.CompilerParams(vmem_limit_bytes=16 * 1024 * 1024),
        cost_estimate=pl.CostEstimate(
            flops=0, bytes_accessed=4 * early * links * tile * comps, transcendentals=0
        ),
        name="fetch_curl",
    )(curl_hbm)
    rows = []
    for j in range(harm):
        block = send(near, "harm", j) if j else near
        beside = from_neighbours(edges, "harm", j)
        rows.append(jnp.concatenate([beside[..., tile:], block, beside[..., :tile]], axis=-1))
    window = jnp.concatenate(rows, axis=0).reshape(parts, -1)
    own, halo = pl.pallas_call(
        shard_kernel,
        out_shape=(
            pltpu.VMEM(source.shape, jnp.float32),
            pltpu.VMEM((parts_here, 2 * tile), jnp.float32),
        ),
        in_specs=[vmem] * 2 + [hbm] * 7,
        out_specs=(vmem, vmem),
        scratch_shapes=[
            pltpu.SMEM((links, tile_count), jnp.int32),
            pltpu.SMEM(region_ids.shape, jnp.int32),
            pltpu.SMEM(material_law.shape, jnp.float32),
            pltpu.VMEM(pieces.shape[1:], jnp.bfloat16),
            pltpu.VMEM(own_columns.shape[1:], jnp.float32),
            pltpu.VMEM(source.shape, jnp.float32),
            pltpu.VMEM((tile_count - early,) + curl_tiles.shape[1:], curl_tiles.dtype),
            pltpu.VMEM((SAMPLES, (tile_count + 2) * tile), jnp.bfloat16),
            pltpu.VMEM((tile_count + 2, parts_here, tile), jnp.float32),
            pltpu.SemaphoreType.DMA((6,)),
            pltpu.SemaphoreType.DMA,
        ],
        compiler_params=pltpu.CompilerParams(vmem_limit_bytes=32 * 1024 * 1024),
        cost_estimate=pl.CostEstimate(
            flops=4 * SAMPLES * tile_count * links * tile * comps,
            bytes_accessed=2 * curl_tiles.size,
            transcendentals=0,
        ),
        name="shard_residual",
    )(
        window,
        pltpu.with_memory_space_constraint(first_curl, pltpu.VMEM),
        curl_hbm,
        *[
            pltpu.with_memory_space_constraint(operand, pltpu.HBM)
            for operand in (
                pattern.T,
                region_ids,
                material_law,
                jnp.asarray(pieces),
                jnp.asarray(own_columns.astype(np.float32)),
                source,
            )
        ],
    )
    return pl.pallas_call(
        halo_kernel,
        out_shape=jax.ShapeDtypeStruct(source.shape, jnp.float32),
        in_specs=[vmem] * 2,
        out_specs=vmem,
        compiler_params=pltpu.CompilerParams(vmem_limit_bytes=16 * 1024 * 1024),
        name="halo_sum",
    )(pltpu.with_memory_space_constraint(own, pltpu.VMEM), from_neighbours(halo, "harm", 0))


def solution(mesh):
    placed = (
        P(GROUP, "space"),
        P("space", None, None, None),
        P("space", None),
        P("space"),
        P(),
        P(GROUP, "space"),
    )
    return jax.shard_map(
        per_device,
        mesh=mesh,
        in_specs=placed,
        out_specs=P(GROUP, "space"),
        check_vma=False,
    )
```

```python
import math

import jax
import jax.numpy as jnp
import ml_dtypes
import numpy as np
from jax import lax
from jax.experimental import pallas as pl
from jax.experimental.pallas import tpu as pltpu
from jax.sharding import PartitionSpec as P

SAMPLES = 64
HALF = SAMPLES // 2
GROUP = ("harm", "samp")
MIB = 1024 * 1024


def half_table(parts):
    sample_ids = np.arange(HALF)[:, None]
    part_ids = np.arange(parts)[None, :]
    phase = ((2 * (part_ids // 2) + 1) * sample_ids % SAMPLES) * (2.0 * math.pi / SAMPLES)
    return np.where(part_ids % 2 == 0, np.cos(phase), np.sin(phase))


def bf16_pieces(table):
    rest = table
    pieces = []
    for _ in range(3):
        piece = rest.astype(ml_dtypes.bfloat16)
        pieces.append(piece)
        rest = rest - piece.astype(np.float64)
    return np.concatenate(pieces, axis=-1)


def shifted(array, axis, by):
    count = lax.axis_size(axis)
    return lax.ppermute(array, axis, [(i, (i + by) % count) for i in range(count)])


def from_neighbours(array, tile):
    if lax.axis_size("space") == 2:
        other = shifted(array, "space", 1)
        return other[:, :tile], other[:, -tile:]
    return shifted(array[:, :tile], "space", -1), shifted(array[:, -tile:], "space", 1)


def fetch_kernel(*refs):
    count = (len(refs) - 1) // 2
    sources, targets, sems = refs[:count], refs[count : 2 * count], refs[-1]
    rank = lax.axis_index(GROUP)
    sources = (sources[0].at[: targets[0].shape[0]], sources[1].at[rank]) + sources[2:]
    copies = [
        pltpu.make_async_copy(source, target, sems.at[i])
        for i, (source, target) in enumerate(zip(sources, targets))
    ]
    for copy in copies:
        copy.start()
    for copy in copies:
        copy.wait()


def shard_kernel(
    window,
    first_curl,
    table,
    pieces,
    source,
    pattern_in,
    region_in,
    law_in,
    curl_hbm,
    out,
    halo,
    pattern,
    region_ids,
    law,
    later_curl,
    timed,
    densities,
    small_sems,
    curl_sem,
    *sums,
):
    tile_count, links, tile, comps = curl_hbm.shape
    early = first_curl.shape[0]
    parts_here = out.shape[0]
    fetched = [(pattern_in, pattern), (region_in, region_ids), (law_in, law)]
    small = [
        pltpu.make_async_copy(src, dst, small_sems.at[i]) for i, (src, dst) in enumerate(fetched)
    ]
    rest = pltpu.make_async_copy(curl_hbm.at[early:], later_curl, curl_sem)
    for copy in small + [rest]:
        copy.start()
    for total in sums:
        total[...] = jnp.zeros_like(total)
    stacked = jnp.concatenate([window[...]] * 3, axis=0)
    samples = jnp.dot(pieces[...], stacked, preferred_element_type=jnp.float32)
    high = samples.astype(jnp.bfloat16)
    timed[:HALF, :] = high
    timed[HALF:, :] = (samples - high.astype(jnp.float32)).astype(jnp.bfloat16)
    columns = [
        jnp.broadcast_to(table[:, part : part + 1], (HALF, comps)) for part in range(parts_here)
    ]
    for copy in small:
        copy.wait()
    places = [[pattern[link, elem] for link in range(links)] for elem in range(tile_count)]

    def blocks(elem):
        curl = first_curl[elem] if elem < early else later_curl[elem - early]
        return curl.reshape(links * tile, comps)

    def find_density(elem):
        picked = jnp.concatenate(
            [timed[:, pl.ds(pl.multiple_of(at * tile, tile), tile)] for at in places[elem]], axis=1
        )
        split = jnp.dot(picked, blocks(elem), preferred_element_type=jnp.float32)
        densities[elem] = split[:HALF] + split[HALF:]

    def project(elem):
        density = densities[elem]
        comp = [density[:, c * tile : (c + 1) * tile] for c in range(comps // tile)]
        square = comp[0] * comp[0]
        for c in comp[1:]:
            square = square + c * c
        region = region_ids[elem]
        reluct = law[0, region] + law[2, region] * square / (square + law[1, region])
        field = jnp.concatenate([reluct * c for c in comp], axis=1)
        rows = [jnp.sum(column * field, axis=0, keepdims=True) for column in columns]
        return (jnp.concatenate(rows, axis=0) * (4.0 / SAMPLES)).astype(jnp.bfloat16)

    def contribute(elem, projected):
        contrib = lax.dot_general(
            projected, blocks(elem), (((1,), (1,)), ((), ())), preferred_element_type=jnp.float32
        )
        for link, at in enumerate(places[elem]):
            sums[link][at] += contrib[:, link * tile : (link + 1) * tile]

    step = 2
    chunks = [range(at, min(at + step, tile_count)) for at in range(0, tile_count, step)]
    projected = {}
    for turn in range(len(chunks) + 2):
        if turn < len(chunks):
            if early in chunks[turn]:
                rest.wait()
            for elem in chunks[turn]:
                find_density(elem)
        if 0 <= turn - 1 < len(chunks):
            for elem in chunks[turn - 1]:
                projected[elem] = project(elem)
        if 0 <= turn - 2:
            for elem in chunks[turn - 2]:
                contribute(elem, projected[elem])

    def window_sum(w):
        total = sums[0][w]
        for other in sums[1:]:
            total = total + other[w]
        return total

    for w in range(tile_count):
        at = slice(w * tile, (w + 1) * tile)
        out[:, at] = window_sum(w + 1) - source[:, at]
    halo[:, :tile] = window_sum(0)
    halo[:, tile:] = window_sum(tile_count + 1)


def halo_kernel(own, from_right, from_left, out):
    tile = from_left.shape[1] // 2
    out[...] = own[...]
    out[:, :tile] += from_left[:, tile:]
    out[:, -tile:] += from_right[:, :tile]


def per_device(coeffs, curl_tiles, pattern, region_ids, material_law, source):
    parts_here = coeffs.shape[0]
    tile_count, links, tile, comps = curl_tiles.shape
    group_size = lax.axis_size(GROUP)
    parts = parts_here * group_size
    table = half_table(parts)
    pieces = jnp.asarray(bf16_pieces(table))
    own_columns = jnp.asarray(
        table.reshape(HALF, group_size, parts_here).transpose(1, 0, 2).astype(np.float32)
    )
    vmem, hbm = pl.BlockSpec(memory_space=pltpu.VMEM), pl.BlockSpec(memory_space=pltpu.HBM)

    def in_vmem(array):
        return pltpu.with_memory_space_constraint(array, pltpu.VMEM)

    def in_hbm(array):
        return pltpu.with_memory_space_constraint(array, pltpu.HBM)

    early = 3 * tile_count // 8
    operands = [
        curl_tiles,
        own_columns,
        coeffs,
        pieces,
        source,
        pattern.T,
        region_ids,
        material_law,
    ]
    shapes = [
        (early,) + curl_tiles.shape[1:],
        own_columns.shape[1:],
    ] + [operand.shape for operand in operands[2:]]
    fetched = pl.pallas_call(
        fetch_kernel,
        out_shape=[pltpu.VMEM(shape, o.dtype) for shape, o in zip(shapes, operands)],
        in_specs=[hbm] * len(operands),
        out_specs=[vmem] * len(operands),
        scratch_shapes=[pltpu.SemaphoreType.DMA((len(operands),))],
        compiler_params=pltpu.CompilerParams(vmem_limit_bytes=16 * MIB),
        cost_estimate=pl.CostEstimate(
            flops=0, bytes_accessed=4 * early * links * tile * comps, transcendentals=0
        ),
        name="fetch_operands",
    )(*[in_hbm(operand) for operand in operands])
    first_curl, columns_here, coeffs_here, pieces_here, *others = fetched

    right, left = from_neighbours(coeffs, tile)
    block = jnp.concatenate([left, coeffs_here, right], axis=1)
    copies = jnp.broadcast_to(block[None], (group_size,) + block.shape)
    window = lax.all_to_all(copies, GROUP, 0, 0).reshape(parts, block.shape[1])
    own, halo = pl.pallas_call(
        shard_kernel,
        out_shape=(
            pltpu.VMEM(source.shape, jnp.float32),
            pltpu.VMEM((parts_here, 2 * tile), jnp.float32),
        ),
        in_specs=[vmem] * 8 + [hbm],
        out_specs=(vmem, vmem),
        scratch_shapes=[
            pltpu.SMEM((links, tile_count), jnp.int32),
            pltpu.SMEM(region_ids.shape, jnp.int32),
            pltpu.SMEM(material_law.shape, jnp.float32),
            pltpu.VMEM((tile_count - early,) + curl_tiles.shape[1:], curl_tiles.dtype),
            pltpu.VMEM((SAMPLES, (tile_count + 2) * tile), jnp.bfloat16),
            pltpu.VMEM((tile_count, HALF, comps), jnp.float32),
            pltpu.SemaphoreType.DMA((3,)),
            pltpu.SemaphoreType.DMA,
        ]
        + [pltpu.VMEM((tile_count + 2, parts_here, tile), jnp.float32)] * links,
        compiler_params=pltpu.CompilerParams(vmem_limit_bytes=32 * MIB),
        cost_estimate=pl.CostEstimate(
            flops=4 * SAMPLES * tile_count * links * tile * comps,
            bytes_accessed=2 * curl_tiles.size,
            transcendentals=0,
        ),
        name="shard_residual",
    )(
        in_vmem(window),
        *[in_vmem(array) for array in (first_curl, columns_here, pieces_here, *others)],
        in_hbm(curl_tiles),
    )
    if lax.axis_size("space") == 2:
        beside = [shifted(halo, "space", 1)] * 2
    else:
        beside = [shifted(halo, "space", -1), shifted(halo, "space", 1)]
    return pl.pallas_call(
        halo_kernel,
        out_shape=jax.ShapeDtypeStruct(source.shape, jnp.float32),
        in_specs=[vmem] * 3,
        out_specs=vmem,
        compiler_params=pltpu.CompilerParams(vmem_limit_bytes=16 * MIB),
        name="halo_sum",
    )(in_vmem(own), *beside)


def solution(mesh):
    placed = (
        P(GROUP, "space"),
        P("space", None, None, None),
        P("space", None),
        P("space"),
        P(),
        P(GROUP, "space"),
    )
    return jax.shard_map(
        per_device,
        mesh=mesh,
        in_specs=placed,
        out_specs=P(GROUP, "space"),
        check_vma=False,
    )
```

```python
import math

import jax
import jax.numpy as jnp
import ml_dtypes
import numpy as np
from jax import lax
from jax.experimental import pallas as pl
from jax.experimental.pallas import tpu as pltpu
from jax.sharding import PartitionSpec as P

SAMPLES = 64
HALF = SAMPLES // 2
GROUP = ("harm", "samp")
MIB = 1024 * 1024


def half_table(parts):
    sample_ids = np.arange(HALF)[:, None]
    part_ids = np.arange(parts)[None, :]
    phase = ((2 * (part_ids // 2) + 1) * sample_ids % SAMPLES) * (2.0 * math.pi / SAMPLES)
    return np.where(part_ids % 2 == 0, np.cos(phase), np.sin(phase))


def bf16_pieces(table):
    rest = table
    pieces = []
    for _ in range(3):
        piece = rest.astype(ml_dtypes.bfloat16)
        pieces.append(piece)
        rest = rest - piece.astype(np.float64)
    return np.concatenate(pieces, axis=-1)


def shifted(array, axis, by):
    count = lax.axis_size(axis)
    return lax.ppermute(array, axis, [(i, (i + by) % count) for i in range(count)])


def from_neighbours(array, tile):
    if lax.axis_size("space") == 2:
        other = shifted(array, "space", 1)
        return other[:, :tile], other[:, -tile:]
    return shifted(array[:, :tile], "space", -1), shifted(array[:, -tile:], "space", 1)


def partner(index, step, size):
    return index ^ step if size & (size - 1) == 0 else (index + step) % size


def sender(index, step, size):
    return index ^ step if size & (size - 1) == 0 else (index - step) % size


def gathered(block, axis):
    size = lax.axis_size(axis)
    blocks = [block]
    for step in range(1, size):
        pairs = [(i, partner(i, step, size)) for i in range(size)]
        blocks.append(lax.ppermute(block, axis, pairs))
    return jnp.concatenate(blocks, axis=0)


def arrival_order(harm, samp, parts_here):
    ranks = [
        [
            sender(h, j, harm) * samp + sender(s, k, samp)
            for j in range(harm)
            for k in range(samp)
        ]
        for h in range(harm)
        for s in range(samp)
    ]
    rows = np.array(ranks)[:, :, None] * parts_here + np.arange(parts_here)
    return rows.reshape(harm * samp, -1)


def fetch_kernel(*refs):
    count = (len(refs) - 1) // 2
    sources, targets, sems = refs[:count], refs[count : 2 * count], refs[-1]
    rank = lax.axis_index(GROUP)
    first = sources[0].at[: targets[0].shape[0]]
    sources = (first, sources[1].at[rank], sources[2].at[rank]) + sources[3:]
    copies = [
        pltpu.make_async_copy(source, target, sems.at[i])
        for i, (source, target) in enumerate(zip(sources, targets))
    ]
    for copy in copies:
        copy.start()
    for copy in copies:
        copy.wait()


def shard_kernel(
    window,
    first_curl,
    table,
    pieces,
    source,
    pattern_in,
    region_in,
    law_in,
    curl_hbm,
    out,
    halo,
    pattern,
    region_ids,
    law,
    later_curl,
    timed,
    densities,
    small_sems,
    curl_sem,
    *sums,
):
    tile_count, links, tile, comps = curl_hbm.shape
    early = first_curl.shape[0]
    parts_here = out.shape[0]
    fetched = [(pattern_in, pattern), (region_in, region_ids), (law_in, law)]
    small = [
        pltpu.make_async_copy(src, dst, small_sems.at[i]) for i, (src, dst) in enumerate(fetched)
    ]
    rest = pltpu.make_async_copy(curl_hbm.at[early:], later_curl, curl_sem)
    for copy in small + [rest]:
        copy.start()
    for total in sums:
        total[...] = jnp.zeros_like(total)
    stacked = jnp.concatenate([window[...]] * 3, axis=0)
    samples = jnp.dot(pieces[...], stacked, preferred_element_type=jnp.float32)
    high = samples.astype(jnp.bfloat16)
    timed[:HALF, :] = high
    timed[HALF:, :] = (samples - high.astype(jnp.float32)).astype(jnp.bfloat16)
    columns = [
        jnp.broadcast_to(table[:, part : part + 1], (HALF, comps)) for part in range(parts_here)
    ]
    for copy in small:
        copy.wait()
    places = [[pattern[link, elem] for link in range(links)] for elem in range(tile_count)]

    def blocks(elem):
        curl = first_curl[elem] if elem < early else later_curl[elem - early]
        return curl.reshape(links * tile, comps)

    def find_density(elem):
        picked = jnp.concatenate(
            [timed[:, pl.ds(pl.multiple_of(at * tile, tile), tile)] for at in places[elem]], axis=1
        )
        split = jnp.dot(picked, blocks(elem), preferred_element_type=jnp.float32)
        densities[elem] = split[:HALF] + split[HALF:]

    def project(elem):
        density = densities[elem]
        comp = [density[:, c * tile : (c + 1) * tile] for c in range(comps // tile)]
        square = comp[0] * comp[0]
        for c in comp[1:]:
            square = square + c * c
        region = region_ids[elem]
        reluct = law[0, region] + law[2, region] * square / (square + law[1, region])
        field = jnp.concatenate([reluct * c for c in comp], axis=1)
        rows = [jnp.sum(column * field, axis=0, keepdims=True) for column in columns]
        return (jnp.concatenate(rows, axis=0) * (4.0 / SAMPLES)).astype(jnp.bfloat16)

    def contribute(elem, projected):
        contrib = lax.dot_general(
            projected, blocks(elem), (((1,), (1,)), ((), ())), preferred_element_type=jnp.float32
        )
        for link, at in enumerate(places[elem]):
            sums[link][at] += contrib[:, link * tile : (link + 1) * tile]

    step = 2
    chunks = [range(at, min(at + step, tile_count)) for at in range(0, tile_count, step)]
    projected = {}
    for turn in range(len(chunks) + 2):
        if turn < len(chunks):
            if early in chunks[turn]:
                rest.wait()
            for elem in chunks[turn]:
                find_density(elem)
        if 0 <= turn - 1 < len(chunks):
            for elem in chunks[turn - 1]:
                projected[elem] = project(elem)
        if 0 <= turn - 2:
            for elem in chunks[turn - 2]:
                contribute(elem, projected[elem])

    def window_sum(w):
        total = sums[0][w]
        for other in sums[1:]:
            total = total + other[w]
        return total

    for w in range(tile_count):
        at = slice(w * tile, (w + 1) * tile)
        out[:, at] = window_sum(w + 1) - source[:, at]
    halo[:, :tile] = window_sum(0)
    halo[:, tile:] = window_sum(tile_count + 1)


def halo_kernel(own, from_right, from_left, out):
    tile = from_left.shape[1] // 2
    out[...] = own[...]
    out[:, :tile] += from_left[:, tile:]
    out[:, -tile:] += from_right[:, :tile]


def per_device(coeffs, curl_tiles, pattern, region_ids, material_law, source):
    parts_here = coeffs.shape[0]
    tile_count, links, tile, comps = curl_tiles.shape
    harm, samp = lax.axis_size("harm"), lax.axis_size("samp")
    parts = parts_here * harm * samp
    table = half_table(parts)[:, arrival_order(harm, samp, parts_here)].transpose(1, 0, 2)
    pieces = jnp.asarray(bf16_pieces(table))
    own_columns = jnp.asarray(table[:, :, :parts_here].astype(np.float32))
    vmem, hbm = pl.BlockSpec(memory_space=pltpu.VMEM), pl.BlockSpec(memory_space=pltpu.HBM)

    def in_vmem(array):
        return pltpu.with_memory_space_constraint(array, pltpu.VMEM)

    def in_hbm(array):
        return pltpu.with_memory_space_constraint(array, pltpu.HBM)

    early = 3 * tile_count // 8
    operands = [
        curl_tiles,
        own_columns,
        pieces,
        coeffs,
        source,
        pattern.T,
        region_ids,
        material_law,
    ]
    shapes = [
        (early,) + curl_tiles.shape[1:],
        own_columns.shape[1:],
        pieces.shape[1:],
    ] + [operand.shape for operand in operands[3:]]
    fetched = pl.pallas_call(
        fetch_kernel,
        out_shape=[pltpu.VMEM(shape, o.dtype) for shape, o in zip(shapes, operands)],
        in_specs=[hbm] * len(operands),
        out_specs=[vmem] * len(operands),
        scratch_shapes=[pltpu.SemaphoreType.DMA((len(operands),))],
        compiler_params=pltpu.CompilerParams(vmem_limit_bytes=16 * MIB),
        cost_estimate=pl.CostEstimate(
            flops=0, bytes_accessed=4 * early * links * tile * comps, transcendentals=0
        ),
        name="fetch_operands",
    )(*[in_hbm(operand) for operand in operands])
    first_curl, columns_here, pieces_here, coeffs_here, *others = fetched

    right, left = from_neighbours(coeffs, tile)
    block = jnp.concatenate([left, coeffs_here, right], axis=1)
    window = gathered(gathered(block[None], "samp"), "harm").reshape(parts, block.shape[1])
    own, halo = pl.pallas_call(
        shard_kernel,
        out_shape=(
            pltpu.VMEM(source.shape, jnp.float32),
            pltpu.VMEM((parts_here, 2 * tile), jnp.float32),
        ),
        in_specs=[vmem] * 8 + [hbm],
        out_specs=(vmem, vmem),
        scratch_shapes=[
            pltpu.SMEM((links, tile_count), jnp.int32),
            pltpu.SMEM(region_ids.shape, jnp.int32),
            pltpu.SMEM(material_law.shape, jnp.float32),
            pltpu.VMEM((tile_count - early,) + curl_tiles.shape[1:], curl_tiles.dtype),
            pltpu.VMEM((SAMPLES, (tile_count + 2) * tile), jnp.bfloat16),
            pltpu.VMEM((tile_count, HALF, comps), jnp.float32),
            pltpu.SemaphoreType.DMA((3,)),
            pltpu.SemaphoreType.DMA,
        ]
        + [pltpu.VMEM((tile_count + 2, parts_here, tile), jnp.float32)] * links,
        compiler_params=pltpu.CompilerParams(vmem_limit_bytes=32 * MIB),
        cost_estimate=pl.CostEstimate(
            flops=4 * SAMPLES * tile_count * links * tile * comps,
            bytes_accessed=2 * curl_tiles.size,
            transcendentals=0,
        ),
        name="shard_residual",
    )(
        in_vmem(window),
        *[in_vmem(array) for array in (first_curl, columns_here, pieces_here, *others)],
        in_hbm(curl_tiles),
    )
    if lax.axis_size("space") == 2:
        beside = [shifted(halo, "space", 1)] * 2
    else:
        beside = [shifted(halo, "space", -1), shifted(halo, "space", 1)]
    return pl.pallas_call(
        halo_kernel,
        out_shape=jax.ShapeDtypeStruct(source.shape, jnp.float32),
        in_specs=[vmem] * 3,
        out_specs=vmem,
        compiler_params=pltpu.CompilerParams(vmem_limit_bytes=16 * MIB),
        name="halo_sum",
    )(in_vmem(own), *beside)


def solution(mesh):
    placed = (
        P(GROUP, "space"),
        P("space", None, None, None),
        P("space", None),
        P("space"),
        P(),
        P(GROUP, "space"),
    )
    return jax.shard_map(
        per_device,
        mesh=mesh,
        in_specs=placed,
        out_specs=P(GROUP, "space"),
        check_vma=False,
    )
```

```python
import math

import jax
import jax.numpy as jnp
import ml_dtypes
import numpy as np
from jax import lax
from jax.experimental import pallas as pl
from jax.experimental.pallas import tpu as pltpu
from jax.sharding import PartitionSpec as P

SAMPLES = 64
HALF = SAMPLES // 2
GROUP = ("chip", "core", "samp")
MIB = 1024 * 1024


def half_table(parts):
    sample_ids = np.arange(HALF)[:, None]
    part_ids = np.arange(parts)[None, :]
    phase = ((2 * (part_ids // 2) + 1) * sample_ids % SAMPLES) * (2.0 * math.pi / SAMPLES)
    return np.where(part_ids % 2 == 0, np.cos(phase), np.sin(phase))


def bf16_pieces(table):
    rest = table
    pieces = []
    for _ in range(3):
        piece = rest.astype(ml_dtypes.bfloat16)
        pieces.append(piece)
        rest = rest - piece.astype(np.float64)
    return np.concatenate(pieces, axis=-1)


def across(array, core_step, space_step):
    cores, shards = lax.axis_size("core"), lax.axis_size("space")
    pairs = [
        (c * shards + s, (c + core_step) % cores * shards + (s + space_step) % shards)
        for c in range(cores)
        for s in range(shards)
    ]
    return lax.ppermute(array, ("core", "space"), pairs)


def from_neighbours(array, tile, core_step):
    if lax.axis_size("space") == 2:
        other = across(array, core_step, 1)
        return other[:, :tile], other[:, -tile:]
    return across(array[:, :tile], core_step, -1), across(array[:, -tile:], core_step, 1)


def arrival_order(chips, cores, samp, parts_here):
    ranks = [
        [
            (chip * cores + (c - step) % cores) * samp + s
            for chip in range(chips)
            for s in range(samp)
            for step in range(cores)
        ]
        for c in range(cores)
    ]
    rows = np.array(ranks)[:, :, None] * parts_here + np.arange(parts_here)
    return rows.reshape(cores, -1)


def fetch_kernel(*refs):
    count = (len(refs) - 1) // 2
    sources, targets, sems = refs[:count], refs[count : 2 * count], refs[-1]
    first = sources[0].at[: targets[0].shape[0]]
    own_columns = sources[1].at[lax.axis_index(GROUP)]
    sources = (first, own_columns, sources[2].at[lax.axis_index("core")]) + sources[3:]
    copies = [
        pltpu.make_async_copy(source, target, sems.at[i])
        for i, (source, target) in enumerate(zip(sources, targets))
    ]
    for copy in copies:
        copy.start()
    for copy in copies:
        copy.wait()


def shard_kernel(
    window,
    first_curl,
    table,
    pieces,
    source,
    pattern_in,
    region_in,
    law_in,
    curl_hbm,
    out,
    halo,
    pattern,
    region_ids,
    law,
    later_curl,
    timed,
    densities,
    small_sems,
    curl_sem,
    *sums,
):
    tile_count, links, tile, comps = curl_hbm.shape
    early = first_curl.shape[0]
    parts_here = out.shape[0]
    fetched = [(pattern_in, pattern), (region_in, region_ids), (law_in, law)]
    small = [
        pltpu.make_async_copy(src, dst, small_sems.at[i]) for i, (src, dst) in enumerate(fetched)
    ]
    rest = pltpu.make_async_copy(curl_hbm.at[early:], later_curl, curl_sem)
    for copy in small + [rest]:
        copy.start()
    for total in sums:
        total[...] = jnp.zeros_like(total)
    stacked = jnp.concatenate([window[...]] * 3, axis=0)
    samples = jnp.dot(pieces[...], stacked, preferred_element_type=jnp.float32)
    high = samples.astype(jnp.bfloat16)
    timed[:HALF, :] = high
    timed[HALF:, :] = (samples - high.astype(jnp.float32)).astype(jnp.bfloat16)
    columns = [
        jnp.broadcast_to(table[:, part : part + 1], (HALF, comps)) for part in range(parts_here)
    ]
    for copy in small:
        copy.wait()
    places = [[pattern[link, elem] for link in range(links)] for elem in range(tile_count)]

    def blocks(elem):
        curl = first_curl[elem] if elem < early else later_curl[elem - early]
        return curl.reshape(links * tile, comps)

    def find_density(elem):
        picked = jnp.concatenate(
            [timed[:, pl.ds(pl.multiple_of(at * tile, tile), tile)] for at in places[elem]], axis=1
        )
        split = jnp.dot(picked, blocks(elem), preferred_element_type=jnp.float32)
        densities[elem] = split[:HALF] + split[HALF:]

    def project(elem):
        density = densities[elem]
        comp = [density[:, c * tile : (c + 1) * tile] for c in range(comps // tile)]
        square = comp[0] * comp[0]
        for c in comp[1:]:
            square = square + c * c
        region = region_ids[elem]
        reluct = law[0, region] + law[2, region] * square / (square + law[1, region])
        field = jnp.concatenate([reluct * c for c in comp], axis=1)
        rows = [jnp.sum(column * field, axis=0, keepdims=True) for column in columns]
        return (jnp.concatenate(rows, axis=0) * (4.0 / SAMPLES)).astype(jnp.bfloat16)

    def contribute(elem, projected):
        contrib = lax.dot_general(
            projected, blocks(elem), (((1,), (1,)), ((), ())), preferred_element_type=jnp.float32
        )
        for link, at in enumerate(places[elem]):
            sums[link][at] += contrib[:, link * tile : (link + 1) * tile]

    step = 2
    chunks = [range(at, min(at + step, tile_count)) for at in range(0, tile_count, step)]
    projected = {}
    for turn in range(len(chunks) + 2):
        if turn < len(chunks):
            if early in chunks[turn]:
                rest.wait()
            for elem in chunks[turn]:
                find_density(elem)
        if 0 <= turn - 1 < len(chunks):
            for elem in chunks[turn - 1]:
                projected[elem] = project(elem)
        if 0 <= turn - 2:
            for elem in chunks[turn - 2]:
                contribute(elem, projected[elem])

    def window_sum(w):
        total = sums[0][w]
        for other in sums[1:]:
            total = total + other[w]
        return total

    for w in range(tile_count):
        at = slice(w * tile, (w + 1) * tile)
        out[:, at] = window_sum(w + 1) - source[:, at]
    halo[:, :tile] = window_sum(0)
    halo[:, tile:] = window_sum(tile_count + 1)


def halo_kernel(own, from_right, from_left, out):
    tile = from_left.shape[1] // 2
    out[...] = own[...]
    out[:, :tile] += from_left[:, tile:]
    out[:, -tile:] += from_right[:, :tile]


def per_device(coeffs, curl_tiles, pattern, region_ids, material_law, source):
    parts_here = coeffs.shape[0]
    tile_count, links, tile, comps = curl_tiles.shape
    chips, cores, samp = (lax.axis_size(axis) for axis in GROUP)
    group_size = chips * cores * samp
    parts = parts_here * group_size
    table = half_table(parts)
    order = arrival_order(chips, cores, samp, parts_here)
    pieces = jnp.asarray(bf16_pieces(table[:, order].transpose(1, 0, 2)))
    own_columns = jnp.asarray(
        table.reshape(HALF, group_size, parts_here).transpose(1, 0, 2).astype(np.float32)
    )
    vmem, hbm = pl.BlockSpec(memory_space=pltpu.VMEM), pl.BlockSpec(memory_space=pltpu.HBM)

    def in_vmem(array):
        return pltpu.with_memory_space_constraint(array, pltpu.VMEM)

    def in_hbm(array):
        return pltpu.with_memory_space_constraint(array, pltpu.HBM)

    early = 3 * tile_count // 8
    operands = [
        curl_tiles,
        own_columns,
        pieces,
        coeffs,
        source,
        pattern.T,
        region_ids,
        material_law,
    ]
    shapes = [
        (early,) + curl_tiles.shape[1:],
        own_columns.shape[1:],
        pieces.shape[1:],
    ] + [operand.shape for operand in operands[3:]]
    fetched = pl.pallas_call(
        fetch_kernel,
        out_shape=[pltpu.VMEM(shape, o.dtype) for shape, o in zip(shapes, operands)],
        in_specs=[hbm] * len(operands),
        out_specs=[vmem] * len(operands),
        scratch_shapes=[pltpu.SemaphoreType.DMA((len(operands),))],
        compiler_params=pltpu.CompilerParams(vmem_limit_bytes=16 * MIB),
        cost_estimate=pl.CostEstimate(
            flops=0, bytes_accessed=4 * early * links * tile * comps, transcendentals=0
        ),
        name="fetch_operands",
    )(*[in_hbm(operand) for operand in operands])
    first_curl, columns_here, pieces_here, coeffs_here, *others = fetched

    blocks = []
    for step in range(cores):
        right, left = from_neighbours(coeffs, tile, step)
        middle = across(coeffs, step, 0) if step else coeffs_here
        blocks.append(jnp.concatenate([left, middle, right], axis=1))
    block = jnp.stack(blocks)
    copies = jnp.broadcast_to(block[None], (chips * samp,) + block.shape)
    window = lax.all_to_all(copies, ("chip", "samp"), 0, 0).reshape(parts, block.shape[-1])
    own, halo = pl.pallas_call(
        shard_kernel,
        out_shape=(
            pltpu.VMEM(source.shape, jnp.float32),
            pltpu.VMEM((parts_here, 2 * tile), jnp.float32),
        ),
        in_specs=[vmem] * 8 + [hbm],
        out_specs=(vmem, vmem),
        scratch_shapes=[
            pltpu.SMEM((links, tile_count), jnp.int32),
            pltpu.SMEM(region_ids.shape, jnp.int32),
            pltpu.SMEM(material_law.shape, jnp.float32),
            pltpu.VMEM((tile_count - early,) + curl_tiles.shape[1:], curl_tiles.dtype),
            pltpu.VMEM((SAMPLES, (tile_count + 2) * tile), jnp.bfloat16),
            pltpu.VMEM((tile_count, HALF, comps), jnp.float32),
            pltpu.SemaphoreType.DMA((3,)),
            pltpu.SemaphoreType.DMA,
        ]
        + [pltpu.VMEM((tile_count + 2, parts_here, tile), jnp.float32)] * links,
        compiler_params=pltpu.CompilerParams(vmem_limit_bytes=32 * MIB),
        cost_estimate=pl.CostEstimate(
            flops=4 * SAMPLES * tile_count * links * tile * comps,
            bytes_accessed=2 * curl_tiles.size,
            transcendentals=0,
        ),
        name="shard_residual",
    )(
        in_vmem(window),
        *[in_vmem(array) for array in (first_curl, columns_here, pieces_here, *others)],
        in_hbm(curl_tiles),
    )
    if lax.axis_size("space") == 2:
        beside = [across(halo, 0, 1)] * 2
    else:
        beside = [across(halo, 0, -1), across(halo, 0, 1)]
    return pl.pallas_call(
        halo_kernel,
        out_shape=jax.ShapeDtypeStruct(source.shape, jnp.float32),
        in_specs=[vmem] * 3,
        out_specs=vmem,
        compiler_params=pltpu.CompilerParams(vmem_limit_bytes=16 * MIB),
        name="halo_sum",
    )(in_vmem(own), *beside)


def solution(mesh):
    at = mesh.axis_names.index("harm")
    harm = mesh.shape["harm"]
    cores = 2 if harm % 2 == 0 else 1
    sizes = mesh.devices.shape
    split = jax.sharding.Mesh(
        mesh.devices.reshape(sizes[:at] + (harm // cores, cores) + sizes[at + 1 :]),
        mesh.axis_names[:at] + ("chip", "core") + mesh.axis_names[at + 1 :],
    )
    placed = (
        P(GROUP, "space"),
        P("space", None, None, None),
        P("space", None),
        P("space"),
        P(),
        P(GROUP, "space"),
    )
    return jax.shard_map(
        per_device,
        mesh=split,
        in_specs=placed,
        out_specs=P(GROUP, "space"),
        check_vma=False,
    )
```

```python
import math

import jax
import jax.numpy as jnp
import ml_dtypes
import numpy as np
from jax import lax
from jax.experimental import pallas as pl
from jax.experimental.pallas import tpu as pltpu
from jax.sharding import PartitionSpec as P

SAMPLES = 64
HALF = SAMPLES // 2
GROUP = ("harm", "samp")
MIB = 1024 * 1024


def half_table(parts):
    sample_ids = np.arange(HALF)[:, None]
    part_ids = np.arange(parts)[None, :]
    phase = ((2 * (part_ids // 2) + 1) * sample_ids % SAMPLES) * (2.0 * math.pi / SAMPLES)
    return np.where(part_ids % 2 == 0, np.cos(phase), np.sin(phase))


def bf16_pieces(table):
    rest = table
    pieces = []
    for _ in range(3):
        piece = rest.astype(ml_dtypes.bfloat16)
        pieces.append(piece)
        rest = rest - piece.astype(np.float64)
    return np.concatenate(pieces, axis=-1)


def shifted(array, axis, by):
    count = lax.axis_size(axis)
    return lax.ppermute(array, axis, [(i, (i + by) % count) for i in range(count)])


def from_neighbours(array, tile):
    if lax.axis_size("space") == 2:
        other = shifted(array, "space", 1)
        return other[:, :tile], other[:, -tile:]
    return shifted(array[:, :tile], "space", -1), shifted(array[:, -tile:], "space", 1)


def fetch_kernel(*refs):
    count = (len(refs) - 1) // 2
    sources, targets, sems = refs[:count], refs[count : 2 * count], refs[-1]
    rank = lax.axis_index(GROUP)
    sources = (sources[0].at[: targets[0].shape[0]], sources[1].at[rank]) + sources[2:]
    copies = [
        pltpu.make_async_copy(source, target, sems.at[i])
        for i, (source, target) in enumerate(zip(sources, targets))
    ]
    for copy in copies:
        copy.start()
    for copy in copies:
        copy.wait()


def shard_kernel(
    window,
    first_curl,
    table,
    pieces,
    source,
    pattern_in,
    region_in,
    law_in,
    curl_hbm,
    out,
    halo,
    pattern,
    region_ids,
    law,
    later_curl,
    timed,
    densities,
    small_sems,
    curl_sem,
    *sums,
):
    tile_count, links, tile, comps = curl_hbm.shape
    early = first_curl.shape[0]
    parts_here = out.shape[0]
    fetched = [(pattern_in, pattern), (region_in, region_ids), (law_in, law)]
    small = [
        pltpu.make_async_copy(src, dst, small_sems.at[i]) for i, (src, dst) in enumerate(fetched)
    ]
    rest = pltpu.make_async_copy(curl_hbm.at[early:], later_curl, curl_sem)
    for copy in small + [rest]:
        copy.start()
    for total in sums:
        total[...] = jnp.zeros_like(total)
    stacked = jnp.concatenate([window[...]] * 3, axis=0)
    samples = jnp.dot(pieces[...], stacked, preferred_element_type=jnp.float32)
    high = samples.astype(jnp.bfloat16)
    timed[:HALF, :] = high
    timed[HALF:, :] = (samples - high.astype(jnp.float32)).astype(jnp.bfloat16)
    columns = [
        jnp.broadcast_to(table[:, part : part + 1], (HALF, comps)) for part in range(parts_here)
    ]
    for copy in small:
        copy.wait()
    places = [[pattern[link, elem] for link in range(links)] for elem in range(tile_count)]

    def blocks(elem):
        curl = first_curl[elem] if elem < early else later_curl[elem - early]
        return curl.reshape(links * tile, comps)

    def find_density(elem):
        picked = jnp.concatenate(
            [timed[:, pl.ds(pl.multiple_of(at * tile, tile), tile)] for at in places[elem]], axis=1
        )
        split = jnp.dot(picked, blocks(elem), preferred_element_type=jnp.float32)
        densities[elem] = split[:HALF] + split[HALF:]

    def project(elem):
        density = densities[elem]
        comp = [density[:, c * tile : (c + 1) * tile] for c in range(comps // tile)]
        square = comp[0] * comp[0]
        for c in comp[1:]:
            square = square + c * c
        region = region_ids[elem]
        reluct = law[0, region] + law[2, region] * square / (square + law[1, region])
        field = jnp.concatenate([reluct * c for c in comp], axis=1)
        rows = [jnp.sum(column * field, axis=0, keepdims=True) for column in columns]
        return (jnp.concatenate(rows, axis=0) * (4.0 / SAMPLES)).astype(jnp.bfloat16)

    def contribute(elem, projected):
        contrib = lax.dot_general(
            projected, blocks(elem), (((1,), (1,)), ((), ())), preferred_element_type=jnp.float32
        )
        for link, at in enumerate(places[elem]):
            sums[link][at] += contrib[:, link * tile : (link + 1) * tile]

    step = 4
    chunks = [range(at, min(at + step, tile_count)) for at in range(0, tile_count, step)]
    projected = {}
    for turn in range(len(chunks) + 2):
        if turn < len(chunks):
            if early in chunks[turn]:
                rest.wait()
            for elem in chunks[turn]:
                find_density(elem)
        if 0 <= turn - 1 < len(chunks):
            for elem in chunks[turn - 1]:
                projected[elem] = project(elem)
        if 0 <= turn - 2:
            for elem in chunks[turn - 2]:
                contribute(elem, projected[elem])

    def window_sum(w):
        total = sums[0][w]
        for other in sums[1:]:
            total = total + other[w]
        return total

    for w in range(tile_count):
        at = slice(w * tile, (w + 1) * tile)
        out[:, at] = window_sum(w + 1) - source[:, at]
    halo[:, :tile] = window_sum(0)
    halo[:, tile:] = window_sum(tile_count + 1)


def halo_kernel(own, from_right, from_left, out):
    tile = from_left.shape[1] // 2
    out[...] = own[...]
    out[:, :tile] += from_left[:, tile:]
    out[:, -tile:] += from_right[:, :tile]


def per_device(coeffs, curl_tiles, pattern, region_ids, material_law, source):
    parts_here = coeffs.shape[0]
    tile_count, links, tile, comps = curl_tiles.shape
    group_size = lax.axis_size(GROUP)
    parts = parts_here * group_size
    table = half_table(parts)
    pieces = jnp.asarray(bf16_pieces(table))
    own_columns = jnp.asarray(
        table.reshape(HALF, group_size, parts_here).transpose(1, 0, 2).astype(np.float32)
    )
    vmem, hbm = pl.BlockSpec(memory_space=pltpu.VMEM), pl.BlockSpec(memory_space=pltpu.HBM)

    def in_vmem(array):
        return pltpu.with_memory_space_constraint(array, pltpu.VMEM)

    def in_hbm(array):
        return pltpu.with_memory_space_constraint(array, pltpu.HBM)

    early = 3 * tile_count // 8
    operands = [
        curl_tiles,
        own_columns,
        coeffs,
        pieces,
        source,
        pattern.T,
        region_ids,
        material_law,
    ]
    shapes = [
        (early,) + curl_tiles.shape[1:],
        own_columns.shape[1:],
    ] + [operand.shape for operand in operands[2:]]
    fetched = pl.pallas_call(
        fetch_kernel,
        out_shape=[pltpu.VMEM(shape, o.dtype) for shape, o in zip(shapes, operands)],
        in_specs=[hbm] * len(operands),
        out_specs=[vmem] * len(operands),
        scratch_shapes=[pltpu.SemaphoreType.DMA((len(operands),))],
        compiler_params=pltpu.CompilerParams(vmem_limit_bytes=16 * MIB),
        cost_estimate=pl.CostEstimate(
            flops=0, bytes_accessed=4 * early * links * tile * comps, transcendentals=0
        ),
        name="fetch_operands",
    )(*[in_hbm(operand) for operand in operands])
    first_curl, columns_here, coeffs_here, pieces_here, *others = fetched

    right, left = from_neighbours(coeffs, tile)
    block = jnp.concatenate([left, coeffs_here, right], axis=1)
    near = lax.all_gather(block, "samp", axis=0, tiled=True)
    window = lax.all_gather(near, "harm", axis=0, tiled=True)
    own, halo = pl.pallas_call(
        shard_kernel,
        out_shape=(
            pltpu.VMEM(source.shape, jnp.float32),
            pltpu.VMEM((parts_here, 2 * tile), jnp.float32),
        ),
        in_specs=[vmem] * 8 + [hbm],
        out_specs=(vmem, vmem),
        scratch_shapes=[
            pltpu.SMEM((links, tile_count), jnp.int32),
            pltpu.SMEM(region_ids.shape, jnp.int32),
            pltpu.SMEM(material_law.shape, jnp.float32),
            pltpu.VMEM((tile_count - early,) + curl_tiles.shape[1:], curl_tiles.dtype),
            pltpu.VMEM((SAMPLES, (tile_count + 2) * tile), jnp.bfloat16),
            pltpu.VMEM((tile_count, HALF, comps), jnp.float32),
            pltpu.SemaphoreType.DMA((3,)),
            pltpu.SemaphoreType.DMA,
        ]
        + [pltpu.VMEM((tile_count + 2, parts_here, tile), jnp.float32)] * links,
        compiler_params=pltpu.CompilerParams(vmem_limit_bytes=32 * MIB),
        cost_estimate=pl.CostEstimate(
            flops=4 * SAMPLES * tile_count * links * tile * comps,
            bytes_accessed=2 * curl_tiles.size,
            transcendentals=0,
        ),
        name="shard_residual",
    )(
        in_vmem(window),
        *[in_vmem(array) for array in (first_curl, columns_here, pieces_here, *others)],
        in_hbm(curl_tiles),
    )
    if lax.axis_size("space") == 2:
        beside = [shifted(halo, "space", 1)] * 2
    else:
        beside = [shifted(halo, "space", -1), shifted(halo, "space", 1)]
    return pl.pallas_call(
        halo_kernel,
        out_shape=jax.ShapeDtypeStruct(source.shape, jnp.float32),
        in_specs=[vmem] * 3,
        out_specs=vmem,
        compiler_params=pltpu.CompilerParams(vmem_limit_bytes=16 * MIB),
        name="halo_sum",
    )(in_vmem(own), *beside)


def solution(mesh):
    placed = (
        P(GROUP, "space"),
        P("space", None, None, None),
        P("space", None),
        P("space"),
        P(),
        P(GROUP, "space"),
    )
    return jax.shard_map(
        per_device,
        mesh=mesh,
        in_specs=placed,
        out_specs=P(GROUP, "space"),
        check_vma=False,
    )
```

```python
import math

import jax
import jax.numpy as jnp
import ml_dtypes
import numpy as np
from jax import lax
from jax.experimental import pallas as pl
from jax.experimental.pallas import tpu as pltpu
from jax.sharding import PartitionSpec as P

SAMPLES = 64
HALF = SAMPLES // 2
GROUP = ("chip", "core", "samp")
MIB = 1024 * 1024


def half_table(parts):
    sample_ids = np.arange(HALF)[:, None]
    part_ids = np.arange(parts)[None, :]
    phase = ((2 * (part_ids // 2) + 1) * sample_ids % SAMPLES) * (2.0 * math.pi / SAMPLES)
    return np.where(part_ids % 2 == 0, np.cos(phase), np.sin(phase))


def bf16_pieces(table):
    rest = table
    pieces = []
    for _ in range(3):
        piece = rest.astype(ml_dtypes.bfloat16)
        pieces.append(piece)
        rest = rest - piece.astype(np.float64)
    return np.concatenate(pieces, axis=-1)


def across(array, core_step, space_step):
    cores, shards = lax.axis_size("core"), lax.axis_size("space")
    pairs = [
        (c * shards + s, (c + core_step) % cores * shards + (s + space_step) % shards)
        for c in range(cores)
        for s in range(shards)
    ]
    return lax.ppermute(array, ("core", "space"), pairs)


def from_neighbours(array, tile, core_step):
    if lax.axis_size("space") == 2:
        other = across(array, core_step, 1)
        return other[..., :tile], other[..., -tile:]
    return across(array[..., :tile], core_step, -1), across(array[..., -tile:], core_step, 1)


def arrival_order(chips, cores, samp, parts_here):
    ranks = [
        [
            (chip * cores + (c - step) % cores) * samp + s
            for step in range(cores)
            for chip in range(chips)
            for s in range(samp)
        ]
        for c in range(cores)
    ]
    rows = np.array(ranks)[:, :, None] * parts_here + np.arange(parts_here)
    return rows.reshape(cores, -1)


def fetch_kernel(*refs):
    count = (len(refs) - 1) // 2
    sources, targets, sems = refs[:count], refs[count : 2 * count], refs[-1]
    first = sources[0].at[: targets[0].shape[0]]
    own_columns = sources[1].at[lax.axis_index(GROUP)]
    sources = (first, own_columns, sources[2].at[lax.axis_index("core")]) + sources[3:]
    copies = [
        pltpu.make_async_copy(source, target, sems.at[i])
        for i, (source, target) in enumerate(zip(sources, targets))
    ]
    for copy in copies:
        copy.start()
    for copy in copies:
        copy.wait()


def shard_kernel(
    window,
    first_curl,
    table,
    pieces,
    source,
    pattern_in,
    region_in,
    law_in,
    curl_hbm,
    out,
    halo,
    pattern,
    region_ids,
    law,
    later_curl,
    timed,
    densities,
    small_sems,
    curl_sem,
    *sums,
):
    tile_count, links, tile, comps = curl_hbm.shape
    early = first_curl.shape[0]
    parts_here = out.shape[0]
    fetched = [(pattern_in, pattern), (region_in, region_ids), (law_in, law)]
    small = [
        pltpu.make_async_copy(src, dst, small_sems.at[i]) for i, (src, dst) in enumerate(fetched)
    ]
    rest = pltpu.make_async_copy(curl_hbm.at[early:], later_curl, curl_sem)
    for copy in small + [rest]:
        copy.start()
    for total in sums:
        total[...] = jnp.zeros_like(total)
    stacked = jnp.concatenate([window[...]] * 3, axis=0)
    samples = jnp.dot(pieces[...], stacked, preferred_element_type=jnp.float32)
    high = samples.astype(jnp.bfloat16)
    timed[:HALF, :] = high
    timed[HALF:, :] = (samples - high.astype(jnp.float32)).astype(jnp.bfloat16)
    columns = [
        jnp.broadcast_to(table[:, part : part + 1], (HALF, comps)) for part in range(parts_here)
    ]
    for copy in small:
        copy.wait()
    places = [[pattern[link, elem] for link in range(links)] for elem in range(tile_count)]

    def blocks(elem):
        curl = first_curl[elem] if elem < early else later_curl[elem - early]
        return curl.reshape(links * tile, comps)

    def find_density(elem):
        picked = jnp.concatenate(
            [timed[:, pl.ds(pl.multiple_of(at * tile, tile), tile)] for at in places[elem]], axis=1
        )
        split = jnp.dot(picked, blocks(elem), preferred_element_type=jnp.float32)
        densities[elem] = split[:HALF] + split[HALF:]

    def project(elem):
        density = densities[elem]
        comp = [density[:, c * tile : (c + 1) * tile] for c in range(comps // tile)]
        square = comp[0] * comp[0]
        for c in comp[1:]:
            square = square + c * c
        region = region_ids[elem]
        reluct = law[0, region] + law[2, region] * square / (square + law[1, region])
        field = jnp.concatenate([reluct * c for c in comp], axis=1)
        rows = [jnp.sum(column * field, axis=0, keepdims=True) for column in columns]
        return (jnp.concatenate(rows, axis=0) * (4.0 / SAMPLES)).astype(jnp.bfloat16)

    def contribute(elem, projected):
        contrib = lax.dot_general(
            projected, blocks(elem), (((1,), (1,)), ((), ())), preferred_element_type=jnp.float32
        )
        for link, at in enumerate(places[elem]):
            sums[link][at] += contrib[:, link * tile : (link + 1) * tile]

    step = 1
    chunks = [range(at, min(at + step, tile_count)) for at in range(0, tile_count, step)]
    projected = {}
    for turn in range(len(chunks) + 2):
        if turn < len(chunks):
            if early in chunks[turn]:
                rest.wait()
            for elem in chunks[turn]:
                find_density(elem)
        if 0 <= turn - 1 < len(chunks):
            for elem in chunks[turn - 1]:
                projected[elem] = project(elem)
        if 0 <= turn - 2:
            for elem in chunks[turn - 2]:
                contribute(elem, projected[elem])

    def window_sum(w):
        total = sums[0][w]
        for other in sums[1:]:
            total = total + other[w]
        return total

    for w in range(tile_count):
        at = slice(w * tile, (w + 1) * tile)
        out[:, at] = window_sum(w + 1) - source[:, at]
    halo[:, :tile] = window_sum(0)
    halo[:, tile:] = window_sum(tile_count + 1)


def halo_kernel(own, from_right, from_left, out):
    tile = from_left.shape[1] // 2
    out[...] = own[...]
    out[:, :tile] += from_left[:, tile:]
    out[:, -tile:] += from_right[:, :tile]


def per_device(coeffs, curl_tiles, pattern, region_ids, material_law, source):
    parts_here = coeffs.shape[0]
    tile_count, links, tile, comps = curl_tiles.shape
    chips, cores, samp = (lax.axis_size(axis) for axis in GROUP)
    group_size = chips * cores * samp
    parts = parts_here * group_size
    table = half_table(parts)
    order = arrival_order(chips, cores, samp, parts_here)
    pieces = jnp.asarray(bf16_pieces(table[:, order].transpose(1, 0, 2)))
    own_columns = jnp.asarray(
        table.reshape(HALF, group_size, parts_here).transpose(1, 0, 2).astype(np.float32)
    )
    vmem, hbm = pl.BlockSpec(memory_space=pltpu.VMEM), pl.BlockSpec(memory_space=pltpu.HBM)

    def in_vmem(array):
        return pltpu.with_memory_space_constraint(array, pltpu.VMEM)

    def in_hbm(array):
        return pltpu.with_memory_space_constraint(array, pltpu.HBM)

    early = 3 * tile_count // 8
    operands = [
        curl_tiles,
        own_columns,
        pieces,
        source,
        pattern.T,
        region_ids,
        material_law,
    ]
    shapes = [
        (early,) + curl_tiles.shape[1:],
        own_columns.shape[1:],
        pieces.shape[1:],
    ] + [operand.shape for operand in operands[3:]]
    fetched = pl.pallas_call(
        fetch_kernel,
        out_shape=[pltpu.VMEM(shape, o.dtype) for shape, o in zip(shapes, operands)],
        in_specs=[hbm] * len(operands),
        out_specs=[vmem] * len(operands),
        scratch_shapes=[pltpu.SemaphoreType.DMA((len(operands),))],
        compiler_params=pltpu.CompilerParams(vmem_limit_bytes=16 * MIB),
        cost_estimate=pl.CostEstimate(
            flops=0, bytes_accessed=4 * early * links * tile * comps, transcendentals=0
        ),
        name="fetch_operands",
    )(*[in_hbm(operand) for operand in operands])
    first_curl, columns_here, pieces_here, *others = fetched

    copies = jnp.broadcast_to(coeffs[None], (chips * samp,) + coeffs.shape)
    near = lax.all_to_all(copies, ("chip", "samp"), 0, 0)
    near, first_curl = lax.optimization_barrier((near, first_curl))
    edges = jnp.concatenate([near[..., :tile], near[..., -tile:]], axis=-1)
    blocks = []
    for step in range(cores):
        right, left = from_neighbours(edges, tile, step)
        middle = across(near, step, 0) if step else near
        blocks.append(jnp.concatenate([left, middle, right], axis=-1))
    window = jnp.concatenate(blocks, axis=0).reshape(parts, -1)
    own, halo = pl.pallas_call(
        shard_kernel,
        out_shape=(
            pltpu.VMEM(source.shape, jnp.float32),
            pltpu.VMEM((parts_here, 2 * tile), jnp.float32),
        ),
        in_specs=[vmem] * 8 + [hbm],
        out_specs=(vmem, vmem),
        scratch_shapes=[
            pltpu.SMEM((links, tile_count), jnp.int32),
            pltpu.SMEM(region_ids.shape, jnp.int32),
            pltpu.SMEM(material_law.shape, jnp.float32),
            pltpu.VMEM((tile_count - early,) + curl_tiles.shape[1:], curl_tiles.dtype),
            pltpu.VMEM((SAMPLES, (tile_count + 2) * tile), jnp.bfloat16),
            pltpu.VMEM((tile_count, HALF, comps), jnp.float32),
            pltpu.SemaphoreType.DMA((3,)),
            pltpu.SemaphoreType.DMA,
        ]
        + [pltpu.VMEM((tile_count + 2, parts_here, tile), jnp.float32)] * links,
        compiler_params=pltpu.CompilerParams(vmem_limit_bytes=32 * MIB),
        cost_estimate=pl.CostEstimate(
            flops=4 * SAMPLES * tile_count * links * tile * comps,
            bytes_accessed=2 * curl_tiles.size,
            transcendentals=0,
        ),
        name="shard_residual",
    )(
        in_vmem(window),
        *[in_vmem(array) for array in (first_curl, columns_here, pieces_here, *others)],
        in_hbm(curl_tiles),
    )
    if lax.axis_size("space") == 2:
        beside = [across(halo, 0, 1)] * 2
    else:
        beside = [across(halo, 0, -1), across(halo, 0, 1)]
    return pl.pallas_call(
        halo_kernel,
        out_shape=jax.ShapeDtypeStruct(source.shape, jnp.float32),
        in_specs=[vmem] * 3,
        out_specs=vmem,
        compiler_params=pltpu.CompilerParams(vmem_limit_bytes=16 * MIB),
        name="halo_sum",
    )(in_vmem(own), *beside)


def solution(mesh):
    at = mesh.axis_names.index("harm")
    harm = mesh.shape["harm"]
    cores = 2 if harm % 2 == 0 else 1
    sizes = mesh.devices.shape
    split = jax.sharding.Mesh(
        mesh.devices.reshape(sizes[:at] + (harm // cores, cores) + sizes[at + 1 :]),
        mesh.axis_names[:at] + ("chip", "core") + mesh.axis_names[at + 1 :],
    )
    placed = (
        P(GROUP, "space"),
        P("space", None, None, None),
        P("space", None),
        P("space"),
        P(),
        P(GROUP, "space"),
    )
    return jax.shard_map(
        per_device,
        mesh=split,
        in_specs=placed,
        out_specs=P(GROUP, "space"),
        check_vma=False,
    )
```

```python
import math

import jax
import jax.numpy as jnp
import ml_dtypes
import numpy as np
from jax import lax
from jax.experimental import pallas as pl
from jax.experimental.pallas import tpu as pltpu
from jax.sharding import PartitionSpec as P

SAMPLES = 64
HALF = SAMPLES // 2
GROUP = ("harm", "samp")
MIB = 1024 * 1024


def half_table(parts):
    sample_ids = np.arange(HALF)[:, None]
    part_ids = np.arange(parts)[None, :]
    phase = ((2 * (part_ids // 2) + 1) * sample_ids % SAMPLES) * (2.0 * math.pi / SAMPLES)
    return np.where(part_ids % 2 == 0, np.cos(phase), np.sin(phase))


def bf16_pieces(table):
    rest = table
    pieces = []
    for _ in range(3):
        piece = rest.astype(ml_dtypes.bfloat16)
        pieces.append(piece)
        rest = rest - piece.astype(np.float64)
    return np.concatenate(pieces, axis=-1)


def shifted(array, axis, by):
    count = lax.axis_size(axis)
    return lax.ppermute(array, axis, [(i, (i + by) % count) for i in range(count)])


def from_neighbours(array, tile):
    if lax.axis_size("space") == 2:
        other = shifted(array, "space", 1)
        return other[:, :tile], other[:, -tile:]
    return shifted(array[:, :tile], "space", -1), shifted(array[:, -tile:], "space", 1)


def fetch_kernel(*refs):
    count = (len(refs) - 1) // 2
    sources, targets, sems = refs[:count], refs[count : 2 * count], refs[-1]
    rank = lax.axis_index(GROUP)
    sources = (sources[0].at[: targets[0].shape[0]], sources[1].at[rank]) + sources[2:]
    copies = [
        pltpu.make_async_copy(source, target, sems.at[i])
        for i, (source, target) in enumerate(zip(sources, targets))
    ]
    for copy in copies:
        copy.start()
    for copy in copies:
        copy.wait()


def shard_kernel(
    window,
    first_curl,
    table,
    pieces,
    source,
    pattern_in,
    region_in,
    law_in,
    curl_hbm,
    out,
    halo,
    pattern,
    region_ids,
    law,
    later_curl,
    timed,
    densities,
    totals,
    small_sems,
    curl_sem,
):
    tile_count, links, tile, comps = curl_hbm.shape
    early = first_curl.shape[0]
    parts_here = out.shape[0]
    slots = links * parts_here
    fetched = [(pattern_in, pattern), (region_in, region_ids), (law_in, law)]
    small = [
        pltpu.make_async_copy(src, dst, small_sems.at[i]) for i, (src, dst) in enumerate(fetched)
    ]
    rest = pltpu.make_async_copy(curl_hbm.at[early:], later_curl, curl_sem)
    for copy in small + [rest]:
        copy.start()
    stacked = jnp.concatenate([window[...]] * 3, axis=0)
    samples = jnp.dot(pieces[...], stacked, preferred_element_type=jnp.float32)
    high = samples.astype(jnp.bfloat16)
    timed[:HALF, :] = high
    timed[HALF:, :] = (samples - high.astype(jnp.float32)).astype(jnp.bfloat16)
    columns = [
        jnp.broadcast_to(table[:, part : part + 1], (HALF, comps)) for part in range(parts_here)
    ]
    for copy in small:
        copy.wait()
    places = [[pattern[link, elem] for link in range(links)] for elem in range(tile_count)]

    def blocks(elem):
        curl = first_curl[elem] if elem < early else later_curl[elem - early]
        return curl.reshape(links * tile, comps)

    def find_density(elem):
        picked = jnp.concatenate(
            [timed[:, pl.ds(pl.multiple_of(at * tile, tile), tile)] for at in places[elem]], axis=1
        )
        split = jnp.dot(picked, blocks(elem), preferred_element_type=jnp.float32)
        densities[elem] = split[:HALF] + split[HALF:]

    def project(elem):
        density = densities[elem]
        comp = [density[:, c * tile : (c + 1) * tile] for c in range(comps // tile)]
        square = comp[0] * comp[0]
        for c in comp[1:]:
            square = square + c * c
        region = region_ids[elem]
        reluct = law[0, region] + law[2, region] * square / (square + law[1, region])
        field = jnp.concatenate([reluct * c for c in comp], axis=1)
        rows = [jnp.sum(column * field, axis=0, keepdims=True) for column in columns]
        return jnp.concatenate(rows * links, axis=0) * (4.0 / SAMPLES)

    def contribute(elem, projected):
        empty = jnp.zeros_like(projected)
        spread = [projected if other == elem else empty for other in range(tile_count)]
        spread = jnp.concatenate(spread, axis=0).astype(jnp.bfloat16)
        contrib = lax.dot_general(
            blocks(elem), spread, (((1,), (1,)), ((), ())), preferred_element_type=jnp.float32
        )
        if elem:
            totals[...] += contrib
        else:
            totals[...] = contrib

    step = 1
    chunks = [range(at, min(at + step, tile_count)) for at in range(0, tile_count, step)]
    projected = {}
    for turn in range(len(chunks) + 2):
        if turn < len(chunks):
            if early in chunks[turn]:
                rest.wait()
            for elem in chunks[turn]:
                find_density(elem)
        if 0 <= turn - 1 < len(chunks):
            for elem in chunks[turn - 1]:
                projected[elem] = project(elem)
        if 0 <= turn - 2:
            for elem in chunks[turn - 2]:
                contribute(elem, projected[elem])

    width = tile_count * slots
    column = lax.broadcasted_iota(jnp.int32, (tile, width), 1)
    kept = jnp.zeros((tile, width), jnp.float32)
    for link in range(links):
        block = totals[link * tile : (link + 1) * tile, :]
        kept = jnp.where(column % slots // parts_here == link, block, kept)
    kept_pieces = []
    for _ in range(3):
        piece = kept.astype(jnp.bfloat16)
        kept_pieces.append(piece)
        kept = kept - piece.astype(jnp.float32)
    rows_out = (tile_count + 2) * parts_here
    row = lax.broadcasted_iota(jnp.int32, (rows_out, width), 0)
    column = lax.broadcasted_iota(jnp.int32, (rows_out, width), 1)
    target = jnp.full((1, width), -1, jnp.int32)
    lane = lax.broadcasted_iota(jnp.int32, (1, width), 1) // parts_here
    for elem in range(tile_count):
        for link in range(links):
            target = jnp.where(lane == elem * links + link, places[elem][link], target)
    hits = (target * parts_here + column % parts_here == row).astype(jnp.bfloat16)
    sums = lax.dot_general(
        jnp.concatenate([hits] * 3, axis=1),
        jnp.concatenate(kept_pieces, axis=1),
        (((1,), (1,)), ((), ())),
        preferred_element_type=jnp.float32,
    )

    def window_sum(w):
        return sums[w * parts_here : (w + 1) * parts_here]

    for w in range(tile_count):
        at = slice(w * tile, (w + 1) * tile)
        out[:, at] = window_sum(w + 1) - source[:, at]
    halo[:, :tile] = window_sum(0)
    halo[:, tile:] = window_sum(tile_count + 1)


def halo_kernel(own, from_right, from_left, out):
    tile = from_left.shape[1] // 2
    out[...] = own[...]
    out[:, :tile] += from_left[:, tile:]
    out[:, -tile:] += from_right[:, :tile]


def per_device(coeffs, curl_tiles, pattern, region_ids, material_law, source):
    parts_here = coeffs.shape[0]
    tile_count, links, tile, comps = curl_tiles.shape
    group_size = lax.axis_size(GROUP)
    parts = parts_here * group_size
    table = half_table(parts)
    pieces = jnp.asarray(bf16_pieces(table))
    own_columns = jnp.asarray(
        table.reshape(HALF, group_size, parts_here).transpose(1, 0, 2).astype(np.float32)
    )
    vmem, hbm = pl.BlockSpec(memory_space=pltpu.VMEM), pl.BlockSpec(memory_space=pltpu.HBM)

    def in_vmem(array):
        return pltpu.with_memory_space_constraint(array, pltpu.VMEM)

    def in_hbm(array):
        return pltpu.with_memory_space_constraint(array, pltpu.HBM)

    early = 3 * tile_count // 8
    operands = [
        curl_tiles,
        own_columns,
        coeffs,
        pieces,
        source,
        pattern.T,
        region_ids,
        material_law,
    ]
    shapes = [
        (early,) + curl_tiles.shape[1:],
        own_columns.shape[1:],
    ] + [operand.shape for operand in operands[2:]]
    fetched = pl.pallas_call(
        fetch_kernel,
        out_shape=[pltpu.VMEM(shape, o.dtype) for shape, o in zip(shapes, operands)],
        in_specs=[hbm] * len(operands),
        out_specs=[vmem] * len(operands),
        scratch_shapes=[pltpu.SemaphoreType.DMA((len(operands),))],
        compiler_params=pltpu.CompilerParams(vmem_limit_bytes=16 * MIB),
        cost_estimate=pl.CostEstimate(
            flops=0, bytes_accessed=4 * early * links * tile * comps, transcendentals=0
        ),
        name="fetch_operands",
    )(*[in_hbm(operand) for operand in operands])
    first_curl, columns_here, coeffs_here, pieces_here, *others = fetched

    right, left = from_neighbours(coeffs, tile)
    block = jnp.concatenate([left, coeffs_here, right], axis=1)
    copies = jnp.broadcast_to(block[None], (group_size,) + block.shape)
    window = lax.all_to_all(copies, GROUP, 0, 0).reshape(parts, block.shape[1])
    own, halo = pl.pallas_call(
        shard_kernel,
        out_shape=(
            pltpu.VMEM(source.shape, jnp.float32),
            pltpu.VMEM((parts_here, 2 * tile), jnp.float32),
        ),
        in_specs=[vmem] * 8 + [hbm],
        out_specs=(vmem, vmem),
        scratch_shapes=[
            pltpu.SMEM((links, tile_count), jnp.int32),
            pltpu.SMEM(region_ids.shape, jnp.int32),
            pltpu.SMEM(material_law.shape, jnp.float32),
            pltpu.VMEM((tile_count - early,) + curl_tiles.shape[1:], curl_tiles.dtype),
            pltpu.VMEM((SAMPLES, (tile_count + 2) * tile), jnp.bfloat16),
            pltpu.VMEM((tile_count, HALF, comps), jnp.float32),
            pltpu.VMEM((links * tile, tile_count * links * parts_here), jnp.float32),
            pltpu.SemaphoreType.DMA((3,)),
            pltpu.SemaphoreType.DMA,
        ],
        compiler_params=pltpu.CompilerParams(vmem_limit_bytes=32 * MIB),
        cost_estimate=pl.CostEstimate(
            flops=4 * SAMPLES * tile_count * links * tile * comps,
            bytes_accessed=2 * curl_tiles.size,
            transcendentals=0,
        ),
        name="shard_residual",
    )(
        in_vmem(window),
        *[in_vmem(array) for array in (first_curl, columns_here, pieces_here, *others)],
        in_hbm(curl_tiles),
    )
    if lax.axis_size("space") == 2:
        beside = [shifted(halo, "space", 1)] * 2
    else:
        beside = [shifted(halo, "space", -1), shifted(halo, "space", 1)]
    return pl.pallas_call(
        halo_kernel,
        out_shape=jax.ShapeDtypeStruct(source.shape, jnp.float32),
        in_specs=[vmem] * 3,
        out_specs=vmem,
        compiler_params=pltpu.CompilerParams(vmem_limit_bytes=16 * MIB),
        name="halo_sum",
    )(in_vmem(own), *beside)


def solution(mesh):
    placed = (
        P(GROUP, "space"),
        P("space", None, None, None),
        P("space", None),
        P("space"),
        P(),
        P(GROUP, "space"),
    )
    return jax.shard_map(
        per_device,
        mesh=mesh,
        in_specs=placed,
        out_specs=P(GROUP, "space"),
        check_vma=False,
    )
```

```python
import math

import jax
import jax.numpy as jnp
import ml_dtypes
import numpy as np
from jax import lax
from jax.experimental import pallas as pl
from jax.experimental.pallas import tpu as pltpu
from jax.sharding import PartitionSpec as P

SAMPLES = 64
HALF = SAMPLES // 2
GROUP = ("harm", "samp")
MIB = 1024 * 1024
CHUNK = 2


def half_table(parts):
    sample_ids = np.arange(HALF)[:, None]
    part_ids = np.arange(parts)[None, :]
    phase = ((2 * (part_ids // 2) + 1) * sample_ids % SAMPLES) * (2.0 * math.pi / SAMPLES)
    return np.where(part_ids % 2 == 0, np.cos(phase), np.sin(phase))


def bf16_pieces(table):
    rest = table
    pieces = []
    for _ in range(3):
        piece = rest.astype(ml_dtypes.bfloat16)
        pieces.append(piece)
        rest = rest - piece.astype(np.float64)
    return np.concatenate(pieces, axis=-1)


def shifted(array, axis, by):
    count = lax.axis_size(axis)
    return lax.ppermute(array, axis, [(i, (i + by) % count) for i in range(count)])


def from_neighbours(array, tile):
    if lax.axis_size("space") == 2:
        other = shifted(array, "space", 1)
        return other[:, :tile], other[:, -tile:]
    return shifted(array[:, :tile], "space", -1), shifted(array[:, -tile:], "space", 1)


def fetch_kernel(*refs):
    count = (len(refs) - 1) // 2
    sources, targets, sems = refs[:count], refs[count : 2 * count], refs[-1]
    rank = lax.axis_index(GROUP)
    sources = (sources[0].at[: targets[0].shape[0]], sources[1].at[rank]) + sources[2:]
    copies = [
        pltpu.make_async_copy(source, target, sems.at[i])
        for i, (source, target) in enumerate(zip(sources, targets))
    ]
    for copy in copies:
        copy.start()
    for copy in copies:
        copy.wait()


def shard_kernel(
    window,
    first_curl,
    table,
    pieces,
    source,
    pattern_in,
    region_in,
    law_in,
    curl_hbm,
    out,
    halo,
    pattern,
    region_ids,
    law,
    later_curl,
    timed,
    densities,
    totals,
    small_sems,
    curl_sems,
):
    tile_count, links, tile, comps = curl_hbm.shape
    early = first_curl.shape[0]
    parts_here = out.shape[0]
    slots = links * parts_here
    fetched = [(pattern_in, pattern), (region_in, region_ids), (law_in, law)]
    small = [
        pltpu.make_async_copy(src, dst, small_sems.at[i]) for i, (src, dst) in enumerate(fetched)
    ]
    later = {
        elem: pltpu.make_async_copy(
            curl_hbm.at[elem : min(elem + CHUNK, tile_count)],
            later_curl.at[elem - early : min(elem + CHUNK, tile_count) - early],
            curl_sems.at[(elem - early) // CHUNK],
        )
        for elem in range(early, tile_count, CHUNK)
    }
    for copy in small + list(later.values()):
        copy.start()
    stacked = jnp.concatenate([window[...]] * 3, axis=0)
    samples = jnp.dot(pieces[...], stacked, preferred_element_type=jnp.float32)
    high = samples.astype(jnp.bfloat16)
    timed[:HALF, :] = high
    timed[HALF:, :] = (samples - high.astype(jnp.float32)).astype(jnp.bfloat16)
    columns = [
        jnp.broadcast_to(table[:, part : part + 1], (HALF, comps)) for part in range(parts_here)
    ]
    for copy in small:
        copy.wait()
    places = [[pattern[link, elem] for link in range(links)] for elem in range(tile_count)]

    def blocks(elem):
        curl = first_curl[elem] if elem < early else later_curl[elem - early]
        return curl.reshape(links * tile, comps)

    def find_density(elem):
        picked = jnp.concatenate(
            [timed[:, pl.ds(pl.multiple_of(at * tile, tile), tile)] for at in places[elem]], axis=1
        )
        split = jnp.dot(picked, blocks(elem), preferred_element_type=jnp.float32)
        densities[elem] = split[:HALF] + split[HALF:]

    def project(elem):
        density = densities[elem]
        comp = [density[:, c * tile : (c + 1) * tile] for c in range(comps // tile)]
        square = comp[0] * comp[0]
        for c in comp[1:]:
            square = square + c * c
        region = region_ids[elem]
        reluct = law[0, region] + law[2, region] * square / (square + law[1, region])
        field = jnp.concatenate([reluct * c for c in comp], axis=1)
        rows = [jnp.sum(column * field, axis=0, keepdims=True) for column in columns]
        return jnp.concatenate(rows * links, axis=0) * (4.0 / SAMPLES)

    def contribute(elem, projected):
        empty = jnp.zeros_like(projected)
        spread = [projected if other == elem else empty for other in range(tile_count)]
        spread = jnp.concatenate(spread, axis=0).astype(jnp.bfloat16)
        contrib = lax.dot_general(
            blocks(elem), spread, (((1,), (1,)), ((), ())), preferred_element_type=jnp.float32
        )
        if elem:
            totals[...] += contrib
        else:
            totals[...] = contrib

    step = 1
    chunks = [range(at, min(at + step, tile_count)) for at in range(0, tile_count, step)]
    projected = {}
    for turn in range(len(chunks) + 2):
        if turn < len(chunks):
            for elem in chunks[turn]:
                if elem in later:
                    later[elem].wait()
                find_density(elem)
        if 0 <= turn - 1 < len(chunks):
            for elem in chunks[turn - 1]:
                projected[elem] = project(elem)
        if 0 <= turn - 2:
            for elem in chunks[turn - 2]:
                contribute(elem, projected[elem])

    width = tile_count * slots
    column = lax.broadcasted_iota(jnp.int32, (tile, width), 1)
    kept = jnp.zeros((tile, width), jnp.float32)
    for link in range(links):
        block = totals[link * tile : (link + 1) * tile, :]
        kept = jnp.where(column % slots // parts_here == link, block, kept)
    kept_pieces = []
    for _ in range(3):
        piece = kept.astype(jnp.bfloat16)
        kept_pieces.append(piece)
        kept = kept - piece.astype(jnp.float32)
    rows_out = (tile_count + 2) * parts_here
    row = lax.broadcasted_iota(jnp.int32, (rows_out, width), 0)
    column = lax.broadcasted_iota(jnp.int32, (rows_out, width), 1)
    target = jnp.full((1, width), -1, jnp.int32)
    lane = lax.broadcasted_iota(jnp.int32, (1, width), 1) // parts_here
    for elem in range(tile_count):
        for link in range(links):
            target = jnp.where(lane == elem * links + link, places[elem][link], target)
    hits = (target * parts_here + column % parts_here == row).astype(jnp.bfloat16)
    sums = lax.dot_general(
        jnp.concatenate([hits] * 3, axis=1),
        jnp.concatenate(kept_pieces, axis=1),
        (((1,), (1,)), ((), ())),
        preferred_element_type=jnp.float32,
    )

    def window_sum(w):
        return sums[w * parts_here : (w + 1) * parts_here]

    for w in range(tile_count):
        at = slice(w * tile, (w + 1) * tile)
        out[:, at] = window_sum(w + 1) - source[:, at]
    halo[:, :tile] = window_sum(0)
    halo[:, tile:] = window_sum(tile_count + 1)


def halo_kernel(own, from_right, from_left, out):
    tile = from_left.shape[1] // 2
    out[...] = own[...]
    out[:, :tile] += from_left[:, tile:]
    out[:, -tile:] += from_right[:, :tile]


def per_device(coeffs, curl_tiles, pattern, region_ids, material_law, source):
    parts_here = coeffs.shape[0]
    tile_count, links, tile, comps = curl_tiles.shape
    group_size = lax.axis_size(GROUP)
    parts = parts_here * group_size
    table = half_table(parts)
    pieces = jnp.asarray(bf16_pieces(table))
    own_columns = jnp.asarray(
        table.reshape(HALF, group_size, parts_here).transpose(1, 0, 2).astype(np.float32)
    )
    vmem, hbm = pl.BlockSpec(memory_space=pltpu.VMEM), pl.BlockSpec(memory_space=pltpu.HBM)

    def in_vmem(array):
        return pltpu.with_memory_space_constraint(array, pltpu.VMEM)

    def in_hbm(array):
        return pltpu.with_memory_space_constraint(array, pltpu.HBM)

    early = 7 * tile_count // 16
    operands = [
        curl_tiles,
        own_columns,
        coeffs,
        pieces,
        source,
        pattern.T,
        region_ids,
        material_law,
    ]
    shapes = [
        (early,) + curl_tiles.shape[1:],
        own_columns.shape[1:],
    ] + [operand.shape for operand in operands[2:]]
    fetched = pl.pallas_call(
        fetch_kernel,
        out_shape=[pltpu.VMEM(shape, o.dtype) for shape, o in zip(shapes, operands)],
        in_specs=[hbm] * len(operands),
        out_specs=[vmem] * len(operands),
        scratch_shapes=[pltpu.SemaphoreType.DMA((len(operands),))],
        compiler_params=pltpu.CompilerParams(vmem_limit_bytes=16 * MIB),
        cost_estimate=pl.CostEstimate(
            flops=0, bytes_accessed=4 * early * links * tile * comps, transcendentals=0
        ),
        name="fetch_operands",
    )(*[in_hbm(operand) for operand in operands])
    first_curl, columns_here, coeffs_here, pieces_here, *others = fetched

    right, left = from_neighbours(coeffs, tile)
    block = jnp.concatenate([left, coeffs_here, right], axis=1)
    copies = jnp.broadcast_to(block[None], (group_size,) + block.shape)
    window = lax.all_to_all(copies, GROUP, 0, 0).reshape(parts, block.shape[1])
    own, halo = pl.pallas_call(
        shard_kernel,
        out_shape=(
            pltpu.VMEM(source.shape, jnp.float32),
            pltpu.VMEM((parts_here, 2 * tile), jnp.float32),
        ),
        in_specs=[vmem] * 8 + [hbm],
        out_specs=(vmem, vmem),
        scratch_shapes=[
            pltpu.SMEM((links, tile_count), jnp.int32),
            pltpu.SMEM(region_ids.shape, jnp.int32),
            pltpu.SMEM(material_law.shape, jnp.float32),
            pltpu.VMEM((tile_count - early,) + curl_tiles.shape[1:], curl_tiles.dtype),
            pltpu.VMEM((SAMPLES, (tile_count + 2) * tile), jnp.bfloat16),
            pltpu.VMEM((tile_count, HALF, comps), jnp.float32),
            pltpu.VMEM((links * tile, tile_count * links * parts_here), jnp.float32),
            pltpu.SemaphoreType.DMA((3,)),
            pltpu.SemaphoreType.DMA((-((early - tile_count) // CHUNK),)),
        ],
        compiler_params=pltpu.CompilerParams(vmem_limit_bytes=32 * MIB),
        cost_estimate=pl.CostEstimate(
            flops=4 * SAMPLES * tile_count * links * tile * comps,
            bytes_accessed=2 * curl_tiles.size,
            transcendentals=0,
        ),
        name="shard_residual",
    )(
        in_vmem(window),
        *[in_vmem(array) for array in (first_curl, columns_here, pieces_here, *others)],
        in_hbm(curl_tiles),
    )
    if lax.axis_size("space") == 2:
        beside = [shifted(halo, "space", 1)] * 2
    else:
        beside = [shifted(halo, "space", -1), shifted(halo, "space", 1)]
    return pl.pallas_call(
        halo_kernel,
        out_shape=jax.ShapeDtypeStruct(source.shape, jnp.float32),
        in_specs=[vmem] * 3,
        out_specs=vmem,
        compiler_params=pltpu.CompilerParams(vmem_limit_bytes=16 * MIB),
        name="halo_sum",
    )(in_vmem(own), *beside)


def solution(mesh):
    placed = (
        P(GROUP, "space"),
        P("space", None, None, None),
        P("space", None),
        P("space"),
        P(),
        P(GROUP, "space"),
    )
    return jax.shard_map(
        per_device,
        mesh=mesh,
        in_specs=placed,
        out_specs=P(GROUP, "space"),
        check_vma=False,
    )
```

```python
import math

import jax
import jax.numpy as jnp
import ml_dtypes
import numpy as np
from jax import lax
from jax.experimental import pallas as pl
from jax.experimental.pallas import tpu as pltpu
from jax.sharding import PartitionSpec as P

SAMPLES = 64
HALF = SAMPLES // 2
GROUP = ("chip", "core", "samp")
MIB = 1024 * 1024


def half_table(parts):
    sample_ids = np.arange(HALF)[:, None]
    part_ids = np.arange(parts)[None, :]
    phase = ((2 * (part_ids // 2) + 1) * sample_ids % SAMPLES) * (2.0 * math.pi / SAMPLES)
    return np.where(part_ids % 2 == 0, np.cos(phase), np.sin(phase))


def bf16_pieces(table):
    rest = table
    pieces = []
    for _ in range(3):
        piece = rest.astype(ml_dtypes.bfloat16)
        pieces.append(piece)
        rest = rest - piece.astype(np.float64)
    return np.concatenate(pieces, axis=-1)


def shifted(array, axis, by):
    count = lax.axis_size(axis)
    return lax.ppermute(array, axis, [(i, (i + by) % count) for i in range(count)])


def from_neighbours(array, tile):
    if lax.axis_size("space") == 2:
        other = shifted(array, "space", 1)
        return other[:, :tile], other[:, -tile:]
    return shifted(array[:, :tile], "space", -1), shifted(array[:, -tile:], "space", 1)


def arrival_order(chips, cores, samp, parts_here):
    ranks = [
        [
            (chip * cores + (c - step) % cores) * samp + s
            for step in range(cores)
            for chip in range(chips)
            for s in range(samp)
        ]
        for c in range(cores)
    ]
    rows = np.array(ranks)[:, :, None] * parts_here + np.arange(parts_here)
    return rows.reshape(cores, -1)


def fetch_kernel(*refs):
    count = (len(refs) - 1) // 2
    sources, targets, sems = refs[:count], refs[count : 2 * count], refs[-1]
    first = sources[0].at[: targets[0].shape[0]]
    own_columns = sources[1].at[lax.axis_index(GROUP)]
    sources = (first, own_columns, sources[2].at[lax.axis_index("core")]) + sources[3:]
    copies = [
        pltpu.make_async_copy(source, target, sems.at[i])
        for i, (source, target) in enumerate(zip(sources, targets))
    ]
    for copy in copies:
        copy.start()
    for copy in copies:
        copy.wait()


def shard_kernel(
    window,
    first_curl,
    table,
    pieces,
    source,
    pattern_in,
    region_in,
    law_in,
    curl_hbm,
    out,
    halo,
    pattern,
    region_ids,
    law,
    later_curl,
    timed,
    densities,
    totals,
    small_sems,
    curl_sem,
):
    tile_count, links, tile, comps = curl_hbm.shape
    early = first_curl.shape[0]
    parts_here = out.shape[0]
    slots = links * parts_here
    fetched = [(pattern_in, pattern), (region_in, region_ids), (law_in, law)]
    small = [
        pltpu.make_async_copy(src, dst, small_sems.at[i]) for i, (src, dst) in enumerate(fetched)
    ]
    rest = pltpu.make_async_copy(curl_hbm.at[early:], later_curl, curl_sem)
    for copy in small + [rest]:
        copy.start()
    stacked = jnp.concatenate([window[...]] * 3, axis=0)
    samples = jnp.dot(pieces[...], stacked, preferred_element_type=jnp.float32)
    high = samples.astype(jnp.bfloat16)
    timed[:HALF, :] = high
    timed[HALF:, :] = (samples - high.astype(jnp.float32)).astype(jnp.bfloat16)
    columns = [
        jnp.broadcast_to(table[:, part : part + 1], (HALF, comps)) for part in range(parts_here)
    ]
    for copy in small:
        copy.wait()
    places = [[pattern[link, elem] for link in range(links)] for elem in range(tile_count)]

    def blocks(elem):
        curl = first_curl[elem] if elem < early else later_curl[elem - early]
        return curl.reshape(links * tile, comps)

    def picked(elem):
        return jnp.concatenate(
            [timed[:, pl.ds(pl.multiple_of(at * tile, tile), tile)] for at in places[elem]], axis=1
        )

    def product(left, right):
        return jnp.dot(left, right, preferred_element_type=jnp.float32)

    def find_densities(one, two):
        cut, rest = 2 * tile, comps - 2 * tile
        samples_one, samples_two = picked(one), picked(two)
        curl_one, curl_two = blocks(one), blocks(two)
        shared = product(
            jnp.concatenate([samples_one, samples_two], axis=0),
            jnp.concatenate([curl_one[:, cut:], curl_two[:, :rest]], axis=1),
        )
        split_one = product(samples_one, curl_one[:, :cut])
        split_two = product(samples_two, curl_two[:, rest:])
        densities[one, :, :cut] = split_one[:HALF] + split_one[HALF:]
        densities[one, :, cut:] = shared[:HALF, :rest] + shared[HALF : 2 * HALF, :rest]
        densities[two, :, :rest] = shared[2 * HALF : 3 * HALF, rest:] + shared[3 * HALF :, rest:]
        densities[two, :, rest:] = split_two[:HALF] + split_two[HALF:]

    def project(elem):
        density = densities[elem]
        comp = [density[:, c * tile : (c + 1) * tile] for c in range(comps // tile)]
        square = comp[0] * comp[0]
        for c in comp[1:]:
            square = square + c * c
        region = region_ids[elem]
        reluct = law[0, region] + law[2, region] * square / (square + law[1, region])
        field = jnp.concatenate([reluct * c for c in comp], axis=1)
        rows = [jnp.sum(column * field, axis=0, keepdims=True) for column in columns]
        return jnp.concatenate(rows * links, axis=0) * (4.0 / SAMPLES)

    def contribute(one, two, rows_one, rows_two):
        empty = jnp.zeros_like(rows_one)
        spread = [
            jnp.concatenate([rows_one if e == one else empty, rows_two if e == two else empty], 1)
            for e in range(tile_count)
        ]
        contrib = lax.dot_general(
            jnp.concatenate([blocks(one), blocks(two)], axis=1),
            jnp.concatenate(spread, axis=0).astype(jnp.bfloat16),
            (((1,), (1,)), ((), ())),
            preferred_element_type=jnp.float32,
        )
        if one:
            totals[...] += contrib
        else:
            totals[...] = contrib

    pairs = [(at, at + 1) for at in range(0, tile_count, 2)]
    projected = {}
    for turn in range(len(pairs) + 2):
        if turn < len(pairs):
            if early in pairs[turn]:
                rest.wait()
            find_densities(*pairs[turn])
        if 0 <= turn - 1 < len(pairs):
            projected[turn - 1] = [project(elem) for elem in pairs[turn - 1]]
        if 0 <= turn - 2:
            contribute(*pairs[turn - 2], *projected[turn - 2])

    width = tile_count * slots
    column = lax.broadcasted_iota(jnp.int32, (tile, width), 1)
    kept = jnp.zeros((tile, width), jnp.float32)
    for link in range(links):
        block = totals[link * tile : (link + 1) * tile, :]
        kept = jnp.where(column % slots // parts_here == link, block, kept)
    kept_pieces = []
    for _ in range(3):
        piece = kept.astype(jnp.bfloat16)
        kept_pieces.append(piece)
        kept = kept - piece.astype(jnp.float32)
    rows_out = (tile_count + 2) * parts_here
    row = lax.broadcasted_iota(jnp.int32, (rows_out, width), 0)
    column = lax.broadcasted_iota(jnp.int32, (rows_out, width), 1)
    target = jnp.full((1, width), -1, jnp.int32)
    lane = lax.broadcasted_iota(jnp.int32, (1, width), 1) // parts_here
    for elem in range(tile_count):
        for link in range(links):
            target = jnp.where(lane == elem * links + link, places[elem][link], target)
    hits = (target * parts_here + column % parts_here == row).astype(jnp.bfloat16)
    sums = lax.dot_general(
        jnp.concatenate([hits] * 3, axis=1),
        jnp.concatenate(kept_pieces, axis=1),
        (((1,), (1,)), ((), ())),
        preferred_element_type=jnp.float32,
    )

    def window_sum(w):
        return sums[w * parts_here : (w + 1) * parts_here]

    for w in range(tile_count):
        at = slice(w * tile, (w + 1) * tile)
        out[:, at] = window_sum(w + 1) - source[:, at]
    halo[:, :tile] = window_sum(0)
    halo[:, tile:] = window_sum(tile_count + 1)


def halo_kernel(own, from_right, from_left, out):
    tile = from_left.shape[1] // 2
    out[...] = own[...]
    out[:, :tile] += from_left[:, tile:]
    out[:, -tile:] += from_right[:, :tile]


def per_device(coeffs, curl_tiles, pattern, region_ids, material_law, source):
    parts_here = coeffs.shape[0]
    tile_count, links, tile, comps = curl_tiles.shape
    chips, cores, samp = (lax.axis_size(axis) for axis in GROUP)
    group_size = chips * cores * samp
    parts = parts_here * group_size
    table = half_table(parts)
    order = arrival_order(chips, cores, samp, parts_here)
    pieces = jnp.asarray(bf16_pieces(table[:, order].transpose(1, 0, 2)))
    own_columns = jnp.asarray(
        table.reshape(HALF, group_size, parts_here).transpose(1, 0, 2).astype(np.float32)
    )
    vmem, hbm = pl.BlockSpec(memory_space=pltpu.VMEM), pl.BlockSpec(memory_space=pltpu.HBM)

    def in_vmem(array):
        return pltpu.with_memory_space_constraint(array, pltpu.VMEM)

    def in_hbm(array):
        return pltpu.with_memory_space_constraint(array, pltpu.HBM)

    early = 3 * tile_count // 8
    operands = [
        curl_tiles,
        own_columns,
        pieces,
        coeffs,
        source,
        pattern.T,
        region_ids,
        material_law,
    ]
    shapes = [
        (early,) + curl_tiles.shape[1:],
        own_columns.shape[1:],
        pieces.shape[1:],
    ] + [operand.shape for operand in operands[3:]]
    fetched = pl.pallas_call(
        fetch_kernel,
        out_shape=[pltpu.VMEM(shape, o.dtype) for shape, o in zip(shapes, operands)],
        in_specs=[hbm] * len(operands),
        out_specs=[vmem] * len(operands),
        scratch_shapes=[pltpu.SemaphoreType.DMA((len(operands),))],
        compiler_params=pltpu.CompilerParams(vmem_limit_bytes=16 * MIB),
        cost_estimate=pl.CostEstimate(
            flops=0, bytes_accessed=4 * early * links * tile * comps, transcendentals=0
        ),
        name="fetch_operands",
    )(*[in_hbm(operand) for operand in operands])
    first_curl, columns_here, pieces_here, coeffs_here, *others = fetched

    right, left = from_neighbours(coeffs, tile)
    block = jnp.concatenate([left, coeffs_here, right], axis=1)
    copies = jnp.broadcast_to(block[None], (chips * samp,) + block.shape)
    near = lax.all_to_all(copies, ("chip", "samp"), 0, 0)
    rows = [near] + [shifted(near, "core", step) for step in range(1, cores)]
    window = jnp.concatenate(rows, axis=0).reshape(parts, block.shape[1])
    own, halo = pl.pallas_call(
        shard_kernel,
        out_shape=(
            pltpu.VMEM(source.shape, jnp.float32),
            pltpu.VMEM((parts_here, 2 * tile), jnp.float32),
        ),
        in_specs=[vmem] * 8 + [hbm],
        out_specs=(vmem, vmem),
        scratch_shapes=[
            pltpu.SMEM((links, tile_count), jnp.int32),
            pltpu.SMEM(region_ids.shape, jnp.int32),
            pltpu.SMEM(material_law.shape, jnp.float32),
            pltpu.VMEM((tile_count - early,) + curl_tiles.shape[1:], curl_tiles.dtype),
            pltpu.VMEM((SAMPLES, (tile_count + 2) * tile), jnp.bfloat16),
            pltpu.VMEM((tile_count, HALF, comps), jnp.float32),
            pltpu.VMEM((links * tile, tile_count * links * parts_here), jnp.float32),
            pltpu.SemaphoreType.DMA((3,)),
            pltpu.SemaphoreType.DMA,
        ],
        compiler_params=pltpu.CompilerParams(vmem_limit_bytes=32 * MIB),
        cost_estimate=pl.CostEstimate(
            flops=4 * SAMPLES * tile_count * links * tile * comps,
            bytes_accessed=2 * curl_tiles.size,
            transcendentals=0,
        ),
        name="shard_residual",
    )(
        in_vmem(window),
        *[in_vmem(array) for array in (first_curl, columns_here, pieces_here, *others)],
        in_hbm(curl_tiles),
    )
    if lax.axis_size("space") == 2:
        beside = [shifted(halo, "space", 1)] * 2
    else:
        beside = [shifted(halo, "space", -1), shifted(halo, "space", 1)]
    return pl.pallas_call(
        halo_kernel,
        out_shape=jax.ShapeDtypeStruct(source.shape, jnp.float32),
        in_specs=[vmem] * 3,
        out_specs=vmem,
        compiler_params=pltpu.CompilerParams(vmem_limit_bytes=16 * MIB),
        name="halo_sum",
    )(in_vmem(own), *beside)


def solution(mesh):
    at = mesh.axis_names.index("harm")
    harm = mesh.shape["harm"]
    cores = 2 if harm % 2 == 0 else 1
    sizes = mesh.devices.shape
    split = jax.sharding.Mesh(
        mesh.devices.reshape(sizes[:at] + (harm // cores, cores) + sizes[at + 1 :]),
        mesh.axis_names[:at] + ("chip", "core") + mesh.axis_names[at + 1 :],
    )
    placed = (
        P(GROUP, "space"),
        P("space", None, None, None),
        P("space", None),
        P("space"),
        P(),
        P(GROUP, "space"),
    )
    return jax.shard_map(
        per_device,
        mesh=split,
        in_specs=placed,
        out_specs=P(GROUP, "space"),
        check_vma=False,
    )
```

```python
import math

import jax
import jax.numpy as jnp
import ml_dtypes
import numpy as np
from jax import lax
from jax.experimental import pallas as pl
from jax.experimental.pallas import tpu as pltpu
from jax.sharding import PartitionSpec as P

SAMPLES = 64
HALF = SAMPLES // 2
GROUP = ("harm", "samp")
MIB = 1024 * 1024


def half_table(parts):
    sample_ids = np.arange(HALF)[:, None]
    part_ids = np.arange(parts)[None, :]
    phase = ((2 * (part_ids // 2) + 1) * sample_ids % SAMPLES) * (2.0 * math.pi / SAMPLES)
    return np.where(part_ids % 2 == 0, np.cos(phase), np.sin(phase))


def bf16_pieces(table):
    rest = table
    pieces = []
    for _ in range(3):
        piece = rest.astype(ml_dtypes.bfloat16)
        pieces.append(piece)
        rest = rest - piece.astype(np.float64)
    return np.concatenate(pieces, axis=-1)


def shifted(array, axis, by):
    count = lax.axis_size(axis)
    return lax.ppermute(array, axis, [(i, (i + by) % count) for i in range(count)])


def from_neighbours(array, tile):
    if lax.axis_size("space") == 2:
        other = shifted(array, "space", 1)
        return other[:, :tile], other[:, -tile:]
    return shifted(array[:, :tile], "space", -1), shifted(array[:, -tile:], "space", 1)


def fetch_kernel(*refs):
    count = (len(refs) - 1) // 2
    sources, targets, sems = refs[:count], refs[count : 2 * count], refs[-1]
    rank = lax.axis_index(GROUP)
    sources = (sources[0].at[rank],) + sources[1:]
    copies = [
        pltpu.make_async_copy(source, target, sems.at[i])
        for i, (source, target) in enumerate(zip(sources, targets))
    ]
    for copy in copies:
        copy.start()
    for copy in copies:
        copy.wait()


def shard_kernel(
    window,
    table,
    pieces,
    source,
    pattern_in,
    region_in,
    law_in,
    curl_hbm,
    out,
    halo,
    pattern,
    region_ids,
    law,
    curl,
    timed,
    small_sems,
    curl_sems,
    *sums,
):
    tile_count, links, tile, comps = curl.shape
    parts_here = out.shape[0]
    fetched = [(pattern_in, pattern), (region_in, region_ids), (law_in, law)]
    small = [
        pltpu.make_async_copy(src, dst, small_sems.at[i]) for i, (src, dst) in enumerate(fetched)
    ]

    def curl_copy(elem):
        return pltpu.make_async_copy(curl_hbm.at[elem], curl.at[elem], curl_sems.at[elem])

    for copy in small + [curl_copy(elem) for elem in range(tile_count)]:
        copy.start()
    for total in sums:
        total[...] = jnp.zeros_like(total)
    stacked = jnp.concatenate([window[...]] * 3, axis=0)
    samples = jnp.dot(pieces[...], stacked, preferred_element_type=jnp.float32)
    high = samples.astype(jnp.bfloat16)
    timed[:HALF, :] = high
    timed[HALF:, :] = (samples - high.astype(jnp.float32)).astype(jnp.bfloat16)
    columns = [
        jnp.broadcast_to(table[:, part : part + 1], (HALF, tile)) for part in range(parts_here)
    ]
    for copy in small:
        copy.wait()

    def blocks(elem):
        return curl[elem].reshape(links * tile, comps)

    def find_density(elem):
        curl_copy(elem).wait()
        picked = jnp.concatenate(
            [
                timed[:, pl.ds(pl.multiple_of(pattern[link, elem] * tile, tile), tile)]
                for link in range(links)
            ],
            axis=1,
        )
        split = jnp.dot(picked, blocks(elem), preferred_element_type=jnp.float32)
        return split[:HALF] + split[HALF:]

    def project(elem, density):
        comp = [density[:, c * tile : (c + 1) * tile] for c in range(comps // tile)]
        square = comp[0] * comp[0]
        for c in comp[1:]:
            square = square + c * c
        region = region_ids[elem]
        reluct = law[0, region] + law[2, region] * square / (square + law[1, region])
        rows = [
            jnp.concatenate(
                [jnp.sum(column * reluct * c, axis=0, keepdims=True) for c in comp], axis=1
            )
            for column in columns
        ]
        return (jnp.concatenate(rows, axis=0) * (4.0 / SAMPLES)).astype(jnp.bfloat16)

    def contribute(elem, projected):
        contrib = lax.dot_general(
            projected, blocks(elem), (((1,), (1,)), ((), ())), preferred_element_type=jnp.float32
        )
        for link in range(links):
            sums[link][pattern[link, elem]] += contrib[:, link * tile : (link + 1) * tile]

    def turn(elem, carry):
        density, projected = carry
        contribute(elem - 2, projected)
        projected = project(elem - 1, density)
        return find_density(elem), projected

    density = find_density(0)
    projected = project(0, density)
    density = find_density(1)
    density, projected = lax.fori_loop(2, tile_count, turn, (density, projected))
    contribute(tile_count - 2, projected)
    contribute(tile_count - 1, project(tile_count - 1, density))

    def window_sum(w):
        total = sums[0][w]
        for other in sums[1:]:
            total = total + other[w]
        return total

    for w in range(tile_count):
        at = slice(w * tile, (w + 1) * tile)
        out[:, at] = window_sum(w + 1) - source[:, at]
    halo[:, :tile] = window_sum(0)
    halo[:, tile:] = window_sum(tile_count + 1)


def halo_kernel(own, from_right, from_left, out):
    tile = from_left.shape[1] // 2
    out[...] = own[...]
    out[:, :tile] += from_left[:, tile:]
    out[:, -tile:] += from_right[:, :tile]


def per_device(coeffs, curl_tiles, pattern, region_ids, material_law, source):
    parts_here = coeffs.shape[0]
    tile_count, links, tile, comps = curl_tiles.shape
    group_size = lax.axis_size(GROUP)
    parts = parts_here * group_size
    table = half_table(parts)
    pieces = jnp.asarray(bf16_pieces(table))
    own_columns = jnp.asarray(
        table.reshape(HALF, group_size, parts_here).transpose(1, 0, 2).astype(np.float32)
    )
    vmem, hbm = pl.BlockSpec(memory_space=pltpu.VMEM), pl.BlockSpec(memory_space=pltpu.HBM)

    def in_vmem(array):
        return pltpu.with_memory_space_constraint(array, pltpu.VMEM)

    def in_hbm(array):
        return pltpu.with_memory_space_constraint(array, pltpu.HBM)

    operands = [
        own_columns,
        coeffs,
        pieces,
        source,
        pattern.T,
        region_ids,
        material_law,
    ]
    shapes = [own_columns.shape[1:]] + [operand.shape for operand in operands[1:]]
    fetched = pl.pallas_call(
        fetch_kernel,
        out_shape=[pltpu.VMEM(shape, o.dtype) for shape, o in zip(shapes, operands)],
        in_specs=[hbm] * len(operands),
        out_specs=[vmem] * len(operands),
        scratch_shapes=[pltpu.SemaphoreType.DMA((len(operands),))],
        compiler_params=pltpu.CompilerParams(vmem_limit_bytes=16 * MIB),
        cost_estimate=pl.CostEstimate(
            flops=0, bytes_accessed=1024 * 1024, transcendentals=0
        ),
        name="fetch_operands",
    )(*[in_hbm(operand) for operand in operands])
    columns_here, coeffs_here, pieces_here, *others = fetched

    right, left = from_neighbours(coeffs, tile)
    block = jnp.concatenate([left, coeffs_here, right], axis=1)
    copies = jnp.broadcast_to(block[None], (group_size,) + block.shape)
    window = lax.all_to_all(copies, GROUP, 0, 0).reshape(parts, block.shape[1])
    own, halo = pl.pallas_call(
        shard_kernel,
        out_shape=(
            pltpu.VMEM(source.shape, jnp.float32),
            pltpu.VMEM((parts_here, 2 * tile), jnp.float32),
        ),
        in_specs=[vmem] * 7 + [hbm],
        out_specs=(vmem, vmem),
        scratch_shapes=[
            pltpu.SMEM((links, tile_count), jnp.int32),
            pltpu.SMEM(region_ids.shape, jnp.int32),
            pltpu.SMEM(material_law.shape, jnp.float32),
            pltpu.VMEM(curl_tiles.shape, curl_tiles.dtype),
            pltpu.VMEM((SAMPLES, (tile_count + 2) * tile), jnp.bfloat16),
            pltpu.SemaphoreType.DMA((3,)),
            pltpu.SemaphoreType.DMA((tile_count,)),
        ]
        + [pltpu.VMEM((tile_count + 2, parts_here, tile), jnp.float32)] * links,
        compiler_params=pltpu.CompilerParams(vmem_limit_bytes=32 * MIB),
        cost_estimate=pl.CostEstimate(
            flops=4 * SAMPLES * tile_count * links * tile * comps,
            bytes_accessed=2 * curl_tiles.size,
            transcendentals=0,
        ),
        name="shard_residual",
    )(
        in_vmem(window),
        *[in_vmem(array) for array in (columns_here, pieces_here, *others)],
        in_hbm(curl_tiles),
    )
    if lax.axis_size("space") == 2:
        beside = [shifted(halo, "space", 1)] * 2
    else:
        beside = [shifted(halo, "space", -1), shifted(halo, "space", 1)]
    return pl.pallas_call(
        halo_kernel,
        out_shape=jax.ShapeDtypeStruct(source.shape, jnp.float32),
        in_specs=[vmem] * 3,
        out_specs=vmem,
        compiler_params=pltpu.CompilerParams(vmem_limit_bytes=16 * MIB),
        name="halo_sum",
    )(in_vmem(own), *beside)


def solution(mesh):
    placed = (
        P(GROUP, "space"),
        P("space", None, None, None),
        P("space", None),
        P("space"),
        P(),
        P(GROUP, "space"),
    )
    return jax.shard_map(
        per_device,
        mesh=mesh,
        in_specs=placed,
        out_specs=P(GROUP, "space"),
        check_vma=False,
    )
```

```python
import math

import jax
import jax.numpy as jnp
import ml_dtypes
import numpy as np
from jax import lax
from jax.experimental import pallas as pl
from jax.experimental.pallas import tpu as pltpu
from jax.sharding import PartitionSpec as P

SAMPLES = 64
HALF = SAMPLES // 2
GROUP = ("harm", "samp")
MIB = 1024 * 1024


def half_table(parts):
    sample_ids = np.arange(HALF)[:, None]
    part_ids = np.arange(parts)[None, :]
    phase = ((2 * (part_ids // 2) + 1) * sample_ids % SAMPLES) * (2.0 * math.pi / SAMPLES)
    return np.where(part_ids % 2 == 0, np.cos(phase), np.sin(phase))


def bf16_pieces(table):
    rest = table
    pieces = []
    for _ in range(3):
        piece = rest.astype(ml_dtypes.bfloat16)
        pieces.append(piece)
        rest = rest - piece.astype(np.float64)
    return np.concatenate(pieces, axis=-1)


def shifted(array, axis, by):
    count = lax.axis_size(axis)
    return lax.ppermute(array, axis, [(i, (i + by) % count) for i in range(count)])


def from_neighbours(array, tile):
    if lax.axis_size("space") == 2:
        other = shifted(array, "space", 1)
        return other[:, :tile], other[:, -tile:]
    return shifted(array[:, :tile], "space", -1), shifted(array[:, -tile:], "space", 1)


def partner(index, step, size):
    return index ^ step if size & (size - 1) == 0 else (index + step) % size


def sender(index, step, size):
    return index ^ step if size & (size - 1) == 0 else (index - step) % size


def exchanged(block, axis):
    size = lax.axis_size(axis)
    blocks = [block]
    for step in range(1, size):
        pairs = [(i, partner(i, step, size)) for i in range(size)]
        blocks.append(lax.ppermute(block, axis, pairs))
    return jnp.concatenate(blocks, axis=0)


def gathered_along(block, axis):
    size = lax.axis_size(axis)
    places = [block] + [None] * (size - 1)
    for step in range(size - 1, 0, -1):
        places[step] = lax.ppermute(block, axis, [(i, i - step) for i in range(step, size)])
    below = [None] * size
    for hop in range(1, size):
        carried = jnp.concatenate(below[size - hop + 1 :] + [block], axis=0)
        arrived = jnp.split(lax.ppermute(carried, axis, [(hop - 1, hop)]), hop, axis=0)
        for place, part in zip(range(size - hop, size), arrived):
            below[place] = part if below[place] is None else below[place] + part
    for step in range(1, size):
        places[step] = places[step] + below[step]
    return jnp.concatenate(places, axis=0)


def arrival_order(harm, samp, parts_here):
    ranks = [
        [
            sender(h, j, harm) * samp + (s + k) % samp
            for j in range(harm)
            for k in range(samp)
        ]
        for h in range(harm)
        for s in range(samp)
    ]
    rows = np.array(ranks)[:, :, None] * parts_here + np.arange(parts_here)
    return rows.reshape(harm * samp, -1)


def fetch_kernel(*refs):
    count = (len(refs) - 1) // 2
    sources, targets, sems = refs[:count], refs[count : 2 * count], refs[-1]
    rank = lax.axis_index(GROUP)
    first = sources[0].at[: targets[0].shape[0]]
    sources = (first, sources[1].at[rank], sources[2].at[rank]) + sources[3:]
    copies = [
        pltpu.make_async_copy(source, target, sems.at[i])
        for i, (source, target) in enumerate(zip(sources, targets))
    ]
    for copy in copies:
        copy.start()
    for copy in copies:
        copy.wait()


def shard_kernel(
    window,
    first_curl,
    table,
    pieces,
    source,
    pattern_in,
    region_in,
    law_in,
    curl_hbm,
    out,
    halo,
    pattern,
    region_ids,
    law,
    later_curl,
    timed,
    densities,
    small_sems,
    curl_sem,
    *sums,
):
    tile_count, links, tile, comps = curl_hbm.shape
    early = first_curl.shape[0]
    parts_here = out.shape[0]
    fetched = [(pattern_in, pattern), (region_in, region_ids), (law_in, law)]
    small = [
        pltpu.make_async_copy(src, dst, small_sems.at[i]) for i, (src, dst) in enumerate(fetched)
    ]
    rest = pltpu.make_async_copy(curl_hbm.at[early:], later_curl, curl_sem)
    for copy in small + [rest]:
        copy.start()
    for total in sums:
        total[...] = jnp.zeros_like(total)
    stacked = jnp.concatenate([window[...]] * 3, axis=0)
    samples = jnp.dot(pieces[...], stacked, preferred_element_type=jnp.float32)
    high = samples.astype(jnp.bfloat16)
    timed[:HALF, :] = high
    timed[HALF:, :] = (samples - high.astype(jnp.float32)).astype(jnp.bfloat16)
    columns = [
        jnp.broadcast_to(table[:, part : part + 1], (HALF, comps)) for part in range(parts_here)
    ]
    for copy in small:
        copy.wait()
    places = [[pattern[link, elem] for link in range(links)] for elem in range(tile_count)]

    def blocks(elem):
        curl = first_curl[elem] if elem < early else later_curl[elem - early]
        return curl.reshape(links * tile, comps)

    def find_density(elem):
        picked = jnp.concatenate(
            [timed[:, pl.ds(pl.multiple_of(at * tile, tile), tile)] for at in places[elem]], axis=1
        )
        split = jnp.dot(picked, blocks(elem), preferred_element_type=jnp.float32)
        densities[elem] = split[:HALF] + split[HALF:]

    def project(elem):
        density = densities[elem]
        comp = [density[:, c * tile : (c + 1) * tile] for c in range(comps // tile)]
        square = comp[0] * comp[0]
        for c in comp[1:]:
            square = square + c * c
        region = region_ids[elem]
        reluct = law[0, region] + law[2, region] * square / (square + law[1, region])
        field = jnp.concatenate([reluct * c for c in comp], axis=1)
        rows = [jnp.sum(column * field, axis=0, keepdims=True) for column in columns]
        return (jnp.concatenate(rows, axis=0) * (4.0 / SAMPLES)).astype(jnp.bfloat16)

    def contribute(elem, projected):
        contrib = lax.dot_general(
            projected, blocks(elem), (((1,), (1,)), ((), ())), preferred_element_type=jnp.float32
        )
        for link, at in enumerate(places[elem]):
            sums[link][at] += contrib[:, link * tile : (link + 1) * tile]

    step = 1
    chunks = [range(at, min(at + step, tile_count)) for at in range(0, tile_count, step)]
    projected = {}
    for turn in range(len(chunks) + 2):
        if turn < len(chunks):
            if early in chunks[turn]:
                rest.wait()
            for elem in chunks[turn]:
                find_density(elem)
        if 0 <= turn - 1 < len(chunks):
            for elem in chunks[turn - 1]:
                projected[elem] = project(elem)
        if 0 <= turn - 2:
            for elem in chunks[turn - 2]:
                contribute(elem, projected[elem])

    def window_sum(w):
        total = sums[0][w]
        for other in sums[1:]:
            total = total + other[w]
        return total

    for w in range(tile_count):
        at = slice(w * tile, (w + 1) * tile)
        out[:, at] = window_sum(w + 1) - source[:, at]
    halo[:, :tile] = window_sum(0)
    halo[:, tile:] = window_sum(tile_count + 1)


def halo_kernel(own, from_right, from_left, out):
    tile = from_left.shape[1] // 2
    out[...] = own[...]
    out[:, :tile] += from_left[:, tile:]
    out[:, -tile:] += from_right[:, :tile]


def per_device(coeffs, curl_tiles, pattern, region_ids, material_law, source):
    parts_here = coeffs.shape[0]
    tile_count, links, tile, comps = curl_tiles.shape
    harm, samp = lax.axis_size("harm"), lax.axis_size("samp")
    parts = parts_here * harm * samp
    table = half_table(parts)[:, arrival_order(harm, samp, parts_here)].transpose(1, 0, 2)
    pieces = jnp.asarray(bf16_pieces(table))
    own_columns = jnp.asarray(table[:, :, :parts_here].astype(np.float32))
    vmem, hbm = pl.BlockSpec(memory_space=pltpu.VMEM), pl.BlockSpec(memory_space=pltpu.HBM)

    def in_vmem(array):
        return pltpu.with_memory_space_constraint(array, pltpu.VMEM)

    def in_hbm(array):
        return pltpu.with_memory_space_constraint(array, pltpu.HBM)

    early = 3 * tile_count // 8
    operands = [
        curl_tiles,
        own_columns,
        pieces,
        coeffs,
        source,
        pattern.T,
        region_ids,
        material_law,
    ]
    shapes = [
        (early,) + curl_tiles.shape[1:],
        own_columns.shape[1:],
        pieces.shape[1:],
    ] + [operand.shape for operand in operands[3:]]
    fetched = pl.pallas_call(
        fetch_kernel,
        out_shape=[pltpu.VMEM(shape, o.dtype) for shape, o in zip(shapes, operands)],
        in_specs=[hbm] * len(operands),
        out_specs=[vmem] * len(operands),
        scratch_shapes=[pltpu.SemaphoreType.DMA((len(operands),))],
        compiler_params=pltpu.CompilerParams(vmem_limit_bytes=16 * MIB),
        cost_estimate=pl.CostEstimate(
            flops=0, bytes_accessed=4 * early * links * tile * comps, transcendentals=0
        ),
        name="fetch_operands",
    )(*[in_hbm(operand) for operand in operands])
    first_curl, columns_here, pieces_here, coeffs_here, *others = fetched

    right, left = from_neighbours(coeffs, tile)
    block = jnp.concatenate([left, coeffs_here, right], axis=1)
    window = exchanged(gathered_along(block[None], "samp"), "harm").reshape(parts, block.shape[1])
    own, halo = pl.pallas_call(
        shard_kernel,
        out_shape=(
            pltpu.VMEM(source.shape, jnp.float32),
            pltpu.VMEM((parts_here, 2 * tile), jnp.float32),
        ),
        in_specs=[vmem] * 8 + [hbm],
        out_specs=(vmem, vmem),
        scratch_shapes=[
            pltpu.SMEM((links, tile_count), jnp.int32),
            pltpu.SMEM(region_ids.shape, jnp.int32),
            pltpu.SMEM(material_law.shape, jnp.float32),
            pltpu.VMEM((tile_count - early,) + curl_tiles.shape[1:], curl_tiles.dtype),
            pltpu.VMEM((SAMPLES, (tile_count + 2) * tile), jnp.bfloat16),
            pltpu.VMEM((tile_count, HALF, comps), jnp.float32),
            pltpu.SemaphoreType.DMA((3,)),
            pltpu.SemaphoreType.DMA,
        ]
        + [pltpu.VMEM((tile_count + 2, parts_here, tile), jnp.float32)] * links,
        compiler_params=pltpu.CompilerParams(vmem_limit_bytes=32 * MIB),
        cost_estimate=pl.CostEstimate(
            flops=4 * SAMPLES * tile_count * links * tile * comps,
            bytes_accessed=2 * curl_tiles.size,
            transcendentals=0,
        ),
        name="shard_residual",
    )(
        in_vmem(window),
        *[in_vmem(array) for array in (first_curl, columns_here, pieces_here, *others)],
        in_hbm(curl_tiles),
    )
    if lax.axis_size("space") == 2:
        beside = [shifted(halo, "space", 1)] * 2
    else:
        beside = [shifted(halo, "space", -1), shifted(halo, "space", 1)]
    return pl.pallas_call(
        halo_kernel,
        out_shape=jax.ShapeDtypeStruct(source.shape, jnp.float32),
        in_specs=[vmem] * 3,
        out_specs=vmem,
        compiler_params=pltpu.CompilerParams(vmem_limit_bytes=16 * MIB),
        name="halo_sum",
    )(in_vmem(own), *beside)


def solution(mesh):
    placed = (
        P(GROUP, "space"),
        P("space", None, None, None),
        P("space", None),
        P("space"),
        P(),
        P(GROUP, "space"),
    )
    return jax.shard_map(
        per_device,
        mesh=mesh,
        in_specs=placed,
        out_specs=P(GROUP, "space"),
        check_vma=False,
    )
```

```python
import math

import jax
import jax.numpy as jnp
import ml_dtypes
import numpy as np
from jax import lax
from jax.experimental import pallas as pl
from jax.experimental.pallas import tpu as pltpu
from jax.sharding import PartitionSpec as P

SAMPLES = 64
HALF = SAMPLES // 2
GROUP = ("harm", "samp")
MIB = 1024 * 1024
LISTED = 4


def half_table(parts):
    sample_ids = np.arange(HALF)[:, None]
    part_ids = np.arange(parts)[None, :]
    phase = ((2 * (part_ids // 2) + 1) * sample_ids % SAMPLES) * (2.0 * math.pi / SAMPLES)
    return np.where(part_ids % 2 == 0, np.cos(phase), np.sin(phase))


def bf16_pieces(table):
    rest = table
    pieces = []
    for _ in range(3):
        piece = rest.astype(ml_dtypes.bfloat16)
        pieces.append(piece)
        rest = rest - piece.astype(np.float64)
    return np.concatenate(pieces, axis=-1)


def shifted(array, axis, by):
    count = lax.axis_size(axis)
    return lax.ppermute(array, axis, [(i, (i + by) % count) for i in range(count)])


def from_neighbours(array, tile):
    if lax.axis_size("space") == 2:
        other = shifted(array, "space", 1)
        return other[:, :tile], other[:, -tile:]
    return shifted(array[:, :tile], "space", -1), shifted(array[:, -tile:], "space", 1)


def fetch_kernel(*refs):
    count = (len(refs) - 1) // 2
    sources, targets, sems = refs[:count], refs[count : 2 * count], refs[-1]
    rank = lax.axis_index(GROUP)
    sources = (sources[0].at[: targets[0].shape[0]], sources[1].at[rank]) + sources[2:]
    copies = [
        pltpu.make_async_copy(source, target, sems.at[i])
        for i, (source, target) in enumerate(zip(sources, targets))
    ]
    for copy in copies:
        copy.start()
    for copy in copies:
        copy.wait()


def curl_copies(curl_hbm, first_curl, later_curl, sem):
    early = first_curl.shape[0]
    links, tile, comps = curl_hbm.shape[1:]
    rest = pltpu.make_async_copy(curl_hbm.at[early:], later_curl, sem)

    def blocks(elem):
        curl = first_curl[elem] if elem < early else later_curl[elem - early]
        return curl.reshape(links * tile, comps)

    return rest, blocks


def weighted(projected, blocks):
    return lax.dot_general(
        projected.astype(jnp.bfloat16),
        blocks,
        (((1,), (1,)), ((), ())),
        preferred_element_type=jnp.float32,
    )


def field_kernel(
    window,
    first_curl,
    table,
    pieces,
    pattern_in,
    region_in,
    law_in,
    curl_hbm,
    projected,
    halo,
    pattern,
    region_ids,
    law,
    outer,
    later_curl,
    timed,
    densities,
    edge_sums,
    small_sems,
    curl_sem,
):
    tile_count, links, tile, comps = curl_hbm.shape
    early = first_curl.shape[0]
    parts_here = halo.shape[0]
    fetched = [(pattern_in, pattern), (region_in, region_ids), (law_in, law)]
    small = [
        pltpu.make_async_copy(src, dst, small_sems.at[i]) for i, (src, dst) in enumerate(fetched)
    ]
    rest, blocks = curl_copies(curl_hbm, first_curl, later_curl, curl_sem)
    for copy in small + [rest]:
        copy.start()
    edge_sums[...] = jnp.zeros_like(edge_sums)
    stacked = jnp.concatenate([window[...]] * 3, axis=0)
    samples = jnp.dot(pieces[...], stacked, preferred_element_type=jnp.float32)
    high = samples.astype(jnp.bfloat16)
    timed[:HALF, :] = high
    timed[HALF:, :] = (samples - high.astype(jnp.float32)).astype(jnp.bfloat16)
    columns = [
        jnp.broadcast_to(table[:, part : part + 1], (HALF, comps)) for part in range(parts_here)
    ]
    for copy in small:
        copy.wait()
    places = [[pattern[link, elem] for link in range(links)] for elem in range(tile_count)]
    count = jnp.int32(0)
    for elem in range(tile_count):
        for link, at in enumerate(places[elem]):
            outer[count] = elem * links + link
            count += jnp.where((at == 0) | (at == tile_count + 1), 1, 0)

    def find_density(elem):
        picked = jnp.concatenate(
            [timed[:, pl.ds(pl.multiple_of(at * tile, tile), tile)] for at in places[elem]], axis=1
        )
        split = jnp.dot(picked, blocks(elem), preferred_element_type=jnp.float32)
        densities[elem] = split[:HALF] + split[HALF:]

    def project(elem):
        density = densities[elem]
        comp = [density[:, c * tile : (c + 1) * tile] for c in range(comps // tile)]
        square = comp[0] * comp[0]
        for c in comp[1:]:
            square = square + c * c
        region = region_ids[elem]
        reluct = law[0, region] + law[2, region] * square / (square + law[1, region])
        field = jnp.concatenate([reluct * c for c in comp], axis=1)
        rows = [jnp.sum(column * field, axis=0, keepdims=True) for column in columns]
        projected[elem] = jnp.concatenate(rows, axis=0) * (4.0 / SAMPLES)

    for turn in range(tile_count + 1):
        if turn < tile_count:
            if turn == early:
                rest.wait()
            find_density(turn)
        if turn:
            project(turn - 1)

    def add_outer(turn, carry):
        for slot in range(LISTED):
            spot = turn * LISTED + slot
            code = jnp.where(spot < count, outer[jnp.minimum(spot, count - 1)], 0)
            elem, link = code // links, code % links
            block = jnp.where(
                elem < early,
                first_curl[jnp.minimum(elem, early - 1), link],
                later_curl[jnp.maximum(elem - early, 0), link],
            )
            contrib = weighted(projected[elem], block)
            side = jnp.where(pattern[link, elem] == 0, 0, 1)
            edge_sums[slot, side] += jnp.where(spot < count, contrib, 0.0)
        return carry

    lax.fori_loop(0, (count + LISTED - 1) // LISTED, add_outer, 0)
    total = edge_sums[0]
    for slot in range(1, LISTED):
        total = total + edge_sums[slot]
    halo[:, :tile] = total[0]
    halo[:, tile:] = total[1]


def sum_kernel(
    projected,
    first_curl,
    source,
    pattern_in,
    curl_hbm,
    out,
    pattern,
    later_curl,
    small_sem,
    curl_sem,
    *sums,
):
    tile_count, links, tile, _ = curl_hbm.shape
    early = first_curl.shape[0]
    small = pltpu.make_async_copy(pattern_in, pattern, small_sem)
    rest, blocks = curl_copies(curl_hbm, first_curl, later_curl, curl_sem)
    small.start()
    rest.start()
    for total in sums:
        total[...] = jnp.zeros_like(total)
    small.wait()
    for elem in range(tile_count):
        if elem == early:
            rest.wait()
        contrib = weighted(projected[elem], blocks(elem))
        for link in range(links):
            sums[link][pattern[link, elem]] += contrib[:, link * tile : (link + 1) * tile]
    for w in range(tile_count):
        at = slice(w * tile, (w + 1) * tile)
        total = sums[0][w + 1]
        for other in sums[1:]:
            total = total + other[w + 1]
        out[:, at] = total - source[:, at]


def halo_kernel(own, from_right, from_left, out):
    tile = from_left.shape[1] // 2
    out[...] = own[...]
    out[:, :tile] += from_left[:, tile:]
    out[:, -tile:] += from_right[:, :tile]


def per_device(coeffs, curl_tiles, pattern, region_ids, material_law, source):
    parts_here = coeffs.shape[0]
    tile_count, links, tile, comps = curl_tiles.shape
    group_size = lax.axis_size(GROUP)
    parts = parts_here * group_size
    table = half_table(parts)
    pieces = jnp.asarray(bf16_pieces(table))
    own_columns = jnp.asarray(
        table.reshape(HALF, group_size, parts_here).transpose(1, 0, 2).astype(np.float32)
    )
    vmem, hbm = pl.BlockSpec(memory_space=pltpu.VMEM), pl.BlockSpec(memory_space=pltpu.HBM)

    def in_vmem(array):
        return pltpu.with_memory_space_constraint(array, pltpu.VMEM)

    def in_hbm(array):
        return pltpu.with_memory_space_constraint(array, pltpu.HBM)

    early = 3 * tile_count // 8
    operands = [
        curl_tiles,
        own_columns,
        coeffs,
        pieces,
        source,
        pattern.T,
        region_ids,
        material_law,
    ]
    shapes = [
        (early,) + curl_tiles.shape[1:],
        own_columns.shape[1:],
    ] + [operand.shape for operand in operands[2:]]
    fetched = pl.pallas_call(
        fetch_kernel,
        out_shape=[pltpu.VMEM(shape, o.dtype) for shape, o in zip(shapes, operands)],
        in_specs=[hbm] * len(operands),
        out_specs=[vmem] * len(operands),
        scratch_shapes=[pltpu.SemaphoreType.DMA((len(operands),))],
        compiler_params=pltpu.CompilerParams(vmem_limit_bytes=16 * MIB),
        cost_estimate=pl.CostEstimate(
            flops=0, bytes_accessed=4 * early * links * tile * comps, transcendentals=0
        ),
        name="fetch_operands",
    )(*[in_hbm(operand) for operand in operands])
    first_curl, columns_here, coeffs_here, pieces_here, source_here, *others = fetched
    pattern_here = others[0]

    right, left = from_neighbours(coeffs, tile)
    block = jnp.concatenate([left, coeffs_here, right], axis=1)
    copies = jnp.broadcast_to(block[None], (group_size,) + block.shape)
    window = lax.all_to_all(copies, GROUP, 0, 0).reshape(parts, block.shape[1])
    later_tiles = pltpu.VMEM((tile_count - early,) + curl_tiles.shape[1:], curl_tiles.dtype)
    pattern_words = pltpu.SMEM((links, tile_count), jnp.int32)
    projected, halo = pl.pallas_call(
        field_kernel,
        out_shape=(
            pltpu.VMEM((tile_count, parts_here, comps), jnp.float32),
            pltpu.VMEM((parts_here, 2 * tile), jnp.float32),
        ),
        in_specs=[vmem] * 7 + [hbm],
        out_specs=(vmem, vmem),
        scratch_shapes=[
            pattern_words,
            pltpu.SMEM(region_ids.shape, jnp.int32),
            pltpu.SMEM(material_law.shape, jnp.float32),
            pltpu.SMEM((links * tile_count + 1,), jnp.int32),
            later_tiles,
            pltpu.VMEM((SAMPLES, (tile_count + 2) * tile), jnp.bfloat16),
            pltpu.VMEM((tile_count, HALF, comps), jnp.float32),
            pltpu.VMEM((LISTED, 2, parts_here, tile), jnp.float32),
            pltpu.SemaphoreType.DMA((3,)),
            pltpu.SemaphoreType.DMA,
        ],
        compiler_params=pltpu.CompilerParams(vmem_limit_bytes=32 * MIB),
        cost_estimate=pl.CostEstimate(
            flops=2 * SAMPLES * tile_count * links * tile * comps,
            bytes_accessed=2 * curl_tiles.size,
            transcendentals=0,
        ),
        name="shard_fields",
    )(
        in_vmem(window),
        *[in_vmem(array) for array in (first_curl, columns_here, pieces_here, *others)],
        in_hbm(curl_tiles),
    )
    if lax.axis_size("space") == 2:
        beside = [shifted(halo, "space", 1)] * 2
    else:
        beside = [shifted(halo, "space", -1), shifted(halo, "space", 1)]
    own = pl.pallas_call(
        sum_kernel,
        out_shape=pltpu.VMEM(source.shape, jnp.float32),
        in_specs=[vmem] * 4 + [hbm],
        out_specs=vmem,
        scratch_shapes=[
            pattern_words,
            later_tiles,
            pltpu.SemaphoreType.DMA,
            pltpu.SemaphoreType.DMA,
        ]
        + [pltpu.VMEM((tile_count + 2, parts_here, tile), jnp.float32)] * links,
        compiler_params=pltpu.CompilerParams(vmem_limit_bytes=32 * MIB),
        cost_estimate=pl.CostEstimate(
            flops=2 * SAMPLES * tile_count * links * tile * comps,
            bytes_accessed=2 * curl_tiles.size,
            transcendentals=0,
        ),
        name="shard_sums",
    )(
        *[in_vmem(array) for array in (projected, first_curl, source_here, pattern_here)],
        in_hbm(curl_tiles),
    )
    return pl.pallas_call(
        halo_kernel,
        out_shape=jax.ShapeDtypeStruct(source.shape, jnp.float32),
        in_specs=[vmem] * 3,
        out_specs=vmem,
        compiler_params=pltpu.CompilerParams(vmem_limit_bytes=16 * MIB),
        name="halo_sum",
    )(in_vmem(own), *beside)


def solution(mesh):
    placed = (
        P(GROUP, "space"),
        P("space", None, None, None),
        P("space", None),
        P("space"),
        P(),
        P(GROUP, "space"),
    )
    return jax.shard_map(
        per_device,
        mesh=mesh,
        in_specs=placed,
        out_specs=P(GROUP, "space"),
        check_vma=False,
    )
```

```python
import math

import jax
import jax.numpy as jnp
import ml_dtypes
import numpy as np
from jax import lax
from jax.experimental import pallas as pl
from jax.experimental.pallas import tpu as pltpu
from jax.sharding import PartitionSpec as P

SAMPLES = 64
HALF = SAMPLES // 2
GROUP = ("harm", "samp")
MIB = 1024 * 1024
LISTED = 4


def half_table(parts):
    sample_ids = np.arange(HALF)[:, None]
    part_ids = np.arange(parts)[None, :]
    phase = ((2 * (part_ids // 2) + 1) * sample_ids % SAMPLES) * (2.0 * math.pi / SAMPLES)
    return np.where(part_ids % 2 == 0, np.cos(phase), np.sin(phase))


def bf16_pieces(table):
    rest = table
    pieces = []
    for _ in range(3):
        piece = rest.astype(ml_dtypes.bfloat16)
        pieces.append(piece)
        rest = rest - piece.astype(np.float64)
    return np.concatenate(pieces, axis=-1)


def shifted(array, axis, by):
    count = lax.axis_size(axis)
    return lax.ppermute(array, axis, [(i, (i + by) % count) for i in range(count)])


def from_neighbours(array, tile):
    if lax.axis_size("space") == 2:
        other = shifted(array, "space", 1)
        return other[:, :tile], other[:, -tile:]
    return shifted(array[:, :tile], "space", -1), shifted(array[:, -tile:], "space", 1)


def fetch_kernel(*refs):
    count = (len(refs) - 1) // 2
    sources, targets, sems = refs[:count], refs[count : 2 * count], refs[-1]
    rank = lax.axis_index(GROUP)
    sources = (sources[0].at[: targets[0].shape[0]], sources[1].at[rank]) + sources[2:]
    copies = [
        pltpu.make_async_copy(source, target, sems.at[i])
        for i, (source, target) in enumerate(zip(sources, targets))
    ]
    for copy in copies:
        copy.start()
    for copy in copies:
        copy.wait()


def curl_copies(curl_hbm, first_curl, later_curl, sem):
    early = first_curl.shape[0]
    links, tile, comps = curl_hbm.shape[1:]
    rest = pltpu.make_async_copy(curl_hbm.at[early:], later_curl, sem)

    def blocks(elem):
        curl = first_curl[elem] if elem < early else later_curl[elem - early]
        return curl.reshape(links * tile, comps)

    return rest, blocks


def weighted(projected, blocks):
    return lax.dot_general(
        projected.astype(jnp.bfloat16),
        blocks,
        (((1,), (1,)), ((), ())),
        preferred_element_type=jnp.float32,
    )


def field_kernel(
    window,
    first_curl,
    table,
    pieces,
    pattern_in,
    region_in,
    law_in,
    curl_hbm,
    projected,
    halo,
    later_curl,
    pattern,
    region_ids,
    law,
    outer,
    timed,
    densities,
    edge_sums,
    small_sems,
    curl_sem,
):
    tile_count, links, tile, comps = curl_hbm.shape
    early = first_curl.shape[0]
    parts_here = halo.shape[0]
    fetched = [(pattern_in, pattern), (region_in, region_ids), (law_in, law)]
    small = [
        pltpu.make_async_copy(src, dst, small_sems.at[i]) for i, (src, dst) in enumerate(fetched)
    ]
    rest, blocks = curl_copies(curl_hbm, first_curl, later_curl, curl_sem)
    for copy in small + [rest]:
        copy.start()
    edge_sums[...] = jnp.zeros_like(edge_sums)
    stacked = jnp.concatenate([window[...]] * 3, axis=0)
    samples = jnp.dot(pieces[...], stacked, preferred_element_type=jnp.float32)
    high = samples.astype(jnp.bfloat16)
    timed[:HALF, :] = high
    timed[HALF:, :] = (samples - high.astype(jnp.float32)).astype(jnp.bfloat16)
    columns = [
        jnp.broadcast_to(table[:, part : part + 1], (HALF, comps)) for part in range(parts_here)
    ]
    for copy in small:
        copy.wait()
    places = [[pattern[link, elem] for link in range(links)] for elem in range(tile_count)]
    count = jnp.int32(0)
    for elem in range(tile_count):
        for link, at in enumerate(places[elem]):
            outer[count] = elem * links + link
            count += jnp.where((at == 0) | (at == tile_count + 1), 1, 0)

    def find_density(elem):
        picked = jnp.concatenate(
            [timed[:, pl.ds(pl.multiple_of(at * tile, tile), tile)] for at in places[elem]], axis=1
        )
        split = jnp.dot(picked, blocks(elem), preferred_element_type=jnp.float32)
        densities[elem] = split[:HALF] + split[HALF:]

    def project(elem):
        density = densities[elem]
        comp = [density[:, c * tile : (c + 1) * tile] for c in range(comps // tile)]
        square = comp[0] * comp[0]
        for c in comp[1:]:
            square = square + c * c
        region = region_ids[elem]
        reluct = law[0, region] + law[2, region] * square / (square + law[1, region])
        field = jnp.concatenate([reluct * c for c in comp], axis=1)
        rows = [jnp.sum(column * field, axis=0, keepdims=True) for column in columns]
        projected[elem] = jnp.concatenate(rows, axis=0) * (4.0 / SAMPLES)

    for turn in range(tile_count + 1):
        if turn < tile_count:
            if turn == early:
                rest.wait()
            find_density(turn)
        if turn:
            project(turn - 1)

    def add_outer(turn, carry):
        for slot in range(LISTED):
            spot = turn * LISTED + slot
            code = jnp.where(spot < count, outer[jnp.minimum(spot, count - 1)], 0)
            elem, link = code // links, code % links
            block = jnp.where(
                elem < early,
                first_curl[jnp.minimum(elem, early - 1), link],
                later_curl[jnp.maximum(elem - early, 0), link],
            )
            contrib = weighted(projected[elem], block)
            side = jnp.where(pattern[link, elem] == 0, 0, 1)
            edge_sums[slot, side] += jnp.where(spot < count, contrib, 0.0)
        return carry

    lax.fori_loop(0, (count + LISTED - 1) // LISTED, add_outer, 0)
    total = edge_sums[0]
    for slot in range(1, LISTED):
        total = total + edge_sums[slot]
    halo[:, :tile] = total[0]
    halo[:, tile:] = total[1]


def sum_kernel(
    projected,
    first_curl,
    later_curl,
    source,
    pattern_in,
    out,
    pattern,
    small_sem,
    *sums,
):
    links, tile, comps = first_curl.shape[1:]
    early = first_curl.shape[0]
    tile_count = early + later_curl.shape[0]
    small = pltpu.make_async_copy(pattern_in, pattern, small_sem)
    small.start()
    for total in sums:
        total[...] = jnp.zeros_like(total)
    small.wait()
    for elem in range(tile_count):
        curl = first_curl[elem] if elem < early else later_curl[elem - early]
        contrib = weighted(projected[elem], curl.reshape(links * tile, comps))
        for link in range(links):
            sums[link][pattern[link, elem]] += contrib[:, link * tile : (link + 1) * tile]
    for w in range(tile_count):
        at = slice(w * tile, (w + 1) * tile)
        total = sums[0][w + 1]
        for other in sums[1:]:
            total = total + other[w + 1]
        out[:, at] = total - source[:, at]


def halo_kernel(own, from_right, from_left, out):
    tile = from_left.shape[1] // 2
    out[...] = own[...]
    out[:, :tile] += from_left[:, tile:]
    out[:, -tile:] += from_right[:, :tile]


def per_device(coeffs, curl_tiles, pattern, region_ids, material_law, source):
    parts_here = coeffs.shape[0]
    tile_count, links, tile, comps = curl_tiles.shape
    group_size = lax.axis_size(GROUP)
    parts = parts_here * group_size
    table = half_table(parts)
    pieces = jnp.asarray(bf16_pieces(table))
    own_columns = jnp.asarray(
        table.reshape(HALF, group_size, parts_here).transpose(1, 0, 2).astype(np.float32)
    )
    vmem, hbm = pl.BlockSpec(memory_space=pltpu.VMEM), pl.BlockSpec(memory_space=pltpu.HBM)

    def in_vmem(array):
        return pltpu.with_memory_space_constraint(array, pltpu.VMEM)

    def in_hbm(array):
        return pltpu.with_memory_space_constraint(array, pltpu.HBM)

    early = 3 * tile_count // 8
    operands = [
        curl_tiles,
        own_columns,
        coeffs,
        pieces,
        source,
        pattern.T,
        region_ids,
        material_law,
    ]
    shapes = [
        (early,) + curl_tiles.shape[1:],
        own_columns.shape[1:],
    ] + [operand.shape for operand in operands[2:]]
    fetched = pl.pallas_call(
        fetch_kernel,
        out_shape=[pltpu.VMEM(shape, o.dtype) for shape, o in zip(shapes, operands)],
        in_specs=[hbm] * len(operands),
        out_specs=[vmem] * len(operands),
        scratch_shapes=[pltpu.SemaphoreType.DMA((len(operands),))],
        compiler_params=pltpu.CompilerParams(vmem_limit_bytes=16 * MIB),
        cost_estimate=pl.CostEstimate(
            flops=0, bytes_accessed=4 * early * links * tile * comps, transcendentals=0
        ),
        name="fetch_operands",
    )(*[in_hbm(operand) for operand in operands])
    first_curl, columns_here, coeffs_here, pieces_here, source_here, *others = fetched
    pattern_here = others[0]

    right, left = from_neighbours(coeffs, tile)
    block = jnp.concatenate([left, coeffs_here, right], axis=1)
    copies = jnp.broadcast_to(block[None], (group_size,) + block.shape)
    window = lax.all_to_all(copies, GROUP, 0, 0).reshape(parts, block.shape[1])
    pattern_words = pltpu.SMEM((links, tile_count), jnp.int32)
    projected, halo, later_curl = pl.pallas_call(
        field_kernel,
        out_shape=(
            pltpu.VMEM((tile_count, parts_here, comps), jnp.float32),
            pltpu.VMEM((parts_here, 2 * tile), jnp.float32),
            pltpu.VMEM((tile_count - early,) + curl_tiles.shape[1:], curl_tiles.dtype),
        ),
        in_specs=[vmem] * 7 + [hbm],
        out_specs=(vmem, vmem, vmem),
        scratch_shapes=[
            pattern_words,
            pltpu.SMEM(region_ids.shape, jnp.int32),
            pltpu.SMEM(material_law.shape, jnp.float32),
            pltpu.SMEM((links * tile_count + 1,), jnp.int32),
            pltpu.VMEM((SAMPLES, (tile_count + 2) * tile), jnp.bfloat16),
            pltpu.VMEM((tile_count, HALF, comps), jnp.float32),
            pltpu.VMEM((LISTED, 2, parts_here, tile), jnp.float32),
            pltpu.SemaphoreType.DMA((3,)),
            pltpu.SemaphoreType.DMA,
        ],
        compiler_params=pltpu.CompilerParams(vmem_limit_bytes=32 * MIB),
        cost_estimate=pl.CostEstimate(
            flops=2 * SAMPLES * tile_count * links * tile * comps,
            bytes_accessed=2 * curl_tiles.size,
            transcendentals=0,
        ),
        name="shard_fields",
    )(
        in_vmem(window),
        *[in_vmem(array) for array in (first_curl, columns_here, pieces_here, *others)],
        in_hbm(curl_tiles),
    )
    if lax.axis_size("space") == 2:
        beside = [shifted(halo, "space", 1)] * 2
    else:
        beside = [shifted(halo, "space", -1), shifted(halo, "space", 1)]
    own = pl.pallas_call(
        sum_kernel,
        out_shape=pltpu.VMEM(source.shape, jnp.float32),
        in_specs=[vmem] * 5,
        out_specs=vmem,
        scratch_shapes=[
            pattern_words,
            pltpu.SemaphoreType.DMA,
        ]
        + [pltpu.VMEM((tile_count + 2, parts_here, tile), jnp.float32)] * links,
        compiler_params=pltpu.CompilerParams(vmem_limit_bytes=32 * MIB),
        cost_estimate=pl.CostEstimate(
            flops=2 * SAMPLES * tile_count * links * tile * comps,
            bytes_accessed=2 * curl_tiles.size,
            transcendentals=0,
        ),
        name="shard_sums",
    )(
        *[in_vmem(a) for a in (projected, first_curl, later_curl, source_here, pattern_here)],
    )
    return pl.pallas_call(
        halo_kernel,
        out_shape=jax.ShapeDtypeStruct(source.shape, jnp.float32),
        in_specs=[vmem] * 3,
        out_specs=vmem,
        compiler_params=pltpu.CompilerParams(vmem_limit_bytes=16 * MIB),
        name="halo_sum",
    )(in_vmem(own), *beside)


def solution(mesh):
    placed = (
        P(GROUP, "space"),
        P("space", None, None, None),
        P("space", None),
        P("space"),
        P(),
        P(GROUP, "space"),
    )
    return jax.shard_map(
        per_device,
        mesh=mesh,
        in_specs=placed,
        out_specs=P(GROUP, "space"),
        check_vma=False,
    )
```

```python
import math

import jax
import jax.numpy as jnp
import ml_dtypes
import numpy as np
from jax import lax
from jax.experimental import pallas as pl
from jax.experimental.pallas import tpu as pltpu
from jax.sharding import PartitionSpec as P

SAMPLES = 64
HALF = SAMPLES // 2
GROUP = ("harm", "samp")
MIB = 1024 * 1024
LISTED = 4
CHUNK = 4


def half_table(parts):
    sample_ids = np.arange(HALF)[:, None]
    part_ids = np.arange(parts)[None, :]
    phase = ((2 * (part_ids // 2) + 1) * sample_ids % SAMPLES) * (2.0 * math.pi / SAMPLES)
    return np.where(part_ids % 2 == 0, np.cos(phase), np.sin(phase))


def bf16_pieces(table):
    rest = table
    pieces = []
    for _ in range(3):
        piece = rest.astype(ml_dtypes.bfloat16)
        pieces.append(piece)
        rest = rest - piece.astype(np.float64)
    return np.concatenate(pieces, axis=-1)


def shifted(array, axis, by):
    count = lax.axis_size(axis)
    return lax.ppermute(array, axis, [(i, (i + by) % count) for i in range(count)])


def from_neighbours(array, tile):
    if lax.axis_size("space") == 2:
        other = shifted(array, "space", 1)
        return other[:, :tile], other[:, -tile:]
    return shifted(array[:, :tile], "space", -1), shifted(array[:, -tile:], "space", 1)


def fetch_kernel(*refs):
    count = (len(refs) - 1) // 2
    sources, targets, sems = refs[:count], refs[count : 2 * count], refs[-1]
    rank = lax.axis_index(GROUP)
    sources = (sources[0].at[: targets[0].shape[0]], sources[1].at[rank]) + sources[2:]
    copies = [
        pltpu.make_async_copy(source, target, sems.at[i])
        for i, (source, target) in enumerate(zip(sources, targets))
    ]
    for copy in copies:
        copy.start()
    for copy in copies:
        copy.wait()


def weighted(projected, blocks):
    return lax.dot_general(
        projected.astype(jnp.bfloat16),
        blocks,
        (((1,), (1,)), ((), ())),
        preferred_element_type=jnp.float32,
    )


def field_kernel(
    window,
    first_curl,
    table,
    pieces,
    pattern_in,
    region_in,
    law_in,
    curl_hbm,
    projected,
    halo,
    later_curl,
    pattern,
    region_ids,
    law,
    outer,
    timed,
    densities,
    edge_sums,
    small_sems,
    curl_sems,
):
    tile_count, links, tile, comps = curl_hbm.shape
    early = first_curl.shape[0]
    parts_here = halo.shape[0]
    fetched = [(pattern_in, pattern), (region_in, region_ids), (law_in, law)]
    small = [
        pltpu.make_async_copy(src, dst, small_sems.at[i]) for i, (src, dst) in enumerate(fetched)
    ]
    later = {
        elem: pltpu.make_async_copy(
            curl_hbm.at[elem : min(elem + CHUNK, tile_count)],
            later_curl.at[elem - early : min(elem + CHUNK, tile_count) - early],
            curl_sems.at[(elem - early) // CHUNK],
        )
        for elem in range(early, tile_count, CHUNK)
    }
    for copy in small + list(later.values()):
        copy.start()
    edge_sums[...] = jnp.zeros_like(edge_sums)
    stacked = jnp.concatenate([window[...]] * 3, axis=0)
    samples = jnp.dot(pieces[...], stacked, preferred_element_type=jnp.float32)
    high = samples.astype(jnp.bfloat16)
    timed[:HALF, :] = high
    timed[HALF:, :] = (samples - high.astype(jnp.float32)).astype(jnp.bfloat16)
    columns = [
        jnp.broadcast_to(table[:, part : part + 1], (HALF, comps)) for part in range(parts_here)
    ]
    for copy in small:
        copy.wait()
    places = [[pattern[link, elem] for link in range(links)] for elem in range(tile_count)]
    count = jnp.int32(0)
    for elem in range(tile_count):
        for link, at in enumerate(places[elem]):
            outer[count] = elem * links + link
            count += jnp.where((at == 0) | (at == tile_count + 1), 1, 0)

    def blocks(elem):
        curl = first_curl[elem] if elem < early else later_curl[elem - early]
        return curl.reshape(links * tile, comps)

    def find_density(elem):
        picked = jnp.concatenate(
            [timed[:, pl.ds(pl.multiple_of(at * tile, tile), tile)] for at in places[elem]], axis=1
        )
        split = jnp.dot(picked, blocks(elem), preferred_element_type=jnp.float32)
        densities[elem] = split[:HALF] + split[HALF:]

    def project(elem):
        density = densities[elem]
        comp = [density[:, c * tile : (c + 1) * tile] for c in range(comps // tile)]
        square = comp[0] * comp[0]
        for c in comp[1:]:
            square = square + c * c
        region = region_ids[elem]
        reluct = law[0, region] + law[2, region] * square / (square + law[1, region])
        field = jnp.concatenate([reluct * c for c in comp], axis=1)
        rows = [jnp.sum(column * field, axis=0, keepdims=True) for column in columns]
        projected[elem] = jnp.concatenate(rows, axis=0) * (4.0 / SAMPLES)

    for turn in range(tile_count + 1):
        if turn < tile_count:
            if turn in later:
                later[turn].wait()
            find_density(turn)
        if turn:
            project(turn - 1)

    def add_outer(turn, carry):
        for slot in range(LISTED):
            spot = turn * LISTED + slot
            code = jnp.where(spot < count, outer[jnp.minimum(spot, count - 1)], 0)
            elem, link = code // links, code % links
            block = jnp.where(
                elem < early,
                first_curl[jnp.minimum(elem, early - 1), link],
                later_curl[jnp.maximum(elem - early, 0), link],
            )
            contrib = weighted(projected[elem], block)
            side = jnp.where(pattern[link, elem] == 0, 0, 1)
            edge_sums[slot, side] += jnp.where(spot < count, contrib, 0.0)
        return carry

    lax.fori_loop(0, (count + LISTED - 1) // LISTED, add_outer, 0)
    total = edge_sums[0]
    for slot in range(1, LISTED):
        total = total + edge_sums[slot]
    halo[:, :tile] = total[0]
    halo[:, tile:] = total[1]


def sum_kernel(
    projected,
    first_curl,
    later_curl,
    source,
    pattern_in,
    out,
    pattern,
    small_sem,
    *sums,
):
    links, tile, comps = first_curl.shape[1:]
    early = first_curl.shape[0]
    tile_count = early + later_curl.shape[0]
    small = pltpu.make_async_copy(pattern_in, pattern, small_sem)
    small.start()
    for total in sums:
        total[...] = jnp.zeros_like(total)
    small.wait()
    for elem in range(tile_count):
        curl = first_curl[elem] if elem < early else later_curl[elem - early]
        contrib = weighted(projected[elem], curl.reshape(links * tile, comps))
        for link in range(links):
            sums[link][pattern[link, elem]] += contrib[:, link * tile : (link + 1) * tile]
    for w in range(tile_count):
        at = slice(w * tile, (w + 1) * tile)
        total = sums[0][w + 1]
        for other in sums[1:]:
            total = total + other[w + 1]
        out[:, at] = total - source[:, at]


def halo_kernel(own, from_right, from_left, out):
    tile = from_left.shape[1] // 2
    out[...] = own[...]
    out[:, :tile] += from_left[:, tile:]
    out[:, -tile:] += from_right[:, :tile]


def per_device(coeffs, curl_tiles, pattern, region_ids, material_law, source):
    parts_here = coeffs.shape[0]
    tile_count, links, tile, comps = curl_tiles.shape
    group_size = lax.axis_size(GROUP)
    parts = parts_here * group_size
    table = half_table(parts)
    pieces = jnp.asarray(bf16_pieces(table))
    own_columns = jnp.asarray(
        table.reshape(HALF, group_size, parts_here).transpose(1, 0, 2).astype(np.float32)
    )
    vmem, hbm = pl.BlockSpec(memory_space=pltpu.VMEM), pl.BlockSpec(memory_space=pltpu.HBM)

    def in_vmem(array):
        return pltpu.with_memory_space_constraint(array, pltpu.VMEM)

    def in_hbm(array):
        return pltpu.with_memory_space_constraint(array, pltpu.HBM)

    early = tile_count // 2
    operands = [
        curl_tiles,
        own_columns,
        coeffs,
        pieces,
        source,
        pattern.T,
        region_ids,
        material_law,
    ]
    shapes = [
        (early,) + curl_tiles.shape[1:],
        own_columns.shape[1:],
    ] + [operand.shape for operand in operands[2:]]
    fetched = pl.pallas_call(
        fetch_kernel,
        out_shape=[pltpu.VMEM(shape, o.dtype) for shape, o in zip(shapes, operands)],
        in_specs=[hbm] * len(operands),
        out_specs=[vmem] * len(operands),
        scratch_shapes=[pltpu.SemaphoreType.DMA((len(operands),))],
        compiler_params=pltpu.CompilerParams(vmem_limit_bytes=16 * MIB),
        cost_estimate=pl.CostEstimate(
            flops=0, bytes_accessed=4 * early * links * tile * comps, transcendentals=0
        ),
        name="fetch_operands",
    )(*[in_hbm(operand) for operand in operands])
    first_curl, columns_here, coeffs_here, pieces_here, source_here, *others = fetched
    pattern_here = others[0]

    right, left = from_neighbours(coeffs, tile)
    block = jnp.concatenate([left, coeffs_here, right], axis=1)
    copies = jnp.broadcast_to(block[None], (group_size,) + block.shape)
    window = lax.all_to_all(copies, GROUP, 0, 0).reshape(parts, block.shape[1])
    pattern_words = pltpu.SMEM((links, tile_count), jnp.int32)
    projected, halo, later_curl = pl.pallas_call(
        field_kernel,
        out_shape=(
            pltpu.VMEM((tile_count, parts_here, comps), jnp.float32),
            pltpu.VMEM((parts_here, 2 * tile), jnp.float32),
            pltpu.VMEM((tile_count - early,) + curl_tiles.shape[1:], curl_tiles.dtype),
        ),
        in_specs=[vmem] * 7 + [hbm],
        out_specs=(vmem, vmem, vmem),
        scratch_shapes=[
            pattern_words,
            pltpu.SMEM(region_ids.shape, jnp.int32),
            pltpu.SMEM(material_law.shape, jnp.float32),
            pltpu.SMEM((links * tile_count + 1,), jnp.int32),
            pltpu.VMEM((SAMPLES, (tile_count + 2) * tile), jnp.bfloat16),
            pltpu.VMEM((tile_count, HALF, comps), jnp.float32),
            pltpu.VMEM((LISTED, 2, parts_here, tile), jnp.float32),
            pltpu.SemaphoreType.DMA((3,)),
            pltpu.SemaphoreType.DMA((pl.cdiv(tile_count - early, CHUNK),)),
        ],
        compiler_params=pltpu.CompilerParams(vmem_limit_bytes=32 * MIB),
        cost_estimate=pl.CostEstimate(
            flops=2 * SAMPLES * tile_count * links * tile * comps,
            bytes_accessed=2 * curl_tiles.size,
            transcendentals=0,
        ),
        name="shard_fields",
    )(
        in_vmem(window),
        *[in_vmem(array) for array in (first_curl, columns_here, pieces_here, *others)],
        in_hbm(curl_tiles),
    )
    if lax.axis_size("space") == 2:
        beside = [shifted(halo, "space", 1)] * 2
    else:
        beside = [shifted(halo, "space", -1), shifted(halo, "space", 1)]
    own = pl.pallas_call(
        sum_kernel,
        out_shape=pltpu.VMEM(source.shape, jnp.float32),
        in_specs=[vmem] * 5,
        out_specs=vmem,
        scratch_shapes=[
            pattern_words,
            pltpu.SemaphoreType.DMA,
        ]
        + [pltpu.VMEM((tile_count + 2, parts_here, tile), jnp.float32)] * links,
        compiler_params=pltpu.CompilerParams(vmem_limit_bytes=32 * MIB),
        cost_estimate=pl.CostEstimate(
            flops=2 * SAMPLES * tile_count * links * tile * comps,
            bytes_accessed=2 * curl_tiles.size,
            transcendentals=0,
        ),
        name="shard_sums",
    )(
        *[in_vmem(a) for a in (projected, first_curl, later_curl, source_here, pattern_here)],
    )
    return pl.pallas_call(
        halo_kernel,
        out_shape=jax.ShapeDtypeStruct(source.shape, jnp.float32),
        in_specs=[vmem] * 3,
        out_specs=vmem,
        compiler_params=pltpu.CompilerParams(vmem_limit_bytes=16 * MIB),
        name="halo_sum",
    )(in_vmem(own), *beside)


def solution(mesh):
    placed = (
        P(GROUP, "space"),
        P("space", None, None, None),
        P("space", None),
        P("space"),
        P(),
        P(GROUP, "space"),
    )
    return jax.shard_map(
        per_device,
        mesh=mesh,
        in_specs=placed,
        out_specs=P(GROUP, "space"),
        check_vma=False,
    )
```

```python
import math

import jax
import jax.numpy as jnp
import ml_dtypes
import numpy as np
from jax import lax
from jax.experimental import pallas as pl
from jax.experimental.pallas import tpu as pltpu
from jax.sharding import PartitionSpec as P

SAMPLES = 64
HALF = SAMPLES // 2
GROUP = ("harm", "samp")
MIB = 1024 * 1024
LISTED = 4
CHUNK = 4


def half_table(parts):
    sample_ids = np.arange(HALF)[:, None]
    part_ids = np.arange(parts)[None, :]
    phase = ((2 * (part_ids // 2) + 1) * sample_ids % SAMPLES) * (2.0 * math.pi / SAMPLES)
    return np.where(part_ids % 2 == 0, np.cos(phase), np.sin(phase))


def bf16_pieces(table):
    rest = table
    pieces = []
    for _ in range(3):
        piece = rest.astype(ml_dtypes.bfloat16)
        pieces.append(piece)
        rest = rest - piece.astype(np.float64)
    return np.concatenate(pieces, axis=-1)


def shifted(array, axis, by):
    count = lax.axis_size(axis)
    return lax.ppermute(array, axis, [(i, (i + by) % count) for i in range(count)])


def from_neighbours(array, tile):
    if lax.axis_size("space") == 2:
        other = shifted(array, "space", 1)
        return other[:, :tile], other[:, -tile:]
    return shifted(array[:, :tile], "space", -1), shifted(array[:, -tile:], "space", 1)


def fetch_kernel(*refs):
    count = (len(refs) - 1) // 2
    sources, targets, sems = refs[:count], refs[count : 2 * count], refs[-1]
    rank = lax.axis_index(GROUP)
    sources = (sources[0].at[: targets[0].shape[0]], sources[1].at[rank]) + sources[2:]
    copies = [
        pltpu.make_async_copy(source, target, sems.at[i])
        for i, (source, target) in enumerate(zip(sources, targets))
    ]
    for copy in copies:
        copy.start()
    for copy in copies:
        copy.wait()


def weighted(projected, blocks):
    return lax.dot_general(
        projected.astype(jnp.bfloat16),
        blocks,
        (((1,), (1,)), ((), ())),
        preferred_element_type=jnp.float32,
    )


def field_kernel(
    window,
    first_curl,
    table,
    pieces,
    pattern_in,
    region_in,
    law_in,
    curl_hbm,
    projected,
    halo,
    later_curl,
    pattern,
    region_ids,
    law,
    outer,
    timed,
    densities,
    edge_sums,
    small_sems,
    curl_sems,
):
    tile_count, links, tile, comps = curl_hbm.shape
    early = first_curl.shape[0]
    parts_here = halo.shape[0]
    fetched = [(pattern_in, pattern), (region_in, region_ids), (law_in, law)]
    small = [
        pltpu.make_async_copy(src, dst, small_sems.at[i]) for i, (src, dst) in enumerate(fetched)
    ]
    later = {
        elem: pltpu.make_async_copy(
            curl_hbm.at[elem : min(elem + CHUNK, tile_count)],
            later_curl.at[elem - early : min(elem + CHUNK, tile_count) - early],
            curl_sems.at[(elem - early) // CHUNK],
        )
        for elem in range(early, tile_count, CHUNK)
    }
    for copy in small + list(later.values()):
        copy.start()
    edge_sums[...] = jnp.zeros_like(edge_sums)
    stacked = jnp.concatenate([window[...]] * 3, axis=0)
    samples = jnp.dot(pieces[...], stacked, preferred_element_type=jnp.float32)
    high = samples.astype(jnp.bfloat16)
    timed[:HALF, :] = high
    timed[HALF:, :] = (samples - high.astype(jnp.float32)).astype(jnp.bfloat16)
    columns = [
        jnp.broadcast_to(table[:, part : part + 1], (HALF, comps)) for part in range(parts_here)
    ]
    for copy in small:
        copy.wait()
    places = [[pattern[link, elem] for link in range(links)] for elem in range(tile_count)]
    count = jnp.int32(0)
    for elem in range(tile_count):
        for link, at in enumerate(places[elem]):
            outer[count] = elem * links + link
            count += jnp.where((at == 0) | (at == tile_count + 1), 1, 0)

    def blocks(elem):
        curl = first_curl[elem] if elem < early else later_curl[elem - early]
        return curl.reshape(links * tile, comps)

    def picked(elem):
        return jnp.concatenate(
            [timed[:, pl.ds(pl.multiple_of(at * tile, tile), tile)] for at in places[elem]], axis=1
        )

    def product(left, right):
        return jnp.dot(left, right, preferred_element_type=jnp.float32)

    def find_densities(one, two):
        cut, rest = 2 * tile, comps - 2 * tile
        samples_one, samples_two = picked(one), picked(two)
        split_one = product(samples_one, blocks(one)[:, :cut])
        densities[one, :, :cut] = split_one[:HALF] + split_one[HALF:]
        shared = product(
            jnp.concatenate([samples_one, samples_two], axis=0),
            jnp.concatenate([blocks(one)[:, cut:], blocks(two)[:, :rest]], axis=1),
        )
        densities[one, :, cut:] = shared[:HALF, :rest] + shared[HALF : 2 * HALF, :rest]
        densities[two, :, :rest] = shared[2 * HALF : 3 * HALF, rest:] + shared[3 * HALF :, rest:]
        split_two = product(samples_two, blocks(two)[:, rest:])
        densities[two, :, rest:] = split_two[:HALF] + split_two[HALF:]

    def project(elem):
        density = densities[elem]
        comp = [density[:, c * tile : (c + 1) * tile] for c in range(comps // tile)]
        square = comp[0] * comp[0]
        for c in comp[1:]:
            square = square + c * c
        region = region_ids[elem]
        reluct = law[0, region] + law[2, region] * square / (square + law[1, region])
        field = jnp.concatenate([reluct * c for c in comp], axis=1)
        rows = [jnp.sum(column * field, axis=0, keepdims=True) for column in columns]
        projected[elem] = jnp.concatenate(rows, axis=0) * (4.0 / SAMPLES)

    for elem in range(0, tile_count + 1, 2):
        if elem < tile_count:
            if elem in later:
                later[elem].wait()
            find_densities(elem, elem + 1)
        if elem:
            project(elem - 2)
            project(elem - 1)

    def add_outer(turn, carry):
        for slot in range(LISTED):
            spot = turn * LISTED + slot
            code = jnp.where(spot < count, outer[jnp.minimum(spot, count - 1)], 0)
            elem, link = code // links, code % links
            block = jnp.where(
                elem < early,
                first_curl[jnp.minimum(elem, early - 1), link],
                later_curl[jnp.maximum(elem - early, 0), link],
            )
            contrib = weighted(projected[elem], block)
            side = jnp.where(pattern[link, elem] == 0, 0, 1)
            edge_sums[slot, side] += jnp.where(spot < count, contrib, 0.0)
        return carry

    lax.fori_loop(0, (count + LISTED - 1) // LISTED, add_outer, 0)
    total = edge_sums[0]
    for slot in range(1, LISTED):
        total = total + edge_sums[slot]
    halo[:, :tile] = total[0]
    halo[:, tile:] = total[1]


def sum_kernel(
    projected,
    first_curl,
    later_curl,
    source,
    pattern_in,
    out,
    pattern,
    small_sem,
    *sums,
):
    links, tile, comps = first_curl.shape[1:]
    early = first_curl.shape[0]
    tile_count = early + later_curl.shape[0]
    small = pltpu.make_async_copy(pattern_in, pattern, small_sem)
    small.start()
    for total in sums:
        total[...] = jnp.zeros_like(total)
    small.wait()
    for elem in range(tile_count):
        curl = first_curl[elem] if elem < early else later_curl[elem - early]
        contrib = weighted(projected[elem], curl.reshape(links * tile, comps))
        for link in range(links):
            sums[link][pattern[link, elem]] += contrib[:, link * tile : (link + 1) * tile]
    for w in range(tile_count):
        at = slice(w * tile, (w + 1) * tile)
        total = sums[0][w + 1]
        for other in sums[1:]:
            total = total + other[w + 1]
        out[:, at] = total - source[:, at]


def halo_kernel(own, from_right, from_left, out):
    tile = from_left.shape[1] // 2
    out[...] = own[...]
    out[:, :tile] += from_left[:, tile:]
    out[:, -tile:] += from_right[:, :tile]


def per_device(coeffs, curl_tiles, pattern, region_ids, material_law, source):
    parts_here = coeffs.shape[0]
    tile_count, links, tile, comps = curl_tiles.shape
    group_size = lax.axis_size(GROUP)
    parts = parts_here * group_size
    table = half_table(parts)
    pieces = jnp.asarray(bf16_pieces(table))
    own_columns = jnp.asarray(
        table.reshape(HALF, group_size, parts_here).transpose(1, 0, 2).astype(np.float32)
    )
    vmem, hbm = pl.BlockSpec(memory_space=pltpu.VMEM), pl.BlockSpec(memory_space=pltpu.HBM)

    def in_vmem(array):
        return pltpu.with_memory_space_constraint(array, pltpu.VMEM)

    def in_hbm(array):
        return pltpu.with_memory_space_constraint(array, pltpu.HBM)

    early = tile_count // 2
    operands = [
        curl_tiles,
        own_columns,
        coeffs,
        pieces,
        source,
        pattern.T,
        region_ids,
        material_law,
    ]
    shapes = [
        (early,) + curl_tiles.shape[1:],
        own_columns.shape[1:],
    ] + [operand.shape for operand in operands[2:]]
    fetched = pl.pallas_call(
        fetch_kernel,
        out_shape=[pltpu.VMEM(shape, o.dtype) for shape, o in zip(shapes, operands)],
        in_specs=[hbm] * len(operands),
        out_specs=[vmem] * len(operands),
        scratch_shapes=[pltpu.SemaphoreType.DMA((len(operands),))],
        compiler_params=pltpu.CompilerParams(vmem_limit_bytes=16 * MIB),
        cost_estimate=pl.CostEstimate(
            flops=0, bytes_accessed=4 * early * links * tile * comps, transcendentals=0
        ),
        name="fetch_operands",
    )(*[in_hbm(operand) for operand in operands])
    first_curl, columns_here, coeffs_here, pieces_here, source_here, *others = fetched
    pattern_here = others[0]

    right, left = from_neighbours(coeffs, tile)
    block = jnp.concatenate([left, coeffs_here, right], axis=1)
    copies = jnp.broadcast_to(block[None], (group_size,) + block.shape)
    window = lax.all_to_all(copies, GROUP, 0, 0).reshape(parts, block.shape[1])
    pattern_words = pltpu.SMEM((links, tile_count), jnp.int32)
    projected, halo, later_curl = pl.pallas_call(
        field_kernel,
        out_shape=(
            pltpu.VMEM((tile_count, parts_here, comps), jnp.float32),
            pltpu.VMEM((parts_here, 2 * tile), jnp.float32),
            pltpu.VMEM((tile_count - early,) + curl_tiles.shape[1:], curl_tiles.dtype),
        ),
        in_specs=[vmem] * 7 + [hbm],
        out_specs=(vmem, vmem, vmem),
        scratch_shapes=[
            pattern_words,
            pltpu.SMEM(region_ids.shape, jnp.int32),
            pltpu.SMEM(material_law.shape, jnp.float32),
            pltpu.SMEM((links * tile_count + 1,), jnp.int32),
            pltpu.VMEM((SAMPLES, (tile_count + 2) * tile), jnp.bfloat16),
            pltpu.VMEM((tile_count, HALF, comps), jnp.float32),
            pltpu.VMEM((LISTED, 2, parts_here, tile), jnp.float32),
            pltpu.SemaphoreType.DMA((3,)),
            pltpu.SemaphoreType.DMA((pl.cdiv(tile_count - early, CHUNK),)),
        ],
        compiler_params=pltpu.CompilerParams(vmem_limit_bytes=32 * MIB),
        cost_estimate=pl.CostEstimate(
            flops=2 * SAMPLES * tile_count * links * tile * comps,
            bytes_accessed=2 * curl_tiles.size,
            transcendentals=0,
        ),
        name="shard_fields",
    )(
        in_vmem(window),
        *[in_vmem(array) for array in (first_curl, columns_here, pieces_here, *others)],
        in_hbm(curl_tiles),
    )
    if lax.axis_size("space") == 2:
        beside = [shifted(halo, "space", 1)] * 2
    else:
        beside = [shifted(halo, "space", -1), shifted(halo, "space", 1)]
    own = pl.pallas_call(
        sum_kernel,
        out_shape=pltpu.VMEM(source.shape, jnp.float32),
        in_specs=[vmem] * 5,
        out_specs=vmem,
        scratch_shapes=[
            pattern_words,
            pltpu.SemaphoreType.DMA,
        ]
        + [pltpu.VMEM((tile_count + 2, parts_here, tile), jnp.float32)] * links,
        compiler_params=pltpu.CompilerParams(vmem_limit_bytes=32 * MIB),
        cost_estimate=pl.CostEstimate(
            flops=2 * SAMPLES * tile_count * links * tile * comps,
            bytes_accessed=2 * curl_tiles.size,
            transcendentals=0,
        ),
        name="shard_sums",
    )(
        *[in_vmem(a) for a in (projected, first_curl, later_curl, source_here, pattern_here)],
    )
    return pl.pallas_call(
        halo_kernel,
        out_shape=jax.ShapeDtypeStruct(source.shape, jnp.float32),
        in_specs=[vmem] * 3,
        out_specs=vmem,
        compiler_params=pltpu.CompilerParams(vmem_limit_bytes=16 * MIB),
        name="halo_sum",
    )(in_vmem(own), *beside)


def solution(mesh):
    placed = (
        P(GROUP, "space"),
        P("space", None, None, None),
        P("space", None),
        P("space"),
        P(),
        P(GROUP, "space"),
    )
    return jax.shard_map(
        per_device,
        mesh=mesh,
        in_specs=placed,
        out_specs=P(GROUP, "space"),
        check_vma=False,
    )
```

```python
import math

import jax
import jax.numpy as jnp
import ml_dtypes
import numpy as np
from jax import lax
from jax.experimental import pallas as pl
from jax.experimental.pallas import tpu as pltpu
from jax.sharding import PartitionSpec as P

SAMPLES = 64
HALF = SAMPLES // 2
GROUP = ("harm", "samp")
MIB = 1024 * 1024
LISTED = 4
CHUNK = 2


def half_table(parts):
    sample_ids = np.arange(HALF)[:, None]
    part_ids = np.arange(parts)[None, :]
    phase = ((2 * (part_ids // 2) + 1) * sample_ids % SAMPLES) * (2.0 * math.pi / SAMPLES)
    return np.where(part_ids % 2 == 0, np.cos(phase), np.sin(phase))


def bf16_pieces(table):
    rest = table
    pieces = []
    for _ in range(3):
        piece = rest.astype(ml_dtypes.bfloat16)
        pieces.append(piece)
        rest = rest - piece.astype(np.float64)
    return np.concatenate(pieces, axis=-1)


def shifted(array, axis, by):
    count = lax.axis_size(axis)
    return lax.ppermute(array, axis, [(i, (i + by) % count) for i in range(count)])


def from_neighbours(array, tile):
    if lax.axis_size("space") == 2:
        other = shifted(array, "space", 1)
        return other[:, :tile], other[:, -tile:]
    return shifted(array[:, :tile], "space", -1), shifted(array[:, -tile:], "space", 1)


def fetch_kernel(*refs):
    count = (len(refs) - 1) // 2
    sources, targets, sems = refs[:count], refs[count : 2 * count], refs[-1]
    rank = lax.axis_index(GROUP)
    sources = (sources[0].at[: targets[0].shape[0]], sources[1].at[rank]) + sources[2:]
    copies = [
        pltpu.make_async_copy(source, target, sems.at[i])
        for i, (source, target) in enumerate(zip(sources, targets))
    ]
    for copy in copies:
        copy.start()
    for copy in copies:
        copy.wait()


def weighted(projected, blocks):
    return lax.dot_general(
        projected.astype(jnp.bfloat16),
        blocks,
        (((1,), (1,)), ((), ())),
        preferred_element_type=jnp.float32,
    )


def field_kernel(
    window,
    first_curl,
    table,
    pieces,
    pattern_in,
    region_in,
    law_in,
    curl_hbm,
    projected,
    halo,
    later_curl,
    pattern,
    region_ids,
    law,
    outer,
    timed,
    densities,
    edge_sums,
    small_sems,
    curl_sems,
):
    tile_count, links, tile, comps = curl_hbm.shape
    early = first_curl.shape[0]
    parts_here = halo.shape[0]
    fetched = [(pattern_in, pattern), (region_in, region_ids), (law_in, law)]
    small = [
        pltpu.make_async_copy(src, dst, small_sems.at[i]) for i, (src, dst) in enumerate(fetched)
    ]
    later = {
        elem: pltpu.make_async_copy(
            curl_hbm.at[elem : min(elem + CHUNK, tile_count)],
            later_curl.at[elem - early : min(elem + CHUNK, tile_count) - early],
            curl_sems.at[(elem - early) // CHUNK],
        )
        for elem in range(early, tile_count, CHUNK)
    }
    for copy in small + list(later.values()):
        copy.start()
    edge_sums[...] = jnp.zeros_like(edge_sums)
    stacked = jnp.concatenate([window[...]] * 3, axis=0)
    samples = jnp.dot(pieces[...], stacked, preferred_element_type=jnp.float32)
    high = samples.astype(jnp.bfloat16)
    timed[:HALF, :] = high
    timed[HALF:, :] = (samples - high.astype(jnp.float32)).astype(jnp.bfloat16)
    columns = [
        jnp.broadcast_to(table[:, part : part + 1], (HALF, comps)) for part in range(parts_here)
    ]
    for copy in small:
        copy.wait()
    places = [[pattern[link, elem] for link in range(links)] for elem in range(tile_count)]
    count = jnp.int32(0)
    for elem in range(tile_count):
        for link, at in enumerate(places[elem]):
            outer[count] = elem * links + link
            count += jnp.where((at == 0) | (at == tile_count + 1), 1, 0)

    def blocks(elem):
        curl = first_curl[elem] if elem < early else later_curl[elem - early]
        return curl.reshape(links * tile, comps)

    def picked(elem):
        return jnp.concatenate(
            [timed[:, pl.ds(pl.multiple_of(at * tile, tile), tile)] for at in places[elem]], axis=1
        )

    def product(left, right):
        return jnp.dot(left, right, preferred_element_type=jnp.float32)

    def find_densities(one, two):
        cut, rest = 2 * tile, comps - 2 * tile
        samples_one, samples_two = picked(one), picked(two)
        split_one = product(samples_one, blocks(one)[:, :cut])
        densities[one, :, :cut] = split_one[:HALF] + split_one[HALF:]
        shared = product(
            jnp.concatenate([samples_one, samples_two], axis=0),
            jnp.concatenate([blocks(one)[:, cut:], blocks(two)[:, :rest]], axis=1),
        )
        densities[one, :, cut:] = shared[:HALF, :rest] + shared[HALF : 2 * HALF, :rest]
        densities[two, :, :rest] = shared[2 * HALF : 3 * HALF, rest:] + shared[3 * HALF :, rest:]
        split_two = product(samples_two, blocks(two)[:, rest:])
        densities[two, :, rest:] = split_two[:HALF] + split_two[HALF:]

    def project(elem):
        density = densities[elem]
        comp = [density[:, c * tile : (c + 1) * tile] for c in range(comps // tile)]
        square = comp[0] * comp[0]
        for c in comp[1:]:
            square = square + c * c
        region = region_ids[elem]
        reluct = law[0, region] + law[2, region] * square / (square + law[1, region])
        field = jnp.concatenate([reluct * c for c in comp], axis=1)
        rows = [jnp.sum(column * field, axis=0, keepdims=True) for column in columns]
        projected[elem] = jnp.concatenate(rows, axis=0) * (4.0 / SAMPLES)

    for elem in range(0, tile_count + 1, 2):
        if elem < tile_count:
            if elem in later:
                later[elem].wait()
            find_densities(elem, elem + 1)
        if elem:
            project(elem - 2)
            project(elem - 1)

    def add_outer(turn, carry):
        for slot in range(LISTED):
            spot = turn * LISTED + slot
            code = jnp.where(spot < count, outer[jnp.minimum(spot, count - 1)], 0)
            elem, link = code // links, code % links
            block = jnp.where(
                elem < early,
                first_curl[jnp.minimum(elem, early - 1), link],
                later_curl[jnp.maximum(elem - early, 0), link],
            )
            contrib = weighted(projected[elem], block)
            side = jnp.where(pattern[link, elem] == 0, 0, 1)
            edge_sums[slot, side] += jnp.where(spot < count, contrib, 0.0)
        return carry

    lax.fori_loop(0, (count + LISTED - 1) // LISTED, add_outer, 0)
    total = edge_sums[0]
    for slot in range(1, LISTED):
        total = total + edge_sums[slot]
    halo[:, :tile] = total[0]
    halo[:, tile:] = total[1]


def sum_kernel(
    projected,
    first_curl,
    later_curl,
    source,
    pattern_in,
    out,
    pattern,
    small_sem,
    *sums,
):
    links, tile, comps = first_curl.shape[1:]
    early = first_curl.shape[0]
    tile_count = early + later_curl.shape[0]
    small = pltpu.make_async_copy(pattern_in, pattern, small_sem)
    small.start()
    for total in sums:
        total[...] = jnp.zeros_like(total)
    small.wait()
    for elem in range(tile_count):
        curl = first_curl[elem] if elem < early else later_curl[elem - early]
        contrib = weighted(projected[elem], curl.reshape(links * tile, comps))
        for link in range(links):
            sums[link][pattern[link, elem]] += contrib[:, link * tile : (link + 1) * tile]
    for w in range(tile_count):
        at = slice(w * tile, (w + 1) * tile)
        total = sums[0][w + 1]
        for other in sums[1:]:
            total = total + other[w + 1]
        out[:, at] = total - source[:, at]


def halo_kernel(own, from_right, from_left, out):
    tile = from_left.shape[1] // 2
    out[...] = own[...]
    out[:, :tile] += from_left[:, tile:]
    out[:, -tile:] += from_right[:, :tile]


def per_device(coeffs, curl_tiles, pattern, region_ids, material_law, source):
    parts_here = coeffs.shape[0]
    tile_count, links, tile, comps = curl_tiles.shape
    group_size = lax.axis_size(GROUP)
    parts = parts_here * group_size
    table = half_table(parts)
    pieces = jnp.asarray(bf16_pieces(table))
    own_columns = jnp.asarray(
        table.reshape(HALF, group_size, parts_here).transpose(1, 0, 2).astype(np.float32)
    )
    vmem, hbm = pl.BlockSpec(memory_space=pltpu.VMEM), pl.BlockSpec(memory_space=pltpu.HBM)

    def in_vmem(array):
        return pltpu.with_memory_space_constraint(array, pltpu.VMEM)

    def in_hbm(array):
        return pltpu.with_memory_space_constraint(array, pltpu.HBM)

    early = tile_count // 2
    operands = [
        curl_tiles,
        own_columns,
        coeffs,
        pieces,
        source,
        pattern.T,
        region_ids,
        material_law,
    ]
    shapes = [
        (early,) + curl_tiles.shape[1:],
        own_columns.shape[1:],
    ] + [operand.shape for operand in operands[2:]]
    fetched = pl.pallas_call(
        fetch_kernel,
        out_shape=[pltpu.VMEM(shape, o.dtype) for shape, o in zip(shapes, operands)],
        in_specs=[hbm] * len(operands),
        out_specs=[vmem] * len(operands),
        scratch_shapes=[pltpu.SemaphoreType.DMA((len(operands),))],
        compiler_params=pltpu.CompilerParams(vmem_limit_bytes=16 * MIB),
        cost_estimate=pl.CostEstimate(
            flops=0, bytes_accessed=4 * early * links * tile * comps, transcendentals=0
        ),
        name="fetch_operands",
    )(*[in_hbm(operand) for operand in operands])
    first_curl, columns_here, coeffs_here, pieces_here, source_here, *others = fetched
    pattern_here = others[0]

    right, left = from_neighbours(coeffs, tile)
    block = jnp.concatenate([left, coeffs_here, right], axis=1)
    copies = jnp.broadcast_to(block[None], (group_size,) + block.shape)
    window = lax.all_to_all(copies, GROUP, 0, 0).reshape(parts, block.shape[1])
    pattern_words = pltpu.SMEM((links, tile_count), jnp.int32)
    projected, halo, later_curl = pl.pallas_call(
        field_kernel,
        out_shape=(
            pltpu.VMEM((tile_count, parts_here, comps), jnp.float32),
            pltpu.VMEM((parts_here, 2 * tile), jnp.float32),
            pltpu.VMEM((tile_count - early,) + curl_tiles.shape[1:], curl_tiles.dtype),
        ),
        in_specs=[vmem] * 7 + [hbm],
        out_specs=(vmem, vmem, vmem),
        scratch_shapes=[
            pattern_words,
            pltpu.SMEM(region_ids.shape, jnp.int32),
            pltpu.SMEM(material_law.shape, jnp.float32),
            pltpu.SMEM((links * tile_count + 1,), jnp.int32),
            pltpu.VMEM((SAMPLES, (tile_count + 2) * tile), jnp.bfloat16),
            pltpu.VMEM((tile_count, HALF, comps), jnp.float32),
            pltpu.VMEM((LISTED, 2, parts_here, tile), jnp.float32),
            pltpu.SemaphoreType.DMA((3,)),
            pltpu.SemaphoreType.DMA((pl.cdiv(tile_count - early, CHUNK),)),
        ],
        compiler_params=pltpu.CompilerParams(vmem_limit_bytes=32 * MIB),
        cost_estimate=pl.CostEstimate(
            flops=2 * SAMPLES * tile_count * links * tile * comps,
            bytes_accessed=2 * curl_tiles.size,
            transcendentals=0,
        ),
        name="shard_fields",
    )(
        in_vmem(window),
        *[in_vmem(array) for array in (first_curl, columns_here, pieces_here, *others)],
        in_hbm(curl_tiles),
    )
    if lax.axis_size("space") == 2:
        beside = [shifted(halo, "space", 1)] * 2
    else:
        beside = [shifted(halo, "space", -1), shifted(halo, "space", 1)]
    own = pl.pallas_call(
        sum_kernel,
        out_shape=pltpu.VMEM(source.shape, jnp.float32),
        in_specs=[vmem] * 5,
        out_specs=vmem,
        scratch_shapes=[
            pattern_words,
            pltpu.SemaphoreType.DMA,
        ]
        + [pltpu.VMEM((tile_count + 2, parts_here, tile), jnp.float32)] * links,
        compiler_params=pltpu.CompilerParams(vmem_limit_bytes=32 * MIB),
        cost_estimate=pl.CostEstimate(
            flops=2 * SAMPLES * tile_count * links * tile * comps,
            bytes_accessed=2 * curl_tiles.size,
            transcendentals=0,
        ),
        name="shard_sums",
    )(
        *[in_vmem(a) for a in (projected, first_curl, later_curl, source_here, pattern_here)],
    )
    return pl.pallas_call(
        halo_kernel,
        out_shape=jax.ShapeDtypeStruct(source.shape, jnp.float32),
        in_specs=[vmem] * 3,
        out_specs=vmem,
        compiler_params=pltpu.CompilerParams(vmem_limit_bytes=16 * MIB),
        name="halo_sum",
    )(in_vmem(own), *beside)


def solution(mesh):
    placed = (
        P(GROUP, "space"),
        P("space", None, None, None),
        P("space", None),
        P("space"),
        P(),
        P(GROUP, "space"),
    )
    return jax.shard_map(
        per_device,
        mesh=mesh,
        in_specs=placed,
        out_specs=P(GROUP, "space"),
        check_vma=False,
    )
```

```python
import math

import jax
import jax.numpy as jnp
import ml_dtypes
import numpy as np
from jax import lax
from jax.experimental import pallas as pl
from jax.experimental.pallas import tpu as pltpu
from jax.sharding import PartitionSpec as P

SAMPLES = 64
HALF = SAMPLES // 2
GROUP = ("harm", "samp")
MIB = 1024 * 1024
LISTED = 4
CHUNK = 4


def half_table(parts):
    sample_ids = np.arange(HALF)[:, None]
    part_ids = np.arange(parts)[None, :]
    phase = ((2 * (part_ids // 2) + 1) * sample_ids % SAMPLES) * (2.0 * math.pi / SAMPLES)
    return np.where(part_ids % 2 == 0, np.cos(phase), np.sin(phase))


def bf16_pieces(table):
    rest = table
    pieces = []
    for _ in range(3):
        piece = rest.astype(ml_dtypes.bfloat16)
        pieces.append(piece)
        rest = rest - piece.astype(np.float64)
    return np.concatenate(pieces, axis=-1)


def shifted(array, axis, by):
    count = lax.axis_size(axis)
    return lax.ppermute(array, axis, [(i, (i + by) % count) for i in range(count)])


def from_neighbours(array, tile):
    first, last = array[..., :tile], array[..., -tile:]
    if lax.axis_size("space") == 2:
        other = shifted(jnp.concatenate([first, last], axis=-1), "space", 1)
        return other[..., :tile], other[..., tile:]
    return shifted(first, "space", -1), shifted(last, "space", 1)


def weighted(projected, blocks):
    return lax.dot_general(
        projected.astype(jnp.bfloat16),
        blocks,
        (((1,), (1,)), ((), ())),
        preferred_element_type=jnp.float32,
    )


def time_samples(pieces, rows):
    stacked = jnp.concatenate([rows] * 3, axis=0)
    samples = jnp.dot(pieces, stacked, preferred_element_type=jnp.float32)
    high = samples.astype(jnp.bfloat16)
    low = (samples - high.astype(jnp.float32)).astype(jnp.bfloat16)
    return jnp.concatenate([high, low], axis=0)


def flux_kernel(
    window,
    curl_hbm,
    pattern_hbm,
    pieces_hbm,
    table_hbm,
    *refs,
):
    others_hbm, refs = refs[:3], refs[3:]
    densities, curl, pieces, table = refs[:4]
    others, (pattern_here, pattern, timed, small_sems, curl_sems) = refs[4:7], refs[7:]
    tile_count, links, tile, comps = curl_hbm.shape
    fetched = [
        (pieces_hbm, pieces),
        (pattern_hbm, pattern),
        (table_hbm.at[lax.axis_index(GROUP)], table),
        (pattern_hbm, pattern_here),
        *zip(others_hbm, others),
    ]
    small = [
        pltpu.make_async_copy(src, dst, small_sems.at[i]) for i, (src, dst) in enumerate(fetched)
    ]
    later = {
        elem: pltpu.make_async_copy(
            curl_hbm.at[elem : min(elem + CHUNK, tile_count)],
            curl.at[elem : min(elem + CHUNK, tile_count)],
            curl_sems.at[elem // CHUNK],
        )
        for elem in range(0, tile_count, CHUNK)
    }
    for copy in small + list(later.values()):
        copy.start()
    outer = jnp.zeros((SAMPLES, tile), jnp.bfloat16)
    timed[:, :tile] = outer
    timed[:, (tile_count + 1) * tile :] = outer
    small[0].wait()
    timed[:, tile : (tile_count + 1) * tile] = time_samples(pieces[...], window[...])
    for copy in small[1:]:
        copy.wait()
    for elem in range(tile_count):
        if elem in later:
            later[elem].wait()
        places = [pattern[link, elem] for link in range(links)]
        picked = jnp.concatenate(
            [timed[:, pl.ds(pl.multiple_of(at * tile, tile), tile)] for at in places], axis=1
        )
        blocks = curl[elem].reshape(links * tile, comps)
        split = jnp.dot(picked, blocks, preferred_element_type=jnp.float32)
        densities[elem] = split[:HALF] + split[HALF:]


def field_kernel(
    partial,
    right,
    left,
    curl,
    pieces,
    table,
    pattern_in,
    region_in,
    law_in,
    projected,
    halo,
    pattern,
    region_ids,
    law,
    outer,
    timed,
    densities,
    edge_sums,
    small_sems,
):
    tile_count, links, tile, comps = curl.shape
    parts_here = halo.shape[0]
    fetched = [(pattern_in, pattern), (region_in, region_ids), (law_in, law)]
    small = [
        pltpu.make_async_copy(src, dst, small_sems.at[i]) for i, (src, dst) in enumerate(fetched)
    ]
    for copy in small:
        copy.start()
    edge_sums[...] = jnp.zeros_like(edge_sums)
    timed[0] = time_samples(pieces[...], left[...])
    timed[1] = time_samples(pieces[...], right[...])
    densities[...] = partial[...]
    columns = [
        jnp.broadcast_to(table[:, part : part + 1], (HALF, comps)) for part in range(parts_here)
    ]
    for copy in small:
        copy.wait()
    count = jnp.int32(0)
    for elem in range(tile_count):
        for link in range(links):
            at = pattern[link, elem]
            outer[count] = elem * links + link
            count += jnp.where((at == 0) | (at == tile_count + 1), 1, 0)

    def entry(turn, slot):
        spot = turn * LISTED + slot
        code = jnp.where(spot < count, outer[jnp.minimum(spot, count - 1)], 0)
        elem, link = code // links, code % links
        side = jnp.where(pattern[link, elem] == 0, 0, 1)
        return spot < count, elem, link, side

    def add_density(turn, carry):
        for slot in range(LISTED):
            listed, elem, link, side = entry(turn, slot)
            split = jnp.dot(timed[side], curl[elem, link], preferred_element_type=jnp.float32)
            densities[elem] += jnp.where(listed, split[:HALF] + split[HALF:], 0.0)
        return carry

    def project(elem):
        density = densities[elem]
        comp = [density[:, c * tile : (c + 1) * tile] for c in range(comps // tile)]
        square = comp[0] * comp[0]
        for c in comp[1:]:
            square = square + c * c
        region = region_ids[elem]
        reluct = law[0, region] + law[2, region] * square / (square + law[1, region])
        field = jnp.concatenate([reluct * c for c in comp], axis=1)
        rows = [jnp.sum(column * field, axis=0, keepdims=True) for column in columns]
        projected[elem] = jnp.concatenate(rows, axis=0) * (4.0 / SAMPLES)

    def add_outer(turn, carry):
        for slot in range(LISTED):
            listed, elem, link, side = entry(turn, slot)
            contrib = weighted(projected[elem], curl[elem, link])
            edge_sums[slot, side] += jnp.where(listed, contrib, 0.0)
        return carry

    turns = (count + LISTED - 1) // LISTED
    lax.fori_loop(0, turns, add_density, 0)
    for elem in range(tile_count):
        project(elem)
    lax.fori_loop(0, turns, add_outer, 0)
    total = edge_sums[0]
    for slot in range(1, LISTED):
        total = total + edge_sums[slot]
    halo[:, :tile] = total[0]
    halo[:, tile:] = total[1]


def sum_kernel(
    projected,
    curl,
    source,
    pattern_in,
    out,
    pattern,
    small_sem,
    *sums,
):
    tile_count, links, tile, comps = curl.shape
    small = pltpu.make_async_copy(pattern_in, pattern, small_sem)
    small.start()
    for total in sums:
        total[...] = jnp.zeros_like(total)
    small.wait()
    for elem in range(tile_count):
        contrib = weighted(projected[elem], curl[elem].reshape(links * tile, comps))
        for link in range(links):
            sums[link][pattern[link, elem]] += contrib[:, link * tile : (link + 1) * tile]
    for w in range(tile_count):
        at = slice(w * tile, (w + 1) * tile)
        total = sums[0][w + 1]
        for other in sums[1:]:
            total = total + other[w + 1]
        out[:, at] = total - source[:, at]


def halo_kernel(own, from_right, from_left, out):
    tile = from_left.shape[1] // 2
    out[...] = own[...]
    out[:, :tile] += from_left[:, tile:]
    out[:, -tile:] += from_right[:, :tile]


def per_device(coeffs, curl_tiles, pattern, region_ids, material_law, source):
    parts_here = coeffs.shape[0]
    tile_count, links, tile, comps = curl_tiles.shape
    group_size = lax.axis_size(GROUP)
    parts = parts_here * group_size
    table = half_table(parts)
    pieces = jnp.asarray(bf16_pieces(table))
    own_columns = jnp.asarray(
        table.reshape(HALF, group_size, parts_here).transpose(1, 0, 2).astype(np.float32)
    )
    vmem, hbm = pl.BlockSpec(memory_space=pltpu.VMEM), pl.BlockSpec(memory_space=pltpu.HBM)

    def in_vmem(array):
        return pltpu.with_memory_space_constraint(array, pltpu.VMEM)

    def in_hbm(array):
        return pltpu.with_memory_space_constraint(array, pltpu.HBM)

    flops = 2 * SAMPLES * tile_count * links * tile * comps
    limits = pltpu.CompilerParams(vmem_limit_bytes=32 * MIB)
    cost = pl.CostEstimate(flops=flops, bytes_accessed=2 * curl_tiles.size, transcendentals=0)
    pattern_words = pltpu.SMEM((links, tile_count), jnp.int32)
    kept = (region_ids, material_law, source)

    copies = jnp.broadcast_to(coeffs[None], (group_size,) + coeffs.shape)
    near = lax.all_to_all(copies, GROUP, 0, 0)
    right, left = from_neighbours(near, tile)
    densities, curl, pieces_here, columns_here, region_here, law_here, source_here, pattern_here = (
        pl.pallas_call(
            flux_kernel,
            out_shape=[
                pltpu.VMEM((tile_count, HALF, comps), jnp.float32),
                pltpu.VMEM(curl_tiles.shape, curl_tiles.dtype),
                pltpu.VMEM(pieces.shape, pieces.dtype),
                pltpu.VMEM(own_columns.shape[1:], jnp.float32),
                *[pltpu.VMEM(operand.shape, operand.dtype) for operand in kept],
                pltpu.VMEM((links, tile_count), jnp.int32),
            ],
            in_specs=[vmem] + [hbm] * 7,
            out_specs=[vmem] * 8,
            scratch_shapes=[
                pattern_words,
                pltpu.VMEM((SAMPLES, (tile_count + 2) * tile), jnp.bfloat16),
                pltpu.SemaphoreType.DMA((7,)),
                pltpu.SemaphoreType.DMA((pl.cdiv(tile_count, CHUNK),)),
            ],
            compiler_params=limits,
            cost_estimate=cost,
            name="shard_flux",
        )(
            in_vmem(near.reshape(parts, -1)),
            *[in_hbm(array) for array in (curl_tiles, pattern.T, pieces, own_columns, *kept)],
        )
    )
    projected, halo = pl.pallas_call(
        field_kernel,
        out_shape=(
            pltpu.VMEM((tile_count, parts_here, comps), jnp.float32),
            pltpu.VMEM((parts_here, 2 * tile), jnp.float32),
        ),
        in_specs=[vmem] * 9,
        out_specs=(vmem, vmem),
        scratch_shapes=[
            pattern_words,
            pltpu.SMEM(region_ids.shape, jnp.int32),
            pltpu.SMEM(material_law.shape, jnp.float32),
            pltpu.SMEM((links * tile_count + 1,), jnp.int32),
            pltpu.VMEM((2, SAMPLES, tile), jnp.bfloat16),
            pltpu.VMEM((tile_count, HALF, comps), jnp.float32),
            pltpu.VMEM((LISTED, 2, parts_here, tile), jnp.float32),
            pltpu.SemaphoreType.DMA((3,)),
        ],
        compiler_params=limits,
        cost_estimate=cost,
        name="shard_fields",
    )(
        *[
            in_vmem(array)
            for array in (
                densities,
                right.reshape(parts, tile),
                left.reshape(parts, tile),
                curl,
                pieces_here,
                columns_here,
                pattern_here,
                region_here,
                law_here,
            )
        ],
    )
    if lax.axis_size("space") == 2:
        beside = [shifted(halo, "space", 1)] * 2
    else:
        beside = [shifted(halo, "space", -1), shifted(halo, "space", 1)]
    own = pl.pallas_call(
        sum_kernel,
        out_shape=pltpu.VMEM(source.shape, jnp.float32),
        in_specs=[vmem] * 4,
        out_specs=vmem,
        scratch_shapes=[
            pattern_words,
            pltpu.SemaphoreType.DMA,
        ]
        + [pltpu.VMEM((tile_count + 2, parts_here, tile), jnp.float32)] * links,
        compiler_params=limits,
        cost_estimate=cost,
        name="shard_sums",
    )(*[in_vmem(array) for array in (projected, curl, source_here, pattern_here)])
    return pl.pallas_call(
        halo_kernel,
        out_shape=jax.ShapeDtypeStruct(source.shape, jnp.float32),
        in_specs=[vmem] * 3,
        out_specs=vmem,
        compiler_params=pltpu.CompilerParams(vmem_limit_bytes=16 * MIB),
        name="halo_sum",
    )(in_vmem(own), *beside)


def solution(mesh):
    placed = (
        P(GROUP, "space"),
        P("space", None, None, None),
        P("space", None),
        P("space"),
        P(),
        P(GROUP, "space"),
    )
    return jax.shard_map(
        per_device,
        mesh=mesh,
        in_specs=placed,
        out_specs=P(GROUP, "space"),
        check_vma=False,
    )
```

```python
import math

import jax
import jax.numpy as jnp
import ml_dtypes
import numpy as np
from jax import lax
from jax.experimental import pallas as pl
from jax.experimental.pallas import tpu as pltpu
from jax.sharding import PartitionSpec as P

SAMPLES = 64
HALF = SAMPLES // 2
GROUP = ("chip", "core", "samp")
MIB = 1024 * 1024
LISTED = 4
CHUNK = 4


def half_table(parts):
    sample_ids = np.arange(HALF)[:, None]
    part_ids = np.arange(parts)[None, :]
    phase = ((2 * (part_ids // 2) + 1) * sample_ids % SAMPLES) * (2.0 * math.pi / SAMPLES)
    return np.where(part_ids % 2 == 0, np.cos(phase), np.sin(phase))


def bf16_pieces(table):
    rest = table
    pieces = []
    for _ in range(3):
        piece = rest.astype(ml_dtypes.bfloat16)
        pieces.append(piece)
        rest = rest - piece.astype(np.float64)
    return np.concatenate(pieces, axis=-1)


def across(array, core_step, space_step):
    cores, shards = lax.axis_size("core"), lax.axis_size("space")
    pairs = [
        (c * shards + s, (c + core_step) % cores * shards + (s + space_step) % shards)
        for c in range(cores)
        for s in range(shards)
    ]
    return lax.ppermute(array, ("core", "space"), pairs)


def from_neighbours(array, tile):
    if lax.axis_size("space") == 2:
        other = across(array, 1, 1)
        return other[:, -tile:], other[:, :tile]
    return across(array[:, -tile:], 1, 1), across(array[:, :tile], 1, -1)


def fetch_kernel(*refs):
    count = (len(refs) - 1) // 2
    sources, targets, sems = refs[:count], refs[count : 2 * count], refs[-1]
    rank = lax.axis_index(GROUP)
    sources = (sources[0].at[: targets[0].shape[0]], sources[1].at[rank]) + sources[2:]
    copies = [
        pltpu.make_async_copy(source, target, sems.at[i])
        for i, (source, target) in enumerate(zip(sources, targets))
    ]
    for copy in copies:
        copy.start()
    for copy in copies:
        copy.wait()


def time_samples(pieces, rows):
    stacked = jnp.concatenate([rows] * 3, axis=0)
    samples = jnp.dot(pieces, stacked, preferred_element_type=jnp.float32)
    high = samples.astype(jnp.bfloat16)
    low = (samples - high.astype(jnp.float32)).astype(jnp.bfloat16)
    return jnp.concatenate([high, low], axis=0)


def weighted(projected, blocks):
    return lax.dot_general(
        projected.astype(jnp.bfloat16),
        blocks,
        (((1,), (1,)), ((), ())),
        preferred_element_type=jnp.float32,
    )


def field_kernel(
    window,
    first_curl,
    table,
    pieces,
    pattern_in,
    region_in,
    law_in,
    curl_hbm,
    projected,
    halo,
    later_curl,
    pattern,
    region_ids,
    law,
    outer,
    timed,
    densities,
    edge_sums,
    small_sems,
    curl_sems,
):
    tile_count, links, tile, comps = curl_hbm.shape
    early = first_curl.shape[0]
    parts_here = halo.shape[0]
    fetched = [(pattern_in, pattern), (region_in, region_ids), (law_in, law)]
    small = [
        pltpu.make_async_copy(src, dst, small_sems.at[i]) for i, (src, dst) in enumerate(fetched)
    ]
    later = {
        elem: pltpu.make_async_copy(
            curl_hbm.at[elem : min(elem + CHUNK, tile_count)],
            later_curl.at[elem - early : min(elem + CHUNK, tile_count) - early],
            curl_sems.at[(elem - early) // CHUNK],
        )
        for elem in range(early, tile_count, CHUNK)
    }
    for copy in small + list(later.values()):
        copy.start()
    edge_sums[...] = jnp.zeros_like(edge_sums)
    own, outer_tiles = pieces[0], pieces[1]
    timed[:, tile:-tile] = time_samples(own, window[:, tile:-tile])
    timed[:, :tile] = time_samples(outer_tiles, window[:, :tile])
    timed[:, -tile:] = time_samples(outer_tiles, window[:, -tile:])
    columns = [
        jnp.broadcast_to(table[:, part : part + 1], (HALF, comps)) for part in range(parts_here)
    ]
    for copy in small:
        copy.wait()
    places = [[pattern[link, elem] for link in range(links)] for elem in range(tile_count)]
    count = jnp.int32(0)
    for elem in range(tile_count):
        for link, at in enumerate(places[elem]):
            outer[count] = elem * links + link
            count += jnp.where((at == 0) | (at == tile_count + 1), 1, 0)

    def blocks(elem):
        curl = first_curl[elem] if elem < early else later_curl[elem - early]
        return curl.reshape(links * tile, comps)

    def find_density(elem):
        picked = jnp.concatenate(
            [timed[:, pl.ds(pl.multiple_of(at * tile, tile), tile)] for at in places[elem]], axis=1
        )
        split = jnp.dot(picked, blocks(elem), preferred_element_type=jnp.float32)
        densities[elem] = split[:HALF] + split[HALF:]

    def project(elem):
        density = densities[elem]
        comp = [density[:, c * tile : (c + 1) * tile] for c in range(comps // tile)]
        square = comp[0] * comp[0]
        for c in comp[1:]:
            square = square + c * c
        region = region_ids[elem]
        reluct = law[0, region] + law[2, region] * square / (square + law[1, region])
        field = jnp.concatenate([reluct * c for c in comp], axis=1)
        rows = [jnp.sum(column * field, axis=0, keepdims=True) for column in columns]
        projected[elem] = jnp.concatenate(rows, axis=0) * (4.0 / SAMPLES)

    for turn in range(tile_count + 1):
        if turn < tile_count:
            if turn in later:
                later[turn].wait()
            find_density(turn)
        if turn:
            project(turn - 1)

    def add_outer(turn, carry):
        for slot in range(LISTED):
            spot = turn * LISTED + slot
            code = jnp.where(spot < count, outer[jnp.minimum(spot, count - 1)], 0)
            elem, link = code // links, code % links
            block = jnp.where(
                elem < early,
                first_curl[jnp.minimum(elem, early - 1), link],
                later_curl[jnp.maximum(elem - early, 0), link],
            )
            contrib = weighted(projected[elem], block)
            side = jnp.where(pattern[link, elem] == 0, 0, 1)
            edge_sums[slot, side] += jnp.where(spot < count, contrib, 0.0)
        return carry

    lax.fori_loop(0, (count + LISTED - 1) // LISTED, add_outer, 0)
    total = edge_sums[0]
    for slot in range(1, LISTED):
        total = total + edge_sums[slot]
    halo[:, :tile] = total[0]
    halo[:, tile:] = total[1]


def sum_kernel(
    projected,
    first_curl,
    later_curl,
    source,
    pattern_in,
    out,
    pattern,
    small_sem,
    *sums,
):
    links, tile, comps = first_curl.shape[1:]
    early = first_curl.shape[0]
    tile_count = early + later_curl.shape[0]
    small = pltpu.make_async_copy(pattern_in, pattern, small_sem)
    small.start()
    for total in sums:
        total[...] = jnp.zeros_like(total)
    small.wait()
    for elem in range(tile_count):
        curl = first_curl[elem] if elem < early else later_curl[elem - early]
        contrib = weighted(projected[elem], curl.reshape(links * tile, comps))
        for link in range(links):
            sums[link][pattern[link, elem]] += contrib[:, link * tile : (link + 1) * tile]
    for w in range(tile_count):
        at = slice(w * tile, (w + 1) * tile)
        total = sums[0][w + 1]
        for other in sums[1:]:
            total = total + other[w + 1]
        out[:, at] = total - source[:, at]


def halo_kernel(own, from_right, from_left, out):
    tile = from_left.shape[1] // 2
    out[...] = own[...]
    out[:, :tile] += from_left[:, tile:]
    out[:, -tile:] += from_right[:, :tile]


def per_device(coeffs, curl_tiles, pattern, region_ids, material_law, source):
    parts_here = coeffs.shape[0]
    tile_count, links, tile, comps = curl_tiles.shape
    chips, cores, samp = (lax.axis_size(axis) for axis in GROUP)
    group_size = chips * cores * samp
    parts = parts_here * group_size
    table = half_table(parts)
    before = np.roll(np.arange(parts).reshape(chips, cores, -1), 1, axis=1).reshape(-1)
    pieces = jnp.asarray(np.stack([bf16_pieces(table), bf16_pieces(table[:, before])]))
    own_columns = jnp.asarray(
        table.reshape(HALF, group_size, parts_here).transpose(1, 0, 2).astype(np.float32)
    )
    vmem, hbm = pl.BlockSpec(memory_space=pltpu.VMEM), pl.BlockSpec(memory_space=pltpu.HBM)

    def in_vmem(array):
        return pltpu.with_memory_space_constraint(array, pltpu.VMEM)

    def in_hbm(array):
        return pltpu.with_memory_space_constraint(array, pltpu.HBM)

    early = tile_count // 2
    operands = [
        curl_tiles,
        own_columns,
        coeffs,
        pieces,
        source,
        pattern.T,
        region_ids,
        material_law,
    ]
    shapes = [
        (early,) + curl_tiles.shape[1:],
        own_columns.shape[1:],
    ] + [operand.shape for operand in operands[2:]]
    fetched = pl.pallas_call(
        fetch_kernel,
        out_shape=[pltpu.VMEM(shape, o.dtype) for shape, o in zip(shapes, operands)],
        in_specs=[hbm] * len(operands),
        out_specs=[vmem] * len(operands),
        scratch_shapes=[pltpu.SemaphoreType.DMA((len(operands),))],
        compiler_params=pltpu.CompilerParams(vmem_limit_bytes=16 * MIB),
        cost_estimate=pl.CostEstimate(
            flops=0, bytes_accessed=4 * early * links * tile * comps, transcendentals=0
        ),
        name="fetch_operands",
    )(*[in_hbm(operand) for operand in operands])
    first_curl, columns_here, coeffs_here, pieces_here, source_here, *others = fetched
    pattern_here = others[0]

    left, right = from_neighbours(coeffs, tile)
    block = jnp.concatenate([left, coeffs_here, right], axis=1)
    copies = jnp.broadcast_to(block[None], (group_size,) + block.shape)
    window = lax.all_to_all(copies, GROUP, 0, 0).reshape(parts, block.shape[1])
    pattern_words = pltpu.SMEM((links, tile_count), jnp.int32)
    projected, halo, later_curl = pl.pallas_call(
        field_kernel,
        out_shape=(
            pltpu.VMEM((tile_count, parts_here, comps), jnp.float32),
            pltpu.VMEM((parts_here, 2 * tile), jnp.float32),
            pltpu.VMEM((tile_count - early,) + curl_tiles.shape[1:], curl_tiles.dtype),
        ),
        in_specs=[vmem] * 7 + [hbm],
        out_specs=(vmem, vmem, vmem),
        scratch_shapes=[
            pattern_words,
            pltpu.SMEM(region_ids.shape, jnp.int32),
            pltpu.SMEM(material_law.shape, jnp.float32),
            pltpu.SMEM((links * tile_count + 1,), jnp.int32),
            pltpu.VMEM((SAMPLES, (tile_count + 2) * tile), jnp.bfloat16),
            pltpu.VMEM((tile_count, HALF, comps), jnp.float32),
            pltpu.VMEM((LISTED, 2, parts_here, tile), jnp.float32),
            pltpu.SemaphoreType.DMA((3,)),
            pltpu.SemaphoreType.DMA((pl.cdiv(tile_count - early, CHUNK),)),
        ],
        compiler_params=pltpu.CompilerParams(vmem_limit_bytes=32 * MIB),
        cost_estimate=pl.CostEstimate(
            flops=2 * SAMPLES * tile_count * links * tile * comps,
            bytes_accessed=2 * curl_tiles.size,
            transcendentals=0,
        ),
        name="shard_fields",
    )(
        in_vmem(window),
        *[in_vmem(array) for array in (first_curl, columns_here, pieces_here, *others)],
        in_hbm(curl_tiles),
    )
    if lax.axis_size("space") == 2:
        beside = [across(halo, 0, 1)] * 2
    else:
        beside = [across(halo, 0, -1), across(halo, 0, 1)]
    own = pl.pallas_call(
        sum_kernel,
        out_shape=pltpu.VMEM(source.shape, jnp.float32),
        in_specs=[vmem] * 5,
        out_specs=vmem,
        scratch_shapes=[
            pattern_words,
            pltpu.SemaphoreType.DMA,
        ]
        + [pltpu.VMEM((tile_count + 2, parts_here, tile), jnp.float32)] * links,
        compiler_params=pltpu.CompilerParams(vmem_limit_bytes=32 * MIB),
        cost_estimate=pl.CostEstimate(
            flops=2 * SAMPLES * tile_count * links * tile * comps,
            bytes_accessed=2 * curl_tiles.size,
            transcendentals=0,
        ),
        name="shard_sums",
    )(
        *[in_vmem(a) for a in (projected, first_curl, later_curl, source_here, pattern_here)],
    )
    return pl.pallas_call(
        halo_kernel,
        out_shape=jax.ShapeDtypeStruct(source.shape, jnp.float32),
        in_specs=[vmem] * 3,
        out_specs=vmem,
        compiler_params=pltpu.CompilerParams(vmem_limit_bytes=16 * MIB),
        name="halo_sum",
    )(in_vmem(own), *beside)


def solution(mesh):
    at = mesh.axis_names.index("harm")
    harm = mesh.shape["harm"]
    cores = 2 if harm % 2 == 0 else 1
    sizes = mesh.devices.shape
    split = jax.sharding.Mesh(
        mesh.devices.reshape(sizes[:at] + (harm // cores, cores) + sizes[at + 1 :]),
        mesh.axis_names[:at] + ("chip", "core") + mesh.axis_names[at + 1 :],
    )
    placed = (
        P(GROUP, "space"),
        P("space", None, None, None),
        P("space", None),
        P("space"),
        P(),
        P(GROUP, "space"),
    )
    return jax.shard_map(
        per_device,
        mesh=split,
        in_specs=placed,
        out_specs=P(GROUP, "space"),
        check_vma=False,
    )
```

```python
import math

import jax
import jax.numpy as jnp
import ml_dtypes
import numpy as np
from jax import lax
from jax.experimental import pallas as pl
from jax.experimental.pallas import tpu as pltpu
from jax.sharding import PartitionSpec as P

SAMPLES = 64
HALF = SAMPLES // 2
GROUP = ("chip", "core", "samp")
MIB = 1024 * 1024
LISTED = 4
CHUNK = 4
AHEAD = 3


def half_table(parts):
    sample_ids = np.arange(HALF)[:, None]
    part_ids = np.arange(parts)[None, :]
    phase = ((2 * (part_ids // 2) + 1) * sample_ids % SAMPLES) * (2.0 * math.pi / SAMPLES)
    return np.where(part_ids % 2 == 0, np.cos(phase), np.sin(phase))


def bf16_pieces(table):
    rest = table
    pieces = []
    for _ in range(3):
        piece = rest.astype(ml_dtypes.bfloat16)
        pieces.append(piece)
        rest = rest - piece.astype(np.float64)
    return np.concatenate(pieces, axis=-1)


def across(array, core_step, space_step):
    cores, shards = lax.axis_size("core"), lax.axis_size("space")
    pairs = [
        (c * shards + s, (c + core_step) % cores * shards + (s + space_step) % shards)
        for c in range(cores)
        for s in range(shards)
    ]
    return lax.ppermute(array, ("core", "space"), pairs)


def from_neighbours(array, tile):
    if lax.axis_size("space") == 2:
        other = across(array, 1, 1)
        return other[:, -tile:], other[:, :tile]
    return across(array[:, -tile:], 1, 1), across(array[:, :tile], 1, -1)


def fetch_kernel(*refs):
    count = (len(refs) - 1) // 2
    sources, targets, sems = refs[:count], refs[count : 2 * count], refs[-1]
    rank = lax.axis_index(GROUP)
    sources = (sources[0].at[: targets[0].shape[0]], sources[1].at[rank]) + sources[2:]
    copies = [
        pltpu.make_async_copy(source, target, sems.at[i])
        for i, (source, target) in enumerate(zip(sources, targets))
    ]
    for copy in copies:
        copy.start()
    for copy in copies:
        copy.wait()


def time_samples(pieces, rows):
    stacked = jnp.concatenate([rows] * 3, axis=0)
    samples = jnp.dot(pieces, stacked, preferred_element_type=jnp.float32)
    high = samples.astype(jnp.bfloat16)
    low = (samples - high.astype(jnp.float32)).astype(jnp.bfloat16)
    return jnp.concatenate([high, low], axis=0)


def weighted(projected, blocks):
    return lax.dot_general(
        projected.astype(jnp.bfloat16),
        blocks,
        (((1,), (1,)), ((), ())),
        preferred_element_type=jnp.float32,
    )


def field_kernel(
    window,
    first_curl,
    table,
    pieces,
    pattern_in,
    region_in,
    law_in,
    curl_hbm,
    projected,
    halo,
    later_curl,
    pattern,
    region_ids,
    law,
    outer,
    timed,
    densities,
    edge_sums,
    small_sems,
    curl_sems,
):
    tile_count, links, tile, comps = curl_hbm.shape
    early = first_curl.shape[0]
    parts_here = halo.shape[0]
    fetched = [(pattern_in, pattern), (region_in, region_ids), (law_in, law)]
    small = [
        pltpu.make_async_copy(src, dst, small_sems.at[i]) for i, (src, dst) in enumerate(fetched)
    ]
    later = {
        elem: pltpu.make_async_copy(
            curl_hbm.at[elem : min(elem + CHUNK, tile_count)],
            later_curl.at[elem - early : min(elem + CHUNK, tile_count) - early],
            curl_sems.at[(elem - early) // CHUNK],
        )
        for elem in range(early, tile_count, CHUNK)
    }
    for copy in small + list(later.values()):
        copy.start()
    edge_sums[...] = jnp.zeros_like(edge_sums)
    own, outer_tiles = pieces[0], pieces[1]
    timed[:, tile:-tile] = time_samples(own, window[:, tile:-tile])
    timed[:, :tile] = time_samples(outer_tiles, window[:, :tile])
    timed[:, -tile:] = time_samples(outer_tiles, window[:, -tile:])
    columns = [
        jnp.broadcast_to(table[:, part : part + 1], (HALF, comps)) for part in range(parts_here)
    ]
    for copy in small:
        copy.wait()
    places = [[pattern[link, elem] for link in range(links)] for elem in range(tile_count)]
    count = jnp.int32(0)
    for elem in range(tile_count):
        for link, at in enumerate(places[elem]):
            outer[count] = elem * links + link
            count += jnp.where((at == 0) | (at == tile_count + 1), 1, 0)

    def blocks(elem):
        curl = first_curl[elem] if elem < early else later_curl[elem - early]
        return curl.reshape(links * tile, comps)

    def find_density(elem):
        picked = jnp.concatenate(
            [timed[:, pl.ds(pl.multiple_of(at * tile, tile), tile)] for at in places[elem]], axis=1
        )
        split = jnp.dot(picked, blocks(elem), preferred_element_type=jnp.float32)
        densities[elem] = split[:HALF] + split[HALF:]

    def project(elem):
        density = densities[elem]
        comp = [density[:, c * tile : (c + 1) * tile] for c in range(comps // tile)]
        square = comp[0] * comp[0]
        for c in comp[1:]:
            square = square + c * c
        region = region_ids[elem]
        reluct = law[0, region] + law[2, region] * square / (square + law[1, region])
        field = jnp.concatenate([reluct * c for c in comp], axis=1)
        rows = [jnp.sum(column * field, axis=0, keepdims=True) for column in columns]
        projected[elem] = jnp.concatenate(rows, axis=0) * (4.0 / SAMPLES)

    for turn in range(tile_count + 1):
        if turn < tile_count:
            if turn in later:
                later[turn].wait()
            find_density(turn)
        if turn:
            project(turn - 1)

    def add_outer(turn, carry):
        for slot in range(LISTED):
            spot = turn * LISTED + slot
            code = jnp.where(spot < count, outer[jnp.minimum(spot, jnp.maximum(count - 1, 0))], 0)
            elem, link = code // links, code % links
            block = jnp.where(
                elem < early,
                first_curl[jnp.minimum(elem, early - 1), link],
                later_curl[jnp.maximum(elem - early, 0), link],
            )
            contrib = weighted(projected[elem], block)
            side = jnp.where(pattern[link, elem] == 0, 0, 1)
            edge_sums[slot, side] += jnp.where(spot < count, contrib, 0.0)
        return carry

    add_outer(0, 0)
    lax.fori_loop(1, (count + LISTED - 1) // LISTED, add_outer, 0)
    total = edge_sums[0]
    for slot in range(1, LISTED):
        total = total + edge_sums[slot]
    halo[:, :tile] = total[0]
    halo[:, tile:] = total[1]


def sum_kernel(
    projected,
    first_curl,
    later_curl,
    source,
    pattern_in,
    out,
    pattern,
    small_sem,
    *sums,
):
    links, tile, comps = first_curl.shape[1:]
    early = first_curl.shape[0]
    tile_count = early + later_curl.shape[0]
    small = pltpu.make_async_copy(pattern_in, pattern, small_sem)
    small.start()
    for total in sums:
        total[...] = jnp.zeros_like(total)

    def contribution(elem):
        curl = first_curl[elem] if elem < early else later_curl[elem - early]
        return weighted(projected[elem], curl.reshape(links * tile, comps))

    ahead = [contribution(elem) for elem in range(AHEAD)]
    small.wait()
    for elem in range(tile_count):
        contrib = ahead[elem] if elem < AHEAD else contribution(elem)
        for link in range(links):
            sums[link][pattern[link, elem]] += contrib[:, link * tile : (link + 1) * tile]
    for w in range(tile_count):
        at = slice(w * tile, (w + 1) * tile)
        total = sums[0][w + 1]
        for other in sums[1:]:
            total = total + other[w + 1]
        out[:, at] = total - source[:, at]


def halo_kernel(own, from_right, from_left, out):
    tile = from_left.shape[1] // 2
    out[...] = own[...]
    out[:, :tile] += from_left[:, tile:]
    out[:, -tile:] += from_right[:, :tile]


def per_device(coeffs, curl_tiles, pattern, region_ids, material_law, source):
    parts_here = coeffs.shape[0]
    tile_count, links, tile, comps = curl_tiles.shape
    chips, cores, samp = (lax.axis_size(axis) for axis in GROUP)
    group_size = chips * cores * samp
    parts = parts_here * group_size
    table = half_table(parts)
    before = np.roll(np.arange(parts).reshape(chips, cores, -1), 1, axis=1).reshape(-1)
    pieces = jnp.asarray(np.stack([bf16_pieces(table), bf16_pieces(table[:, before])]))
    own_columns = jnp.asarray(
        table.reshape(HALF, group_size, parts_here).transpose(1, 0, 2).astype(np.float32)
    )
    vmem, hbm = pl.BlockSpec(memory_space=pltpu.VMEM), pl.BlockSpec(memory_space=pltpu.HBM)

    def in_vmem(array):
        return pltpu.with_memory_space_constraint(array, pltpu.VMEM)

    def in_hbm(array):
        return pltpu.with_memory_space_constraint(array, pltpu.HBM)

    early = tile_count // 2
    operands = [
        curl_tiles,
        own_columns,
        coeffs,
        pieces,
        source,
        pattern.T,
        region_ids,
        material_law,
    ]
    shapes = [
        (early,) + curl_tiles.shape[1:],
        own_columns.shape[1:],
    ] + [operand.shape for operand in operands[2:]]
    fetched = pl.pallas_call(
        fetch_kernel,
        out_shape=[pltpu.VMEM(shape, o.dtype) for shape, o in zip(shapes, operands)],
        in_specs=[hbm] * len(operands),
        out_specs=[vmem] * len(operands),
        scratch_shapes=[pltpu.SemaphoreType.DMA((len(operands),))],
        compiler_params=pltpu.CompilerParams(vmem_limit_bytes=16 * MIB),
        cost_estimate=pl.CostEstimate(
            flops=0, bytes_accessed=4 * early * links * tile * comps, transcendentals=0
        ),
        name="fetch_operands",
    )(*[in_hbm(operand) for operand in operands])
    first_curl, columns_here, coeffs_here, pieces_here, source_here, *others = fetched
    pattern_here = others[0]

    left, right = from_neighbours(coeffs, tile)
    block = jnp.concatenate([left, coeffs_here, right], axis=1)
    copies = jnp.broadcast_to(block[None], (group_size,) + block.shape)
    window = lax.all_to_all(copies, GROUP, 0, 0).reshape(parts, block.shape[1])
    pattern_words = pltpu.SMEM((links, tile_count), jnp.int32)
    projected, halo, later_curl = pl.pallas_call(
        field_kernel,
        out_shape=(
            pltpu.VMEM((tile_count, parts_here, comps), jnp.float32),
            pltpu.VMEM((parts_here, 2 * tile), jnp.float32),
            pltpu.VMEM((tile_count - early,) + curl_tiles.shape[1:], curl_tiles.dtype),
        ),
        in_specs=[vmem] * 7 + [hbm],
        out_specs=(vmem, vmem, vmem),
        scratch_shapes=[
            pattern_words,
            pltpu.SMEM(region_ids.shape, jnp.int32),
            pltpu.SMEM(material_law.shape, jnp.float32),
            pltpu.SMEM((links * tile_count + 1,), jnp.int32),
            pltpu.VMEM((SAMPLES, (tile_count + 2) * tile), jnp.bfloat16),
            pltpu.VMEM((tile_count, HALF, comps), jnp.float32),
            pltpu.VMEM((LISTED, 2, parts_here, tile), jnp.float32),
            pltpu.SemaphoreType.DMA((3,)),
            pltpu.SemaphoreType.DMA((pl.cdiv(tile_count - early, CHUNK),)),
        ],
        compiler_params=pltpu.CompilerParams(vmem_limit_bytes=32 * MIB),
        cost_estimate=pl.CostEstimate(
            flops=2 * SAMPLES * tile_count * links * tile * comps,
            bytes_accessed=2 * curl_tiles.size,
            transcendentals=0,
        ),
        name="shard_fields",
    )(
        in_vmem(window),
        *[in_vmem(array) for array in (first_curl, columns_here, pieces_here, *others)],
        in_hbm(curl_tiles),
    )
    if lax.axis_size("space") == 2:
        beside = [across(halo, 0, 1)] * 2
    else:
        beside = [across(halo, 0, -1), across(halo, 0, 1)]
    own = pl.pallas_call(
        sum_kernel,
        out_shape=pltpu.VMEM(source.shape, jnp.float32),
        in_specs=[vmem] * 5,
        out_specs=vmem,
        scratch_shapes=[
            pattern_words,
            pltpu.SemaphoreType.DMA,
        ]
        + [pltpu.VMEM((tile_count + 2, parts_here, tile), jnp.float32)] * links,
        compiler_params=pltpu.CompilerParams(vmem_limit_bytes=32 * MIB),
        cost_estimate=pl.CostEstimate(
            flops=2 * SAMPLES * tile_count * links * tile * comps,
            bytes_accessed=2 * curl_tiles.size,
            transcendentals=0,
        ),
        name="shard_sums",
    )(
        *[in_vmem(a) for a in (projected, first_curl, later_curl, source_here, pattern_here)],
    )
    return pl.pallas_call(
        halo_kernel,
        out_shape=jax.ShapeDtypeStruct(source.shape, jnp.float32),
        in_specs=[vmem] * 3,
        out_specs=vmem,
        compiler_params=pltpu.CompilerParams(vmem_limit_bytes=16 * MIB),
        name="halo_sum",
    )(in_vmem(own), *beside)


def solution(mesh):
    at = mesh.axis_names.index("harm")
    harm = mesh.shape["harm"]
    cores = 2 if harm % 2 == 0 else 1
    sizes = mesh.devices.shape
    split = jax.sharding.Mesh(
        mesh.devices.reshape(sizes[:at] + (harm // cores, cores) + sizes[at + 1 :]),
        mesh.axis_names[:at] + ("chip", "core") + mesh.axis_names[at + 1 :],
    )
    placed = (
        P(GROUP, "space"),
        P("space", None, None, None),
        P("space", None),
        P("space"),
        P(),
        P(GROUP, "space"),
    )
    return jax.shard_map(
        per_device,
        mesh=split,
        in_specs=placed,
        out_specs=P(GROUP, "space"),
        check_vma=False,
    )
```

```python
import math

import jax
import jax.numpy as jnp
import ml_dtypes
import numpy as np
from jax import lax
from jax.experimental import pallas as pl
from jax.experimental.pallas import tpu as pltpu
from jax.sharding import PartitionSpec as P

SAMPLES = 64
HALF = SAMPLES // 2
GROUP = ("chip", "core", "samp")
MIB = 1024 * 1024
LISTED = 4
CHUNK = 4
AHEAD = 3


def half_table(parts):
    sample_ids = np.arange(HALF)[:, None]
    part_ids = np.arange(parts)[None, :]
    phase = ((2 * (part_ids // 2) + 1) * sample_ids % SAMPLES) * (2.0 * math.pi / SAMPLES)
    return np.where(part_ids % 2 == 0, np.cos(phase), np.sin(phase))


def bf16_pieces(table):
    rest = table
    pieces = []
    for _ in range(3):
        piece = rest.astype(ml_dtypes.bfloat16)
        pieces.append(piece)
        rest = rest - piece.astype(np.float64)
    return np.concatenate(pieces, axis=-1)


def across(array, core_step, space_step):
    cores, shards = lax.axis_size("core"), lax.axis_size("space")
    pairs = [
        (c * shards + s, (c + core_step) % cores * shards + (s + space_step) % shards)
        for c in range(cores)
        for s in range(shards)
    ]
    return lax.ppermute(array, ("core", "space"), pairs)


def from_neighbours(array, tile):
    if lax.axis_size("space") == 2:
        other = across(array, 1, 1)
        return other[:, -tile:], other[:, :tile]
    return across(array[:, -tile:], 1, 1), across(array[:, :tile], 1, -1)


def fetch_kernel(*refs):
    count = (len(refs) - 1) // 2
    sources, targets, sems = refs[:count], refs[count : 2 * count], refs[-1]
    rank = lax.axis_index(GROUP)
    sources = (sources[0].at[: targets[0].shape[0]], sources[1].at[rank]) + sources[2:]
    copies = [
        pltpu.make_async_copy(source, target, sems.at[i])
        for i, (source, target) in enumerate(zip(sources, targets))
    ]
    for copy in copies:
        copy.start()
    for copy in copies:
        copy.wait()


def time_samples(pieces, rows):
    stacked = jnp.concatenate([rows] * 3, axis=0)
    samples = jnp.dot(pieces, stacked, preferred_element_type=jnp.float32)
    high = samples.astype(jnp.bfloat16)
    low = (samples - high.astype(jnp.float32)).astype(jnp.bfloat16)
    return jnp.concatenate([high, low], axis=0)


def weighted(projected, blocks):
    return lax.dot_general(
        projected.astype(jnp.bfloat16),
        blocks,
        (((1,), (1,)), ((), ())),
        preferred_element_type=jnp.float32,
    )


def field_kernel(
    window,
    first_curl,
    table,
    pieces,
    pattern_in,
    region_in,
    law_in,
    curl_hbm,
    projected,
    halo,
    later_curl,
    pattern,
    region_ids,
    law,
    outer,
    timed,
    densities,
    edge_sums,
    small_sems,
    curl_sems,
):
    tile_count, links, tile, comps = curl_hbm.shape
    early = first_curl.shape[0]
    parts_here = halo.shape[0]
    fetched = [(pattern_in, pattern), (region_in, region_ids), (law_in, law)]
    small = [
        pltpu.make_async_copy(src, dst, small_sems.at[i]) for i, (src, dst) in enumerate(fetched)
    ]
    later = {
        elem: pltpu.make_async_copy(
            curl_hbm.at[elem : min(elem + CHUNK, tile_count)],
            later_curl.at[elem - early : min(elem + CHUNK, tile_count) - early],
            curl_sems.at[(elem - early) // CHUNK],
        )
        for elem in range(early, tile_count, CHUNK)
    }
    for copy in small + list(later.values()):
        copy.start()
    edge_sums[...] = jnp.zeros_like(edge_sums)
    own, outer_tiles = pieces[0], pieces[1]
    timed[:, tile:-tile] = time_samples(own, window[:, tile:-tile])
    timed[:, :tile] = time_samples(outer_tiles, window[:, :tile])
    timed[:, -tile:] = time_samples(outer_tiles, window[:, -tile:])
    columns = [
        jnp.broadcast_to(table[:, part : part + 1], (HALF, comps)) for part in range(parts_here)
    ]
    for copy in small:
        copy.wait()
    places = [[pattern[link, elem] for link in range(links)] for elem in range(tile_count)]
    count = jnp.int32(0)
    for elem in range(tile_count):
        for link, at in enumerate(places[elem]):
            outer[count] = elem * links + link
            count += jnp.where((at == 0) | (at == tile_count + 1), 1, 0)

    def blocks(elem):
        curl = first_curl[elem] if elem < early else later_curl[elem - early]
        return curl.reshape(links * tile, comps)

    def find_density(elem):
        picked = jnp.concatenate(
            [timed[:, pl.ds(pl.multiple_of(at * tile, tile), tile)] for at in places[elem]], axis=1
        )
        split = jnp.dot(picked, blocks(elem), preferred_element_type=jnp.float32)
        densities[elem] = split[:HALF] + split[HALF:]

    def project(elem):
        density = densities[elem]
        comp = [density[:, c * tile : (c + 1) * tile] for c in range(comps // tile)]
        square = comp[0] * comp[0]
        for c in comp[1:]:
            square = square + c * c
        region = region_ids[elem]
        reluct = law[0, region] + law[2, region] * square / (square + law[1, region])
        field = jnp.concatenate([reluct * c for c in comp], axis=1)
        rows = [jnp.sum(column * field, axis=0, keepdims=True) for column in columns]
        projected[elem] = jnp.concatenate(rows, axis=0) * (4.0 / SAMPLES)

    for turn in range(tile_count + 1):
        if turn < tile_count:
            if turn in later:
                later[turn].wait()
            find_density(turn)
        if turn:
            project(turn - 1)

    def add_outer(turn, carry):
        for slot in range(LISTED):
            spot = turn * LISTED + slot
            code = jnp.where(spot < count, outer[jnp.minimum(spot, jnp.maximum(count - 1, 0))], 0)
            elem, link = code // links, code % links
            block = jnp.where(
                elem < early,
                first_curl[jnp.minimum(elem, early - 1), link],
                later_curl[jnp.maximum(elem - early, 0), link],
            )
            contrib = weighted(projected[elem], block)
            side = jnp.where(pattern[link, elem] == 0, 0, 1)
            edge_sums[slot, side] += jnp.where(spot < count, contrib, 0.0)
        return carry

    add_outer(0, 0)
    lax.fori_loop(1, (count + LISTED - 1) // LISTED, add_outer, 0)
    total = edge_sums[0]
    for slot in range(1, LISTED):
        total = total + edge_sums[slot]
    halo[:, :tile] = total[0]
    halo[:, tile:] = total[1]


def sum_kernel(
    projected,
    first_curl,
    later_curl,
    source,
    pattern_in,
    out,
    pattern,
    small_sem,
    *sums,
):
    links, tile, comps = first_curl.shape[1:]
    early = first_curl.shape[0]
    tile_count = early + later_curl.shape[0]
    small = pltpu.make_async_copy(pattern_in, pattern, small_sem)
    small.start()
    for total in sums:
        total[...] = jnp.zeros_like(total)

    def contribution(elem):
        curl = first_curl[elem] if elem < early else later_curl[elem - early]
        return weighted(projected[elem], curl.reshape(links * tile, comps))

    ahead = [contribution(elem) for elem in range(AHEAD)]
    small.wait()
    for elem in range(tile_count):
        contrib = ahead[elem] if elem < AHEAD else contribution(elem)
        for link in range(links):
            sums[link][pattern[link, elem]] += contrib[:, link * tile : (link + 1) * tile]
    for w in range(tile_count):
        at = slice(w * tile, (w + 1) * tile)
        total = sums[0][w + 1]
        for other in sums[1:]:
            total = total + other[w + 1]
        out[:, at] = total - source[:, at]


def halo_kernel(own, from_right, from_left, out):
    tile = from_left.shape[1] // 2
    out[...] = own[...]
    out[:, :tile] += from_left[:, tile:]
    out[:, -tile:] += from_right[:, :tile]


def per_device(coeffs, curl_tiles, pattern, region_ids, material_law, source):
    parts_here = coeffs.shape[0]
    tile_count, links, tile, comps = curl_tiles.shape
    chips, cores, samp = (lax.axis_size(axis) for axis in GROUP)
    group_size = chips * cores * samp
    parts = parts_here * group_size
    table = half_table(parts)
    by_rank = np.arange(parts).reshape(chips, cores, samp, parts_here)
    orders = [
        by_core.transpose(2, 0, 1, 3).reshape(-1) for by_core in (by_rank, np.roll(by_rank, 1, 1))
    ]
    pieces = jnp.asarray(np.stack([bf16_pieces(table[:, order]) for order in orders]))
    own_columns = jnp.asarray(
        table.reshape(HALF, group_size, parts_here).transpose(1, 0, 2).astype(np.float32)
    )
    vmem, hbm = pl.BlockSpec(memory_space=pltpu.VMEM), pl.BlockSpec(memory_space=pltpu.HBM)

    def in_vmem(array):
        return pltpu.with_memory_space_constraint(array, pltpu.VMEM)

    def in_hbm(array):
        return pltpu.with_memory_space_constraint(array, pltpu.HBM)

    early = tile_count // 2
    operands = [
        curl_tiles,
        own_columns,
        coeffs,
        pieces,
        source,
        pattern.T,
        region_ids,
        material_law,
    ]
    shapes = [
        (early,) + curl_tiles.shape[1:],
        own_columns.shape[1:],
    ] + [operand.shape for operand in operands[2:]]
    fetched = pl.pallas_call(
        fetch_kernel,
        out_shape=[pltpu.VMEM(shape, o.dtype) for shape, o in zip(shapes, operands)],
        in_specs=[hbm] * len(operands),
        out_specs=[vmem] * len(operands),
        scratch_shapes=[pltpu.SemaphoreType.DMA((len(operands),))],
        compiler_params=pltpu.CompilerParams(vmem_limit_bytes=16 * MIB),
        cost_estimate=pl.CostEstimate(
            flops=0, bytes_accessed=4 * early * links * tile * comps, transcendentals=0
        ),
        name="fetch_operands",
    )(*[in_hbm(operand) for operand in operands])
    first_curl, columns_here, coeffs_here, pieces_here, source_here, *others = fetched
    pattern_here = others[0]

    left, right = from_neighbours(coeffs, tile)
    block = jnp.concatenate([left, coeffs_here, right], axis=1)
    copies = jnp.broadcast_to(block[None], (group_size,) + block.shape)
    window = lax.all_to_all(copies, ("samp", "chip", "core"), 0, 0).reshape(parts, block.shape[1])
    pattern_words = pltpu.SMEM((links, tile_count), jnp.int32)
    projected, halo, later_curl = pl.pallas_call(
        field_kernel,
        out_shape=(
            pltpu.VMEM((tile_count, parts_here, comps), jnp.float32),
            pltpu.VMEM((parts_here, 2 * tile), jnp.float32),
            pltpu.VMEM((tile_count - early,) + curl_tiles.shape[1:], curl_tiles.dtype),
        ),
        in_specs=[vmem] * 7 + [hbm],
        out_specs=(vmem, vmem, vmem),
        scratch_shapes=[
            pattern_words,
            pltpu.SMEM(region_ids.shape, jnp.int32),
            pltpu.SMEM(material_law.shape, jnp.float32),
            pltpu.SMEM((links * tile_count + 1,), jnp.int32),
            pltpu.VMEM((SAMPLES, (tile_count + 2) * tile), jnp.bfloat16),
            pltpu.VMEM((tile_count, HALF, comps), jnp.float32),
            pltpu.VMEM((LISTED, 2, parts_here, tile), jnp.float32),
            pltpu.SemaphoreType.DMA((3,)),
            pltpu.SemaphoreType.DMA((pl.cdiv(tile_count - early, CHUNK),)),
        ],
        compiler_params=pltpu.CompilerParams(vmem_limit_bytes=32 * MIB),
        cost_estimate=pl.CostEstimate(
            flops=2 * SAMPLES * tile_count * links * tile * comps,
            bytes_accessed=2 * curl_tiles.size,
            transcendentals=0,
        ),
        name="shard_fields",
    )(
        in_vmem(window),
        *[in_vmem(array) for array in (first_curl, columns_here, pieces_here, *others)],
        in_hbm(curl_tiles),
    )
    if lax.axis_size("space") == 2:
        beside = [across(halo, 0, 1)] * 2
    else:
        beside = [across(halo, 0, -1), across(halo, 0, 1)]
    own = pl.pallas_call(
        sum_kernel,
        out_shape=pltpu.VMEM(source.shape, jnp.float32),
        in_specs=[vmem] * 5,
        out_specs=vmem,
        scratch_shapes=[
            pattern_words,
            pltpu.SemaphoreType.DMA,
        ]
        + [pltpu.VMEM((tile_count + 2, parts_here, tile), jnp.float32)] * links,
        compiler_params=pltpu.CompilerParams(vmem_limit_bytes=32 * MIB),
        cost_estimate=pl.CostEstimate(
            flops=2 * SAMPLES * tile_count * links * tile * comps,
            bytes_accessed=2 * curl_tiles.size,
            transcendentals=0,
        ),
        name="shard_sums",
    )(
        *[in_vmem(a) for a in (projected, first_curl, later_curl, source_here, pattern_here)],
    )
    return pl.pallas_call(
        halo_kernel,
        out_shape=jax.ShapeDtypeStruct(source.shape, jnp.float32),
        in_specs=[vmem] * 3,
        out_specs=vmem,
        compiler_params=pltpu.CompilerParams(vmem_limit_bytes=16 * MIB),
        name="halo_sum",
    )(in_vmem(own), *beside)


def solution(mesh):
    at = mesh.axis_names.index("harm")
    harm = mesh.shape["harm"]
    cores = 2 if harm % 2 == 0 else 1
    sizes = mesh.devices.shape
    split = jax.sharding.Mesh(
        mesh.devices.reshape(sizes[:at] + (harm // cores, cores) + sizes[at + 1 :]),
        mesh.axis_names[:at] + ("chip", "core") + mesh.axis_names[at + 1 :],
    )
    placed = (
        P(GROUP, "space"),
        P("space", None, None, None),
        P("space", None),
        P("space"),
        P(),
        P(GROUP, "space"),
    )
    return jax.shard_map(
        per_device,
        mesh=split,
        in_specs=placed,
        out_specs=P(GROUP, "space"),
        check_vma=False,
    )
```

```python
import math

import jax
import jax.numpy as jnp
import ml_dtypes
import numpy as np
from jax import lax
from jax.experimental import pallas as pl
from jax.experimental.pallas import tpu as pltpu
from jax.sharding import PartitionSpec as P

SAMPLES = 64
HALF = SAMPLES // 2
GROUP = ("chip", "core", "samp")
ARRIVAL = ("samp", "core", "chip")
MIB = 1024 * 1024
LISTED = 4
CHUNK = 4
AHEAD = 3


def half_table(parts):
    sample_ids = np.arange(HALF)[:, None]
    part_ids = np.arange(parts)[None, :]
    phase = ((2 * (part_ids // 2) + 1) * sample_ids % SAMPLES) * (2.0 * math.pi / SAMPLES)
    return np.where(part_ids % 2 == 0, np.cos(phase), np.sin(phase))


def bf16_pieces(table):
    rest = table
    pieces = []
    for _ in range(3):
        piece = rest.astype(ml_dtypes.bfloat16)
        pieces.append(piece)
        rest = rest - piece.astype(np.float64)
    return np.concatenate(pieces, axis=-1)


def across(array, core_step, space_step):
    cores, shards = lax.axis_size("core"), lax.axis_size("space")
    pairs = [
        (c * shards + s, (c + core_step) % cores * shards + (s + space_step) % shards)
        for c in range(cores)
        for s in range(shards)
    ]
    return lax.ppermute(array, ("core", "space"), pairs)


def from_neighbours(array, tile):
    if lax.axis_size("space") == 2:
        other = across(array, 1, 1)
        return other[:, -tile:], other[:, :tile]
    return across(array[:, -tile:], 1, 1), across(array[:, :tile], 1, -1)


def fetch_kernel(*refs):
    count = (len(refs) - 1) // 2
    sources, targets, sems = refs[:count], refs[count : 2 * count], refs[-1]
    rank = lax.axis_index(GROUP)
    sources = (sources[0].at[: targets[0].shape[0]], sources[1].at[rank]) + sources[2:]
    copies = [
        pltpu.make_async_copy(source, target, sems.at[i])
        for i, (source, target) in enumerate(zip(sources, targets))
    ]
    for copy in copies:
        copy.start()
    for copy in copies:
        copy.wait()


def time_samples(pieces, rows):
    stacked = jnp.concatenate([rows] * 3, axis=0)
    samples = jnp.dot(pieces, stacked, preferred_element_type=jnp.float32)
    high = samples.astype(jnp.bfloat16)
    low = (samples - high.astype(jnp.float32)).astype(jnp.bfloat16)
    return jnp.concatenate([high, low], axis=0)


def weighted(projected, blocks):
    return lax.dot_general(
        projected.astype(jnp.bfloat16),
        blocks,
        (((1,), (1,)), ((), ())),
        preferred_element_type=jnp.float32,
    )


def field_kernel(
    window,
    first_curl,
    table,
    pieces,
    pattern_in,
    region_in,
    law_in,
    curl_hbm,
    projected,
    halo,
    later_curl,
    pattern,
    region_ids,
    law,
    outer,
    timed,
    densities,
    edge_sums,
    small_sems,
    curl_sems,
):
    tile_count, links, tile, comps = curl_hbm.shape
    early = first_curl.shape[0]
    parts_here = halo.shape[0]
    fetched = [(pattern_in, pattern), (region_in, region_ids), (law_in, law)]
    small = [
        pltpu.make_async_copy(src, dst, small_sems.at[i]) for i, (src, dst) in enumerate(fetched)
    ]
    later = {
        elem: pltpu.make_async_copy(
            curl_hbm.at[elem : min(elem + CHUNK, tile_count)],
            later_curl.at[elem - early : min(elem + CHUNK, tile_count) - early],
            curl_sems.at[(elem - early) // CHUNK],
        )
        for elem in range(early, tile_count, CHUNK)
    }
    for copy in small + list(later.values()):
        copy.start()
    edge_sums[...] = jnp.zeros_like(edge_sums)
    own, outer_tiles = pieces[0], pieces[1]
    timed[:, tile:-tile] = time_samples(own, window[:, tile:-tile])
    timed[:, :tile] = time_samples(outer_tiles, window[:, :tile])
    timed[:, -tile:] = time_samples(outer_tiles, window[:, -tile:])
    columns = [
        jnp.broadcast_to(table[:, part : part + 1], (HALF, comps)) for part in range(parts_here)
    ]
    for copy in small:
        copy.wait()
    places = [[pattern[link, elem] for link in range(links)] for elem in range(tile_count)]
    count = jnp.int32(0)
    for elem in range(tile_count):
        for link, at in enumerate(places[elem]):
            outer[count] = elem * links + link
            count += jnp.where((at == 0) | (at == tile_count + 1), 1, 0)

    def blocks(elem):
        curl = first_curl[elem] if elem < early else later_curl[elem - early]
        return curl.reshape(links * tile, comps)

    def find_density(elem):
        picked = jnp.concatenate(
            [timed[:, pl.ds(pl.multiple_of(at * tile, tile), tile)] for at in places[elem]], axis=1
        )
        split = jnp.dot(picked, blocks(elem), preferred_element_type=jnp.float32)
        densities[elem] = split[:HALF] + split[HALF:]

    def project(elem):
        density = densities[elem]
        comp = [density[:, c * tile : (c + 1) * tile] for c in range(comps // tile)]
        square = comp[0] * comp[0]
        for c in comp[1:]:
            square = square + c * c
        region = region_ids[elem]
        reluct = law[0, region] + law[2, region] * square / (square + law[1, region])
        field = jnp.concatenate([reluct * c for c in comp], axis=1)
        rows = [jnp.sum(column * field, axis=0, keepdims=True) for column in columns]
        projected[elem] = jnp.concatenate(rows, axis=0) * (4.0 / SAMPLES)

    for turn in range(tile_count + 1):
        if turn < tile_count:
            if turn in later:
                later[turn].wait()
            find_density(turn)
        if turn:
            project(turn - 1)

    def add_outer(turn, carry):
        for slot in range(LISTED):
            spot = turn * LISTED + slot
            code = jnp.where(spot < count, outer[jnp.minimum(spot, jnp.maximum(count - 1, 0))], 0)
            elem, link = code // links, code % links
            block = jnp.where(
                elem < early,
                first_curl[jnp.minimum(elem, early - 1), link],
                later_curl[jnp.maximum(elem - early, 0), link],
            )
            contrib = weighted(projected[elem], block)
            side = jnp.where(pattern[link, elem] == 0, 0, 1)
            edge_sums[slot, side] += jnp.where(spot < count, contrib, 0.0)
        return carry

    add_outer(0, 0)
    lax.fori_loop(1, (count + LISTED - 1) // LISTED, add_outer, 0)
    total = edge_sums[0]
    for slot in range(1, LISTED):
        total = total + edge_sums[slot]
    halo[:, :tile] = total[0]
    halo[:, tile:] = total[1]


def sum_kernel(
    projected,
    first_curl,
    later_curl,
    source,
    pattern_in,
    out,
    pattern,
    small_sem,
    *sums,
):
    links, tile, comps = first_curl.shape[1:]
    early = first_curl.shape[0]
    tile_count = early + later_curl.shape[0]
    small = pltpu.make_async_copy(pattern_in, pattern, small_sem)
    small.start()
    for total in sums:
        total[...] = jnp.zeros_like(total)

    def contribution(elem):
        curl = first_curl[elem] if elem < early else later_curl[elem - early]
        return weighted(projected[elem], curl.reshape(links * tile, comps))

    ahead = [contribution(elem) for elem in range(AHEAD)]
    small.wait()
    for elem in range(tile_count):
        contrib = ahead[elem] if elem < AHEAD else contribution(elem)
        for link in range(links):
            sums[link][pattern[link, elem]] += contrib[:, link * tile : (link + 1) * tile]
    for w in range(tile_count):
        at = slice(w * tile, (w + 1) * tile)
        total = sums[0][w + 1]
        for other in sums[1:]:
            total = total + other[w + 1]
        out[:, at] = total - source[:, at]


def halo_kernel(own, from_right, from_left, out):
    tile = from_left.shape[1] // 2
    out[...] = own[...]
    out[:, :tile] += from_left[:, tile:]
    out[:, -tile:] += from_right[:, :tile]


def per_device(coeffs, curl_tiles, pattern, region_ids, material_law, source):
    parts_here = coeffs.shape[0]
    tile_count, links, tile, comps = curl_tiles.shape
    chips, cores, samp = (lax.axis_size(axis) for axis in GROUP)
    group_size = chips * cores * samp
    parts = parts_here * group_size
    table = half_table(parts)
    by_rank = np.arange(parts).reshape(chips, cores, samp, parts_here)
    orders = [
        by_core.transpose([GROUP.index(axis) for axis in ARRIVAL] + [3]).reshape(-1)
        for by_core in (by_rank, np.roll(by_rank, 1, 1))
    ]
    pieces = jnp.asarray(np.stack([bf16_pieces(table[:, order]) for order in orders]))
    own_columns = jnp.asarray(
        table.reshape(HALF, group_size, parts_here).transpose(1, 0, 2).astype(np.float32)
    )
    vmem, hbm = pl.BlockSpec(memory_space=pltpu.VMEM), pl.BlockSpec(memory_space=pltpu.HBM)

    def in_vmem(array):
        return pltpu.with_memory_space_constraint(array, pltpu.VMEM)

    def in_hbm(array):
        return pltpu.with_memory_space_constraint(array, pltpu.HBM)

    early = tile_count // 2
    operands = [
        curl_tiles,
        own_columns,
        coeffs,
        pieces,
        source,
        pattern.T,
        region_ids,
        material_law,
    ]
    shapes = [
        (early,) + curl_tiles.shape[1:],
        own_columns.shape[1:],
    ] + [operand.shape for operand in operands[2:]]
    fetched = pl.pallas_call(
        fetch_kernel,
        out_shape=[pltpu.VMEM(shape, o.dtype) for shape, o in zip(shapes, operands)],
        in_specs=[hbm] * len(operands),
        out_specs=[vmem] * len(operands),
        scratch_shapes=[pltpu.SemaphoreType.DMA((len(operands),))],
        compiler_params=pltpu.CompilerParams(vmem_limit_bytes=16 * MIB),
        cost_estimate=pl.CostEstimate(
            flops=0, bytes_accessed=4 * early * links * tile * comps, transcendentals=0
        ),
        name="fetch_operands",
    )(*[in_hbm(operand) for operand in operands])
    first_curl, columns_here, coeffs_here, pieces_here, source_here, *others = fetched
    pattern_here = others[0]

    left, right = from_neighbours(coeffs, tile)
    block = jnp.concatenate([left, coeffs_here, right], axis=1)
    copies = jnp.broadcast_to(block[None], (group_size,) + block.shape)
    window = lax.all_to_all(copies, ARRIVAL, 0, 0).reshape(parts, block.shape[1])
    pattern_words = pltpu.SMEM((links, tile_count), jnp.int32)
    projected, halo, later_curl = pl.pallas_call(
        field_kernel,
        out_shape=(
            pltpu.VMEM((tile_count, parts_here, comps), jnp.float32),
            pltpu.VMEM((parts_here, 2 * tile), jnp.float32),
            pltpu.VMEM((tile_count - early,) + curl_tiles.shape[1:], curl_tiles.dtype),
        ),
        in_specs=[vmem] * 7 + [hbm],
        out_specs=(vmem, vmem, vmem),
        scratch_shapes=[
            pattern_words,
            pltpu.SMEM(region_ids.shape, jnp.int32),
            pltpu.SMEM(material_law.shape, jnp.float32),
            pltpu.SMEM((links * tile_count + 1,), jnp.int32),
            pltpu.VMEM((SAMPLES, (tile_count + 2) * tile), jnp.bfloat16),
            pltpu.VMEM((tile_count, HALF, comps), jnp.float32),
            pltpu.VMEM((LISTED, 2, parts_here, tile), jnp.float32),
            pltpu.SemaphoreType.DMA((3,)),
            pltpu.SemaphoreType.DMA((pl.cdiv(tile_count - early, CHUNK),)),
        ],
        compiler_params=pltpu.CompilerParams(vmem_limit_bytes=32 * MIB),
        cost_estimate=pl.CostEstimate(
            flops=2 * SAMPLES * tile_count * links * tile * comps,
            bytes_accessed=2 * curl_tiles.size,
            transcendentals=0,
        ),
        name="shard_fields",
    )(
        in_vmem(window),
        *[in_vmem(array) for array in (first_curl, columns_here, pieces_here, *others)],
        in_hbm(curl_tiles),
    )
    if lax.axis_size("space") == 2:
        beside = [across(halo, 0, 1)] * 2
    else:
        beside = [across(halo, 0, -1), across(halo, 0, 1)]
    own = pl.pallas_call(
        sum_kernel,
        out_shape=pltpu.VMEM(source.shape, jnp.float32),
        in_specs=[vmem] * 5,
        out_specs=vmem,
        scratch_shapes=[
            pattern_words,
            pltpu.SemaphoreType.DMA,
        ]
        + [pltpu.VMEM((tile_count + 2, parts_here, tile), jnp.float32)] * links,
        compiler_params=pltpu.CompilerParams(vmem_limit_bytes=32 * MIB),
        cost_estimate=pl.CostEstimate(
            flops=2 * SAMPLES * tile_count * links * tile * comps,
            bytes_accessed=2 * curl_tiles.size,
            transcendentals=0,
        ),
        name="shard_sums",
    )(
        *[in_vmem(a) for a in (projected, first_curl, later_curl, source_here, pattern_here)],
    )
    return pl.pallas_call(
        halo_kernel,
        out_shape=jax.ShapeDtypeStruct(source.shape, jnp.float32),
        in_specs=[vmem] * 3,
        out_specs=vmem,
        compiler_params=pltpu.CompilerParams(vmem_limit_bytes=16 * MIB),
        name="halo_sum",
    )(in_vmem(own), *beside)


def solution(mesh):
    at = mesh.axis_names.index("harm")
    harm = mesh.shape["harm"]
    cores = 2 if harm % 2 == 0 else 1
    sizes = mesh.devices.shape
    split = jax.sharding.Mesh(
        mesh.devices.reshape(sizes[:at] + (harm // cores, cores) + sizes[at + 1 :]),
        mesh.axis_names[:at] + ("chip", "core") + mesh.axis_names[at + 1 :],
    )
    placed = (
        P(GROUP, "space"),
        P("space", None, None, None),
        P("space", None),
        P("space"),
        P(),
        P(GROUP, "space"),
    )
    return jax.shard_map(
        per_device,
        mesh=split,
        in_specs=placed,
        out_specs=P(GROUP, "space"),
        check_vma=False,
    )
```

```python
import math

import jax
import jax.numpy as jnp
import ml_dtypes
import numpy as np
from jax import lax
from jax.experimental import pallas as pl
from jax.experimental.pallas import tpu as pltpu
from jax.sharding import PartitionSpec as P

SAMPLES = 64
HALF = SAMPLES // 2
GROUP = ("chip", "core", "samp")
MIB = 1024 * 1024
LISTED = 4
CHUNK = 4
AHEAD = 3


def half_table(parts):
    sample_ids = np.arange(HALF)[:, None]
    part_ids = np.arange(parts)[None, :]
    phase = ((2 * (part_ids // 2) + 1) * sample_ids % SAMPLES) * (2.0 * math.pi / SAMPLES)
    return np.where(part_ids % 2 == 0, np.cos(phase), np.sin(phase))


def bf16_pieces(table):
    rest = table
    pieces = []
    for _ in range(3):
        piece = rest.astype(ml_dtypes.bfloat16)
        pieces.append(piece)
        rest = rest - piece.astype(np.float64)
    return np.concatenate(pieces, axis=-1)


def across(array, core_step, space_step):
    cores, shards = lax.axis_size("core"), lax.axis_size("space")
    pairs = [
        (c * shards + s, (c + core_step) % cores * shards + (s + space_step) % shards)
        for c in range(cores)
        for s in range(shards)
    ]
    return lax.ppermute(array, ("core", "space"), pairs)


def from_neighbours(array, tile):
    if lax.axis_size("space") == 2:
        other = across(array, 1, 1)
        return other[:, -tile:], other[:, :tile]
    return across(array[:, -tile:], 1, 1), across(array[:, :tile], 1, -1)


def fetch_kernel(*refs):
    count = (len(refs) - 1) // 2
    sources, targets, sems = refs[:count], refs[count : 2 * count], refs[-1]
    early = targets[0].shape[0]
    sources = [sources[0].at[i] for i in range(early)] + [
        sources[1].at[lax.axis_index(GROUP)],
        *sources[2:],
    ]
    targets = [targets[0].at[i] for i in range(early)] + list(targets[1:])
    copies = [
        pltpu.make_async_copy(source, target, sems.at[i])
        for i, (source, target) in enumerate(zip(sources, targets))
    ]
    for copy in copies:
        copy.start()
    for copy in copies:
        copy.wait()


def time_samples(pieces, rows):
    stacked = jnp.concatenate([rows] * 3, axis=0)
    samples = jnp.dot(pieces, stacked, preferred_element_type=jnp.float32)
    high = samples.astype(jnp.bfloat16)
    low = (samples - high.astype(jnp.float32)).astype(jnp.bfloat16)
    return jnp.concatenate([high, low], axis=0)


def weighted(projected, blocks):
    return lax.dot_general(
        projected.astype(jnp.bfloat16),
        blocks,
        (((1,), (1,)), ((), ())),
        preferred_element_type=jnp.float32,
    )


def field_kernel(
    window,
    first_curl,
    table,
    pieces,
    pattern_in,
    region_in,
    law_in,
    curl_hbm,
    projected,
    halo,
    later_curl,
    pattern,
    region_ids,
    law,
    outer,
    timed,
    densities,
    edge_sums,
    small_sems,
    curl_sems,
):
    tile_count, links, tile, comps = curl_hbm.shape
    early = first_curl.shape[0]
    parts_here = halo.shape[0]
    fetched = [(pattern_in, pattern), (region_in, region_ids), (law_in, law)]
    small = [
        pltpu.make_async_copy(src, dst, small_sems.at[i]) for i, (src, dst) in enumerate(fetched)
    ]
    later = {
        elem: pltpu.make_async_copy(
            curl_hbm.at[elem], later_curl.at[elem - early], curl_sems.at[elem - early]
        )
        for elem in range(early, tile_count)
    }
    for copy in small + list(later.values()):
        copy.start()
    edge_sums[...] = jnp.zeros_like(edge_sums)
    own, outer_tiles = pieces[0], pieces[1]
    timed[:, tile:-tile] = time_samples(own, window[:, tile:-tile])
    timed[:, :tile] = time_samples(outer_tiles, window[:, :tile])
    timed[:, -tile:] = time_samples(outer_tiles, window[:, -tile:])
    columns = [
        jnp.broadcast_to(table[:, part : part + 1], (HALF, comps)) for part in range(parts_here)
    ]
    for copy in small:
        copy.wait()
    places = [[pattern[link, elem] for link in range(links)] for elem in range(tile_count)]
    count = jnp.int32(0)
    for elem in range(tile_count):
        for link, at in enumerate(places[elem]):
            outer[count] = elem * links + link
            count += jnp.where((at == 0) | (at == tile_count + 1), 1, 0)

    def blocks(elem):
        curl = first_curl[elem] if elem < early else later_curl[elem - early]
        return curl.reshape(links * tile, comps)

    def find_density(elem):
        picked = jnp.concatenate(
            [timed[:, pl.ds(pl.multiple_of(at * tile, tile), tile)] for at in places[elem]], axis=1
        )
        split = jnp.dot(picked, blocks(elem), preferred_element_type=jnp.float32)
        densities[elem] = split[:HALF] + split[HALF:]

    def project(elem):
        density = densities[elem]
        comp = [density[:, c * tile : (c + 1) * tile] for c in range(comps // tile)]
        square = comp[0] * comp[0]
        for c in comp[1:]:
            square = square + c * c
        region = region_ids[elem]
        reluct = law[0, region] + law[2, region] * square / (square + law[1, region])
        field = jnp.concatenate([reluct * c for c in comp], axis=1)
        rows = [jnp.sum(column * field, axis=0, keepdims=True) for column in columns]
        projected[elem] = jnp.concatenate(rows, axis=0) * (4.0 / SAMPLES)

    for turn in range(tile_count + 1):
        if turn < tile_count:
            if turn >= early and (turn - early) % CHUNK == 0:
                for elem in range(turn, min(turn + CHUNK, tile_count)):
                    later[elem].wait()
            find_density(turn)
        if turn:
            project(turn - 1)

    def add_outer(turn, carry):
        for slot in range(LISTED):
            spot = turn * LISTED + slot
            code = jnp.where(spot < count, outer[jnp.minimum(spot, jnp.maximum(count - 1, 0))], 0)
            elem, link = code // links, code % links
            block = jnp.where(
                elem < early,
                first_curl[jnp.minimum(elem, early - 1), link],
                later_curl[jnp.maximum(elem - early, 0), link],
            )
            contrib = weighted(projected[elem], block)
            side = jnp.where(pattern[link, elem] == 0, 0, 1)
            edge_sums[slot, side] += jnp.where(spot < count, contrib, 0.0)
        return carry

    add_outer(0, 0)
    lax.fori_loop(1, (count + LISTED - 1) // LISTED, add_outer, 0)
    total = edge_sums[0]
    for slot in range(1, LISTED):
        total = total + edge_sums[slot]
    halo[:, :tile] = total[0]
    halo[:, tile:] = total[1]


def sum_kernel(
    projected,
    first_curl,
    later_curl,
    source,
    pattern_in,
    out,
    pattern,
    small_sem,
    *sums,
):
    links, tile, comps = first_curl.shape[1:]
    early = first_curl.shape[0]
    tile_count = early + later_curl.shape[0]
    small = pltpu.make_async_copy(pattern_in, pattern, small_sem)
    small.start()
    for total in sums:
        total[...] = jnp.zeros_like(total)

    def contribution(elem):
        curl = first_curl[elem] if elem < early else later_curl[elem - early]
        return weighted(projected[elem], curl.reshape(links * tile, comps))

    ahead = [contribution(elem) for elem in range(AHEAD)]
    small.wait()
    for elem in range(tile_count):
        contrib = ahead[elem] if elem < AHEAD else contribution(elem)
        for link in range(links):
            sums[link][pattern[link, elem]] += contrib[:, link * tile : (link + 1) * tile]
    for w in range(tile_count):
        at = slice(w * tile, (w + 1) * tile)
        total = sums[0][w + 1]
        for other in sums[1:]:
            total = total + other[w + 1]
        out[:, at] = total - source[:, at]


def halo_kernel(own, from_right, from_left, out):
    tile = from_left.shape[1] // 2
    out[...] = own[...]
    out[:, :tile] += from_left[:, tile:]
    out[:, -tile:] += from_right[:, :tile]


def per_device(coeffs, curl_tiles, pattern, region_ids, material_law, source):
    parts_here = coeffs.shape[0]
    tile_count, links, tile, comps = curl_tiles.shape
    chips, cores, samp = (lax.axis_size(axis) for axis in GROUP)
    group_size = chips * cores * samp
    parts = parts_here * group_size
    table = half_table(parts)
    before = np.roll(np.arange(parts).reshape(chips, cores, -1), 1, axis=1).reshape(-1)
    pieces = jnp.asarray(np.stack([bf16_pieces(table), bf16_pieces(table[:, before])]))
    own_columns = jnp.asarray(
        table.reshape(HALF, group_size, parts_here).transpose(1, 0, 2).astype(np.float32)
    )
    vmem, hbm = pl.BlockSpec(memory_space=pltpu.VMEM), pl.BlockSpec(memory_space=pltpu.HBM)

    def in_vmem(array):
        return pltpu.with_memory_space_constraint(array, pltpu.VMEM)

    def in_hbm(array):
        return pltpu.with_memory_space_constraint(array, pltpu.HBM)

    early = tile_count // 2
    operands = [
        curl_tiles,
        own_columns,
        coeffs,
        pieces,
        source,
        pattern.T,
        region_ids,
        material_law,
    ]
    shapes = [
        (early,) + curl_tiles.shape[1:],
        own_columns.shape[1:],
    ] + [operand.shape for operand in operands[2:]]
    fetched = pl.pallas_call(
        fetch_kernel,
        out_shape=[pltpu.VMEM(shape, o.dtype) for shape, o in zip(shapes, operands)],
        in_specs=[hbm] * len(operands),
        out_specs=[vmem] * len(operands),
        scratch_shapes=[pltpu.SemaphoreType.DMA((early + len(operands) - 1,))],
        compiler_params=pltpu.CompilerParams(vmem_limit_bytes=16 * MIB),
        cost_estimate=pl.CostEstimate(
            flops=0, bytes_accessed=4 * early * links * tile * comps, transcendentals=0
        ),
        name="fetch_operands",
    )(*[in_hbm(operand) for operand in operands])
    first_curl, columns_here, coeffs_here, pieces_here, source_here, *others = fetched
    pattern_here = others[0]

    left, right = from_neighbours(coeffs, tile)
    block = jnp.concatenate([left, coeffs_here, right], axis=1)
    copies = jnp.broadcast_to(block[None], (group_size,) + block.shape)
    window = lax.all_to_all(copies, GROUP, 0, 0).reshape(parts, block.shape[1])
    pattern_words = pltpu.SMEM((links, tile_count), jnp.int32)
    projected, halo, later_curl = pl.pallas_call(
        field_kernel,
        out_shape=(
            pltpu.VMEM((tile_count, parts_here, comps), jnp.float32),
            pltpu.VMEM((parts_here, 2 * tile), jnp.float32),
            pltpu.VMEM((tile_count - early,) + curl_tiles.shape[1:], curl_tiles.dtype),
        ),
        in_specs=[vmem] * 7 + [hbm],
        out_specs=(vmem, vmem, vmem),
        scratch_shapes=[
            pattern_words,
            pltpu.SMEM(region_ids.shape, jnp.int32),
            pltpu.SMEM(material_law.shape, jnp.float32),
            pltpu.SMEM((links * tile_count + 1,), jnp.int32),
            pltpu.VMEM((SAMPLES, (tile_count + 2) * tile), jnp.bfloat16),
            pltpu.VMEM((tile_count, HALF, comps), jnp.float32),
            pltpu.VMEM((LISTED, 2, parts_here, tile), jnp.float32),
            pltpu.SemaphoreType.DMA((3,)),
            pltpu.SemaphoreType.DMA((tile_count - early,)),
        ],
        compiler_params=pltpu.CompilerParams(vmem_limit_bytes=32 * MIB),
        cost_estimate=pl.CostEstimate(
            flops=2 * SAMPLES * tile_count * links * tile * comps,
            bytes_accessed=2 * curl_tiles.size,
            transcendentals=0,
        ),
        name="shard_fields",
    )(
        in_vmem(window),
        *[in_vmem(array) for array in (first_curl, columns_here, pieces_here, *others)],
        in_hbm(curl_tiles),
    )
    if lax.axis_size("space") == 2:
        beside = [across(halo, 0, 1)] * 2
    else:
        beside = [across(halo, 0, -1), across(halo, 0, 1)]
    own = pl.pallas_call(
        sum_kernel,
        out_shape=pltpu.VMEM(source.shape, jnp.float32),
        in_specs=[vmem] * 5,
        out_specs=vmem,
        scratch_shapes=[
            pattern_words,
            pltpu.SemaphoreType.DMA,
        ]
        + [pltpu.VMEM((tile_count + 2, parts_here, tile), jnp.float32)] * links,
        compiler_params=pltpu.CompilerParams(vmem_limit_bytes=32 * MIB),
        cost_estimate=pl.CostEstimate(
            flops=2 * SAMPLES * tile_count * links * tile * comps,
            bytes_accessed=2 * curl_tiles.size,
            transcendentals=0,
        ),
        name="shard_sums",
    )(
        *[in_vmem(a) for a in (projected, first_curl, later_curl, source_here, pattern_here)],
    )
    return pl.pallas_call(
        halo_kernel,
        out_shape=jax.ShapeDtypeStruct(source.shape, jnp.float32),
        in_specs=[vmem] * 3,
        out_specs=vmem,
        compiler_params=pltpu.CompilerParams(vmem_limit_bytes=16 * MIB),
        name="halo_sum",
    )(in_vmem(own), *beside)


def solution(mesh):
    at = mesh.axis_names.index("harm")
    harm = mesh.shape["harm"]
    cores = 2 if harm % 2 == 0 else 1
    sizes = mesh.devices.shape
    split = jax.sharding.Mesh(
        mesh.devices.reshape(sizes[:at] + (harm // cores, cores) + sizes[at + 1 :]),
        mesh.axis_names[:at] + ("chip", "core") + mesh.axis_names[at + 1 :],
    )
    placed = (
        P(GROUP, "space"),
        P("space", None, None, None),
        P("space", None),
        P("space"),
        P(),
        P(GROUP, "space"),
    )
    return jax.shard_map(
        per_device,
        mesh=split,
        in_specs=placed,
        out_specs=P(GROUP, "space"),
        check_vma=False,
    )
```

```python
import math

import jax
import jax.numpy as jnp
import ml_dtypes
import numpy as np
from jax import lax
from jax.experimental import pallas as pl
from jax.experimental.pallas import tpu as pltpu
from jax.sharding import PartitionSpec as P

SAMPLES = 64
HALF = SAMPLES // 2
GROUP = ("chip", "core", "samp")
ARRIVAL = ("core", "chip", "samp")
MIB = 1024 * 1024
LISTED = 4
CHUNK = 4
AHEAD = 3


def half_table(parts):
    sample_ids = np.arange(HALF)[:, None]
    part_ids = np.arange(parts)[None, :]
    phase = ((2 * (part_ids // 2) + 1) * sample_ids % SAMPLES) * (2.0 * math.pi / SAMPLES)
    return np.where(part_ids % 2 == 0, np.cos(phase), np.sin(phase))


def bf16_pieces(table):
    rest = table
    pieces = []
    for _ in range(3):
        piece = rest.astype(ml_dtypes.bfloat16)
        pieces.append(piece)
        rest = rest - piece.astype(np.float64)
    return np.concatenate(pieces, axis=-1)


def across(array, core_step, space_step):
    cores, shards = lax.axis_size("core"), lax.axis_size("space")
    pairs = [
        (c * shards + s, (c + core_step) % cores * shards + (s + space_step) % shards)
        for c in range(cores)
        for s in range(shards)
    ]
    return lax.ppermute(array, ("core", "space"), pairs)


def from_neighbours(array, tile):
    if lax.axis_size("space") == 2:
        other = across(array, 1, 1)
        return other[:, -tile:], other[:, :tile]
    return across(array[:, -tile:], 1, 1), across(array[:, :tile], 1, -1)


def fetch_kernel(*refs):
    count = (len(refs) - 1) // 2
    sources, targets, sems = refs[:count], refs[count : 2 * count], refs[-1]
    rank = lax.axis_index(GROUP)
    sources = (sources[0].at[: targets[0].shape[0]], sources[1].at[rank]) + sources[2:]
    copies = [
        pltpu.make_async_copy(source, target, sems.at[i])
        for i, (source, target) in enumerate(zip(sources, targets))
    ]
    for copy in copies:
        copy.start()
    for copy in copies:
        copy.wait()


def time_samples(pieces, rows):
    stacked = jnp.concatenate([rows] * 3, axis=0)
    samples = jnp.dot(pieces, stacked, preferred_element_type=jnp.float32)
    high = samples.astype(jnp.bfloat16)
    low = (samples - high.astype(jnp.float32)).astype(jnp.bfloat16)
    return jnp.concatenate([high, low], axis=0)


def weighted(projected, blocks):
    return lax.dot_general(
        projected.astype(jnp.bfloat16),
        blocks,
        (((1,), (1,)), ((), ())),
        preferred_element_type=jnp.float32,
    )


def field_kernel(
    window,
    first_curl,
    table,
    pieces,
    pattern_in,
    region_in,
    law_in,
    curl_hbm,
    projected,
    halo,
    later_curl,
    pattern,
    region_ids,
    law,
    outer,
    timed,
    densities,
    edge_sums,
    small_sems,
    curl_sems,
):
    tile_count, links, tile, comps = curl_hbm.shape
    early = first_curl.shape[0]
    parts_here = halo.shape[0]
    fetched = [(pattern_in, pattern), (region_in, region_ids), (law_in, law)]
    small = [
        pltpu.make_async_copy(src, dst, small_sems.at[i]) for i, (src, dst) in enumerate(fetched)
    ]
    later = {
        elem: pltpu.make_async_copy(
            curl_hbm.at[elem : min(elem + CHUNK, tile_count)],
            later_curl.at[elem - early : min(elem + CHUNK, tile_count) - early],
            curl_sems.at[(elem - early) // CHUNK],
        )
        for elem in range(early, tile_count, CHUNK)
    }
    for copy in small + list(later.values()):
        copy.start()
    edge_sums[...] = jnp.zeros_like(edge_sums)
    own, outer_tiles = pieces[0], pieces[1]
    timed[:, tile:-tile] = time_samples(own, window[:, tile:-tile])
    timed[:, :tile] = time_samples(outer_tiles, window[:, :tile])
    timed[:, -tile:] = time_samples(outer_tiles, window[:, -tile:])
    columns = [
        jnp.broadcast_to(table[:, part : part + 1], (HALF, comps)) for part in range(parts_here)
    ]
    for copy in small:
        copy.wait()
    places = [[pattern[link, elem] for link in range(links)] for elem in range(tile_count)]
    count = jnp.int32(0)
    for elem in range(tile_count):
        for link, at in enumerate(places[elem]):
            outer[count] = elem * links + link
            count += jnp.where((at == 0) | (at == tile_count + 1), 1, 0)

    def blocks(elem):
        curl = first_curl[elem] if elem < early else later_curl[elem - early]
        return curl.reshape(links * tile, comps)

    def find_density(elem):
        picked = jnp.concatenate(
            [timed[:, pl.ds(pl.multiple_of(at * tile, tile), tile)] for at in places[elem]], axis=1
        )
        split = jnp.dot(picked, blocks(elem), preferred_element_type=jnp.float32)
        densities[elem] = split[:HALF] + split[HALF:]

    def project(elem):
        density = densities[elem]
        comp = [density[:, c * tile : (c + 1) * tile] for c in range(comps // tile)]
        square = comp[0] * comp[0]
        for c in comp[1:]:
            square = square + c * c
        region = region_ids[elem]
        reluct = law[0, region] + law[2, region] * square / (square + law[1, region])
        field = jnp.concatenate([reluct * c for c in comp], axis=1)
        rows = [jnp.sum(column * field, axis=0, keepdims=True) for column in columns]
        projected[elem] = jnp.concatenate(rows, axis=0) * (4.0 / SAMPLES)

    for turn in range(tile_count + 1):
        if turn < tile_count:
            if turn in later:
                later[turn].wait()
            find_density(turn)
        if turn:
            project(turn - 1)

    def add_outer(turn, carry):
        for slot in range(LISTED):
            spot = turn * LISTED + slot
            code = jnp.where(spot < count, outer[jnp.minimum(spot, jnp.maximum(count - 1, 0))], 0)
            elem, link = code // links, code % links
            block = jnp.where(
                elem < early,
                first_curl[jnp.minimum(elem, early - 1), link],
                later_curl[jnp.maximum(elem - early, 0), link],
            )
            contrib = weighted(projected[elem], block)
            side = jnp.where(pattern[link, elem] == 0, 0, 1)
            edge_sums[slot, side] += jnp.where(spot < count, contrib, 0.0)
        return carry

    add_outer(0, 0)
    lax.fori_loop(1, (count + LISTED - 1) // LISTED, add_outer, 0)
    total = edge_sums[0]
    for slot in range(1, LISTED):
        total = total + edge_sums[slot]
    halo[:, :tile] = total[0]
    halo[:, tile:] = total[1]


def sum_kernel(
    projected,
    first_curl,
    later_curl,
    source,
    pattern_in,
    out,
    pattern,
    small_sem,
    *sums,
):
    links, tile, comps = first_curl.shape[1:]
    early = first_curl.shape[0]
    tile_count = early + later_curl.shape[0]
    small = pltpu.make_async_copy(pattern_in, pattern, small_sem)
    small.start()
    for total in sums:
        total[...] = jnp.zeros_like(total)

    def contribution(elem):
        curl = first_curl[elem] if elem < early else later_curl[elem - early]
        return weighted(projected[elem], curl.reshape(links * tile, comps))

    ahead = [contribution(elem) for elem in range(AHEAD)]
    small.wait()
    for elem in range(tile_count):
        contrib = ahead[elem] if elem < AHEAD else contribution(elem)
        for link in range(links):
            sums[link][pattern[link, elem]] += contrib[:, link * tile : (link + 1) * tile]
    for w in range(tile_count):
        at = slice(w * tile, (w + 1) * tile)
        total = sums[0][w + 1]
        for other in sums[1:]:
            total = total + other[w + 1]
        out[:, at] = total - source[:, at]


def halo_kernel(own, from_right, from_left, out):
    tile = from_left.shape[1] // 2
    out[...] = own[...]
    out[:, :tile] += from_left[:, tile:]
    out[:, -tile:] += from_right[:, :tile]


def per_device(coeffs, curl_tiles, pattern, region_ids, material_law, source):
    parts_here = coeffs.shape[0]
    tile_count, links, tile, comps = curl_tiles.shape
    chips, cores, samp = (lax.axis_size(axis) for axis in GROUP)
    group_size = chips * cores * samp
    parts = parts_here * group_size
    table = half_table(parts)
    by_rank = np.arange(parts).reshape(chips, cores, samp, parts_here)
    orders = [
        by_core.transpose([GROUP.index(axis) for axis in ARRIVAL] + [3]).reshape(-1)
        for by_core in (by_rank, np.roll(by_rank, 1, 1))
    ]
    pieces = jnp.asarray(np.stack([bf16_pieces(table[:, order]) for order in orders]))
    own_columns = jnp.asarray(
        table.reshape(HALF, group_size, parts_here).transpose(1, 0, 2).astype(np.float32)
    )
    vmem, hbm = pl.BlockSpec(memory_space=pltpu.VMEM), pl.BlockSpec(memory_space=pltpu.HBM)

    def in_vmem(array):
        return pltpu.with_memory_space_constraint(array, pltpu.VMEM)

    def in_hbm(array):
        return pltpu.with_memory_space_constraint(array, pltpu.HBM)

    early = tile_count // 2
    operands = [
        curl_tiles,
        own_columns,
        coeffs,
        pieces,
        source,
        pattern.T,
        region_ids,
        material_law,
    ]
    shapes = [
        (early,) + curl_tiles.shape[1:],
        own_columns.shape[1:],
    ] + [operand.shape for operand in operands[2:]]
    fetched = pl.pallas_call(
        fetch_kernel,
        out_shape=[pltpu.VMEM(shape, o.dtype) for shape, o in zip(shapes, operands)],
        in_specs=[hbm] * len(operands),
        out_specs=[vmem] * len(operands),
        scratch_shapes=[pltpu.SemaphoreType.DMA((len(operands),))],
        compiler_params=pltpu.CompilerParams(vmem_limit_bytes=16 * MIB),
        cost_estimate=pl.CostEstimate(
            flops=0, bytes_accessed=4 * early * links * tile * comps, transcendentals=0
        ),
        name="fetch_operands",
    )(*[in_hbm(operand) for operand in operands])
    first_curl, columns_here, coeffs_here, pieces_here, source_here, *others = fetched
    pattern_here = others[0]

    left, right = from_neighbours(coeffs, tile)
    block = jnp.concatenate([left, coeffs_here, right], axis=1)
    copies = jnp.broadcast_to(block[None], (group_size,) + block.shape)
    window = lax.all_to_all(copies, ARRIVAL, 0, 0).reshape(parts, block.shape[1])
    pattern_words = pltpu.SMEM((links, tile_count), jnp.int32)
    projected, halo, later_curl = pl.pallas_call(
        field_kernel,
        out_shape=(
            pltpu.VMEM((tile_count, parts_here, comps), jnp.float32),
            pltpu.VMEM((parts_here, 2 * tile), jnp.float32),
            pltpu.VMEM((tile_count - early,) + curl_tiles.shape[1:], curl_tiles.dtype),
        ),
        in_specs=[vmem] * 7 + [hbm],
        out_specs=(vmem, vmem, vmem),
        scratch_shapes=[
            pattern_words,
            pltpu.SMEM(region_ids.shape, jnp.int32),
            pltpu.SMEM(material_law.shape, jnp.float32),
            pltpu.SMEM((links * tile_count + 1,), jnp.int32),
            pltpu.VMEM((SAMPLES, (tile_count + 2) * tile), jnp.bfloat16),
            pltpu.VMEM((tile_count, HALF, comps), jnp.float32),
            pltpu.VMEM((LISTED, 2, parts_here, tile), jnp.float32),
            pltpu.SemaphoreType.DMA((3,)),
            pltpu.SemaphoreType.DMA((pl.cdiv(tile_count - early, CHUNK),)),
        ],
        compiler_params=pltpu.CompilerParams(vmem_limit_bytes=32 * MIB),
        cost_estimate=pl.CostEstimate(
            flops=2 * SAMPLES * tile_count * links * tile * comps,
            bytes_accessed=2 * curl_tiles.size,
            transcendentals=0,
        ),
        name="shard_fields",
    )(
        in_vmem(window),
        *[in_vmem(array) for array in (first_curl, columns_here, pieces_here, *others)],
        in_hbm(curl_tiles),
    )
    if lax.axis_size("space") == 2:
        beside = [across(halo, 0, 1)] * 2
    else:
        beside = [across(halo, 0, -1), across(halo, 0, 1)]
    own = pl.pallas_call(
        sum_kernel,
        out_shape=pltpu.VMEM(source.shape, jnp.float32),
        in_specs=[vmem] * 5,
        out_specs=vmem,
        scratch_shapes=[
            pattern_words,
            pltpu.SemaphoreType.DMA,
        ]
        + [pltpu.VMEM((tile_count + 2, parts_here, tile), jnp.float32)] * links,
        compiler_params=pltpu.CompilerParams(vmem_limit_bytes=32 * MIB),
        cost_estimate=pl.CostEstimate(
            flops=2 * SAMPLES * tile_count * links * tile * comps,
            bytes_accessed=2 * curl_tiles.size,
            transcendentals=0,
        ),
        name="shard_sums",
    )(
        *[in_vmem(a) for a in (projected, first_curl, later_curl, source_here, pattern_here)],
    )
    return pl.pallas_call(
        halo_kernel,
        out_shape=jax.ShapeDtypeStruct(source.shape, jnp.float32),
        in_specs=[vmem] * 3,
        out_specs=vmem,
        compiler_params=pltpu.CompilerParams(vmem_limit_bytes=16 * MIB),
        name="halo_sum",
    )(in_vmem(own), *beside)


def solution(mesh):
    at = mesh.axis_names.index("harm")
    harm = mesh.shape["harm"]
    cores = 2 if harm % 2 == 0 else 1
    sizes = mesh.devices.shape
    split = jax.sharding.Mesh(
        mesh.devices.reshape(sizes[:at] + (harm // cores, cores) + sizes[at + 1 :]),
        mesh.axis_names[:at] + ("chip", "core") + mesh.axis_names[at + 1 :],
    )
    placed = (
        P(GROUP, "space"),
        P("space", None, None, None),
        P("space", None),
        P("space"),
        P(),
        P(GROUP, "space"),
    )
    return jax.shard_map(
        per_device,
        mesh=split,
        in_specs=placed,
        out_specs=P(GROUP, "space"),
        check_vma=False,
    )
```

```python
import math

import jax
import jax.numpy as jnp
import ml_dtypes
import numpy as np
from jax import lax
from jax.experimental import pallas as pl
from jax.experimental.pallas import tpu as pltpu
from jax.sharding import PartitionSpec as P

SAMPLES = 64
HALF = SAMPLES // 2
GROUP = ("chip", "core", "samp")
MIB = 1024 * 1024
LISTED = 6
CHUNK = 5
AHEAD = 3


def half_table(parts):
    sample_ids = np.arange(HALF)[:, None]
    part_ids = np.arange(parts)[None, :]
    phase = ((2 * (part_ids // 2) + 1) * sample_ids % SAMPLES) * (2.0 * math.pi / SAMPLES)
    return np.where(part_ids % 2 == 0, np.cos(phase), np.sin(phase))


def bf16_pieces(table):
    rest = table
    pieces = []
    for _ in range(3):
        piece = rest.astype(ml_dtypes.bfloat16)
        pieces.append(piece)
        rest = rest - piece.astype(np.float64)
    return np.concatenate(pieces, axis=-1)


def across(array, core_step, space_step):
    cores, shards = lax.axis_size("core"), lax.axis_size("space")
    pairs = [
        (c * shards + s, (c + core_step) % cores * shards + (s + space_step) % shards)
        for c in range(cores)
        for s in range(shards)
    ]
    return lax.ppermute(array, ("core", "space"), pairs)


def from_neighbours(array, tile):
    if lax.axis_size("space") == 2:
        other = across(array, 1, 1)
        return other[:, -tile:], other[:, :tile]
    return across(array[:, -tile:], 1, 1), across(array[:, :tile], 1, -1)


def fetch_kernel(*refs):
    count = (len(refs) - 1) // 2
    sources, targets, sems = refs[:count], refs[count : 2 * count], refs[-1]
    early = targets[0].shape[0]
    sources = [sources[0].at[i] for i in range(early)] + [
        sources[1].at[lax.axis_index(GROUP)],
        *sources[2:],
    ]
    targets = [targets[0].at[i] for i in range(early)] + list(targets[1:])
    copies = [
        pltpu.make_async_copy(source, target, sems.at[i])
        for i, (source, target) in enumerate(zip(sources, targets))
    ]
    for copy in copies:
        copy.start()
    for copy in copies:
        copy.wait()


def time_samples(pieces, rows):
    stacked = jnp.concatenate([rows] * 3, axis=0)
    samples = jnp.dot(pieces, stacked, preferred_element_type=jnp.float32)
    high = samples.astype(jnp.bfloat16)
    low = (samples - high.astype(jnp.float32)).astype(jnp.bfloat16)
    return jnp.concatenate([high, low], axis=0)


def weighted(projected, blocks):
    return lax.dot_general(
        projected.astype(jnp.bfloat16),
        blocks,
        (((1,), (1,)), ((), ())),
        preferred_element_type=jnp.float32,
    )


def field_kernel(
    window,
    first_curl,
    table,
    pieces,
    pattern_in,
    region_in,
    law_in,
    curl_hbm,
    projected,
    halo,
    later_curl,
    pattern,
    region_ids,
    law,
    outer,
    timed,
    densities,
    edge_sums,
    small_sems,
    curl_sems,
):
    tile_count, links, tile, comps = curl_hbm.shape
    early = first_curl.shape[0]
    parts_here = halo.shape[0]
    fetched = [(pattern_in, pattern), (region_in, region_ids), (law_in, law)]
    small = [
        pltpu.make_async_copy(src, dst, small_sems.at[i]) for i, (src, dst) in enumerate(fetched)
    ]
    later = {
        elem: pltpu.make_async_copy(
            curl_hbm.at[elem], later_curl.at[elem - early], curl_sems.at[elem - early]
        )
        for elem in range(early, tile_count)
    }
    for copy in small + list(later.values()):
        copy.start()
    edge_sums[...] = jnp.zeros_like(edge_sums)
    own, outer_tiles = pieces[0], pieces[1]
    timed[:, tile:-tile] = time_samples(own, window[:, tile:-tile])
    timed[:, :tile] = time_samples(outer_tiles, window[:, :tile])
    timed[:, -tile:] = time_samples(outer_tiles, window[:, -tile:])
    columns = [
        jnp.broadcast_to(table[:, part : part + 1], (HALF, comps)) for part in range(parts_here)
    ]
    for copy in small:
        copy.wait()
    places = [[pattern[link, elem] for link in range(links)] for elem in range(tile_count)]
    count = jnp.int32(0)
    for elem in range(tile_count):
        for link, at in enumerate(places[elem]):
            outer[count] = elem * links + link
            count += jnp.where((at == 0) | (at == tile_count + 1), 1, 0)

    def blocks(elem):
        curl = first_curl[elem] if elem < early else later_curl[elem - early]
        return curl.reshape(links * tile, comps)

    def find_density(elem):
        picked = jnp.concatenate(
            [timed[:, pl.ds(pl.multiple_of(at * tile, tile), tile)] for at in places[elem]], axis=1
        )
        split = jnp.dot(picked, blocks(elem), preferred_element_type=jnp.float32)
        densities[elem] = split[:HALF] + split[HALF:]

    def project(elem):
        density = densities[elem]
        comp = [density[:, c * tile : (c + 1) * tile] for c in range(comps // tile)]
        square = comp[0] * comp[0]
        for c in comp[1:]:
            square = square + c * c
        region = region_ids[elem]
        reluct = law[0, region] + law[2, region] * square / (square + law[1, region])
        field = jnp.concatenate([reluct * c for c in comp], axis=1)
        rows = [jnp.sum(column * field, axis=0, keepdims=True) for column in columns]
        projected[elem] = jnp.concatenate(rows, axis=0) * (4.0 / SAMPLES)

    for turn in range(tile_count + 1):
        if turn < tile_count:
            if turn >= early and (turn - early) % CHUNK == 0:
                for elem in range(turn, min(turn + CHUNK, tile_count)):
                    later[elem].wait()
            find_density(turn)
        if turn:
            project(turn - 1)

    def add_outer(turn, carry):
        for slot in range(LISTED):
            spot = turn * LISTED + slot
            code = jnp.where(spot < count, outer[jnp.minimum(spot, jnp.maximum(count - 1, 0))], 0)
            elem, link = code // links, code % links
            block = jnp.where(
                elem < early,
                first_curl[jnp.minimum(elem, early - 1), link],
                later_curl[jnp.maximum(elem - early, 0), link],
            )
            contrib = weighted(projected[elem], block)
            side = jnp.where(pattern[link, elem] == 0, 0, 1)
            edge_sums[slot, side] += jnp.where(spot < count, contrib, 0.0)
        return carry

    add_outer(0, 0)
    lax.fori_loop(1, (count + LISTED - 1) // LISTED, add_outer, 0)
    total = edge_sums[0]
    for slot in range(1, LISTED):
        total = total + edge_sums[slot]
    halo[:, :tile] = total[0]
    halo[:, tile:] = total[1]


def sum_kernel(
    projected,
    first_curl,
    later_curl,
    source,
    pattern_in,
    out,
    pattern,
    small_sem,
    *sums,
):
    links, tile, comps = first_curl.shape[1:]
    early = first_curl.shape[0]
    tile_count = early + later_curl.shape[0]
    small = pltpu.make_async_copy(pattern_in, pattern, small_sem)
    small.start()
    for total in sums:
        total[...] = jnp.zeros_like(total)

    def contribution(elem):
        curl = first_curl[elem] if elem < early else later_curl[elem - early]
        return weighted(projected[elem], curl.reshape(links * tile, comps))

    ahead = [contribution(elem) for elem in range(AHEAD)]
    small.wait()
    for elem in range(tile_count):
        contrib = ahead[elem] if elem < AHEAD else contribution(elem)
        for link in range(links):
            sums[link][pattern[link, elem]] += contrib[:, link * tile : (link + 1) * tile]
    for w in range(tile_count):
        at = slice(w * tile, (w + 1) * tile)
        total = sums[0][w + 1]
        for other in sums[1:]:
            total = total + other[w + 1]
        out[:, at] = total - source[:, at]


def halo_kernel(own, from_right, from_left, out):
    tile = from_left.shape[1] // 2
    out[...] = own[...]
    out[:, :tile] += from_left[:, tile:]
    out[:, -tile:] += from_right[:, :tile]


def per_device(coeffs, curl_tiles, pattern, region_ids, material_law, source):
    parts_here = coeffs.shape[0]
    tile_count, links, tile, comps = curl_tiles.shape
    chips, cores, samp = (lax.axis_size(axis) for axis in GROUP)
    group_size = chips * cores * samp
    parts = parts_here * group_size
    table = half_table(parts)
    before = np.roll(np.arange(parts).reshape(chips, cores, -1), 1, axis=1).reshape(-1)
    pieces = jnp.asarray(np.stack([bf16_pieces(table), bf16_pieces(table[:, before])]))
    own_columns = jnp.asarray(
        table.reshape(HALF, group_size, parts_here).transpose(1, 0, 2).astype(np.float32)
    )
    vmem, hbm = pl.BlockSpec(memory_space=pltpu.VMEM), pl.BlockSpec(memory_space=pltpu.HBM)

    def in_vmem(array):
        return pltpu.with_memory_space_constraint(array, pltpu.VMEM)

    def in_hbm(array):
        return pltpu.with_memory_space_constraint(array, pltpu.HBM)

    early = tile_count // 2
    operands = [
        curl_tiles,
        own_columns,
        coeffs,
        pieces,
        source,
        pattern.T,
        region_ids,
        material_law,
    ]
    shapes = [
        (early,) + curl_tiles.shape[1:],
        own_columns.shape[1:],
    ] + [operand.shape for operand in operands[2:]]
    fetched = pl.pallas_call(
        fetch_kernel,
        out_shape=[pltpu.VMEM(shape, o.dtype) for shape, o in zip(shapes, operands)],
        in_specs=[hbm] * len(operands),
        out_specs=[vmem] * len(operands),
        scratch_shapes=[pltpu.SemaphoreType.DMA((early + len(operands) - 1,))],
        compiler_params=pltpu.CompilerParams(vmem_limit_bytes=16 * MIB),
        cost_estimate=pl.CostEstimate(
            flops=0, bytes_accessed=4 * early * links * tile * comps, transcendentals=0
        ),
        name="fetch_operands",
    )(*[in_hbm(operand) for operand in operands])
    first_curl, columns_here, coeffs_here, pieces_here, source_here, *others = fetched
    pattern_here = others[0]

    left, right = from_neighbours(coeffs, tile)
    block = jnp.concatenate([left, coeffs_here, right], axis=1)
    copies = jnp.broadcast_to(block[None], (group_size,) + block.shape)
    window = lax.all_to_all(copies, GROUP, 0, 0).reshape(parts, block.shape[1])
    pattern_words = pltpu.SMEM((links, tile_count), jnp.int32)
    projected, halo, later_curl = pl.pallas_call(
        field_kernel,
        out_shape=(
            pltpu.VMEM((tile_count, parts_here, comps), jnp.float32),
            pltpu.VMEM((parts_here, 2 * tile), jnp.float32),
            pltpu.VMEM((tile_count - early,) + curl_tiles.shape[1:], curl_tiles.dtype),
        ),
        in_specs=[vmem] * 7 + [hbm],
        out_specs=(vmem, vmem, vmem),
        scratch_shapes=[
            pattern_words,
            pltpu.SMEM(region_ids.shape, jnp.int32),
            pltpu.SMEM(material_law.shape, jnp.float32),
            pltpu.SMEM((links * tile_count + 1,), jnp.int32),
            pltpu.VMEM((SAMPLES, (tile_count + 2) * tile), jnp.bfloat16),
            pltpu.VMEM((tile_count, HALF, comps), jnp.float32),
            pltpu.VMEM((LISTED, 2, parts_here, tile), jnp.float32),
            pltpu.SemaphoreType.DMA((3,)),
            pltpu.SemaphoreType.DMA((tile_count - early,)),
        ],
        compiler_params=pltpu.CompilerParams(vmem_limit_bytes=32 * MIB),
        cost_estimate=pl.CostEstimate(
            flops=2 * SAMPLES * tile_count * links * tile * comps,
            bytes_accessed=2 * curl_tiles.size,
            transcendentals=0,
        ),
        name="shard_fields",
    )(
        in_vmem(window),
        *[in_vmem(array) for array in (first_curl, columns_here, pieces_here, *others)],
        in_hbm(curl_tiles),
    )
    if lax.axis_size("space") == 2:
        beside = [across(halo, 0, 1)] * 2
    else:
        beside = [across(halo, 0, -1), across(halo, 0, 1)]
    own = pl.pallas_call(
        sum_kernel,
        out_shape=pltpu.VMEM(source.shape, jnp.float32),
        in_specs=[vmem] * 5,
        out_specs=vmem,
        scratch_shapes=[
            pattern_words,
            pltpu.SemaphoreType.DMA,
        ]
        + [pltpu.VMEM((tile_count + 2, parts_here, tile), jnp.float32)] * links,
        compiler_params=pltpu.CompilerParams(vmem_limit_bytes=32 * MIB),
        cost_estimate=pl.CostEstimate(
            flops=2 * SAMPLES * tile_count * links * tile * comps,
            bytes_accessed=2 * curl_tiles.size,
            transcendentals=0,
        ),
        name="shard_sums",
    )(
        *[in_vmem(a) for a in (projected, first_curl, later_curl, source_here, pattern_here)],
    )
    return pl.pallas_call(
        halo_kernel,
        out_shape=jax.ShapeDtypeStruct(source.shape, jnp.float32),
        in_specs=[vmem] * 3,
        out_specs=vmem,
        compiler_params=pltpu.CompilerParams(vmem_limit_bytes=16 * MIB),
        name="halo_sum",
    )(in_vmem(own), *beside)


def solution(mesh):
    at = mesh.axis_names.index("harm")
    harm = mesh.shape["harm"]
    cores = 2 if harm % 2 == 0 else 1
    sizes = mesh.devices.shape
    split = jax.sharding.Mesh(
        mesh.devices.reshape(sizes[:at] + (harm // cores, cores) + sizes[at + 1 :]),
        mesh.axis_names[:at] + ("chip", "core") + mesh.axis_names[at + 1 :],
    )
    placed = (
        P(GROUP, "space"),
        P("space", None, None, None),
        P("space", None),
        P("space"),
        P(),
        P(GROUP, "space"),
    )
    return jax.shard_map(
        per_device,
        mesh=split,
        in_specs=placed,
        out_specs=P(GROUP, "space"),
        check_vma=False,
    )
```

```python
import math

import jax
import jax.numpy as jnp
import ml_dtypes
import numpy as np
from jax import lax
from jax.experimental import pallas as pl
from jax.experimental.pallas import tpu as pltpu
from jax.sharding import PartitionSpec as P

SAMPLES = 64
HALF = SAMPLES // 2
GROUP = ("chip", "core", "samp")
MIB = 1024 * 1024
LISTED = 4
CHUNK = 4
AHEAD = 3


def half_table(parts):
    sample_ids = np.arange(HALF)[:, None]
    part_ids = np.arange(parts)[None, :]
    phase = ((2 * (part_ids // 2) + 1) * sample_ids % SAMPLES) * (2.0 * math.pi / SAMPLES)
    return np.where(part_ids % 2 == 0, np.cos(phase), np.sin(phase))


def bf16_pieces(table):
    rest = table
    pieces = []
    for _ in range(3):
        piece = rest.astype(ml_dtypes.bfloat16)
        pieces.append(piece)
        rest = rest - piece.astype(np.float64)
    return np.concatenate(pieces, axis=-1)


def across(array, core_step, space_step):
    cores, shards = lax.axis_size("core"), lax.axis_size("space")
    pairs = [
        (c * shards + s, (c + core_step) % cores * shards + (s + space_step) % shards)
        for c in range(cores)
        for s in range(shards)
    ]
    return lax.ppermute(array, ("core", "space"), pairs)


def from_neighbours(array, tile):
    if lax.axis_size("space") == 2:
        other = across(array, 1, 1)
        return other[:, -tile:], other[:, :tile]
    return across(array[:, -tile:], 1, 1), across(array[:, :tile], 1, -1)


def fetch_kernel(*refs):
    count = (len(refs) - 1) // 2
    sources, targets, sems = refs[:count], refs[count : 2 * count], refs[-1]
    rank = lax.axis_index(GROUP)
    sources = (sources[0].at[: targets[0].shape[0]], sources[1].at[rank]) + sources[2:]
    copies = [
        pltpu.make_async_copy(source, target, sems.at[i])
        for i, (source, target) in enumerate(zip(sources, targets))
    ]
    for copy in copies:
        copy.start()
    for copy in copies:
        copy.wait()


def time_samples(pieces, rows):
    stacked = jnp.concatenate([rows] * 3, axis=0)
    samples = jnp.dot(pieces, stacked, preferred_element_type=jnp.float32)
    high = samples.astype(jnp.bfloat16)
    low = (samples - high.astype(jnp.float32)).astype(jnp.bfloat16)
    return jnp.concatenate([high, low], axis=0)


def weighted(projected, blocks):
    return lax.dot_general(
        projected.astype(jnp.bfloat16),
        blocks,
        (((1,), (1,)), ((), ())),
        preferred_element_type=jnp.float32,
    )


def field_kernel(
    window,
    first_curl,
    table,
    pieces,
    pattern_in,
    region_in,
    law_in,
    curl_hbm,
    projected,
    halo,
    later_curl,
    pattern,
    region_ids,
    law,
    outer,
    timed,
    densities,
    edge_sums,
    small_sems,
    curl_sems,
):
    tile_count, links, tile, comps = curl_hbm.shape
    early = first_curl.shape[0]
    parts_here = halo.shape[0]
    fetched = [(pattern_in, pattern), (region_in, region_ids), (law_in, law)]
    small = [
        pltpu.make_async_copy(src, dst, small_sems.at[i]) for i, (src, dst) in enumerate(fetched)
    ]
    later = {
        elem: pltpu.make_async_copy(
            curl_hbm.at[elem : min(elem + CHUNK, tile_count)],
            later_curl.at[elem - early : min(elem + CHUNK, tile_count) - early],
            curl_sems.at[(elem - early) // CHUNK],
        )
        for elem in range(early, tile_count, CHUNK)
    }
    for copy in small + list(later.values()):
        copy.start()
    edge_sums[...] = jnp.zeros_like(edge_sums)
    own, outer_tiles = pieces[0], pieces[1]
    timed[:, tile:-tile] = time_samples(own, window[:, tile:-tile])
    timed[:, :tile] = time_samples(outer_tiles, window[:, :tile])
    timed[:, -tile:] = time_samples(outer_tiles, window[:, -tile:])
    columns = [
        jnp.broadcast_to(table[:, part : part + 1], (HALF, comps)) for part in range(parts_here)
    ]
    for copy in small:
        copy.wait()
    places = [[pattern[link, elem] for link in range(links)] for elem in range(tile_count)]
    count = jnp.int32(0)
    for elem in range(tile_count):
        for link, at in enumerate(places[elem]):
            outer[count] = elem * links + link
            count += jnp.where((at == 0) | (at == tile_count + 1), 1, 0)

    def blocks(elem):
        curl = first_curl[elem] if elem < early else later_curl[elem - early]
        return curl.reshape(links * tile, comps)

    def find_density(elem):
        picked = jnp.concatenate(
            [timed[:, pl.ds(pl.multiple_of(at * tile, tile), tile)] for at in places[elem]], axis=1
        )
        split = jnp.dot(picked, blocks(elem), preferred_element_type=jnp.float32)
        densities[elem] = split[:HALF] + split[HALF:]

    def project(elem):
        density = densities[elem]
        comp = [density[:, c * tile : (c + 1) * tile] for c in range(comps // tile)]
        square = comp[0] * comp[0]
        for c in comp[1:]:
            square = square + c * c
        region = region_ids[elem]
        reluct = law[0, region] + law[2, region] * square / (square + law[1, region])
        field = jnp.concatenate([reluct * c for c in comp], axis=1)
        rows = [jnp.sum(column * field, axis=0, keepdims=True) for column in columns]
        projected[elem] = jnp.concatenate(rows, axis=0) * (4.0 / SAMPLES)

    for turn in range(tile_count + 1):
        if turn < tile_count:
            if turn in later:
                later[turn].wait()
            find_density(turn)
        if turn:
            project(turn - 1)

    def add_outer(turn, carry):
        listed, sides, rows, curls = [], [], [], []
        for slot in range(LISTED):
            spot = turn * LISTED + slot
            code = jnp.where(spot < count, outer[jnp.minimum(spot, jnp.maximum(count - 1, 0))], 0)
            elem, link = code // links, code % links
            curls.append(
                jnp.where(
                    elem < early,
                    first_curl[jnp.minimum(elem, early - 1), link],
                    later_curl[jnp.maximum(elem - early, 0), link],
                )
            )
            rows.append(projected[elem])
            sides.append(jnp.where(pattern[link, elem] == 0, 0, 1))
            listed.append(spot < count)
        contrib = weighted(jnp.concatenate(rows, axis=0), jnp.concatenate(curls, axis=0))
        for slot in range(LISTED):
            block = contrib[
                slot * parts_here : (slot + 1) * parts_here, slot * tile : (slot + 1) * tile
            ]
            edge_sums[slot, sides[slot]] += jnp.where(listed[slot], block, 0.0)
        return carry

    add_outer(0, 0)
    lax.fori_loop(1, (count + LISTED - 1) // LISTED, add_outer, 0)
    total = edge_sums[0]
    for slot in range(1, LISTED):
        total = total + edge_sums[slot]
    halo[:, :tile] = total[0]
    halo[:, tile:] = total[1]


def sum_kernel(
    projected,
    first_curl,
    later_curl,
    source,
    pattern_in,
    out,
    pattern,
    small_sem,
    *sums,
):
    links, tile, comps = first_curl.shape[1:]
    early = first_curl.shape[0]
    tile_count = early + later_curl.shape[0]
    small = pltpu.make_async_copy(pattern_in, pattern, small_sem)
    small.start()
    for total in sums:
        total[...] = jnp.zeros_like(total)

    def contribution(elem):
        curl = first_curl[elem] if elem < early else later_curl[elem - early]
        return weighted(projected[elem], curl.reshape(links * tile, comps))

    ahead = [contribution(elem) for elem in range(AHEAD)]
    small.wait()
    for elem in range(tile_count):
        contrib = ahead[elem] if elem < AHEAD else contribution(elem)
        for link in range(links):
            sums[link][pattern[link, elem]] += contrib[:, link * tile : (link + 1) * tile]
    for w in range(tile_count):
        at = slice(w * tile, (w + 1) * tile)
        total = sums[0][w + 1]
        for other in sums[1:]:
            total = total + other[w + 1]
        out[:, at] = total - source[:, at]


def halo_kernel(own, from_right, from_left, out):
    tile = from_left.shape[1] // 2
    out[...] = own[...]
    out[:, :tile] += from_left[:, tile:]
    out[:, -tile:] += from_right[:, :tile]


def per_device(coeffs, curl_tiles, pattern, region_ids, material_law, source):
    parts_here = coeffs.shape[0]
    tile_count, links, tile, comps = curl_tiles.shape
    chips, cores, samp = (lax.axis_size(axis) for axis in GROUP)
    group_size = chips * cores * samp
    parts = parts_here * group_size
    table = half_table(parts)
    before = np.roll(np.arange(parts).reshape(chips, cores, -1), 1, axis=1).reshape(-1)
    pieces = jnp.asarray(np.stack([bf16_pieces(table), bf16_pieces(table[:, before])]))
    own_columns = jnp.asarray(
        table.reshape(HALF, group_size, parts_here).transpose(1, 0, 2).astype(np.float32)
    )
    vmem, hbm = pl.BlockSpec(memory_space=pltpu.VMEM), pl.BlockSpec(memory_space=pltpu.HBM)

    def in_vmem(array):
        return pltpu.with_memory_space_constraint(array, pltpu.VMEM)

    def in_hbm(array):
        return pltpu.with_memory_space_constraint(array, pltpu.HBM)

    early = tile_count // 2
    operands = [
        curl_tiles,
        own_columns,
        coeffs,
        pieces,
        source,
        pattern.T,
        region_ids,
        material_law,
    ]
    shapes = [
        (early,) + curl_tiles.shape[1:],
        own_columns.shape[1:],
    ] + [operand.shape for operand in operands[2:]]
    fetched = pl.pallas_call(
        fetch_kernel,
        out_shape=[pltpu.VMEM(shape, o.dtype) for shape, o in zip(shapes, operands)],
        in_specs=[hbm] * len(operands),
        out_specs=[vmem] * len(operands),
        scratch_shapes=[pltpu.SemaphoreType.DMA((len(operands),))],
        compiler_params=pltpu.CompilerParams(vmem_limit_bytes=16 * MIB),
        cost_estimate=pl.CostEstimate(
            flops=0, bytes_accessed=4 * early * links * tile * comps, transcendentals=0
        ),
        name="fetch_operands",
    )(*[in_hbm(operand) for operand in operands])
    first_curl, columns_here, coeffs_here, pieces_here, source_here, *others = fetched
    pattern_here = others[0]

    left, right = from_neighbours(coeffs, tile)
    block = jnp.concatenate([left, coeffs_here, right], axis=1)
    copies = jnp.broadcast_to(block[None], (group_size,) + block.shape)
    window = lax.all_to_all(copies, GROUP, 0, 0).reshape(parts, block.shape[1])
    pattern_words = pltpu.SMEM((links, tile_count), jnp.int32)
    projected, halo, later_curl = pl.pallas_call(
        field_kernel,
        out_shape=(
            pltpu.VMEM((tile_count, parts_here, comps), jnp.float32),
            pltpu.VMEM((parts_here, 2 * tile), jnp.float32),
            pltpu.VMEM((tile_count - early,) + curl_tiles.shape[1:], curl_tiles.dtype),
        ),
        in_specs=[vmem] * 7 + [hbm],
        out_specs=(vmem, vmem, vmem),
        scratch_shapes=[
            pattern_words,
            pltpu.SMEM(region_ids.shape, jnp.int32),
            pltpu.SMEM(material_law.shape, jnp.float32),
            pltpu.SMEM((links * tile_count + 1,), jnp.int32),
            pltpu.VMEM((SAMPLES, (tile_count + 2) * tile), jnp.bfloat16),
            pltpu.VMEM((tile_count, HALF, comps), jnp.float32),
            pltpu.VMEM((LISTED, 2, parts_here, tile), jnp.float32),
            pltpu.SemaphoreType.DMA((3,)),
            pltpu.SemaphoreType.DMA((pl.cdiv(tile_count - early, CHUNK),)),
        ],
        compiler_params=pltpu.CompilerParams(vmem_limit_bytes=32 * MIB),
        cost_estimate=pl.CostEstimate(
            flops=2 * SAMPLES * tile_count * links * tile * comps,
            bytes_accessed=2 * curl_tiles.size,
            transcendentals=0,
        ),
        name="shard_fields",
    )(
        in_vmem(window),
        *[in_vmem(array) for array in (first_curl, columns_here, pieces_here, *others)],
        in_hbm(curl_tiles),
    )
    if lax.axis_size("space") == 2:
        beside = [across(halo, 0, 1)] * 2
    else:
        beside = [across(halo, 0, -1), across(halo, 0, 1)]
    own = pl.pallas_call(
        sum_kernel,
        out_shape=pltpu.VMEM(source.shape, jnp.float32),
        in_specs=[vmem] * 5,
        out_specs=vmem,
        scratch_shapes=[
            pattern_words,
            pltpu.SemaphoreType.DMA,
        ]
        + [pltpu.VMEM((tile_count + 2, parts_here, tile), jnp.float32)] * links,
        compiler_params=pltpu.CompilerParams(vmem_limit_bytes=32 * MIB),
        cost_estimate=pl.CostEstimate(
            flops=2 * SAMPLES * tile_count * links * tile * comps,
            bytes_accessed=2 * curl_tiles.size,
            transcendentals=0,
        ),
        name="shard_sums",
    )(
        *[in_vmem(a) for a in (projected, first_curl, later_curl, source_here, pattern_here)],
    )
    return pl.pallas_call(
        halo_kernel,
        out_shape=jax.ShapeDtypeStruct(source.shape, jnp.float32),
        in_specs=[vmem] * 3,
        out_specs=vmem,
        compiler_params=pltpu.CompilerParams(vmem_limit_bytes=16 * MIB),
        name="halo_sum",
    )(in_vmem(own), *beside)


def solution(mesh):
    at = mesh.axis_names.index("harm")
    harm = mesh.shape["harm"]
    cores = 2 if harm % 2 == 0 else 1
    sizes = mesh.devices.shape
    split = jax.sharding.Mesh(
        mesh.devices.reshape(sizes[:at] + (harm // cores, cores) + sizes[at + 1 :]),
        mesh.axis_names[:at] + ("chip", "core") + mesh.axis_names[at + 1 :],
    )
    placed = (
        P(GROUP, "space"),
        P("space", None, None, None),
        P("space", None),
        P("space"),
        P(),
        P(GROUP, "space"),
    )
    return jax.shard_map(
        per_device,
        mesh=split,
        in_specs=placed,
        out_specs=P(GROUP, "space"),
        check_vma=False,
    )
```

```python
import math

import jax
import jax.numpy as jnp
import ml_dtypes
import numpy as np
from jax import lax
from jax.experimental import pallas as pl
from jax.experimental.pallas import tpu as pltpu
from jax.sharding import PartitionSpec as P

SAMPLES = 64
HALF = SAMPLES // 2
GROUP = ("chip", "core", "samp")
MIB = 1024 * 1024
LISTED = 4
CHUNK = 4
AHEAD = 3


def half_table(parts):
    sample_ids = np.arange(HALF)[:, None]
    part_ids = np.arange(parts)[None, :]
    phase = ((2 * (part_ids // 2) + 1) * sample_ids % SAMPLES) * (2.0 * math.pi / SAMPLES)
    return np.where(part_ids % 2 == 0, np.cos(phase), np.sin(phase))


def bf16_pieces(table):
    rest = table
    pieces = []
    for _ in range(3):
        piece = rest.astype(ml_dtypes.bfloat16)
        pieces.append(piece)
        rest = rest - piece.astype(np.float64)
    return np.concatenate(pieces, axis=-1)


def across(array, core_step, space_step):
    cores, shards = lax.axis_size("core"), lax.axis_size("space")
    pairs = [
        (c * shards + s, (c + core_step) % cores * shards + (s + space_step) % shards)
        for c in range(cores)
        for s in range(shards)
    ]
    return lax.ppermute(array, ("core", "space"), pairs)


def from_neighbours(array, tile):
    if lax.axis_size("space") == 2:
        other = across(array, 1, 1)
        return other[:, -tile:], other[:, :tile]
    return across(array[:, -tile:], 1, 1), across(array[:, :tile], 1, -1)


def fetch_kernel(*refs):
    count = (len(refs) - 1) // 2
    sources, targets, sems = refs[:count], refs[count : 2 * count], refs[-1]
    rank = lax.axis_index(GROUP)
    sources = (sources[0].at[: targets[0].shape[0]], sources[1].at[rank]) + sources[2:]
    copies = [
        pltpu.make_async_copy(source, target, sems.at[i])
        for i, (source, target) in enumerate(zip(sources, targets))
    ]
    for copy in copies:
        copy.start()
    for copy in copies:
        copy.wait()


def time_samples(pieces, rows):
    stacked = jnp.concatenate([rows] * 3, axis=0)
    samples = jnp.dot(pieces, stacked, preferred_element_type=jnp.float32)
    high = samples.astype(jnp.bfloat16)
    low = (samples - high.astype(jnp.float32)).astype(jnp.bfloat16)
    return jnp.concatenate([high, low], axis=0)


def weighted(projected, blocks):
    return lax.dot_general(
        projected.astype(jnp.bfloat16),
        blocks,
        (((1,), (1,)), ((), ())),
        preferred_element_type=jnp.float32,
    )


def field_kernel(
    window,
    first_curl,
    table,
    pieces,
    pattern_in,
    region_in,
    law_in,
    curl_hbm,
    projected,
    halo,
    later_curl,
    pattern,
    region_ids,
    law,
    outer,
    timed,
    edge_sums,
    small_sems,
    curl_sems,
):
    tile_count, links, tile, comps = curl_hbm.shape
    early = first_curl.shape[0]
    parts_here = halo.shape[0]
    fetched = [(pattern_in, pattern), (region_in, region_ids), (law_in, law)]
    small = [
        pltpu.make_async_copy(src, dst, small_sems.at[i]) for i, (src, dst) in enumerate(fetched)
    ]
    later = {
        elem: pltpu.make_async_copy(
            curl_hbm.at[elem : min(elem + CHUNK, tile_count)],
            later_curl.at[elem - early : min(elem + CHUNK, tile_count) - early],
            curl_sems.at[(elem - early) // CHUNK],
        )
        for elem in range(early, tile_count, CHUNK)
    }
    for copy in small + list(later.values()):
        copy.start()
    edge_sums[...] = jnp.zeros_like(edge_sums)
    own, outer_tiles = pieces[0], pieces[1]
    timed[:, tile:-tile] = time_samples(own, window[:, tile:-tile])
    timed[:, :tile] = time_samples(outer_tiles, window[:, :tile])
    timed[:, -tile:] = time_samples(outer_tiles, window[:, -tile:])
    columns = [
        jnp.broadcast_to(table[:, part : part + 1], (HALF, comps)) for part in range(parts_here)
    ]
    for copy in small:
        copy.wait()
    places = [[pattern[link, elem] for link in range(links)] for elem in range(tile_count)]
    count = jnp.int32(0)
    for elem in range(tile_count):
        for link, at in enumerate(places[elem]):
            outer[count] = elem * links + link
            count += jnp.where((at == 0) | (at == tile_count + 1), 1, 0)

    def blocks(elem):
        curl = first_curl[elem] if elem < early else later_curl[elem - early]
        return curl.reshape(links * tile, comps)

    def find_density(elem):
        picked = jnp.concatenate(
            [timed[:, pl.ds(pl.multiple_of(at * tile, tile), tile)] for at in places[elem]], axis=1
        )
        split = jnp.dot(picked, blocks(elem), preferred_element_type=jnp.float32)
        return split[:HALF] + split[HALF:]

    def project(elem, density):
        comp = [density[:, c * tile : (c + 1) * tile] for c in range(comps // tile)]
        square = comp[0] * comp[0]
        for c in comp[1:]:
            square = square + c * c
        region = region_ids[elem]
        reluct = law[0, region] + law[2, region] * square / (square + law[1, region])
        field = jnp.concatenate([reluct * c for c in comp], axis=1)
        rows = [jnp.sum(column * field, axis=0, keepdims=True) for column in columns]
        projected[elem] = jnp.concatenate(rows, axis=0) * (4.0 / SAMPLES)

    density = None
    for turn in range(tile_count + 1):
        last = density
        if turn < tile_count:
            if turn in later:
                later[turn].wait()
            density = find_density(turn)
        if turn:
            project(turn - 1, last)

    def add_outer(turn, carry):
        listed, sides, rows, curls = [], [], [], []
        for slot in range(LISTED):
            spot = turn * LISTED + slot
            code = jnp.where(spot < count, outer[jnp.minimum(spot, jnp.maximum(count - 1, 0))], 0)
            elem, link = code // links, code % links
            curls.append(
                jnp.where(
                    elem < early,
                    first_curl[jnp.minimum(elem, early - 1), link],
                    later_curl[jnp.maximum(elem - early, 0), link],
                )
            )
            rows.append(projected[elem])
            sides.append(jnp.where(pattern[link, elem] == 0, 0, 1))
            listed.append(spot < count)
        contrib = weighted(jnp.concatenate(rows, axis=0), jnp.concatenate(curls, axis=0))
        for slot in range(LISTED):
            block = contrib[
                slot * parts_here : (slot + 1) * parts_here, slot * tile : (slot + 1) * tile
            ]
            edge_sums[slot, sides[slot]] += jnp.where(listed[slot], block, 0.0)
        return carry

    add_outer(0, 0)
    lax.fori_loop(1, (count + LISTED - 1) // LISTED, add_outer, 0)
    total = edge_sums[0]
    for slot in range(1, LISTED):
        total = total + edge_sums[slot]
    halo[:, :tile] = total[0]
    halo[:, tile:] = total[1]


def sum_kernel(
    projected,
    first_curl,
    later_curl,
    source,
    pattern_in,
    out,
    pattern,
    small_sem,
    *sums,
):
    links, tile, comps = first_curl.shape[1:]
    early = first_curl.shape[0]
    tile_count = early + later_curl.shape[0]
    small = pltpu.make_async_copy(pattern_in, pattern, small_sem)
    small.start()
    for total in sums:
        total[...] = jnp.zeros_like(total)

    def contribution(elem):
        curl = first_curl[elem] if elem < early else later_curl[elem - early]
        return weighted(projected[elem], curl.reshape(links * tile, comps))

    ahead = [contribution(elem) for elem in range(AHEAD)]
    small.wait()
    for elem in range(tile_count):
        contrib = ahead[elem] if elem < AHEAD else contribution(elem)
        for link in range(links):
            sums[link][pattern[link, elem]] += contrib[:, link * tile : (link + 1) * tile]
    for w in range(tile_count):
        at = slice(w * tile, (w + 1) * tile)
        total = sums[0][w + 1]
        for other in sums[1:]:
            total = total + other[w + 1]
        out[:, at] = total - source[:, at]


def halo_kernel(own, from_right, from_left, out):
    tile = from_left.shape[1] // 2
    out[...] = own[...]
    out[:, :tile] += from_left[:, tile:]
    out[:, -tile:] += from_right[:, :tile]


def per_device(coeffs, curl_tiles, pattern, region_ids, material_law, source):
    parts_here = coeffs.shape[0]
    tile_count, links, tile, comps = curl_tiles.shape
    chips, cores, samp = (lax.axis_size(axis) for axis in GROUP)
    group_size = chips * cores * samp
    parts = parts_here * group_size
    table = half_table(parts)
    before = np.roll(np.arange(parts).reshape(chips, cores, -1), 1, axis=1).reshape(-1)
    pieces = jnp.asarray(np.stack([bf16_pieces(table), bf16_pieces(table[:, before])]))
    own_columns = jnp.asarray(
        table.reshape(HALF, group_size, parts_here).transpose(1, 0, 2).astype(np.float32)
    )
    vmem, hbm = pl.BlockSpec(memory_space=pltpu.VMEM), pl.BlockSpec(memory_space=pltpu.HBM)

    def in_vmem(array):
        return pltpu.with_memory_space_constraint(array, pltpu.VMEM)

    def in_hbm(array):
        return pltpu.with_memory_space_constraint(array, pltpu.HBM)

    early = tile_count // 2
    operands = [
        curl_tiles,
        own_columns,
        coeffs,
        pieces,
        source,
        pattern.T,
        region_ids,
        material_law,
    ]
    shapes = [
        (early,) + curl_tiles.shape[1:],
        own_columns.shape[1:],
    ] + [operand.shape for operand in operands[2:]]
    fetched = pl.pallas_call(
        fetch_kernel,
        out_shape=[pltpu.VMEM(shape, o.dtype) for shape, o in zip(shapes, operands)],
        in_specs=[hbm] * len(operands),
        out_specs=[vmem] * len(operands),
        scratch_shapes=[pltpu.SemaphoreType.DMA((len(operands),))],
        compiler_params=pltpu.CompilerParams(vmem_limit_bytes=16 * MIB),
        cost_estimate=pl.CostEstimate(
            flops=0, bytes_accessed=4 * early * links * tile * comps, transcendentals=0
        ),
        name="fetch_operands",
    )(*[in_hbm(operand) for operand in operands])
    first_curl, columns_here, coeffs_here, pieces_here, source_here, *others = fetched
    pattern_here = others[0]

    left, right = from_neighbours(coeffs, tile)
    block = jnp.concatenate([left, coeffs_here, right], axis=1)
    copies = jnp.broadcast_to(block[None], (group_size,) + block.shape)
    window = lax.all_to_all(copies, GROUP, 0, 0).reshape(parts, block.shape[1])
    pattern_words = pltpu.SMEM((links, tile_count), jnp.int32)
    projected, halo, later_curl = pl.pallas_call(
        field_kernel,
        out_shape=(
            pltpu.VMEM((tile_count, parts_here, comps), jnp.float32),
            pltpu.VMEM((parts_here, 2 * tile), jnp.float32),
            pltpu.VMEM((tile_count - early,) + curl_tiles.shape[1:], curl_tiles.dtype),
        ),
        in_specs=[vmem] * 7 + [hbm],
        out_specs=(vmem, vmem, vmem),
        scratch_shapes=[
            pattern_words,
            pltpu.SMEM(region_ids.shape, jnp.int32),
            pltpu.SMEM(material_law.shape, jnp.float32),
            pltpu.SMEM((links * tile_count + 1,), jnp.int32),
            pltpu.VMEM((SAMPLES, (tile_count + 2) * tile), jnp.bfloat16),
            pltpu.VMEM((LISTED, 2, parts_here, tile), jnp.float32),
            pltpu.SemaphoreType.DMA((3,)),
            pltpu.SemaphoreType.DMA((pl.cdiv(tile_count - early, CHUNK),)),
        ],
        compiler_params=pltpu.CompilerParams(vmem_limit_bytes=32 * MIB),
        cost_estimate=pl.CostEstimate(
            flops=2 * SAMPLES * tile_count * links * tile * comps,
            bytes_accessed=2 * curl_tiles.size,
            transcendentals=0,
        ),
        name="shard_fields",
    )(
        in_vmem(window),
        *[in_vmem(array) for array in (first_curl, columns_here, pieces_here, *others)],
        in_hbm(curl_tiles),
    )
    if lax.axis_size("space") == 2:
        beside = [across(halo, 0, 1)] * 2
    else:
        beside = [across(halo, 0, -1), across(halo, 0, 1)]
    own = pl.pallas_call(
        sum_kernel,
        out_shape=pltpu.VMEM(source.shape, jnp.float32),
        in_specs=[vmem] * 5,
        out_specs=vmem,
        scratch_shapes=[
            pattern_words,
            pltpu.SemaphoreType.DMA,
        ]
        + [pltpu.VMEM((tile_count + 2, parts_here, tile), jnp.float32)] * links,
        compiler_params=pltpu.CompilerParams(vmem_limit_bytes=32 * MIB),
        cost_estimate=pl.CostEstimate(
            flops=2 * SAMPLES * tile_count * links * tile * comps,
            bytes_accessed=2 * curl_tiles.size,
            transcendentals=0,
        ),
        name="shard_sums",
    )(
        *[in_vmem(a) for a in (projected, first_curl, later_curl, source_here, pattern_here)],
    )
    return pl.pallas_call(
        halo_kernel,
        out_shape=jax.ShapeDtypeStruct(source.shape, jnp.float32),
        in_specs=[vmem] * 3,
        out_specs=vmem,
        compiler_params=pltpu.CompilerParams(vmem_limit_bytes=16 * MIB),
        name="halo_sum",
    )(in_vmem(own), *beside)


def solution(mesh):
    at = mesh.axis_names.index("harm")
    harm = mesh.shape["harm"]
    cores = 2 if harm % 2 == 0 else 1
    sizes = mesh.devices.shape
    split = jax.sharding.Mesh(
        mesh.devices.reshape(sizes[:at] + (harm // cores, cores) + sizes[at + 1 :]),
        mesh.axis_names[:at] + ("chip", "core") + mesh.axis_names[at + 1 :],
    )
    placed = (
        P(GROUP, "space"),
        P("space", None, None, None),
        P("space", None),
        P("space"),
        P(),
        P(GROUP, "space"),
    )
    return jax.shard_map(
        per_device,
        mesh=split,
        in_specs=placed,
        out_specs=P(GROUP, "space"),
        check_vma=False,
    )
```

```python
import math

import jax
import jax.numpy as jnp
import ml_dtypes
import numpy as np
from jax import lax
from jax.experimental import pallas as pl
from jax.experimental.pallas import tpu as pltpu
from jax.sharding import PartitionSpec as P

SAMPLES = 64
HALF = SAMPLES // 2
GROUP = ("chip", "core", "samp")
MIB = 1024 * 1024
LISTED = 4
CHUNK = 4
AHEAD = 3


def half_table(parts):
    sample_ids = np.arange(HALF)[:, None]
    part_ids = np.arange(parts)[None, :]
    phase = ((2 * (part_ids // 2) + 1) * sample_ids % SAMPLES) * (2.0 * math.pi / SAMPLES)
    return np.where(part_ids % 2 == 0, np.cos(phase), np.sin(phase))


def bf16_pieces(table):
    rest = table
    pieces = []
    for _ in range(3):
        piece = rest.astype(ml_dtypes.bfloat16)
        pieces.append(piece)
        rest = rest - piece.astype(np.float64)
    return np.concatenate(pieces, axis=-1)


def across(array, core_step, space_step):
    cores, shards = lax.axis_size("core"), lax.axis_size("space")
    pairs = [
        (c * shards + s, (c + core_step) % cores * shards + (s + space_step) % shards)
        for c in range(cores)
        for s in range(shards)
    ]
    return lax.ppermute(array, ("core", "space"), pairs)


def from_neighbours(array, tile):
    if lax.axis_size("space") == 2:
        other = across(array, 1, 1)
        return other[:, -tile:], other[:, :tile]
    return across(array[:, -tile:], 1, 1), across(array[:, :tile], 1, -1)


def fetch_kernel(*refs):
    count = (len(refs) - 1) // 2
    sources, targets, sems = refs[:count], refs[count : 2 * count], refs[-1]
    rank = lax.axis_index(GROUP)
    sources = (sources[0].at[: targets[0].shape[0]], sources[1].at[rank]) + sources[2:]
    copies = [
        pltpu.make_async_copy(source, target, sems.at[i])
        for i, (source, target) in enumerate(zip(sources, targets))
    ]
    for copy in copies:
        copy.start()
    for copy in copies:
        copy.wait()


def time_samples(pieces, rows):
    stacked = jnp.concatenate([rows] * 3, axis=0)
    samples = jnp.dot(pieces, stacked, preferred_element_type=jnp.float32)
    high = samples.astype(jnp.bfloat16)
    low = (samples - high.astype(jnp.float32)).astype(jnp.bfloat16)
    return jnp.concatenate([high, low], axis=0)


def weighted(projected, blocks):
    return lax.dot_general(
        projected.astype(jnp.bfloat16),
        blocks,
        (((1,), (1,)), ((), ())),
        preferred_element_type=jnp.float32,
    )


def field_kernel(
    window,
    first_curl,
    table,
    pieces,
    pattern_in,
    region_in,
    law_in,
    curl_hbm,
    projected,
    halo,
    later_curl,
    pattern,
    region_ids,
    law,
    outer,
    timed,
    edge_sums,
    small_sems,
    curl_sems,
):
    tile_count, links, tile, comps = curl_hbm.shape
    early = first_curl.shape[0]
    parts_here = halo.shape[0]
    fetched = [(pattern_in, pattern), (region_in, region_ids), (law_in, law)]
    small = [
        pltpu.make_async_copy(src, dst, small_sems.at[i]) for i, (src, dst) in enumerate(fetched)
    ]
    later = {
        elem: pltpu.make_async_copy(
            curl_hbm.at[elem : min(elem + CHUNK, tile_count)],
            later_curl.at[elem - early : min(elem + CHUNK, tile_count) - early],
            curl_sems.at[(elem - early) // CHUNK],
        )
        for elem in range(early, tile_count, CHUNK)
    }
    for copy in small + list(later.values()):
        copy.start()
    edge_sums[...] = jnp.zeros_like(edge_sums)
    own, outer_tiles = pieces[0], pieces[1]
    timed[:, tile:-tile] = time_samples(own, window[:, tile:-tile])
    ends = time_samples(
        outer_tiles, jnp.concatenate([window[:, :tile], window[:, -tile:]], axis=1)
    )
    timed[:, :tile] = ends[:, :tile]
    timed[:, -tile:] = ends[:, tile:]
    columns = [
        jnp.broadcast_to(table[:, part : part + 1], (HALF, comps)) for part in range(parts_here)
    ]
    for copy in small:
        copy.wait()
    places = [[pattern[link, elem] for link in range(links)] for elem in range(tile_count)]
    count = jnp.int32(0)
    for elem in range(tile_count):
        for link, at in enumerate(places[elem]):
            outer[count] = elem * links + link
            count += jnp.where((at == 0) | (at == tile_count + 1), 1, 0)

    def blocks(elem):
        curl = first_curl[elem] if elem < early else later_curl[elem - early]
        return curl.reshape(links * tile, comps)

    def find_density(elem):
        picked = jnp.concatenate(
            [timed[:, pl.ds(pl.multiple_of(at * tile, tile), tile)] for at in places[elem]], axis=1
        )
        split = jnp.dot(picked, blocks(elem), preferred_element_type=jnp.float32)
        return split[:HALF] + split[HALF:]

    def project(elem, density):
        comp = [density[:, c * tile : (c + 1) * tile] for c in range(comps // tile)]
        square = comp[0] * comp[0]
        for c in comp[1:]:
            square = square + c * c
        region = region_ids[elem]
        reluct = law[0, region] + law[2, region] * square / (square + law[1, region])
        field = jnp.concatenate([reluct * c for c in comp], axis=1)
        rows = [jnp.sum(column * field, axis=0, keepdims=True) for column in columns]
        projected[elem] = jnp.concatenate(rows, axis=0) * (4.0 / SAMPLES)

    density = None
    for turn in range(tile_count + 1):
        last = density
        if turn < tile_count:
            if turn in later:
                later[turn].wait()
            density = find_density(turn)
        if turn:
            project(turn - 1, last)

    def add_outer(turn, carry):
        listed, sides, rows, curls = [], [], [], []
        for slot in range(LISTED):
            spot = turn * LISTED + slot
            code = jnp.where(spot < count, outer[jnp.minimum(spot, jnp.maximum(count - 1, 0))], 0)
            elem, link = code // links, code % links
            curls.append(
                jnp.where(
                    elem < early,
                    first_curl[jnp.minimum(elem, early - 1), link],
                    later_curl[jnp.maximum(elem - early, 0), link],
                )
            )
            rows.append(projected[elem])
            sides.append(jnp.where(pattern[link, elem] == 0, 0, 1))
            listed.append(spot < count)
        contrib = weighted(jnp.concatenate(rows, axis=0), jnp.concatenate(curls, axis=0))
        for slot in range(LISTED):
            block = contrib[
                slot * parts_here : (slot + 1) * parts_here, slot * tile : (slot + 1) * tile
            ]
            edge_sums[slot, sides[slot]] += jnp.where(listed[slot], block, 0.0)
        return carry

    add_outer(0, 0)
    lax.fori_loop(1, (count + LISTED - 1) // LISTED, add_outer, 0)
    total = edge_sums[0]
    for slot in range(1, LISTED):
        total = total + edge_sums[slot]
    halo[:, :tile] = total[0]
    halo[:, tile:] = total[1]


def sum_kernel(
    projected,
    first_curl,
    later_curl,
    source,
    pattern_in,
    out,
    pattern,
    small_sem,
    *sums,
):
    links, tile, comps = first_curl.shape[1:]
    early = first_curl.shape[0]
    tile_count = early + later_curl.shape[0]
    small = pltpu.make_async_copy(pattern_in, pattern, small_sem)
    small.start()
    for total in sums:
        total[...] = jnp.zeros_like(total)

    def contribution(elem):
        curl = first_curl[elem] if elem < early else later_curl[elem - early]
        return weighted(projected[elem], curl.reshape(links * tile, comps))

    ahead = [contribution(elem) for elem in range(AHEAD)]
    small.wait()
    for elem in range(tile_count):
        contrib = ahead[elem] if elem < AHEAD else contribution(elem)
        for link in range(links):
            sums[link][pattern[link, elem]] += contrib[:, link * tile : (link + 1) * tile]
    for w in range(tile_count):
        at = slice(w * tile, (w + 1) * tile)
        total = sums[0][w + 1]
        for other in sums[1:]:
            total = total + other[w + 1]
        out[:, at] = total - source[:, at]


def halo_kernel(own, from_right, from_left, out):
    tile = from_left.shape[1] // 2
    out[...] = own[...]
    out[:, :tile] += from_left[:, tile:]
    out[:, -tile:] += from_right[:, :tile]


def per_device(coeffs, curl_tiles, pattern, region_ids, material_law, source):
    parts_here = coeffs.shape[0]
    tile_count, links, tile, comps = curl_tiles.shape
    chips, cores, samp = (lax.axis_size(axis) for axis in GROUP)
    group_size = chips * cores * samp
    parts = parts_here * group_size
    table = half_table(parts)
    before = np.roll(np.arange(parts).reshape(chips, cores, -1), 1, axis=1).reshape(-1)
    pieces = jnp.asarray(np.stack([bf16_pieces(table), bf16_pieces(table[:, before])]))
    own_columns = jnp.asarray(
        table.reshape(HALF, group_size, parts_here).transpose(1, 0, 2).astype(np.float32)
    )
    vmem, hbm = pl.BlockSpec(memory_space=pltpu.VMEM), pl.BlockSpec(memory_space=pltpu.HBM)

    def in_vmem(array):
        return pltpu.with_memory_space_constraint(array, pltpu.VMEM)

    def in_hbm(array):
        return pltpu.with_memory_space_constraint(array, pltpu.HBM)

    early = tile_count // 2
    operands = [
        curl_tiles,
        own_columns,
        coeffs,
        pieces,
        source,
        pattern.T,
        region_ids,
        material_law,
    ]
    shapes = [
        (early,) + curl_tiles.shape[1:],
        own_columns.shape[1:],
    ] + [operand.shape for operand in operands[2:]]
    fetched = pl.pallas_call(
        fetch_kernel,
        out_shape=[pltpu.VMEM(shape, o.dtype) for shape, o in zip(shapes, operands)],
        in_specs=[hbm] * len(operands),
        out_specs=[vmem] * len(operands),
        scratch_shapes=[pltpu.SemaphoreType.DMA((len(operands),))],
        compiler_params=pltpu.CompilerParams(vmem_limit_bytes=16 * MIB),
        cost_estimate=pl.CostEstimate(
            flops=0, bytes_accessed=4 * early * links * tile * comps, transcendentals=0
        ),
        name="fetch_operands",
    )(*[in_hbm(operand) for operand in operands])
    first_curl, columns_here, coeffs_here, pieces_here, source_here, *others = fetched
    pattern_here = others[0]

    left, right = from_neighbours(coeffs, tile)
    block = jnp.concatenate([left, coeffs_here, right], axis=1)
    copies = jnp.broadcast_to(block[None], (group_size,) + block.shape)
    window = lax.all_to_all(copies, GROUP, 0, 0).reshape(parts, block.shape[1])
    pattern_words = pltpu.SMEM((links, tile_count), jnp.int32)
    projected, halo, later_curl = pl.pallas_call(
        field_kernel,
        out_shape=(
            pltpu.VMEM((tile_count, parts_here, comps), jnp.float32),
            pltpu.VMEM((parts_here, 2 * tile), jnp.float32),
            pltpu.VMEM((tile_count - early,) + curl_tiles.shape[1:], curl_tiles.dtype),
        ),
        in_specs=[vmem] * 7 + [hbm],
        out_specs=(vmem, vmem, vmem),
        scratch_shapes=[
            pattern_words,
            pltpu.SMEM(region_ids.shape, jnp.int32),
            pltpu.SMEM(material_law.shape, jnp.float32),
            pltpu.SMEM((links * tile_count + 1,), jnp.int32),
            pltpu.VMEM((SAMPLES, (tile_count + 2) * tile), jnp.bfloat16),
            pltpu.VMEM((LISTED, 2, parts_here, tile), jnp.float32),
            pltpu.SemaphoreType.DMA((3,)),
            pltpu.SemaphoreType.DMA((pl.cdiv(tile_count - early, CHUNK),)),
        ],
        compiler_params=pltpu.CompilerParams(vmem_limit_bytes=32 * MIB),
        cost_estimate=pl.CostEstimate(
            flops=2 * SAMPLES * tile_count * links * tile * comps,
            bytes_accessed=2 * curl_tiles.size,
            transcendentals=0,
        ),
        name="shard_fields",
    )(
        in_vmem(window),
        *[in_vmem(array) for array in (first_curl, columns_here, pieces_here, *others)],
        in_hbm(curl_tiles),
    )
    if lax.axis_size("space") == 2:
        beside = [across(halo, 0, 1)] * 2
    else:
        beside = [across(halo, 0, -1), across(halo, 0, 1)]
    own = pl.pallas_call(
        sum_kernel,
        out_shape=pltpu.VMEM(source.shape, jnp.float32),
        in_specs=[vmem] * 5,
        out_specs=vmem,
        scratch_shapes=[
            pattern_words,
            pltpu.SemaphoreType.DMA,
        ]
        + [pltpu.VMEM((tile_count + 2, parts_here, tile), jnp.float32)] * links,
        compiler_params=pltpu.CompilerParams(vmem_limit_bytes=32 * MIB),
        cost_estimate=pl.CostEstimate(
            flops=2 * SAMPLES * tile_count * links * tile * comps,
            bytes_accessed=2 * curl_tiles.size,
            transcendentals=0,
        ),
        name="shard_sums",
    )(
        *[in_vmem(a) for a in (projected, first_curl, later_curl, source_here, pattern_here)],
    )
    return pl.pallas_call(
        halo_kernel,
        out_shape=jax.ShapeDtypeStruct(source.shape, jnp.float32),
        in_specs=[vmem] * 3,
        out_specs=vmem,
        compiler_params=pltpu.CompilerParams(vmem_limit_bytes=16 * MIB),
        name="halo_sum",
    )(in_vmem(own), *beside)


def solution(mesh):
    at = mesh.axis_names.index("harm")
    harm = mesh.shape["harm"]
    cores = 2 if harm % 2 == 0 else 1
    sizes = mesh.devices.shape
    split = jax.sharding.Mesh(
        mesh.devices.reshape(sizes[:at] + (harm // cores, cores) + sizes[at + 1 :]),
        mesh.axis_names[:at] + ("chip", "core") + mesh.axis_names[at + 1 :],
    )
    placed = (
        P(GROUP, "space"),
        P("space", None, None, None),
        P("space", None),
        P("space"),
        P(),
        P(GROUP, "space"),
    )
    return jax.shard_map(
        per_device,
        mesh=split,
        in_specs=placed,
        out_specs=P(GROUP, "space"),
        check_vma=False,
    )
```

```python
import math

import jax
import jax.numpy as jnp
import ml_dtypes
import numpy as np
from jax import lax
from jax.experimental import pallas as pl
from jax.experimental.pallas import tpu as pltpu
from jax.sharding import PartitionSpec as P

SAMPLES = 64
HALF = SAMPLES // 2
GROUP = ("chip", "core", "samp")
MIB = 1024 * 1024
LISTED = 4
CHUNK = 5
AHEAD = 3


def half_table(parts):
    sample_ids = np.arange(HALF)[:, None]
    part_ids = np.arange(parts)[None, :]
    phase = ((2 * (part_ids // 2) + 1) * sample_ids % SAMPLES) * (2.0 * math.pi / SAMPLES)
    return np.where(part_ids % 2 == 0, np.cos(phase), np.sin(phase))


def bf16_pieces(table):
    rest = table
    pieces = []
    for _ in range(3):
        piece = rest.astype(ml_dtypes.bfloat16)
        pieces.append(piece)
        rest = rest - piece.astype(np.float64)
    return np.concatenate(pieces, axis=-1)


def across(array, core_step, space_step):
    cores, shards = lax.axis_size("core"), lax.axis_size("space")
    pairs = [
        (c * shards + s, (c + core_step) % cores * shards + (s + space_step) % shards)
        for c in range(cores)
        for s in range(shards)
    ]
    return lax.ppermute(array, ("core", "space"), pairs)


def from_neighbours(array, tile):
    if lax.axis_size("space") == 2:
        other = across(array, 1, 1)
        return other[:, -tile:], other[:, :tile]
    return across(array[:, -tile:], 1, 1), across(array[:, :tile], 1, -1)


def fetch_kernel(*refs):
    count = (len(refs) - 1) // 2
    sources, targets, sems = refs[:count], refs[count : 2 * count], refs[-1]
    rank = lax.axis_index(GROUP)
    sources = (sources[0].at[: targets[0].shape[0]], sources[1].at[rank]) + sources[2:]
    copies = [
        pltpu.make_async_copy(source, target, sems.at[i])
        for i, (source, target) in enumerate(zip(sources, targets))
    ]
    for copy in copies:
        copy.start()
    for copy in copies:
        copy.wait()


def time_samples(pieces, rows):
    stacked = jnp.concatenate([rows] * 3, axis=0)
    samples = jnp.dot(pieces, stacked, preferred_element_type=jnp.float32)
    high = samples.astype(jnp.bfloat16)
    low = (samples - high.astype(jnp.float32)).astype(jnp.bfloat16)
    return jnp.concatenate([high, low], axis=0)


def weighted(projected, blocks):
    return lax.dot_general(
        projected.astype(jnp.bfloat16),
        blocks,
        (((1,), (1,)), ((), ())),
        preferred_element_type=jnp.float32,
    )


def field_kernel(
    window,
    first_curl,
    table,
    pieces,
    pattern_in,
    region_in,
    law_in,
    curl_hbm,
    projected,
    halo,
    later_curl,
    pattern,
    region_ids,
    law,
    outer,
    timed,
    edge_sums,
    small_sems,
    curl_sems,
):
    tile_count, links, tile, comps = curl_hbm.shape
    early = first_curl.shape[0]
    parts_here = halo.shape[0]
    fetched = [(pattern_in, pattern), (region_in, region_ids), (law_in, law)]
    small = [
        pltpu.make_async_copy(src, dst, small_sems.at[i]) for i, (src, dst) in enumerate(fetched)
    ]
    later = {
        elem: pltpu.make_async_copy(
            curl_hbm.at[elem : min(elem + CHUNK, tile_count)],
            later_curl.at[elem - early : min(elem + CHUNK, tile_count) - early],
            curl_sems.at[(elem - early) // CHUNK],
        )
        for elem in range(early, tile_count, CHUNK)
    }
    for copy in small + list(later.values()):
        copy.start()
    edge_sums[...] = jnp.zeros_like(edge_sums)
    own, outer_tiles = pieces[0], pieces[1]
    timed[:, tile:-tile] = time_samples(own, window[:, tile:-tile])
    ends = time_samples(
        outer_tiles, jnp.concatenate([window[:, :tile], window[:, -tile:]], axis=1)
    )
    timed[:, :tile] = ends[:, :tile]
    timed[:, -tile:] = ends[:, tile:]
    columns = [
        jnp.broadcast_to(table[:, part : part + 1], (HALF, comps)) for part in range(parts_here)
    ]
    for copy in small:
        copy.wait()
    places = [[pattern[link, elem] for link in range(links)] for elem in range(tile_count)]
    count = jnp.int32(0)
    for elem in range(tile_count):
        for link, at in enumerate(places[elem]):
            outer[count] = elem * links + link
            count += jnp.where((at == 0) | (at == tile_count + 1), 1, 0)

    def blocks(elem):
        curl = first_curl[elem] if elem < early else later_curl[elem - early]
        return curl.reshape(links * tile, comps)

    def find_density(elem):
        picked = jnp.concatenate(
            [timed[:, pl.ds(pl.multiple_of(at * tile, tile), tile)] for at in places[elem]], axis=1
        )
        split = jnp.dot(picked, blocks(elem), preferred_element_type=jnp.float32)
        return split[:HALF] + split[HALF:]

    def project(elem, density):
        comp = [density[:, c * tile : (c + 1) * tile] for c in range(comps // tile)]
        square = comp[0] * comp[0]
        for c in comp[1:]:
            square = square + c * c
        region = region_ids[elem]
        reluct = law[0, region] + law[2, region] * square / (square + law[1, region])
        field = jnp.concatenate([reluct * c for c in comp], axis=1)
        rows = [jnp.sum(column * field, axis=0, keepdims=True) for column in columns]
        projected[elem] = jnp.concatenate(rows, axis=0) * (4.0 / SAMPLES)

    density = None
    for turn in range(tile_count + 1):
        last = density
        if turn < tile_count:
            if turn in later:
                later[turn].wait()
            density = find_density(turn)
        if turn:
            project(turn - 1, last)

    def add_outer(turn, carry):
        listed, sides, rows, curls = [], [], [], []
        for slot in range(LISTED):
            spot = turn * LISTED + slot
            code = jnp.where(spot < count, outer[jnp.minimum(spot, jnp.maximum(count - 1, 0))], 0)
            elem, link = code // links, code % links
            curls.append(
                jnp.where(
                    elem < early,
                    first_curl[jnp.minimum(elem, early - 1), link],
                    later_curl[jnp.maximum(elem - early, 0), link],
                )
            )
            rows.append(projected[elem])
            sides.append(jnp.where(pattern[link, elem] == 0, 0, 1))
            listed.append(spot < count)
        contrib = weighted(jnp.concatenate(rows, axis=0), jnp.concatenate(curls, axis=0))
        for slot in range(LISTED):
            block = contrib[
                slot * parts_here : (slot + 1) * parts_here, slot * tile : (slot + 1) * tile
            ]
            edge_sums[slot, sides[slot]] += jnp.where(listed[slot], block, 0.0)
        return carry

    add_outer(0, 0)
    lax.fori_loop(1, (count + LISTED - 1) // LISTED, add_outer, 0)
    total = edge_sums[0]
    for slot in range(1, LISTED):
        total = total + edge_sums[slot]
    halo[:, :tile] = total[0]
    halo[:, tile:] = total[1]


def sum_kernel(
    projected,
    first_curl,
    later_curl,
    source,
    pattern_in,
    out,
    pattern,
    small_sem,
    *sums,
):
    links, tile, comps = first_curl.shape[1:]
    early = first_curl.shape[0]
    tile_count = early + later_curl.shape[0]
    small = pltpu.make_async_copy(pattern_in, pattern, small_sem)
    small.start()
    for total in sums:
        total[...] = jnp.zeros_like(total)

    def contribution(elem):
        curl = first_curl[elem] if elem < early else later_curl[elem - early]
        return weighted(projected[elem], curl.reshape(links * tile, comps))

    ahead = [contribution(elem) for elem in range(AHEAD)]
    small.wait()
    for elem in range(tile_count):
        contrib = ahead[elem] if elem < AHEAD else contribution(elem)
        for link in range(links):
            sums[link][pattern[link, elem]] += contrib[:, link * tile : (link + 1) * tile]
    for w in range(tile_count):
        at = slice(w * tile, (w + 1) * tile)
        total = sums[0][w + 1]
        for other in sums[1:]:
            total = total + other[w + 1]
        out[:, at] = total - source[:, at]


def halo_kernel(own, from_right, from_left, out):
    tile = from_left.shape[1] // 2
    out[...] = own[...]
    out[:, :tile] += from_left[:, tile:]
    out[:, -tile:] += from_right[:, :tile]


def per_device(coeffs, curl_tiles, pattern, region_ids, material_law, source):
    parts_here = coeffs.shape[0]
    tile_count, links, tile, comps = curl_tiles.shape
    chips, cores, samp = (lax.axis_size(axis) for axis in GROUP)
    group_size = chips * cores * samp
    parts = parts_here * group_size
    table = half_table(parts)
    before = np.roll(np.arange(parts).reshape(chips, cores, -1), 1, axis=1).reshape(-1)
    pieces = jnp.asarray(np.stack([bf16_pieces(table), bf16_pieces(table[:, before])]))
    own_columns = jnp.asarray(
        table.reshape(HALF, group_size, parts_here).transpose(1, 0, 2).astype(np.float32)
    )
    vmem, hbm = pl.BlockSpec(memory_space=pltpu.VMEM), pl.BlockSpec(memory_space=pltpu.HBM)

    def in_vmem(array):
        return pltpu.with_memory_space_constraint(array, pltpu.VMEM)

    def in_hbm(array):
        return pltpu.with_memory_space_constraint(array, pltpu.HBM)

    early = tile_count // 2
    operands = [
        curl_tiles,
        own_columns,
        coeffs,
        pieces,
        source,
        pattern.T,
        region_ids,
        material_law,
    ]
    shapes = [
        (early,) + curl_tiles.shape[1:],
        own_columns.shape[1:],
    ] + [operand.shape for operand in operands[2:]]
    fetched = pl.pallas_call(
        fetch_kernel,
        out_shape=[pltpu.VMEM(shape, o.dtype) for shape, o in zip(shapes, operands)],
        in_specs=[hbm] * len(operands),
        out_specs=[vmem] * len(operands),
        scratch_shapes=[pltpu.SemaphoreType.DMA((len(operands),))],
        compiler_params=pltpu.CompilerParams(vmem_limit_bytes=16 * MIB),
        cost_estimate=pl.CostEstimate(
            flops=0, bytes_accessed=4 * early * links * tile * comps, transcendentals=0
        ),
        name="fetch_operands",
    )(*[in_hbm(operand) for operand in operands])
    first_curl, columns_here, coeffs_here, pieces_here, source_here, *others = fetched
    pattern_here = others[0]

    left, right = from_neighbours(coeffs, tile)
    block = jnp.concatenate([left, coeffs_here, right], axis=1)
    copies = jnp.broadcast_to(block[None], (group_size,) + block.shape)
    window = lax.all_to_all(copies, GROUP, 0, 0).reshape(parts, block.shape[1])
    pattern_words = pltpu.SMEM((links, tile_count), jnp.int32)
    projected, halo, later_curl = pl.pallas_call(
        field_kernel,
        out_shape=(
            pltpu.VMEM((tile_count, parts_here, comps), jnp.float32),
            pltpu.VMEM((parts_here, 2 * tile), jnp.float32),
            pltpu.VMEM((tile_count - early,) + curl_tiles.shape[1:], curl_tiles.dtype),
        ),
        in_specs=[vmem] * 7 + [hbm],
        out_specs=(vmem, vmem, vmem),
        scratch_shapes=[
            pattern_words,
            pltpu.SMEM(region_ids.shape, jnp.int32),
            pltpu.SMEM(material_law.shape, jnp.float32),
            pltpu.SMEM((links * tile_count + 1,), jnp.int32),
            pltpu.VMEM((SAMPLES, (tile_count + 2) * tile), jnp.bfloat16),
            pltpu.VMEM((LISTED, 2, parts_here, tile), jnp.float32),
            pltpu.SemaphoreType.DMA((3,)),
            pltpu.SemaphoreType.DMA((pl.cdiv(tile_count - early, CHUNK),)),
        ],
        compiler_params=pltpu.CompilerParams(vmem_limit_bytes=32 * MIB),
        cost_estimate=pl.CostEstimate(
            flops=2 * SAMPLES * tile_count * links * tile * comps,
            bytes_accessed=2 * curl_tiles.size,
            transcendentals=0,
        ),
        name="shard_fields",
    )(
        in_vmem(window),
        *[in_vmem(array) for array in (first_curl, columns_here, pieces_here, *others)],
        in_hbm(curl_tiles),
    )
    if lax.axis_size("space") == 2:
        beside = [across(halo, 0, 1)] * 2
    else:
        beside = [across(halo, 0, -1), across(halo, 0, 1)]
    own = pl.pallas_call(
        sum_kernel,
        out_shape=pltpu.VMEM(source.shape, jnp.float32),
        in_specs=[vmem] * 5,
        out_specs=vmem,
        scratch_shapes=[
            pattern_words,
            pltpu.SemaphoreType.DMA,
        ]
        + [pltpu.VMEM((tile_count + 2, parts_here, tile), jnp.float32)] * links,
        compiler_params=pltpu.CompilerParams(vmem_limit_bytes=32 * MIB),
        cost_estimate=pl.CostEstimate(
            flops=2 * SAMPLES * tile_count * links * tile * comps,
            bytes_accessed=2 * curl_tiles.size,
            transcendentals=0,
        ),
        name="shard_sums",
    )(
        *[in_vmem(a) for a in (projected, first_curl, later_curl, source_here, pattern_here)],
    )
    return pl.pallas_call(
        halo_kernel,
        out_shape=jax.ShapeDtypeStruct(source.shape, jnp.float32),
        in_specs=[vmem] * 3,
        out_specs=vmem,
        compiler_params=pltpu.CompilerParams(vmem_limit_bytes=16 * MIB),
        name="halo_sum",
    )(in_vmem(own), *beside)


def solution(mesh):
    at = mesh.axis_names.index("harm")
    harm = mesh.shape["harm"]
    cores = 2 if harm % 2 == 0 else 1
    sizes = mesh.devices.shape
    split = jax.sharding.Mesh(
        mesh.devices.reshape(sizes[:at] + (harm // cores, cores) + sizes[at + 1 :]),
        mesh.axis_names[:at] + ("chip", "core") + mesh.axis_names[at + 1 :],
    )
    placed = (
        P(GROUP, "space"),
        P("space", None, None, None),
        P("space", None),
        P("space"),
        P(),
        P(GROUP, "space"),
    )
    return jax.shard_map(
        per_device,
        mesh=split,
        in_specs=placed,
        out_specs=P(GROUP, "space"),
        check_vma=False,
    )
```

```python
import math

import jax
import jax.numpy as jnp
import ml_dtypes
import numpy as np
from jax import lax
from jax.experimental import pallas as pl
from jax.experimental.pallas import tpu as pltpu
from jax.sharding import PartitionSpec as P

SAMPLES = 64
HALF = SAMPLES // 2
GROUP = ("chip", "core", "samp")
MIB = 1024 * 1024
LISTED = 4
FIRST = 3
AHEAD = 3


def half_table(parts):
    sample_ids = np.arange(HALF)[:, None]
    part_ids = np.arange(parts)[None, :]
    phase = ((2 * (part_ids // 2) + 1) * sample_ids % SAMPLES) * (2.0 * math.pi / SAMPLES)
    return np.where(part_ids % 2 == 0, np.cos(phase), np.sin(phase))


def bf16_pieces(table):
    rest = table
    pieces = []
    for _ in range(3):
        piece = rest.astype(ml_dtypes.bfloat16)
        pieces.append(piece)
        rest = rest - piece.astype(np.float64)
    return np.concatenate(pieces, axis=-1)


def across(array, core_step, space_step):
    cores, shards = lax.axis_size("core"), lax.axis_size("space")
    pairs = [
        (c * shards + s, (c + core_step) % cores * shards + (s + space_step) % shards)
        for c in range(cores)
        for s in range(shards)
    ]
    return lax.ppermute(array, ("core", "space"), pairs)


def from_neighbours(array, tile):
    if lax.axis_size("space") == 2:
        other = across(array, 1, 1)
        return other[:, -tile:], other[:, :tile]
    return across(array[:, -tile:], 1, 1), across(array[:, :tile], 1, -1)


def fetch_kernel(*refs):
    count = (len(refs) - 1) // 2
    sources, targets, sems = refs[:count], refs[count : 2 * count], refs[-1]
    rank = lax.axis_index(GROUP)
    sources = (sources[0].at[: targets[0].shape[0]], sources[1].at[rank]) + sources[2:]
    copies = [
        pltpu.make_async_copy(source, target, sems.at[i])
        for i, (source, target) in enumerate(zip(sources, targets))
    ]
    for copy in copies:
        copy.start()
    for copy in copies:
        copy.wait()


def time_samples(pieces, rows):
    stacked = jnp.concatenate([rows] * 3, axis=0)
    samples = jnp.dot(pieces, stacked, preferred_element_type=jnp.float32)
    high = samples.astype(jnp.bfloat16)
    low = (samples - high.astype(jnp.float32)).astype(jnp.bfloat16)
    return jnp.concatenate([high, low], axis=0)


def weighted(projected, blocks):
    return lax.dot_general(
        projected.astype(jnp.bfloat16),
        blocks,
        (((1,), (1,)), ((), ())),
        preferred_element_type=jnp.float32,
    )


def field_kernel(
    window,
    first_curl,
    table,
    pieces,
    pattern_in,
    region_in,
    law_in,
    curl_hbm,
    projected,
    halo,
    later_curl,
    pattern,
    region_ids,
    law,
    outer,
    timed,
    densities,
    edge_sums,
    small_sems,
    curl_sems,
):
    tile_count, links, tile, comps = curl_hbm.shape
    early = first_curl.shape[0]
    parts_here = halo.shape[0]
    fetched = [(pattern_in, pattern), (region_in, region_ids), (law_in, law)]
    small = [
        pltpu.make_async_copy(src, dst, small_sems.at[i]) for i, (src, dst) in enumerate(fetched)
    ]
    middle = early + FIRST
    later = {
        at: pltpu.make_async_copy(
            curl_hbm.at[at:end], later_curl.at[at - early : end - early], curl_sems.at[i]
        )
        for i, (at, end) in enumerate([(early, middle), (middle, tile_count)])
    }
    for copy in small + list(later.values()):
        copy.start()
    edge_sums[...] = jnp.zeros_like(edge_sums)
    own, outer_tiles = pieces[0], pieces[1]
    timed[:, tile:-tile] = time_samples(own, window[:, tile:-tile])
    timed[:, :tile] = time_samples(outer_tiles, window[:, :tile])
    timed[:, -tile:] = time_samples(outer_tiles, window[:, -tile:])
    columns = [
        jnp.broadcast_to(table[:, part : part + 1], (HALF, comps)) for part in range(parts_here)
    ]
    for copy in small:
        copy.wait()
    places = [[pattern[link, elem] for link in range(links)] for elem in range(tile_count)]
    count = jnp.int32(0)
    for elem in range(tile_count):
        for link, at in enumerate(places[elem]):
            outer[count] = elem * links + link
            count += jnp.where((at == 0) | (at == tile_count + 1), 1, 0)

    def blocks(elem):
        curl = first_curl[elem] if elem < early else later_curl[elem - early]
        return curl.reshape(links * tile, comps)

    def find_density(elem):
        picked = jnp.concatenate(
            [timed[:, pl.ds(pl.multiple_of(at * tile, tile), tile)] for at in places[elem]], axis=1
        )
        split = jnp.dot(picked, blocks(elem), preferred_element_type=jnp.float32)
        densities[elem] = split[:HALF] + split[HALF:]

    def project(elem):
        density = densities[elem]
        comp = [density[:, c * tile : (c + 1) * tile] for c in range(comps // tile)]
        square = comp[0] * comp[0]
        for c in comp[1:]:
            square = square + c * c
        region = region_ids[elem]
        reluct = law[0, region] + law[2, region] * square / (square + law[1, region])
        field = jnp.concatenate([reluct * c for c in comp], axis=1)
        rows = [jnp.sum(column * field, axis=0, keepdims=True) for column in columns]
        projected[elem] = jnp.concatenate(rows, axis=0) * (4.0 / SAMPLES)

    for turn in range(tile_count + 1):
        if turn < tile_count:
            if turn in later:
                later[turn].wait()
            find_density(turn)
        if turn:
            project(turn - 1)

    def add_outer(turn, carry):
        listed, sides, rows, curls = [], [], [], []
        for slot in range(LISTED):
            spot = turn * LISTED + slot
            code = jnp.where(spot < count, outer[jnp.minimum(spot, jnp.maximum(count - 1, 0))], 0)
            elem, link = code // links, code % links
            curls.append(
                jnp.where(
                    elem < early,
                    first_curl[jnp.minimum(elem, early - 1), link],
                    later_curl[jnp.maximum(elem - early, 0), link],
                )
            )
            rows.append(projected[elem])
            sides.append(jnp.where(pattern[link, elem] == 0, 0, 1))
            listed.append(spot < count)
        contrib = weighted(jnp.concatenate(rows, axis=0), jnp.concatenate(curls, axis=0))
        for slot in range(LISTED):
            block = contrib[
                slot * parts_here : (slot + 1) * parts_here, slot * tile : (slot + 1) * tile
            ]
            edge_sums[slot, sides[slot]] += jnp.where(listed[slot], block, 0.0)
        return carry

    add_outer(0, 0)
    lax.fori_loop(1, (count + LISTED - 1) // LISTED, add_outer, 0)
    total = edge_sums[0]
    for slot in range(1, LISTED):
        total = total + edge_sums[slot]
    halo[:, :tile] = total[0]
    halo[:, tile:] = total[1]


def sum_kernel(
    projected,
    first_curl,
    later_curl,
    source,
    pattern_in,
    out,
    pattern,
    small_sem,
    *sums,
):
    links, tile, comps = first_curl.shape[1:]
    early = first_curl.shape[0]
    tile_count = early + later_curl.shape[0]
    small = pltpu.make_async_copy(pattern_in, pattern, small_sem)
    small.start()
    for total in sums:
        total[...] = jnp.zeros_like(total)

    def contribution(elem):
        curl = first_curl[elem] if elem < early else later_curl[elem - early]
        return weighted(projected[elem], curl.reshape(links * tile, comps))

    ahead = [contribution(elem) for elem in range(AHEAD)]
    small.wait()
    for elem in range(tile_count):
        contrib = ahead[elem] if elem < AHEAD else contribution(elem)
        for link in range(links):
            sums[link][pattern[link, elem]] += contrib[:, link * tile : (link + 1) * tile]
    for w in range(tile_count):
        at = slice(w * tile, (w + 1) * tile)
        total = sums[0][w + 1]
        for other in sums[1:]:
            total = total + other[w + 1]
        out[:, at] = total - source[:, at]


def halo_kernel(own, from_right, from_left, out):
    tile = from_left.shape[1] // 2
    out[...] = own[...]
    out[:, :tile] += from_left[:, tile:]
    out[:, -tile:] += from_right[:, :tile]


def per_device(coeffs, curl_tiles, pattern, region_ids, material_law, source):
    parts_here = coeffs.shape[0]
    tile_count, links, tile, comps = curl_tiles.shape
    chips, cores, samp = (lax.axis_size(axis) for axis in GROUP)
    group_size = chips * cores * samp
    parts = parts_here * group_size
    table = half_table(parts)
    before = np.roll(np.arange(parts).reshape(chips, cores, -1), 1, axis=1).reshape(-1)
    pieces = jnp.asarray(np.stack([bf16_pieces(table), bf16_pieces(table[:, before])]))
    own_columns = jnp.asarray(
        table.reshape(HALF, group_size, parts_here).transpose(1, 0, 2).astype(np.float32)
    )
    vmem, hbm = pl.BlockSpec(memory_space=pltpu.VMEM), pl.BlockSpec(memory_space=pltpu.HBM)

    def in_vmem(array):
        return pltpu.with_memory_space_constraint(array, pltpu.VMEM)

    def in_hbm(array):
        return pltpu.with_memory_space_constraint(array, pltpu.HBM)

    early = tile_count // 2
    operands = [
        curl_tiles,
        own_columns,
        coeffs,
        pieces,
        source,
        pattern.T,
        region_ids,
        material_law,
    ]
    shapes = [
        (early,) + curl_tiles.shape[1:],
        own_columns.shape[1:],
    ] + [operand.shape for operand in operands[2:]]
    fetched = pl.pallas_call(
        fetch_kernel,
        out_shape=[pltpu.VMEM(shape, o.dtype) for shape, o in zip(shapes, operands)],
        in_specs=[hbm] * len(operands),
        out_specs=[vmem] * len(operands),
        scratch_shapes=[pltpu.SemaphoreType.DMA((len(operands),))],
        compiler_params=pltpu.CompilerParams(vmem_limit_bytes=16 * MIB),
        cost_estimate=pl.CostEstimate(
            flops=0, bytes_accessed=4 * early * links * tile * comps, transcendentals=0
        ),
        name="fetch_operands",
    )(*[in_hbm(operand) for operand in operands])
    first_curl, columns_here, coeffs_here, pieces_here, source_here, *others = fetched
    pattern_here = others[0]

    left, right = from_neighbours(coeffs, tile)
    block = jnp.concatenate([left, coeffs_here, right], axis=1)
    copies = jnp.broadcast_to(block[None], (group_size,) + block.shape)
    window = lax.all_to_all(copies, GROUP, 0, 0).reshape(parts, block.shape[1])
    pattern_words = pltpu.SMEM((links, tile_count), jnp.int32)
    projected, halo, later_curl = pl.pallas_call(
        field_kernel,
        out_shape=(
            pltpu.VMEM((tile_count, parts_here, comps), jnp.float32),
            pltpu.VMEM((parts_here, 2 * tile), jnp.float32),
            pltpu.VMEM((tile_count - early,) + curl_tiles.shape[1:], curl_tiles.dtype),
        ),
        in_specs=[vmem] * 7 + [hbm],
        out_specs=(vmem, vmem, vmem),
        scratch_shapes=[
            pattern_words,
            pltpu.SMEM(region_ids.shape, jnp.int32),
            pltpu.SMEM(material_law.shape, jnp.float32),
            pltpu.SMEM((links * tile_count + 1,), jnp.int32),
            pltpu.VMEM((SAMPLES, (tile_count + 2) * tile), jnp.bfloat16),
            pltpu.VMEM((tile_count, HALF, comps), jnp.float32),
            pltpu.VMEM((LISTED, 2, parts_here, tile), jnp.float32),
            pltpu.SemaphoreType.DMA((3,)),
            pltpu.SemaphoreType.DMA((2,)),
        ],
        compiler_params=pltpu.CompilerParams(vmem_limit_bytes=32 * MIB),
        cost_estimate=pl.CostEstimate(
            flops=2 * SAMPLES * tile_count * links * tile * comps,
            bytes_accessed=2 * curl_tiles.size,
            transcendentals=0,
        ),
        name="shard_fields",
    )(
        in_vmem(window),
        *[in_vmem(array) for array in (first_curl, columns_here, pieces_here, *others)],
        in_hbm(curl_tiles),
    )
    if lax.axis_size("space") == 2:
        beside = [across(halo, 0, 1)] * 2
    else:
        beside = [across(halo, 0, -1), across(halo, 0, 1)]
    own = pl.pallas_call(
        sum_kernel,
        out_shape=pltpu.VMEM(source.shape, jnp.float32),
        in_specs=[vmem] * 5,
        out_specs=vmem,
        scratch_shapes=[
            pattern_words,
            pltpu.SemaphoreType.DMA,
        ]
        + [pltpu.VMEM((tile_count + 2, parts_here, tile), jnp.float32)] * links,
        compiler_params=pltpu.CompilerParams(vmem_limit_bytes=32 * MIB),
        cost_estimate=pl.CostEstimate(
            flops=2 * SAMPLES * tile_count * links * tile * comps,
            bytes_accessed=2 * curl_tiles.size,
            transcendentals=0,
        ),
        name="shard_sums",
    )(
        *[in_vmem(a) for a in (projected, first_curl, later_curl, source_here, pattern_here)],
    )
    return pl.pallas_call(
        halo_kernel,
        out_shape=jax.ShapeDtypeStruct(source.shape, jnp.float32),
        in_specs=[vmem] * 3,
        out_specs=vmem,
        compiler_params=pltpu.CompilerParams(vmem_limit_bytes=16 * MIB),
        name="halo_sum",
    )(in_vmem(own), *beside)


def solution(mesh):
    at = mesh.axis_names.index("harm")
    harm = mesh.shape["harm"]
    cores = 2 if harm % 2 == 0 else 1
    sizes = mesh.devices.shape
    split = jax.sharding.Mesh(
        mesh.devices.reshape(sizes[:at] + (harm // cores, cores) + sizes[at + 1 :]),
        mesh.axis_names[:at] + ("chip", "core") + mesh.axis_names[at + 1 :],
    )
    placed = (
        P(GROUP, "space"),
        P("space", None, None, None),
        P("space", None),
        P("space"),
        P(),
        P(GROUP, "space"),
    )
    return jax.shard_map(
        per_device,
        mesh=split,
        in_specs=placed,
        out_specs=P(GROUP, "space"),
        check_vma=False,
    )
```

```python
import math

import jax
import jax.numpy as jnp
import ml_dtypes
import numpy as np
from jax import lax
from jax.experimental import pallas as pl
from jax.experimental.pallas import tpu as pltpu
from jax.sharding import PartitionSpec as P

SAMPLES = 64
HALF = SAMPLES // 2
GROUP = ("chip", "core", "samp")
MIB = 1024 * 1024
LISTED = 4
CHUNK = 4
AHEAD = 3


def half_table(parts):
    sample_ids = np.arange(HALF)[:, None]
    part_ids = np.arange(parts)[None, :]
    phase = ((2 * (part_ids // 2) + 1) * sample_ids % SAMPLES) * (2.0 * math.pi / SAMPLES)
    return np.where(part_ids % 2 == 0, np.cos(phase), np.sin(phase))


def bf16_pieces(table):
    rest = table
    pieces = []
    for _ in range(3):
        piece = rest.astype(ml_dtypes.bfloat16)
        pieces.append(piece)
        rest = rest - piece.astype(np.float64)
    return np.concatenate(pieces, axis=-1)


def across(array, core_step, space_step):
    cores, shards = lax.axis_size("core"), lax.axis_size("space")
    pairs = [
        (c * shards + s, (c + core_step) % cores * shards + (s + space_step) % shards)
        for c in range(cores)
        for s in range(shards)
    ]
    return lax.ppermute(array, ("core", "space"), pairs)


def from_neighbours(array, tile):
    if lax.axis_size("space") == 2:
        other = across(array, 1, 1)
        return other[:, -tile:], other[:, :tile]
    return across(array[:, -tile:], 1, 1), across(array[:, :tile], 1, -1)


def fetch_kernel(*refs):
    count = (len(refs) - 1) // 2
    sources, targets, sems = refs[:count], refs[count : 2 * count], refs[-1]
    rank = lax.axis_index(GROUP)
    sources = (sources[0].at[: targets[0].shape[0]], sources[1].at[rank]) + sources[2:]
    copies = [
        pltpu.make_async_copy(source, target, sems.at[i])
        for i, (source, target) in enumerate(zip(sources, targets))
    ]
    for copy in copies:
        copy.start()
    for copy in copies:
        copy.wait()


def time_samples(pieces, rows):
    stacked = jnp.concatenate([rows] * 3, axis=0)
    samples = jnp.dot(pieces, stacked, preferred_element_type=jnp.float32)
    high = samples.astype(jnp.bfloat16)
    low = (samples - high.astype(jnp.float32)).astype(jnp.bfloat16)
    return jnp.concatenate([high, low], axis=0)


def weighted(projected, blocks):
    return lax.dot_general(
        projected.astype(jnp.bfloat16),
        blocks,
        (((1,), (1,)), ((), ())),
        preferred_element_type=jnp.float32,
    )


def field_kernel(
    window,
    first_curl,
    table,
    pieces,
    pattern_in,
    region_in,
    law_in,
    curl_hbm,
    projected,
    halo,
    later_curl,
    pattern,
    region_ids,
    law,
    outer,
    timed,
    densities,
    edge_sums,
    small_sems,
    curl_sems,
):
    tile_count, links, tile, comps = curl_hbm.shape
    early = first_curl.shape[0]
    parts_here = halo.shape[0]
    fetched = [(pattern_in, pattern), (region_in, region_ids), (law_in, law)]
    small = [
        pltpu.make_async_copy(src, dst, small_sems.at[i]) for i, (src, dst) in enumerate(fetched)
    ]
    later = {
        elem: pltpu.make_async_copy(
            curl_hbm.at[elem : min(elem + CHUNK, tile_count)],
            later_curl.at[elem - early : min(elem + CHUNK, tile_count) - early],
            curl_sems.at[(elem - early) // CHUNK],
        )
        for elem in range(early, tile_count, CHUNK)
    }
    for copy in small + list(later.values()):
        copy.start()
    edge_sums[...] = jnp.zeros_like(edge_sums)
    own, outer_tiles = pieces[0], pieces[1]
    timed[:, tile:-tile] = time_samples(own, window[:, tile:-tile])
    timed[:, :tile] = time_samples(outer_tiles, window[:, :tile])
    timed[:, -tile:] = time_samples(outer_tiles, window[:, -tile:])
    columns = [
        jnp.broadcast_to(table[:, part : part + 1], (HALF, tile)) for part in range(parts_here)
    ]
    for copy in small:
        copy.wait()
    places = [[pattern[link, elem] for link in range(links)] for elem in range(tile_count)]
    count = jnp.int32(0)
    for elem in range(tile_count):
        for link, at in enumerate(places[elem]):
            outer[count] = elem * links + link
            count += jnp.where((at == 0) | (at == tile_count + 1), 1, 0)

    def blocks(elem):
        curl = first_curl[elem] if elem < early else later_curl[elem - early]
        return curl.reshape(links * tile, comps)

    def find_density(elem):
        picked = jnp.concatenate(
            [timed[:, pl.ds(pl.multiple_of(at * tile, tile), tile)] for at in places[elem]], axis=1
        )
        split = jnp.dot(picked, blocks(elem), preferred_element_type=jnp.float32)
        densities[elem] = split[:HALF] + split[HALF:]

    def project(elem):
        density = densities[elem]
        comp = [density[:, c * tile : (c + 1) * tile] for c in range(comps // tile)]
        square = comp[0] * comp[0]
        for c in comp[1:]:
            square = square + c * c
        region = region_ids[elem]
        reluct = law[0, region] + law[2, region] * square / (square + law[1, region])
        field = [reluct * c for c in comp]
        rows = [
            jnp.concatenate([jnp.sum(column * f, axis=0, keepdims=True) for f in field], axis=1)
            for column in columns
        ]
        projected[elem] = jnp.concatenate(rows, axis=0) * (4.0 / SAMPLES)

    for turn in range(tile_count + 1):
        if turn < tile_count:
            if turn in later:
                later[turn].wait()
            find_density(turn)
        if turn:
            project(turn - 1)

    def add_outer(turn, carry):
        listed, sides, rows, curls = [], [], [], []
        for slot in range(LISTED):
            spot = turn * LISTED + slot
            code = jnp.where(spot < count, outer[jnp.minimum(spot, jnp.maximum(count - 1, 0))], 0)
            elem, link = code // links, code % links
            curls.append(
                jnp.where(
                    elem < early,
                    first_curl[jnp.minimum(elem, early - 1), link],
                    later_curl[jnp.maximum(elem - early, 0), link],
                )
            )
            rows.append(projected[elem])
            sides.append(jnp.where(pattern[link, elem] == 0, 0, 1))
            listed.append(spot < count)
        contrib = weighted(jnp.concatenate(rows, axis=0), jnp.concatenate(curls, axis=0))
        for slot in range(LISTED):
            block = contrib[
                slot * parts_here : (slot + 1) * parts_here, slot * tile : (slot + 1) * tile
            ]
            edge_sums[slot, sides[slot]] += jnp.where(listed[slot], block, 0.0)
        return carry

    add_outer(0, 0)
    lax.fori_loop(1, (count + LISTED - 1) // LISTED, add_outer, 0)
    total = edge_sums[0]
    for slot in range(1, LISTED):
        total = total + edge_sums[slot]
    halo[:, :tile] = total[0]
    halo[:, tile:] = total[1]


def sum_kernel(
    projected,
    first_curl,
    later_curl,
    source,
    pattern_in,
    out,
    pattern,
    small_sem,
    *sums,
):
    links, tile, comps = first_curl.shape[1:]
    early = first_curl.shape[0]
    tile_count = early + later_curl.shape[0]
    small = pltpu.make_async_copy(pattern_in, pattern, small_sem)
    small.start()
    for total in sums:
        total[...] = jnp.zeros_like(total)

    def contribution(elem):
        curl = first_curl[elem] if elem < early else later_curl[elem - early]
        return weighted(projected[elem], curl.reshape(links * tile, comps))

    ahead = [contribution(elem) for elem in range(AHEAD)]
    small.wait()
    for elem in range(tile_count):
        contrib = ahead[elem] if elem < AHEAD else contribution(elem)
        for link in range(links):
            sums[link][pattern[link, elem]] += contrib[:, link * tile : (link + 1) * tile]
    for w in range(tile_count):
        at = slice(w * tile, (w + 1) * tile)
        total = sums[0][w + 1]
        for other in sums[1:]:
            total = total + other[w + 1]
        out[:, at] = total - source[:, at]


def halo_kernel(own, from_right, from_left, out):
    tile = from_left.shape[1] // 2
    out[...] = own[...]
    out[:, :tile] += from_left[:, tile:]
    out[:, -tile:] += from_right[:, :tile]


def per_device(coeffs, curl_tiles, pattern, region_ids, material_law, source):
    parts_here = coeffs.shape[0]
    tile_count, links, tile, comps = curl_tiles.shape
    chips, cores, samp = (lax.axis_size(axis) for axis in GROUP)
    group_size = chips * cores * samp
    parts = parts_here * group_size
    table = half_table(parts)
    before = np.roll(np.arange(parts).reshape(chips, cores, -1), 1, axis=1).reshape(-1)
    pieces = jnp.asarray(np.stack([bf16_pieces(table), bf16_pieces(table[:, before])]))
    own_columns = jnp.asarray(
        table.reshape(HALF, group_size, parts_here).transpose(1, 0, 2).astype(np.float32)
    )
    vmem, hbm = pl.BlockSpec(memory_space=pltpu.VMEM), pl.BlockSpec(memory_space=pltpu.HBM)

    def in_vmem(array):
        return pltpu.with_memory_space_constraint(array, pltpu.VMEM)

    def in_hbm(array):
        return pltpu.with_memory_space_constraint(array, pltpu.HBM)

    early = tile_count // 2
    operands = [
        curl_tiles,
        own_columns,
        coeffs,
        pieces,
        source,
        pattern.T,
        region_ids,
        material_law,
    ]
    shapes = [
        (early,) + curl_tiles.shape[1:],
        own_columns.shape[1:],
    ] + [operand.shape for operand in operands[2:]]
    fetched = pl.pallas_call(
        fetch_kernel,
        out_shape=[pltpu.VMEM(shape, o.dtype) for shape, o in zip(shapes, operands)],
        in_specs=[hbm] * len(operands),
        out_specs=[vmem] * len(operands),
        scratch_shapes=[pltpu.SemaphoreType.DMA((len(operands),))],
        compiler_params=pltpu.CompilerParams(vmem_limit_bytes=16 * MIB),
        cost_estimate=pl.CostEstimate(
            flops=0, bytes_accessed=4 * early * links * tile * comps, transcendentals=0
        ),
        name="fetch_operands",
    )(*[in_hbm(operand) for operand in operands])
    first_curl, columns_here, coeffs_here, pieces_here, source_here, *others = fetched
    pattern_here = others[0]

    left, right = from_neighbours(coeffs, tile)
    block = jnp.concatenate([left, coeffs_here, right], axis=1)
    copies = jnp.broadcast_to(block[None], (group_size,) + block.shape)
    window = lax.all_to_all(copies, GROUP, 0, 0).reshape(parts, block.shape[1])
    pattern_words = pltpu.SMEM((links, tile_count), jnp.int32)
    projected, halo, later_curl = pl.pallas_call(
        field_kernel,
        out_shape=(
            pltpu.VMEM((tile_count, parts_here, comps), jnp.float32),
            pltpu.VMEM((parts_here, 2 * tile), jnp.float32),
            pltpu.VMEM((tile_count - early,) + curl_tiles.shape[1:], curl_tiles.dtype),
        ),
        in_specs=[vmem] * 7 + [hbm],
        out_specs=(vmem, vmem, vmem),
        scratch_shapes=[
            pattern_words,
            pltpu.SMEM(region_ids.shape, jnp.int32),
            pltpu.SMEM(material_law.shape, jnp.float32),
            pltpu.SMEM((links * tile_count + 1,), jnp.int32),
            pltpu.VMEM((SAMPLES, (tile_count + 2) * tile), jnp.bfloat16),
            pltpu.VMEM((tile_count, HALF, comps), jnp.float32),
            pltpu.VMEM((LISTED, 2, parts_here, tile), jnp.float32),
            pltpu.SemaphoreType.DMA((3,)),
            pltpu.SemaphoreType.DMA((pl.cdiv(tile_count - early, CHUNK),)),
        ],
        compiler_params=pltpu.CompilerParams(vmem_limit_bytes=32 * MIB),
        cost_estimate=pl.CostEstimate(
            flops=2 * SAMPLES * tile_count * links * tile * comps,
            bytes_accessed=2 * curl_tiles.size,
            transcendentals=0,
        ),
        name="shard_fields",
    )(
        in_vmem(window),
        *[in_vmem(array) for array in (first_curl, columns_here, pieces_here, *others)],
        in_hbm(curl_tiles),
    )
    if lax.axis_size("space") == 2:
        beside = [across(halo, 0, 1)] * 2
    else:
        beside = [across(halo, 0, -1), across(halo, 0, 1)]
    own = pl.pallas_call(
        sum_kernel,
        out_shape=pltpu.VMEM(source.shape, jnp.float32),
        in_specs=[vmem] * 5,
        out_specs=vmem,
        scratch_shapes=[
            pattern_words,
            pltpu.SemaphoreType.DMA,
        ]
        + [pltpu.VMEM((tile_count + 2, parts_here, tile), jnp.float32)] * links,
        compiler_params=pltpu.CompilerParams(vmem_limit_bytes=32 * MIB),
        cost_estimate=pl.CostEstimate(
            flops=2 * SAMPLES * tile_count * links * tile * comps,
            bytes_accessed=2 * curl_tiles.size,
            transcendentals=0,
        ),
        name="shard_sums",
    )(
        *[in_vmem(a) for a in (projected, first_curl, later_curl, source_here, pattern_here)],
    )
    return pl.pallas_call(
        halo_kernel,
        out_shape=jax.ShapeDtypeStruct(source.shape, jnp.float32),
        in_specs=[vmem] * 3,
        out_specs=vmem,
        compiler_params=pltpu.CompilerParams(vmem_limit_bytes=16 * MIB),
        name="halo_sum",
    )(in_vmem(own), *beside)


def solution(mesh):
    at = mesh.axis_names.index("harm")
    harm = mesh.shape["harm"]
    cores = 2 if harm % 2 == 0 else 1
    sizes = mesh.devices.shape
    split = jax.sharding.Mesh(
        mesh.devices.reshape(sizes[:at] + (harm // cores, cores) + sizes[at + 1 :]),
        mesh.axis_names[:at] + ("chip", "core") + mesh.axis_names[at + 1 :],
    )
    placed = (
        P(GROUP, "space"),
        P("space", None, None, None),
        P("space", None),
        P("space"),
        P(),
        P(GROUP, "space"),
    )
    return jax.shard_map(
        per_device,
        mesh=split,
        in_specs=placed,
        out_specs=P(GROUP, "space"),
        check_vma=False,
    )
```

```python
import math

import jax
import jax.numpy as jnp
import ml_dtypes
import numpy as np
from jax import lax
from jax.experimental import pallas as pl
from jax.experimental.pallas import tpu as pltpu
from jax.sharding import PartitionSpec as P

SAMPLES = 64
HALF = SAMPLES // 2
GROUP = ("chip", "core", "samp")
MIB = 1024 * 1024
LISTED = 4
CHUNK = 4
AHEAD = 3


def half_table(parts):
    sample_ids = np.arange(HALF)[:, None]
    part_ids = np.arange(parts)[None, :]
    phase = ((2 * (part_ids // 2) + 1) * sample_ids % SAMPLES) * (2.0 * math.pi / SAMPLES)
    return np.where(part_ids % 2 == 0, np.cos(phase), np.sin(phase))


def bf16_pieces(table):
    rest = table
    pieces = []
    for _ in range(3):
        piece = rest.astype(ml_dtypes.bfloat16)
        pieces.append(piece)
        rest = rest - piece.astype(np.float64)
    return np.concatenate(pieces, axis=-1)


def across(array, core_step, space_step):
    cores, shards = lax.axis_size("core"), lax.axis_size("space")
    pairs = [
        (c * shards + s, (c + core_step) % cores * shards + (s + space_step) % shards)
        for c in range(cores)
        for s in range(shards)
    ]
    return lax.ppermute(array, ("core", "space"), pairs)


def from_neighbours(array, tile):
    if lax.axis_size("space") == 2:
        other = across(array, 1, 1)
        return other[:, -tile:], other[:, :tile]
    return across(array[:, -tile:], 1, 1), across(array[:, :tile], 1, -1)


def fetch_kernel(*refs):
    count = (len(refs) - 1) // 2
    sources, targets, sems = refs[:count], refs[count : 2 * count], refs[-1]
    rank = lax.axis_index(GROUP)
    sources = (sources[0].at[: targets[0].shape[0]], sources[1].at[rank]) + sources[2:]
    copies = [
        pltpu.make_async_copy(source, target, sems.at[i])
        for i, (source, target) in enumerate(zip(sources, targets))
    ]
    for copy in copies:
        copy.start()
    for copy in copies:
        copy.wait()


def time_samples(pieces, rows):
    stacked = jnp.concatenate([rows] * 3, axis=0)
    samples = jnp.dot(pieces, stacked, preferred_element_type=jnp.float32)
    high = samples.astype(jnp.bfloat16)
    low = (samples - high.astype(jnp.float32)).astype(jnp.bfloat16)
    return jnp.concatenate([high, low], axis=0)


def weighted(projected, blocks):
    return lax.dot_general(
        projected.astype(jnp.bfloat16),
        blocks,
        (((1,), (1,)), ((), ())),
        preferred_element_type=jnp.float32,
    )


def field_kernel(
    window,
    first_curl,
    table,
    pieces,
    pattern_in,
    region_in,
    law_in,
    curl_hbm,
    projected,
    halo,
    later_curl,
    pattern,
    region_ids,
    law,
    outer,
    timed,
    densities,
    edge_sums,
    small_sems,
    curl_sems,
):
    tile_count, links, tile, comps = curl_hbm.shape
    early = first_curl.shape[0]
    parts_here = halo.shape[0]
    fetched = [(pattern_in, pattern), (region_in, region_ids), (law_in, law)]
    small = [
        pltpu.make_async_copy(src, dst, small_sems.at[i]) for i, (src, dst) in enumerate(fetched)
    ]
    later = {
        elem: pltpu.make_async_copy(
            curl_hbm.at[elem : min(elem + CHUNK, tile_count)],
            later_curl.at[elem - early : min(elem + CHUNK, tile_count) - early],
            curl_sems.at[(elem - early) // CHUNK],
        )
        for elem in range(early, tile_count, CHUNK)
    }
    for copy in small + list(later.values()):
        copy.start()
    edge_sums[...] = jnp.zeros_like(edge_sums)
    own, outer_tiles = pieces[0], pieces[1]
    timed[:, tile:-tile] = time_samples(own, window[:, tile:-tile])
    timed[:, :tile] = time_samples(outer_tiles, window[:, :tile])
    timed[:, -tile:] = time_samples(outer_tiles, window[:, -tile:])
    columns = [
        jnp.broadcast_to(table[:, part : part + 1], (HALF, tile)) for part in range(parts_here)
    ]
    for copy in small:
        copy.wait()
    places = [[pattern[link, elem] for link in range(links)] for elem in range(tile_count)]
    count = jnp.int32(0)

    def blocks(elem):
        curl = first_curl[elem] if elem < early else later_curl[elem - early]
        return curl.reshape(links * tile, comps)

    def find_density(elem):
        picked = jnp.concatenate(
            [timed[:, pl.ds(pl.multiple_of(at * tile, tile), tile)] for at in places[elem]], axis=1
        )
        split = jnp.dot(picked, blocks(elem), preferred_element_type=jnp.float32)
        densities[elem] = split[:HALF] + split[HALF:]

    def project(elem):
        density = densities[elem]
        comp = [density[:, c * tile : (c + 1) * tile] for c in range(comps // tile)]
        square = comp[0] * comp[0]
        for c in comp[1:]:
            square = square + c * c
        region = region_ids[elem]
        reluct = law[0, region] + law[2, region] * square / (square + law[1, region])
        field = [reluct * c for c in comp]
        rows = [
            jnp.concatenate([jnp.sum(column * f, axis=0, keepdims=True) for f in field], axis=1)
            for column in columns
        ]
        projected[elem] = jnp.concatenate(rows, axis=0) * (4.0 / SAMPLES)

    for turn in range(tile_count + 1):
        if turn < tile_count:
            if turn in later:
                later[turn].wait()
            find_density(turn)
            for link, at in enumerate(places[turn]):
                outer[count] = turn * links + link
                count += jnp.where((at == 0) | (at == tile_count + 1), 1, 0)
        if turn:
            project(turn - 1)

    def add_outer(turn, carry):
        listed, sides, rows, curls = [], [], [], []
        for slot in range(LISTED):
            spot = turn * LISTED + slot
            code = jnp.where(spot < count, outer[jnp.minimum(spot, jnp.maximum(count - 1, 0))], 0)
            elem, link = code // links, code % links
            curls.append(
                jnp.where(
                    elem < early,
                    first_curl[jnp.minimum(elem, early - 1), link],
                    later_curl[jnp.maximum(elem - early, 0), link],
                )
            )
            rows.append(projected[elem])
            sides.append(jnp.where(pattern[link, elem] == 0, 0, 1))
            listed.append(spot < count)
        contrib = weighted(jnp.concatenate(rows, axis=0), jnp.concatenate(curls, axis=0))
        for slot in range(LISTED):
            block = contrib[
                slot * parts_here : (slot + 1) * parts_here, slot * tile : (slot + 1) * tile
            ]
            edge_sums[slot, sides[slot]] += jnp.where(listed[slot], block, 0.0)
        return carry

    add_outer(0, 0)
    lax.fori_loop(1, (count + LISTED - 1) // LISTED, add_outer, 0)
    total = edge_sums[0]
    for slot in range(1, LISTED):
        total = total + edge_sums[slot]
    halo[:, :tile] = total[0]
    halo[:, tile:] = total[1]


def sum_kernel(
    projected,
    first_curl,
    later_curl,
    source,
    pattern_in,
    out,
    pattern,
    small_sem,
    *sums,
):
    links, tile, comps = first_curl.shape[1:]
    early = first_curl.shape[0]
    tile_count = early + later_curl.shape[0]
    small = pltpu.make_async_copy(pattern_in, pattern, small_sem)
    small.start()
    for total in sums:
        total[...] = jnp.zeros_like(total)

    def contribution(elem):
        curl = first_curl[elem] if elem < early else later_curl[elem - early]
        return weighted(projected[elem], curl.reshape(links * tile, comps))

    ahead = [contribution(elem) for elem in range(AHEAD)]
    small.wait()
    for elem in range(tile_count):
        contrib = ahead[elem] if elem < AHEAD else contribution(elem)
        for link in range(links):
            sums[link][pattern[link, elem]] += contrib[:, link * tile : (link + 1) * tile]
    for w in range(tile_count):
        at = slice(w * tile, (w + 1) * tile)
        total = sums[0][w + 1]
        for other in sums[1:]:
            total = total + other[w + 1]
        out[:, at] = total - source[:, at]


def halo_kernel(own, from_right, from_left, out):
    tile = from_left.shape[1] // 2
    out[...] = own[...]
    out[:, :tile] += from_left[:, tile:]
    out[:, -tile:] += from_right[:, :tile]


def per_device(coeffs, curl_tiles, pattern, region_ids, material_law, source):
    parts_here = coeffs.shape[0]
    tile_count, links, tile, comps = curl_tiles.shape
    chips, cores, samp = (lax.axis_size(axis) for axis in GROUP)
    group_size = chips * cores * samp
    parts = parts_here * group_size
    table = half_table(parts)
    before = np.roll(np.arange(parts).reshape(chips, cores, -1), 1, axis=1).reshape(-1)
    pieces = jnp.asarray(np.stack([bf16_pieces(table), bf16_pieces(table[:, before])]))
    own_columns = jnp.asarray(
        table.reshape(HALF, group_size, parts_here).transpose(1, 0, 2).astype(np.float32)
    )
    vmem, hbm = pl.BlockSpec(memory_space=pltpu.VMEM), pl.BlockSpec(memory_space=pltpu.HBM)

    def in_vmem(array):
        return pltpu.with_memory_space_constraint(array, pltpu.VMEM)

    def in_hbm(array):
        return pltpu.with_memory_space_constraint(array, pltpu.HBM)

    early = tile_count // 2
    operands = [
        curl_tiles,
        own_columns,
        coeffs,
        pieces,
        source,
        pattern.T,
        region_ids,
        material_law,
    ]
    shapes = [
        (early,) + curl_tiles.shape[1:],
        own_columns.shape[1:],
    ] + [operand.shape for operand in operands[2:]]
    fetched = pl.pallas_call(
        fetch_kernel,
        out_shape=[pltpu.VMEM(shape, o.dtype) for shape, o in zip(shapes, operands)],
        in_specs=[hbm] * len(operands),
        out_specs=[vmem] * len(operands),
        scratch_shapes=[pltpu.SemaphoreType.DMA((len(operands),))],
        compiler_params=pltpu.CompilerParams(vmem_limit_bytes=16 * MIB),
        cost_estimate=pl.CostEstimate(
            flops=0, bytes_accessed=4 * early * links * tile * comps, transcendentals=0
        ),
        name="fetch_operands",
    )(*[in_hbm(operand) for operand in operands])
    first_curl, columns_here, coeffs_here, pieces_here, source_here, *others = fetched
    pattern_here = others[0]

    left, right = from_neighbours(coeffs, tile)
    block = jnp.concatenate([left, coeffs_here, right], axis=1)
    copies = jnp.broadcast_to(block[None], (group_size,) + block.shape)
    window = lax.all_to_all(copies, GROUP, 0, 0).reshape(parts, block.shape[1])
    pattern_words = pltpu.SMEM((links, tile_count), jnp.int32)
    projected, halo, later_curl = pl.pallas_call(
        field_kernel,
        out_shape=(
            pltpu.VMEM((tile_count, parts_here, comps), jnp.float32),
            pltpu.VMEM((parts_here, 2 * tile), jnp.float32),
            pltpu.VMEM((tile_count - early,) + curl_tiles.shape[1:], curl_tiles.dtype),
        ),
        in_specs=[vmem] * 7 + [hbm],
        out_specs=(vmem, vmem, vmem),
        scratch_shapes=[
            pattern_words,
            pltpu.SMEM(region_ids.shape, jnp.int32),
            pltpu.SMEM(material_law.shape, jnp.float32),
            pltpu.SMEM((links * tile_count + 1,), jnp.int32),
            pltpu.VMEM((SAMPLES, (tile_count + 2) * tile), jnp.bfloat16),
            pltpu.VMEM((tile_count, HALF, comps), jnp.float32),
            pltpu.VMEM((LISTED, 2, parts_here, tile), jnp.float32),
            pltpu.SemaphoreType.DMA((3,)),
            pltpu.SemaphoreType.DMA((pl.cdiv(tile_count - early, CHUNK),)),
        ],
        compiler_params=pltpu.CompilerParams(vmem_limit_bytes=32 * MIB),
        cost_estimate=pl.CostEstimate(
            flops=2 * SAMPLES * tile_count * links * tile * comps,
            bytes_accessed=2 * curl_tiles.size,
            transcendentals=0,
        ),
        name="shard_fields",
    )(
        in_vmem(window),
        *[in_vmem(array) for array in (first_curl, columns_here, pieces_here, *others)],
        in_hbm(curl_tiles),
    )
    if lax.axis_size("space") == 2:
        beside = [across(halo, 0, 1)] * 2
    else:
        beside = [across(halo, 0, -1), across(halo, 0, 1)]
    own = pl.pallas_call(
        sum_kernel,
        out_shape=pltpu.VMEM(source.shape, jnp.float32),
        in_specs=[vmem] * 5,
        out_specs=vmem,
        scratch_shapes=[
            pattern_words,
            pltpu.SemaphoreType.DMA,
        ]
        + [pltpu.VMEM((tile_count + 2, parts_here, tile), jnp.float32)] * links,
        compiler_params=pltpu.CompilerParams(vmem_limit_bytes=32 * MIB),
        cost_estimate=pl.CostEstimate(
            flops=2 * SAMPLES * tile_count * links * tile * comps,
            bytes_accessed=2 * curl_tiles.size,
            transcendentals=0,
        ),
        name="shard_sums",
    )(
        *[in_vmem(a) for a in (projected, first_curl, later_curl, source_here, pattern_here)],
    )
    return pl.pallas_call(
        halo_kernel,
        out_shape=jax.ShapeDtypeStruct(source.shape, jnp.float32),
        in_specs=[vmem] * 3,
        out_specs=vmem,
        compiler_params=pltpu.CompilerParams(vmem_limit_bytes=16 * MIB),
        name="halo_sum",
    )(in_vmem(own), *beside)


def solution(mesh):
    at = mesh.axis_names.index("harm")
    harm = mesh.shape["harm"]
    cores = 2 if harm % 2 == 0 else 1
    sizes = mesh.devices.shape
    split = jax.sharding.Mesh(
        mesh.devices.reshape(sizes[:at] + (harm // cores, cores) + sizes[at + 1 :]),
        mesh.axis_names[:at] + ("chip", "core") + mesh.axis_names[at + 1 :],
    )
    placed = (
        P(GROUP, "space"),
        P("space", None, None, None),
        P("space", None),
        P("space"),
        P(),
        P(GROUP, "space"),
    )
    return jax.shard_map(
        per_device,
        mesh=split,
        in_specs=placed,
        out_specs=P(GROUP, "space"),
        check_vma=False,
    )
```

```python
import math

import jax
import jax.numpy as jnp
import ml_dtypes
import numpy as np
from jax import lax
from jax.experimental import pallas as pl
from jax.experimental.pallas import tpu as pltpu
from jax.sharding import PartitionSpec as P

SAMPLES = 64
HALF = SAMPLES // 2
GROUP = ("chip", "core", "samp")
MIB = 1024 * 1024
LISTED = 4
CHUNK = 4
AHEAD = 3


def half_table(parts):
    sample_ids = np.arange(HALF)[:, None]
    part_ids = np.arange(parts)[None, :]
    phase = ((2 * (part_ids // 2) + 1) * sample_ids % SAMPLES) * (2.0 * math.pi / SAMPLES)
    return np.where(part_ids % 2 == 0, np.cos(phase), np.sin(phase))


def bf16_pieces(table):
    rest = table
    pieces = []
    for _ in range(2):
        piece = rest.astype(ml_dtypes.bfloat16)
        pieces.append(piece)
        rest = rest - piece.astype(np.float64)
    return np.concatenate(pieces, axis=-1)


def across(array, core_step, space_step):
    cores, shards = lax.axis_size("core"), lax.axis_size("space")
    pairs = [
        (c * shards + s, (c + core_step) % cores * shards + (s + space_step) % shards)
        for c in range(cores)
        for s in range(shards)
    ]
    return lax.ppermute(array, ("core", "space"), pairs)


def from_neighbours(array, tile):
    if lax.axis_size("space") == 2:
        other = across(array, 1, 1)
        return other[:, -tile:], other[:, :tile]
    return across(array[:, -tile:], 1, 1), across(array[:, :tile], 1, -1)


def fetch_kernel(*refs):
    count = (len(refs) - 1) // 2
    sources, targets, sems = refs[:count], refs[count : 2 * count], refs[-1]
    rank = lax.axis_index(GROUP)
    sources = (sources[0].at[: targets[0].shape[0]], sources[1].at[rank]) + sources[2:]
    copies = [
        pltpu.make_async_copy(source, target, sems.at[i])
        for i, (source, target) in enumerate(zip(sources, targets))
    ]
    for copy in copies:
        copy.start()
    for copy in copies:
        copy.wait()


def time_samples(pieces, rows):
    stacked = jnp.concatenate([rows] * 2, axis=0)
    samples = jnp.dot(pieces, stacked, preferred_element_type=jnp.float32)
    high = samples.astype(jnp.bfloat16)
    low = (samples - high.astype(jnp.float32)).astype(jnp.bfloat16)
    return jnp.concatenate([high, low], axis=0)


def weighted(projected, blocks):
    return lax.dot_general(
        projected.astype(jnp.bfloat16),
        blocks,
        (((1,), (1,)), ((), ())),
        preferred_element_type=jnp.float32,
    )


def field_kernel(
    window,
    first_curl,
    table,
    pieces,
    pattern_in,
    region_in,
    law_in,
    curl_hbm,
    projected,
    halo,
    later_curl,
    pattern,
    region_ids,
    law,
    outer,
    timed,
    densities,
    edge_sums,
    small_sems,
    curl_sems,
):
    tile_count, links, tile, comps = curl_hbm.shape
    early = first_curl.shape[0]
    parts_here = halo.shape[0]
    fetched = [(pattern_in, pattern), (region_in, region_ids), (law_in, law)]
    small = [
        pltpu.make_async_copy(src, dst, small_sems.at[i]) for i, (src, dst) in enumerate(fetched)
    ]
    later = {
        elem: pltpu.make_async_copy(
            curl_hbm.at[elem : min(elem + CHUNK, tile_count)],
            later_curl.at[elem - early : min(elem + CHUNK, tile_count) - early],
            curl_sems.at[(elem - early) // CHUNK],
        )
        for elem in range(early, tile_count, CHUNK)
    }
    for copy in small + list(later.values()):
        copy.start()
    edge_sums[...] = jnp.zeros_like(edge_sums)
    own, outer_tiles = pieces[0], pieces[1]
    timed[:, tile:-tile] = time_samples(own, window[:, tile:-tile])
    timed[:, :tile] = time_samples(outer_tiles, window[:, :tile])
    timed[:, -tile:] = time_samples(outer_tiles, window[:, -tile:])
    columns = [
        jnp.broadcast_to(table[:, part : part + 1], (HALF, tile)) for part in range(parts_here)
    ]
    for copy in small:
        copy.wait()
    places = [[pattern[link, elem] for link in range(links)] for elem in range(tile_count)]
    count = jnp.int32(0)

    def blocks(elem):
        curl = first_curl[elem] if elem < early else later_curl[elem - early]
        return curl.reshape(links * tile, comps)

    def find_density(elem):
        picked = jnp.concatenate(
            [timed[:, pl.ds(pl.multiple_of(at * tile, tile), tile)] for at in places[elem]], axis=1
        )
        split = jnp.dot(picked, blocks(elem), preferred_element_type=jnp.float32)
        densities[elem] = split[:HALF] + split[HALF:]

    def project(elem):
        density = densities[elem]
        comp = [density[:, c * tile : (c + 1) * tile] for c in range(comps // tile)]
        square = comp[0] * comp[0]
        for c in comp[1:]:
            square = square + c * c
        region = region_ids[elem]
        reluct = law[0, region] + law[2, region] * square / (square + law[1, region])
        field = [reluct * c for c in comp]
        rows = [
            jnp.concatenate([jnp.sum(column * f, axis=0, keepdims=True) for f in field], axis=1)
            for column in columns
        ]
        projected[elem] = jnp.concatenate(rows, axis=0) * (4.0 / SAMPLES)

    for turn in range(tile_count + 1):
        if turn < tile_count:
            if turn in later:
                later[turn].wait()
            find_density(turn)
            for link, at in enumerate(places[turn]):
                outer[count] = turn * links + link
                count += jnp.where((at == 0) | (at == tile_count + 1), 1, 0)
        if turn:
            project(turn - 1)

    def add_outer(turn, carry):
        listed, sides, rows, curls = [], [], [], []
        for slot in range(LISTED):
            spot = turn * LISTED + slot
            code = jnp.where(spot < count, outer[jnp.minimum(spot, jnp.maximum(count - 1, 0))], 0)
            elem, link = code // links, code % links
            curls.append(
                jnp.where(
                    elem < early,
                    first_curl[jnp.minimum(elem, early - 1), link],
                    later_curl[jnp.maximum(elem - early, 0), link],
                )
            )
            rows.append(projected[elem])
            sides.append(jnp.where(pattern[link, elem] == 0, 0, 1))
            listed.append(spot < count)
        contrib = weighted(jnp.concatenate(rows, axis=0), jnp.concatenate(curls, axis=0))
        for slot in range(LISTED):
            block = contrib[
                slot * parts_here : (slot + 1) * parts_here, slot * tile : (slot + 1) * tile
            ]
            edge_sums[slot, sides[slot]] += jnp.where(listed[slot], block, 0.0)
        return carry

    add_outer(0, 0)
    lax.fori_loop(1, (count + LISTED - 1) // LISTED, add_outer, 0)
    total = edge_sums[0]
    for slot in range(1, LISTED):
        total = total + edge_sums[slot]
    halo[:, :tile] = total[0]
    halo[:, tile:] = total[1]


def sum_kernel(
    projected,
    first_curl,
    later_curl,
    source,
    pattern_in,
    out,
    pattern,
    small_sem,
    *sums,
):
    links, tile, comps = first_curl.shape[1:]
    early = first_curl.shape[0]
    tile_count = early + later_curl.shape[0]
    small = pltpu.make_async_copy(pattern_in, pattern, small_sem)
    small.start()
    for total in sums:
        total[...] = jnp.zeros_like(total)

    def contribution(elem):
        curl = first_curl[elem] if elem < early else later_curl[elem - early]
        return weighted(projected[elem], curl.reshape(links * tile, comps))

    ahead = [contribution(elem) for elem in range(AHEAD)]
    small.wait()
    for elem in range(tile_count):
        contrib = ahead[elem] if elem < AHEAD else contribution(elem)
        for link in range(links):
            sums[link][pattern[link, elem]] += contrib[:, link * tile : (link + 1) * tile]
    for w in range(tile_count):
        at = slice(w * tile, (w + 1) * tile)
        total = sums[0][w + 1]
        for other in sums[1:]:
            total = total + other[w + 1]
        out[:, at] = total - source[:, at]


def halo_kernel(own, from_right, from_left, out):
    tile = from_left.shape[1] // 2
    out[...] = own[...]
    out[:, :tile] += from_left[:, tile:]
    out[:, -tile:] += from_right[:, :tile]


def per_device(coeffs, curl_tiles, pattern, region_ids, material_law, source):
    parts_here = coeffs.shape[0]
    tile_count, links, tile, comps = curl_tiles.shape
    chips, cores, samp = (lax.axis_size(axis) for axis in GROUP)
    group_size = chips * cores * samp
    parts = parts_here * group_size
    table = half_table(parts)
    before = np.roll(np.arange(parts).reshape(chips, cores, -1), 1, axis=1).reshape(-1)
    pieces = jnp.asarray(np.stack([bf16_pieces(table), bf16_pieces(table[:, before])]))
    own_columns = jnp.asarray(
        table.reshape(HALF, group_size, parts_here).transpose(1, 0, 2).astype(np.float32)
    )
    vmem, hbm = pl.BlockSpec(memory_space=pltpu.VMEM), pl.BlockSpec(memory_space=pltpu.HBM)

    def in_vmem(array):
        return pltpu.with_memory_space_constraint(array, pltpu.VMEM)

    def in_hbm(array):
        return pltpu.with_memory_space_constraint(array, pltpu.HBM)

    early = tile_count // 2
    operands = [
        curl_tiles,
        own_columns,
        coeffs,
        pieces,
        source,
        pattern.T,
        region_ids,
        material_law,
    ]
    shapes = [
        (early,) + curl_tiles.shape[1:],
        own_columns.shape[1:],
    ] + [operand.shape for operand in operands[2:]]
    fetched = pl.pallas_call(
        fetch_kernel,
        out_shape=[pltpu.VMEM(shape, o.dtype) for shape, o in zip(shapes, operands)],
        in_specs=[hbm] * len(operands),
        out_specs=[vmem] * len(operands),
        scratch_shapes=[pltpu.SemaphoreType.DMA((len(operands),))],
        compiler_params=pltpu.CompilerParams(vmem_limit_bytes=16 * MIB),
        cost_estimate=pl.CostEstimate(
            flops=0, bytes_accessed=4 * early * links * tile * comps, transcendentals=0
        ),
        name="fetch_operands",
    )(*[in_hbm(operand) for operand in operands])
    first_curl, columns_here, coeffs_here, pieces_here, source_here, *others = fetched
    pattern_here = others[0]

    left, right = from_neighbours(coeffs, tile)
    block = jnp.concatenate([left, coeffs_here, right], axis=1)
    copies = jnp.broadcast_to(block[None], (group_size,) + block.shape)
    window = lax.all_to_all(copies, GROUP, 0, 0).reshape(parts, block.shape[1])
    pattern_words = pltpu.SMEM((links, tile_count), jnp.int32)
    projected, halo, later_curl = pl.pallas_call(
        field_kernel,
        out_shape=(
            pltpu.VMEM((tile_count, parts_here, comps), jnp.float32),
            pltpu.VMEM((parts_here, 2 * tile), jnp.float32),
            pltpu.VMEM((tile_count - early,) + curl_tiles.shape[1:], curl_tiles.dtype),
        ),
        in_specs=[vmem] * 7 + [hbm],
        out_specs=(vmem, vmem, vmem),
        scratch_shapes=[
            pattern_words,
            pltpu.SMEM(region_ids.shape, jnp.int32),
            pltpu.SMEM(material_law.shape, jnp.float32),
            pltpu.SMEM((links * tile_count + 1,), jnp.int32),
            pltpu.VMEM((SAMPLES, (tile_count + 2) * tile), jnp.bfloat16),
            pltpu.VMEM((tile_count, HALF, comps), jnp.float32),
            pltpu.VMEM((LISTED, 2, parts_here, tile), jnp.float32),
            pltpu.SemaphoreType.DMA((3,)),
            pltpu.SemaphoreType.DMA((pl.cdiv(tile_count - early, CHUNK),)),
        ],
        compiler_params=pltpu.CompilerParams(vmem_limit_bytes=32 * MIB),
        cost_estimate=pl.CostEstimate(
            flops=2 * SAMPLES * tile_count * links * tile * comps,
            bytes_accessed=2 * curl_tiles.size,
            transcendentals=0,
        ),
        name="shard_fields",
    )(
        in_vmem(window),
        *[in_vmem(array) for array in (first_curl, columns_here, pieces_here, *others)],
        in_hbm(curl_tiles),
    )
    if lax.axis_size("space") == 2:
        beside = [across(halo, 0, 1)] * 2
    else:
        beside = [across(halo, 0, -1), across(halo, 0, 1)]
    own = pl.pallas_call(
        sum_kernel,
        out_shape=pltpu.VMEM(source.shape, jnp.float32),
        in_specs=[vmem] * 5,
        out_specs=vmem,
        scratch_shapes=[
            pattern_words,
            pltpu.SemaphoreType.DMA,
        ]
        + [pltpu.VMEM((tile_count + 2, parts_here, tile), jnp.float32)] * links,
        compiler_params=pltpu.CompilerParams(vmem_limit_bytes=32 * MIB),
        cost_estimate=pl.CostEstimate(
            flops=2 * SAMPLES * tile_count * links * tile * comps,
            bytes_accessed=2 * curl_tiles.size,
            transcendentals=0,
        ),
        name="shard_sums",
    )(
        *[in_vmem(a) for a in (projected, first_curl, later_curl, source_here, pattern_here)],
    )
    return pl.pallas_call(
        halo_kernel,
        out_shape=jax.ShapeDtypeStruct(source.shape, jnp.float32),
        in_specs=[vmem] * 3,
        out_specs=vmem,
        compiler_params=pltpu.CompilerParams(vmem_limit_bytes=16 * MIB),
        name="halo_sum",
    )(in_vmem(own), *beside)


def solution(mesh):
    at = mesh.axis_names.index("harm")
    harm = mesh.shape["harm"]
    cores = 2 if harm % 2 == 0 else 1
    sizes = mesh.devices.shape
    split = jax.sharding.Mesh(
        mesh.devices.reshape(sizes[:at] + (harm // cores, cores) + sizes[at + 1 :]),
        mesh.axis_names[:at] + ("chip", "core") + mesh.axis_names[at + 1 :],
    )
    placed = (
        P(GROUP, "space"),
        P("space", None, None, None),
        P("space", None),
        P("space"),
        P(),
        P(GROUP, "space"),
    )
    return jax.shard_map(
        per_device,
        mesh=split,
        in_specs=placed,
        out_specs=P(GROUP, "space"),
        check_vma=False,
    )
```

```python
import math

import jax
import jax.numpy as jnp
import ml_dtypes
import numpy as np
from jax import lax
from jax.experimental import pallas as pl
from jax.experimental.pallas import tpu as pltpu
from jax.sharding import PartitionSpec as P

SAMPLES = 64
HALF = SAMPLES // 2
GROUP = ("chip", "core", "samp")
MIB = 1024 * 1024
LISTED = 4
CHUNK = 4
AHEAD = 6


def half_table(parts):
    sample_ids = np.arange(HALF)[:, None]
    part_ids = np.arange(parts)[None, :]
    phase = ((2 * (part_ids // 2) + 1) * sample_ids % SAMPLES) * (2.0 * math.pi / SAMPLES)
    return np.where(part_ids % 2 == 0, np.cos(phase), np.sin(phase))


def bf16_pieces(table):
    rest = table
    pieces = []
    for _ in range(3):
        piece = rest.astype(ml_dtypes.bfloat16)
        pieces.append(piece)
        rest = rest - piece.astype(np.float64)
    return np.concatenate(pieces, axis=-1)


def across(array, core_step, space_step):
    cores, shards = lax.axis_size("core"), lax.axis_size("space")
    pairs = [
        (c * shards + s, (c + core_step) % cores * shards + (s + space_step) % shards)
        for c in range(cores)
        for s in range(shards)
    ]
    return lax.ppermute(array, ("core", "space"), pairs)


def from_neighbours(array, tile):
    if lax.axis_size("space") == 2:
        other = across(array, 1, 1)
        return other[:, -tile:], other[:, :tile]
    return across(array[:, -tile:], 1, 1), across(array[:, :tile], 1, -1)


def fetch_kernel(*refs):
    count = (len(refs) - 1) // 2
    sources, targets, sems = refs[:count], refs[count : 2 * count], refs[-1]
    rank = lax.axis_index(GROUP)
    sources = (sources[0].at[: targets[0].shape[0]], sources[1].at[rank]) + sources[2:]
    copies = [
        pltpu.make_async_copy(source, target, sems.at[i])
        for i, (source, target) in enumerate(zip(sources, targets))
    ]
    for copy in copies:
        copy.start()
    for copy in copies:
        copy.wait()


def time_samples(pieces, rows):
    stacked = jnp.concatenate([rows] * 3, axis=0)
    samples = jnp.dot(pieces, stacked, preferred_element_type=jnp.float32)
    high = samples.astype(jnp.bfloat16)
    low = (samples - high.astype(jnp.float32)).astype(jnp.bfloat16)
    return jnp.concatenate([high, low], axis=0)


def weighted(projected, blocks):
    return lax.dot_general(
        projected.astype(jnp.bfloat16),
        blocks,
        (((1,), (1,)), ((), ())),
        preferred_element_type=jnp.float32,
    )


def field_kernel(
    window,
    first_curl,
    table,
    pieces,
    pattern_in,
    region_in,
    law_in,
    curl_hbm,
    projected,
    halo,
    later_curl,
    pattern,
    region_ids,
    law,
    outer,
    timed,
    densities,
    edge_sums,
    small_sems,
    curl_sems,
):
    tile_count, links, tile, comps = curl_hbm.shape
    early = first_curl.shape[0]
    parts_here = halo.shape[0]
    fetched = [(pattern_in, pattern), (region_in, region_ids), (law_in, law)]
    small = [
        pltpu.make_async_copy(src, dst, small_sems.at[i]) for i, (src, dst) in enumerate(fetched)
    ]
    later = {
        elem: pltpu.make_async_copy(
            curl_hbm.at[elem : min(elem + CHUNK, tile_count)],
            later_curl.at[elem - early : min(elem + CHUNK, tile_count) - early],
            curl_sems.at[(elem - early) // CHUNK],
        )
        for elem in range(early, tile_count, CHUNK)
    }
    for copy in small + list(later.values()):
        copy.start()
    edge_sums[...] = jnp.zeros_like(edge_sums)
    own, outer_tiles = pieces[0], pieces[1]
    timed[:, tile:-tile] = time_samples(own, window[:, tile:-tile])
    timed[:, :tile] = time_samples(outer_tiles, window[:, :tile])
    timed[:, -tile:] = time_samples(outer_tiles, window[:, -tile:])
    columns = [
        jnp.broadcast_to(table[:, part : part + 1], (HALF, tile)) for part in range(parts_here)
    ]
    for copy in small:
        copy.wait()
    places = [[pattern[link, elem] for link in range(links)] for elem in range(tile_count)]
    count = jnp.int32(0)

    def blocks(elem):
        curl = first_curl[elem] if elem < early else later_curl[elem - early]
        return curl.reshape(links * tile, comps)

    def find_density(elem):
        picked = jnp.concatenate(
            [timed[:, pl.ds(pl.multiple_of(at * tile, tile), tile)] for at in places[elem]], axis=1
        )
        split = jnp.dot(picked, blocks(elem), preferred_element_type=jnp.float32)
        densities[elem] = split[:HALF] + split[HALF:]

    def project(elem):
        density = densities[elem]
        comp = [density[:, c * tile : (c + 1) * tile] for c in range(comps // tile)]
        square = comp[0] * comp[0]
        for c in comp[1:]:
            square = square + c * c
        region = region_ids[elem]
        reluct = law[0, region] + law[2, region] * square / (square + law[1, region])
        field = [reluct * c for c in comp]
        rows = [
            jnp.concatenate([jnp.sum(column * f, axis=0, keepdims=True) for f in field], axis=1)
            for column in columns
        ]
        projected[elem] = jnp.concatenate(rows, axis=0) * (4.0 / SAMPLES)

    for turn in range(tile_count + 1):
        if turn < tile_count:
            if turn in later:
                later[turn].wait()
            find_density(turn)
            for link, at in enumerate(places[turn]):
                outer[count] = turn * links + link
                count += jnp.where((at == 0) | (at == tile_count + 1), 1, 0)
        if turn:
            project(turn - 1)

    def add_outer(turn, carry):
        listed, sides, rows, curls = [], [], [], []
        for slot in range(LISTED):
            spot = turn * LISTED + slot
            code = jnp.where(spot < count, outer[jnp.minimum(spot, jnp.maximum(count - 1, 0))], 0)
            elem, link = code // links, code % links
            curls.append(
                jnp.where(
                    elem < early,
                    first_curl[jnp.minimum(elem, early - 1), link],
                    later_curl[jnp.maximum(elem - early, 0), link],
                )
            )
            rows.append(projected[elem])
            sides.append(jnp.where(pattern[link, elem] == 0, 0, 1))
            listed.append(spot < count)
        contrib = weighted(jnp.concatenate(rows, axis=0), jnp.concatenate(curls, axis=0))
        for slot in range(LISTED):
            block = contrib[
                slot * parts_here : (slot + 1) * parts_here, slot * tile : (slot + 1) * tile
            ]
            edge_sums[slot, sides[slot]] += jnp.where(listed[slot], block, 0.0)
        return carry

    add_outer(0, 0)
    lax.fori_loop(1, (count + LISTED - 1) // LISTED, add_outer, 0)
    total = edge_sums[0]
    for slot in range(1, LISTED):
        total = total + edge_sums[slot]
    halo[:, :tile] = total[0]
    halo[:, tile:] = total[1]


def sum_kernel(
    projected,
    first_curl,
    later_curl,
    source,
    pattern_in,
    out,
    pattern,
    small_sem,
    *sums,
):
    links, tile, comps = first_curl.shape[1:]
    early = first_curl.shape[0]
    tile_count = early + later_curl.shape[0]
    small = pltpu.make_async_copy(pattern_in, pattern, small_sem)
    small.start()
    for total in sums:
        total[...] = jnp.zeros_like(total)

    def contribution(elem):
        curl = first_curl[elem] if elem < early else later_curl[elem - early]
        return weighted(projected[elem], curl.reshape(links * tile, comps))

    ahead = [contribution(elem) for elem in range(AHEAD)]
    small.wait()
    for elem in range(tile_count):
        contrib = ahead[elem] if elem < AHEAD else contribution(elem)
        for link in range(links):
            sums[link][pattern[link, elem]] += contrib[:, link * tile : (link + 1) * tile]
    for w in range(tile_count):
        at = slice(w * tile, (w + 1) * tile)
        total = sums[0][w + 1]
        for other in sums[1:]:
            total = total + other[w + 1]
        out[:, at] = total - source[:, at]


def halo_kernel(own, from_right, from_left, out):
    tile = from_left.shape[1] // 2
    out[...] = own[...]
    out[:, :tile] += from_left[:, tile:]
    out[:, -tile:] += from_right[:, :tile]


def per_device(coeffs, curl_tiles, pattern, region_ids, material_law, source):
    parts_here = coeffs.shape[0]
    tile_count, links, tile, comps = curl_tiles.shape
    chips, cores, samp = (lax.axis_size(axis) for axis in GROUP)
    group_size = chips * cores * samp
    parts = parts_here * group_size
    table = half_table(parts)
    before = np.roll(np.arange(parts).reshape(chips, cores, -1), 1, axis=1).reshape(-1)
    pieces = jnp.asarray(np.stack([bf16_pieces(table), bf16_pieces(table[:, before])]))
    own_columns = jnp.asarray(
        table.reshape(HALF, group_size, parts_here).transpose(1, 0, 2).astype(np.float32)
    )
    vmem, hbm = pl.BlockSpec(memory_space=pltpu.VMEM), pl.BlockSpec(memory_space=pltpu.HBM)

    def in_vmem(array):
        return pltpu.with_memory_space_constraint(array, pltpu.VMEM)

    def in_hbm(array):
        return pltpu.with_memory_space_constraint(array, pltpu.HBM)

    early = tile_count // 2
    operands = [
        curl_tiles,
        own_columns,
        coeffs,
        pieces,
        source,
        pattern.T,
        region_ids,
        material_law,
    ]
    shapes = [
        (early,) + curl_tiles.shape[1:],
        own_columns.shape[1:],
    ] + [operand.shape for operand in operands[2:]]
    fetched = pl.pallas_call(
        fetch_kernel,
        out_shape=[pltpu.VMEM(shape, o.dtype) for shape, o in zip(shapes, operands)],
        in_specs=[hbm] * len(operands),
        out_specs=[vmem] * len(operands),
        scratch_shapes=[pltpu.SemaphoreType.DMA((len(operands),))],
        compiler_params=pltpu.CompilerParams(vmem_limit_bytes=16 * MIB),
        cost_estimate=pl.CostEstimate(
            flops=0, bytes_accessed=4 * early * links * tile * comps, transcendentals=0
        ),
        name="fetch_operands",
    )(*[in_hbm(operand) for operand in operands])
    first_curl, columns_here, coeffs_here, pieces_here, source_here, *others = fetched
    pattern_here = others[0]

    left, right = from_neighbours(coeffs, tile)
    block = jnp.concatenate([left, coeffs_here, right], axis=1)
    copies = jnp.broadcast_to(block[None], (group_size,) + block.shape)
    window = lax.all_to_all(copies, GROUP, 0, 0).reshape(parts, block.shape[1])
    pattern_words = pltpu.SMEM((links, tile_count), jnp.int32)
    projected, halo, later_curl = pl.pallas_call(
        field_kernel,
        out_shape=(
            pltpu.VMEM((tile_count, parts_here, comps), jnp.float32),
            pltpu.VMEM((parts_here, 2 * tile), jnp.float32),
            pltpu.VMEM((tile_count - early,) + curl_tiles.shape[1:], curl_tiles.dtype),
        ),
        in_specs=[vmem] * 7 + [hbm],
        out_specs=(vmem, vmem, vmem),
        scratch_shapes=[
            pattern_words,
            pltpu.SMEM(region_ids.shape, jnp.int32),
            pltpu.SMEM(material_law.shape, jnp.float32),
            pltpu.SMEM((links * tile_count + 1,), jnp.int32),
            pltpu.VMEM((SAMPLES, (tile_count + 2) * tile), jnp.bfloat16),
            pltpu.VMEM((tile_count, HALF, comps), jnp.float32),
            pltpu.VMEM((LISTED, 2, parts_here, tile), jnp.float32),
            pltpu.SemaphoreType.DMA((3,)),
            pltpu.SemaphoreType.DMA((pl.cdiv(tile_count - early, CHUNK),)),
        ],
        compiler_params=pltpu.CompilerParams(vmem_limit_bytes=32 * MIB),
        cost_estimate=pl.CostEstimate(
            flops=2 * SAMPLES * tile_count * links * tile * comps,
            bytes_accessed=2 * curl_tiles.size,
            transcendentals=0,
        ),
        name="shard_fields",
    )(
        in_vmem(window),
        *[in_vmem(array) for array in (first_curl, columns_here, pieces_here, *others)],
        in_hbm(curl_tiles),
    )
    if lax.axis_size("space") == 2:
        beside = [across(halo, 0, 1)] * 2
    else:
        beside = [across(halo, 0, -1), across(halo, 0, 1)]
    own = pl.pallas_call(
        sum_kernel,
        out_shape=pltpu.VMEM(source.shape, jnp.float32),
        in_specs=[vmem] * 5,
        out_specs=vmem,
        scratch_shapes=[
            pattern_words,
            pltpu.SemaphoreType.DMA,
        ]
        + [pltpu.VMEM((tile_count + 2, parts_here, tile), jnp.float32)] * links,
        compiler_params=pltpu.CompilerParams(vmem_limit_bytes=32 * MIB),
        cost_estimate=pl.CostEstimate(
            flops=2 * SAMPLES * tile_count * links * tile * comps,
            bytes_accessed=2 * curl_tiles.size,
            transcendentals=0,
        ),
        name="shard_sums",
    )(
        *[in_vmem(a) for a in (projected, first_curl, later_curl, source_here, pattern_here)],
    )
    return pl.pallas_call(
        halo_kernel,
        out_shape=jax.ShapeDtypeStruct(source.shape, jnp.float32),
        in_specs=[vmem] * 3,
        out_specs=vmem,
        compiler_params=pltpu.CompilerParams(vmem_limit_bytes=16 * MIB),
        name="halo_sum",
    )(in_vmem(own), *beside)


def solution(mesh):
    at = mesh.axis_names.index("harm")
    harm = mesh.shape["harm"]
    cores = 2 if harm % 2 == 0 else 1
    sizes = mesh.devices.shape
    split = jax.sharding.Mesh(
        mesh.devices.reshape(sizes[:at] + (harm // cores, cores) + sizes[at + 1 :]),
        mesh.axis_names[:at] + ("chip", "core") + mesh.axis_names[at + 1 :],
    )
    placed = (
        P(GROUP, "space"),
        P("space", None, None, None),
        P("space", None),
        P("space"),
        P(),
        P(GROUP, "space"),
    )
    return jax.shard_map(
        per_device,
        mesh=split,
        in_specs=placed,
        out_specs=P(GROUP, "space"),
        check_vma=False,
    )
```

```python
import math

import jax
import jax.numpy as jnp
import ml_dtypes
import numpy as np
from jax import lax
from jax.experimental import pallas as pl
from jax.experimental.pallas import tpu as pltpu
from jax.sharding import PartitionSpec as P

SAMPLES = 64
HALF = SAMPLES // 2
GROUP = ("chip", "core", "samp")
MIB = 1024 * 1024
LISTED = 6
CHUNK = 4
AHEAD = 6


def half_table(parts):
    sample_ids = np.arange(HALF)[:, None]
    part_ids = np.arange(parts)[None, :]
    phase = ((2 * (part_ids // 2) + 1) * sample_ids % SAMPLES) * (2.0 * math.pi / SAMPLES)
    return np.where(part_ids % 2 == 0, np.cos(phase), np.sin(phase))


def bf16_pieces(table):
    rest = table
    pieces = []
    for _ in range(3):
        piece = rest.astype(ml_dtypes.bfloat16)
        pieces.append(piece)
        rest = rest - piece.astype(np.float64)
    return np.concatenate(pieces, axis=-1)


def across(array, core_step, space_step):
    cores, shards = lax.axis_size("core"), lax.axis_size("space")
    pairs = [
        (c * shards + s, (c + core_step) % cores * shards + (s + space_step) % shards)
        for c in range(cores)
        for s in range(shards)
    ]
    return lax.ppermute(array, ("core", "space"), pairs)


def from_neighbours(array, tile):
    if lax.axis_size("space") == 2:
        other = across(array, 1, 1)
        return other[:, -tile:], other[:, :tile]
    return across(array[:, -tile:], 1, 1), across(array[:, :tile], 1, -1)


def fetch_kernel(*refs):
    count = (len(refs) - 1) // 2
    sources, targets, sems = refs[:count], refs[count : 2 * count], refs[-1]
    rank = lax.axis_index(GROUP)
    sources = (sources[0].at[: targets[0].shape[0]], sources[1].at[rank]) + sources[2:]
    copies = [
        pltpu.make_async_copy(source, target, sems.at[i])
        for i, (source, target) in enumerate(zip(sources, targets))
    ]
    for copy in copies:
        copy.start()
    for copy in copies:
        copy.wait()


def time_samples(pieces, rows):
    stacked = jnp.concatenate([rows] * 3, axis=0)
    samples = jnp.dot(pieces, stacked, preferred_element_type=jnp.float32)
    high = samples.astype(jnp.bfloat16)
    low = (samples - high.astype(jnp.float32)).astype(jnp.bfloat16)
    return jnp.concatenate([high, low], axis=0)


def weighted(projected, blocks):
    return lax.dot_general(
        projected.astype(jnp.bfloat16),
        blocks,
        (((1,), (1,)), ((), ())),
        preferred_element_type=jnp.float32,
    )


def field_kernel(
    window,
    first_curl,
    table,
    pieces,
    pattern_in,
    region_in,
    law_in,
    curl_hbm,
    projected,
    halo,
    later_curl,
    pattern,
    region_ids,
    law,
    outer,
    timed,
    densities,
    edge_sums,
    small_sems,
    curl_sems,
):
    tile_count, links, tile, comps = curl_hbm.shape
    early = first_curl.shape[0]
    parts_here = halo.shape[0]
    fetched = [(pattern_in, pattern), (region_in, region_ids), (law_in, law)]
    small = [
        pltpu.make_async_copy(src, dst, small_sems.at[i]) for i, (src, dst) in enumerate(fetched)
    ]
    later = {
        elem: pltpu.make_async_copy(
            curl_hbm.at[elem : min(elem + CHUNK, tile_count)],
            later_curl.at[elem - early : min(elem + CHUNK, tile_count) - early],
            curl_sems.at[(elem - early) // CHUNK],
        )
        for elem in range(early, tile_count, CHUNK)
    }
    for copy in small + list(later.values()):
        copy.start()
    edge_sums[...] = jnp.zeros_like(edge_sums)
    own, outer_tiles = pieces[0], pieces[1]
    timed[:, tile:-tile] = time_samples(own, window[:, tile:-tile])
    timed[:, :tile] = time_samples(outer_tiles, window[:, :tile])
    timed[:, -tile:] = time_samples(outer_tiles, window[:, -tile:])
    columns = [
        jnp.broadcast_to(table[:, part : part + 1], (HALF, tile)) for part in range(parts_here)
    ]
    for copy in small:
        copy.wait()
    places = [[pattern[link, elem] for link in range(links)] for elem in range(tile_count)]
    count = jnp.int32(0)

    def blocks(elem):
        curl = first_curl[elem] if elem < early else later_curl[elem - early]
        return curl.reshape(links * tile, comps)

    def find_density(elem):
        picked = jnp.concatenate(
            [timed[:, pl.ds(pl.multiple_of(at * tile, tile), tile)] for at in places[elem]], axis=1
        )
        split = jnp.dot(picked, blocks(elem), preferred_element_type=jnp.float32)
        densities[elem] = split[:HALF] + split[HALF:]

    def project(elem):
        density = densities[elem]
        comp = [density[:, c * tile : (c + 1) * tile] for c in range(comps // tile)]
        square = comp[0] * comp[0]
        for c in comp[1:]:
            square = square + c * c
        region = region_ids[elem]
        reluct = law[0, region] + law[2, region] * square / (square + law[1, region])
        field = [reluct * c for c in comp]
        rows = [
            jnp.concatenate([jnp.sum(column * f, axis=0, keepdims=True) for f in field], axis=1)
            for column in columns
        ]
        projected[elem] = jnp.concatenate(rows, axis=0) * (4.0 / SAMPLES)

    for turn in range(tile_count + 1):
        if turn < tile_count:
            if turn in later:
                later[turn].wait()
            find_density(turn)
            for link, at in enumerate(places[turn]):
                outer[count] = turn * links + link
                count += jnp.where((at == 0) | (at == tile_count + 1), 1, 0)
        if turn:
            project(turn - 1)

    def add_outer(turn, carry):
        listed, sides, rows, curls = [], [], [], []
        for slot in range(LISTED):
            spot = turn * LISTED + slot
            code = jnp.where(spot < count, outer[jnp.minimum(spot, jnp.maximum(count - 1, 0))], 0)
            elem, link = code // links, code % links
            curls.append(
                jnp.where(
                    elem < early,
                    first_curl[jnp.minimum(elem, early - 1), link],
                    later_curl[jnp.maximum(elem - early, 0), link],
                )
            )
            rows.append(projected[elem])
            sides.append(jnp.where(pattern[link, elem] == 0, 0, 1))
            listed.append(spot < count)
        contrib = weighted(jnp.concatenate(rows, axis=0), jnp.concatenate(curls, axis=0))
        for slot in range(LISTED):
            block = contrib[
                slot * parts_here : (slot + 1) * parts_here, slot * tile : (slot + 1) * tile
            ]
            edge_sums[slot, sides[slot]] += jnp.where(listed[slot], block, 0.0)
        return carry

    add_outer(0, 0)
    lax.fori_loop(1, (count + LISTED - 1) // LISTED, add_outer, 0)
    total = edge_sums[0]
    for slot in range(1, LISTED):
        total = total + edge_sums[slot]
    halo[:, :tile] = total[0]
    halo[:, tile:] = total[1]


def sum_kernel(
    projected,
    first_curl,
    later_curl,
    source,
    pattern_in,
    out,
    pattern,
    small_sem,
    *sums,
):
    links, tile, comps = first_curl.shape[1:]
    early = first_curl.shape[0]
    tile_count = early + later_curl.shape[0]
    small = pltpu.make_async_copy(pattern_in, pattern, small_sem)
    small.start()
    for total in sums:
        total[...] = jnp.zeros_like(total)

    def contribution(elem):
        curl = first_curl[elem] if elem < early else later_curl[elem - early]
        return weighted(projected[elem], curl.reshape(links * tile, comps))

    ahead = [contribution(elem) for elem in range(AHEAD)]
    small.wait()
    for elem in range(tile_count):
        contrib = ahead[elem] if elem < AHEAD else contribution(elem)
        for link in range(links):
            sums[link][pattern[link, elem]] += contrib[:, link * tile : (link + 1) * tile]
    for w in range(tile_count):
        at = slice(w * tile, (w + 1) * tile)
        total = sums[0][w + 1]
        for other in sums[1:]:
            total = total + other[w + 1]
        out[:, at] = total - source[:, at]


def halo_kernel(own, from_right, from_left, out):
    tile = from_left.shape[1] // 2
    out[...] = own[...]
    out[:, :tile] += from_left[:, tile:]
    out[:, -tile:] += from_right[:, :tile]


def per_device(coeffs, curl_tiles, pattern, region_ids, material_law, source):
    parts_here = coeffs.shape[0]
    tile_count, links, tile, comps = curl_tiles.shape
    chips, cores, samp = (lax.axis_size(axis) for axis in GROUP)
    group_size = chips * cores * samp
    parts = parts_here * group_size
    table = half_table(parts)
    before = np.roll(np.arange(parts).reshape(chips, cores, -1), 1, axis=1).reshape(-1)
    pieces = jnp.asarray(np.stack([bf16_pieces(table), bf16_pieces(table[:, before])]))
    own_columns = jnp.asarray(
        table.reshape(HALF, group_size, parts_here).transpose(1, 0, 2).astype(np.float32)
    )
    vmem, hbm = pl.BlockSpec(memory_space=pltpu.VMEM), pl.BlockSpec(memory_space=pltpu.HBM)

    def in_vmem(array):
        return pltpu.with_memory_space_constraint(array, pltpu.VMEM)

    def in_hbm(array):
        return pltpu.with_memory_space_constraint(array, pltpu.HBM)

    early = tile_count // 2
    operands = [
        curl_tiles,
        own_columns,
        coeffs,
        pieces,
        source,
        pattern.T,
        region_ids,
        material_law,
    ]
    shapes = [
        (early,) + curl_tiles.shape[1:],
        own_columns.shape[1:],
    ] + [operand.shape for operand in operands[2:]]
    fetched = pl.pallas_call(
        fetch_kernel,
        out_shape=[pltpu.VMEM(shape, o.dtype) for shape, o in zip(shapes, operands)],
        in_specs=[hbm] * len(operands),
        out_specs=[vmem] * len(operands),
        scratch_shapes=[pltpu.SemaphoreType.DMA((len(operands),))],
        compiler_params=pltpu.CompilerParams(vmem_limit_bytes=16 * MIB),
        cost_estimate=pl.CostEstimate(
            flops=0, bytes_accessed=4 * early * links * tile * comps, transcendentals=0
        ),
        name="fetch_operands",
    )(*[in_hbm(operand) for operand in operands])
    first_curl, columns_here, coeffs_here, pieces_here, source_here, *others = fetched
    pattern_here = others[0]

    left, right = from_neighbours(coeffs, tile)
    block = jnp.concatenate([left, coeffs_here, right], axis=1)
    copies = jnp.broadcast_to(block[None], (group_size,) + block.shape)
    window = lax.all_to_all(copies, GROUP, 0, 0).reshape(parts, block.shape[1])
    pattern_words = pltpu.SMEM((links, tile_count), jnp.int32)
    projected, halo, later_curl = pl.pallas_call(
        field_kernel,
        out_shape=(
            pltpu.VMEM((tile_count, parts_here, comps), jnp.float32),
            pltpu.VMEM((parts_here, 2 * tile), jnp.float32),
            pltpu.VMEM((tile_count - early,) + curl_tiles.shape[1:], curl_tiles.dtype),
        ),
        in_specs=[vmem] * 7 + [hbm],
        out_specs=(vmem, vmem, vmem),
        scratch_shapes=[
            pattern_words,
            pltpu.SMEM(region_ids.shape, jnp.int32),
            pltpu.SMEM(material_law.shape, jnp.float32),
            pltpu.SMEM((links * tile_count + 1,), jnp.int32),
            pltpu.VMEM((SAMPLES, (tile_count + 2) * tile), jnp.bfloat16),
            pltpu.VMEM((tile_count, HALF, comps), jnp.float32),
            pltpu.VMEM((LISTED, 2, parts_here, tile), jnp.float32),
            pltpu.SemaphoreType.DMA((3,)),
            pltpu.SemaphoreType.DMA((pl.cdiv(tile_count - early, CHUNK),)),
        ],
        compiler_params=pltpu.CompilerParams(vmem_limit_bytes=32 * MIB),
        cost_estimate=pl.CostEstimate(
            flops=2 * SAMPLES * tile_count * links * tile * comps,
            bytes_accessed=2 * curl_tiles.size,
            transcendentals=0,
        ),
        name="shard_fields",
    )(
        in_vmem(window),
        *[in_vmem(array) for array in (first_curl, columns_here, pieces_here, *others)],
        in_hbm(curl_tiles),
    )
    if lax.axis_size("space") == 2:
        beside = [across(halo, 0, 1)] * 2
    else:
        beside = [across(halo, 0, -1), across(halo, 0, 1)]
    own = pl.pallas_call(
        sum_kernel,
        out_shape=pltpu.VMEM(source.shape, jnp.float32),
        in_specs=[vmem] * 5,
        out_specs=vmem,
        scratch_shapes=[
            pattern_words,
            pltpu.SemaphoreType.DMA,
        ]
        + [pltpu.VMEM((tile_count + 2, parts_here, tile), jnp.float32)] * links,
        compiler_params=pltpu.CompilerParams(vmem_limit_bytes=32 * MIB),
        cost_estimate=pl.CostEstimate(
            flops=2 * SAMPLES * tile_count * links * tile * comps,
            bytes_accessed=2 * curl_tiles.size,
            transcendentals=0,
        ),
        name="shard_sums",
    )(
        *[in_vmem(a) for a in (projected, first_curl, later_curl, source_here, pattern_here)],
    )
    return pl.pallas_call(
        halo_kernel,
        out_shape=jax.ShapeDtypeStruct(source.shape, jnp.float32),
        in_specs=[vmem] * 3,
        out_specs=vmem,
        compiler_params=pltpu.CompilerParams(vmem_limit_bytes=16 * MIB),
        name="halo_sum",
    )(in_vmem(own), *beside)


def solution(mesh):
    at = mesh.axis_names.index("harm")
    harm = mesh.shape["harm"]
    cores = 2 if harm % 2 == 0 else 1
    sizes = mesh.devices.shape
    split = jax.sharding.Mesh(
        mesh.devices.reshape(sizes[:at] + (harm // cores, cores) + sizes[at + 1 :]),
        mesh.axis_names[:at] + ("chip", "core") + mesh.axis_names[at + 1 :],
    )
    placed = (
        P(GROUP, "space"),
        P("space", None, None, None),
        P("space", None),
        P("space"),
        P(),
        P(GROUP, "space"),
    )
    return jax.shard_map(
        per_device,
        mesh=split,
        in_specs=placed,
        out_specs=P(GROUP, "space"),
        check_vma=False,
    )
```
